32 devices in a mesh: dp: 4 (over z), ctx: 4 (over y, x), exp: 2 (over core).
Axes of the slice: x: 2, y: 2, z: 4, core: 2. Of those that a mesh axis runs over, the one named last changes fastest.
Arguments:
- tokens: bfloat16 [8, 1024, 2048], P(('dp', 'exp'), 'ctx'), may hold values from -6 to 6
- attention_gain: float32 [2048], P(('dp', 'ctx', 'exp')), may hold values from 0.5 to 1.5
- query_weight: float32 [2048, 4096], P(('dp', 'ctx', 'exp')), may hold values from -0.125 to 0.125
- key_weight: float32 [2048, 512], P(('dp', 'ctx', 'exp')), may hold values from -0.125 to 0.125
- value_weight: float32 [2048, 512], P(('dp', 'ctx', 'exp')), may hold values from -0.125 to 0.125
- query_gain: float32 [128], P(('dp', 'ctx', 'exp')), may hold values from 0.5 to 1.5
- key_gain: float32 [128], P(('dp', 'ctx', 'exp')), may hold values from 0.5 to 1.5
- output_weight: float32 [4096, 2048], P(('dp', 'ctx', 'exp')), may hold values from -0.5 to 0.5
- mixture_gain: float32 [2048], P(('dp', 'ctx', 'exp')), may hold values from 0.5 to 1.5
- router_weight: float32 [2048, 32], P(('dp', 'ctx', 'exp')), may hold values from -0.0625 to 0.0625
- gate_weight: bfloat16 [32, 2048, 768], P(('dp', 'ctx', 'exp')), may hold values from -0.125 to 0.125
- up_weight: bfloat16 [32, 2048, 768], P(('dp', 'ctx', 'exp')), may hold values from -0.125 to 0.125
- down_weight: bfloat16 [32, 768, 2048], P(('dp', 'ctx', 'exp')), may hold values from -0.625 to 0.625
- routes: int32 [8, 1024, 8], P(('dp', 'exp'), 'ctx'), may hold values from 0 to 31, all different within a row; in each aligned block of 256 rows (0 to 255, 256 to 511, ..., all dimensions but the last counted through in order) at most 72 rows name the same one
- bounds: int32 [8, 2], P(('dp', 'exp')), may hold values from 1 to 1023, as said below
- cotangent: bfloat16 [8, 1024, 2048], P(('dp', 'exp'), 'ctx'), may hold values from -6 to 6
Outputs:
- output: bfloat16 [8, 1024, 2048], P(('dp', 'exp'), 'ctx')
- tokens_grad: bfloat16 [8, 1024, 2048], P(('dp', 'exp'), 'ctx')
- attention_gain_grad: float32 [2048], P(('dp', 'ctx', 'exp'))
- query_weight_grad: float32 [2048, 4096], P(('dp', 'ctx', 'exp'))
- key_weight_grad: float32 [2048, 512], P(('dp', 'ctx', 'exp'))
- value_weight_grad: float32 [2048, 512], P(('dp', 'ctx', 'exp'))
- query_gain_grad: float32 [128], P(('dp', 'ctx', 'exp'))
- key_gain_grad: float32 [128], P(('dp', 'ctx', 'exp'))
- output_weight_grad: float32 [4096, 2048], P(('dp', 'ctx', 'exp'))
- mixture_gain_grad: float32 [2048], P(('dp', 'ctx', 'exp'))
- router_weight_grad: float32 [2048, 32], P(('dp', 'ctx', 'exp'))
- gate_weight_grad: float32 [32, 2048, 768], P(('dp', 'ctx', 'exp'))
- up_weight_grad: float32 [32, 2048, 768], P(('dp', 'ctx', 'exp'))
- down_weight_grad: float32 [32, 768, 2048], P(('dp', 'ctx', 'exp'))
The draws below stay inside these ranges and needn't reach their ends.
Inputs may be any that keep to these rules, and one draw needn't show every extreme that they name: `routes`: each row names 8 different experts. Among the 256 tokens of one device no expert is named more than 72 times, and in some devices' tokens some expert exactly 72 times. A sequence's documents are [0, bounds[s, 0]), [bounds[s, 0], bounds[s, 1]) and [bounds[s, 1], 1024); bounds[s, 0] is at most 128 and bounds[s, 1] at least 896.
All inputs are finite; a program needn't handle non-finite values.
Results may differ from the reference program's by a relative error of at most 0.02.
Values may be sent and summed in bfloat16 or wider, within the bound.
A program may use at most 448 MiB of HBM per device.

```python
import math
from functools import partial
import jax
import jax.numpy as jnp
import numpy as np
from jax import lax

D = 2048
HEADS = 32
KV_HEADS = 4
HD = 128
FF = 768
TOPK = 8
TOK = 256
EXPERTS = 32
SEQ_LEN = 1024
SEQS = 8
CAP = 72
N_CTX = 4


def draw_bounds(key, part):
    key = jax.random.fold_in(key, 7)
    first_key, second_key, chosen_key = jax.random.split(key, 3)
    first = 1 + jax.random.randint(first_key, (SEQS,), 0, TOK // 2)
    second = SEQ_LEN - 1 - jax.random.randint(second_key, (SEQS,), 0, TOK // 2)
    chosen = jax.random.randint(chosen_key, (), 0, SEQS)
    sequence = jnp.arange(SEQS)
    first = jnp.where(sequence == chosen, 1, first)
    second = jnp.where(sequence == chosen, SEQ_LEN - 1, second)
    return jnp.stack([first, second], axis=1).astype(jnp.int32)


def level_of(rng, extent, pieces, low, largest):
    level, own = 1.0, jax.random.fold_in(rng, 6)
    for position, blocks in pieces:
        steps = jnp.exp(jax.random.uniform(jax.random.fold_in(own, position), (blocks,), jnp.float32, low / len(pieces), largest / len(pieces)))
        level = level * jnp.repeat(steps, extent[position] // blocks).reshape([-1 if axis == position else 1 for axis in range(len(extent))])
    return level


def assign_block(rng, own, number, rows, count, top, limit, lean):
    order = jax.random.permutation(rng, count)
    crowded, common = load_shares(count, rows * top, limit, lean, True), load_shares(count, rows * top, limit, lean, False)
    places = jnp.arange(count)

    def named(sizes, offset_by):
        used = int((sizes > 0).sum())
        fixed = max(1, used // 4)
        shifted = fixed + (places - fixed + offset_by * (used - fixed)) % max(1, count - fixed)
        return jnp.zeros((count,), jnp.int32).at[order[jnp.where(places < fixed, places, shifted)]].set(jnp.asarray(sizes, jnp.int32))

    sizes = jnp.where(number % 4 == 0, named(crowded, number // 4), named(common, number - number // 4 - 1))
    mixed = jax.random.permutation(jax.random.fold_in(own, 3), count)
    source_of, sink = mixed[0:count // 2 * 2:2], mixed[1:count // 2 * 2:2]
    room = jnp.minimum(sizes[source_of] - 1, limit - sizes[sink]) // 2
    room = jnp.where((source_of == order[0]) | (sink == order[0]) | (sizes[sink] == 0), 0, jnp.maximum(room, 0))
    shifted = jax.random.randint(jax.random.fold_in(own, 4), (count // 2,), 0, 1 << 20) % (room + 1)
    sizes = sizes.at[source_of].add(-shifted).at[sink].add(shifted)
    labels = jnp.searchsorted(jnp.cumsum(sizes), jnp.arange(rows * top), side="right").astype(jnp.int32)
    listing = labels.reshape(top, rows).T
    listing = listing[jax.random.permutation(jax.random.fold_in(own, 1), rows)]
    offset_by = jax.random.randint(jax.random.fold_in(own, 2), (rows, 1), 0, top)
    return jnp.take_along_axis(listing, (jnp.arange(top)[None, :] + offset_by) % top, axis=1)


def load_shares(number_of, total, limit, slope, full):
    portions = [(1 << 20) // math.isqrt(rank ** slope) + 1 for rank in range(1, number_of + 1)]
    largest = limit if full else min(limit, max(-(-total // number_of), total * portions[0] // sum(portions)))
    least = 1 if total - largest >= number_of - 1 else 0
    given, rest = [largest] + [least] * (number_of - 1), total - largest - least * (number_of - 1)
    while rest > 0:
        movable = [i for i in range(1, number_of) if given[i] < largest] or [i for i in range(1, number_of) if given[i] < limit]
        mass, budget = sum([portions[i] for i in movable]), rest
        for i in movable:
            more = min(limit - given[i], max(1, budget * portions[i] // mass), rest)
            given[i] = given[i] + more
            rest = rest - more
    return np.array(given)


def centred(rng, shape, scale, most, cuts=(), held_as=jnp.bfloat16):
    level = level_of(rng, shape, cuts, -0.22, 0.18) if cuts else 1.0
    values = jax.random.normal(rng, shape, jnp.float32) * scale * level
    return jnp.minimum(jnp.maximum(values, -most), most).astype(held_as)


def setup_inputs(seed: int = 0) -> dict:
    key_list = jax.random.split(jax.random.key(seed), 17)
    tokens = centred(key_list[0], (SEQS, SEQ_LEN, D), 1.0, 6.0, ((0, 8), (1, 4)))
    attention_gain = jnp.clip(1.0 + 0.1 * jax.random.normal(key_list[1], (D,), jnp.float32), 0.5, 1.5)
    query_weight = centred(key_list[2], (D, HEADS * HD), D ** -0.5, 0.125, ((0, 32),), jnp.float32)
    key_weight = centred(key_list[3], (D, KV_HEADS * HD), D ** -0.5, 0.125, ((0, 32),), jnp.float32)
    value_weight = centred(key_list[4], (D, KV_HEADS * HD), D ** -0.5, 0.125, ((0, 32),), jnp.float32)
    query_gain = jnp.clip(1.0 + 0.1 * jax.random.normal(key_list[5], (HD,), jnp.float32), 0.5, 1.5)
    key_gain = jnp.clip(1.0 + 0.1 * jax.random.normal(key_list[6], (HD,), jnp.float32), 0.5, 1.5)
    output_weight = centred(key_list[7], (HEADS * HD, D), (HEADS * HD // 32) ** -0.5, 0.5, ((0, 32),), jnp.float32)
    mixture_gain = jnp.clip(1.0 + 0.1 * jax.random.normal(key_list[8], (D,), jnp.float32), 0.5, 1.5)
    router_weight = centred(key_list[9], (D, EXPERTS), (4 * D) ** -0.5, 0.0625, ((0, 32),), jnp.float32)
    gate_weight = centred(key_list[10], (EXPERTS, D, FF), D ** -0.5, 0.125, ((0, 32),))
    up_weight = centred(key_list[11], (EXPERTS, D, FF), D ** -0.5, 0.125, ((0, 32),))
    down_weight = centred(key_list[12], (EXPERTS, FF, D), (FF // 8) ** -0.5, 0.625, ((0, 32),))
    routes_keys = jax.random.split(jax.random.fold_in(key_list[13], 1), SEQS * SEQ_LEN // TOK)
    routes_turns = jax.random.permutation(jax.random.fold_in(key_list[13], 3), SEQS * SEQ_LEN // TOK)
    routes = jax.vmap(lambda own, number: assign_block(jax.random.fold_in(key_list[13], 2), own, number, TOK, EXPERTS, TOPK, CAP, 1))(routes_keys, routes_turns).reshape((SEQS, SEQ_LEN, TOPK))
    bounds = draw_bounds(jax.random.fold_in(key_list[16], 71), 0)
    cotangent = centred(key_list[15], (SEQS, SEQ_LEN, D), 1.0, 6.0, ((0, 8), (1, 4)))
    return dict(tokens=tokens, attention_gain=attention_gain, query_weight=query_weight, key_weight=key_weight, value_weight=value_weight, query_gain=query_gain, key_gain=key_gain, output_weight=output_weight, mixture_gain=mixture_gain, router_weight=router_weight, gate_weight=gate_weight, up_weight=up_weight, down_weight=down_weight, routes=routes, bounds=bounds, cotangent=cotangent)


@jax.custom_vjp
def low(v):
    return lax.optimization_barrier(v.astype(jnp.bfloat16)).astype(jnp.float32)

@jax.custom_vjp
def low_back(v):
    return v

def low_keep(v):
    return (low(v), None)

def low_pass(kept, grad):
    return (grad,)

def back_keep(v):
    return (v, None)

def back_low(kept, grad):
    return (low(grad),)
low.defvjp(low_keep, low_pass)
low_back.defvjp(back_keep, back_low)
eps_norm = 1e-06
rope_base = 1000000.0
masked_score = -1e+30

def dot_high(left, right):
    return jnp.dot(left, right, precision=lax.Precision.HIGHEST, preferred_element_type=jnp.float32)

def rms_scale(values, gain):
    return values * lax.rsqrt(lax.optimization_barrier(jnp.mean(values * values, axis=-1, keepdims=True)) + eps_norm) * gain

def rotate(values, cosine, sine):
    half = values.shape[-1] // 2
    turned = jnp.concatenate([-values[..., half:], values[..., :half]], axis=-1)
    return values * cosine + turned * sine

def rope_tables(positions, width):
    exponents = jnp.arange(width // 2, dtype=jnp.float32) * (2.0 / width)
    frequency = rope_base ** (-exponents)
    angles = positions.astype(jnp.float32)[:, None] * frequency[None, :]
    angles = jnp.concatenate([angles, angles], axis=-1)
    return (jnp.cos(angles), jnp.sin(angles))

def build_tables(flat, most_rows):
    total = flat.shape[0]
    order = jnp.argsort(flat, stable=True).astype(jnp.int32)
    counts = lax.optimization_barrier(jnp.sum((flat[:, None] == jnp.arange(EXPERTS, dtype=jnp.int32)[None, :]).astype(jnp.int32), axis=0))
    offsets = jnp.cumsum(counts) - counts
    within = jnp.arange(most_rows, dtype=jnp.int32)
    picked = jnp.clip(offsets[:, None] + within[None, :], 0, total - 1)
    slot_rows = order[picked] // TOPK
    slot_valid = within[None, :] < counts[:, None]
    ranks = jnp.zeros((total,), jnp.int32).at[order].set(jnp.arange(total, dtype=jnp.int32))
    slot_of = flat * most_rows + ranks - offsets[flat]
    return (slot_rows, slot_valid, slot_of)

def attend_sequence(items):
    queries, keys, values, ends = items
    length = queries.shape[0]
    positions = jnp.arange(length, dtype=jnp.int32)
    document = (positions >= ends[0]).astype(jnp.int32) + (positions >= ends[1]).astype(jnp.int32)
    allowed = (positions[None, :] <= positions[:, None]) & (document[None, :] == document[:, None])
    grouped = queries.reshape(length, keys.shape[1], -1, queries.shape[2])
    scores = jnp.einsum('tkgd,skd->kgts', grouped, keys, precision=lax.Precision.HIGHEST) * queries.shape[2] ** (-0.5)
    scores = low_back(scores)
    scores = jnp.where(allowed[None, None], scores, masked_score)
    shares = low(jax.nn.softmax(scores, axis=-1))
    attended = jnp.einsum('kgts,skd->tkgd', shares, values, precision=lax.Precision.HIGHEST)
    return attended.reshape(queries.shape)

def run_expert(mixed_low, items):
    gate_matrix, up_matrix, down_matrix, rows_index, valid = items
    inputs = jnp.where(valid[:, None], low_back(mixed_low[rows_index]), 0.0)
    gate_pre = low_back(dot_high(inputs, gate_matrix))
    up_pre = low_back(dot_high(inputs, up_matrix))
    activated = low(jax.nn.silu(gate_pre) * up_pre)
    return low(low_back(dot_high(activated, down_matrix)))

def layer_block(weights, items):
    first_gain, query_matrix, key_matrix, value_matrix, query_scale, key_scale, output_matrix, second_gain, router_matrix, gate_all, up_all, down_all = weights
    inputs, block_routes, block_bounds, slot_rows, slot_valid, slot_of = items
    seqs_here, length, width = inputs.shape
    flat_rows = seqs_here * length
    flat_in = inputs.reshape(flat_rows, width)
    hidden = low(rms_scale(flat_in, low(first_gain)))
    positions = jnp.tile(jnp.arange(length, dtype=jnp.int32), seqs_here)
    cosine, sine = rope_tables(positions, HD)
    cosine = cosine[:, None, :]
    sine = sine[:, None, :]
    query_raw = low_back(dot_high(hidden, low(query_matrix))).reshape(flat_rows, HEADS, HD)
    key_raw = low_back(dot_high(hidden, low(key_matrix))).reshape(flat_rows, KV_HEADS, HD)
    value_raw = low_back(dot_high(hidden, low(value_matrix))).reshape(flat_rows, KV_HEADS, HD)
    queries = low(rotate(rms_scale(query_raw, low(query_scale)), cosine, sine))
    keys = low(rotate(rms_scale(key_raw, low(key_scale)), cosine, sine))
    values = low(value_raw)
    attended = lax.map(jax.checkpoint(attend_sequence), (queries.reshape(seqs_here, length, HEADS, HD), keys.reshape(seqs_here, length, KV_HEADS, HD), values.reshape(seqs_here, length, KV_HEADS, HD), block_bounds))
    attended = low(low_back(attended.reshape(flat_rows, HEADS * HD)))
    middle = flat_in + low_back(dot_high(attended, low(output_matrix)))
    mixed_low = low(rms_scale(middle, low(second_gain)))
    logits = low_back(dot_high(mixed_low, low(router_matrix)))
    selected = block_routes.reshape(flat_rows, TOPK)
    gates = jax.nn.softmax(jnp.take_along_axis(logits, selected, axis=1), axis=-1)
    expert_rows = lax.map(jax.checkpoint(partial(run_expert, mixed_low)), (gate_all, up_all, down_all, slot_rows, slot_valid))
    picked = expert_rows.reshape(-1, width)[slot_of].reshape(flat_rows, TOPK, width)
    result = middle + lax.optimization_barrier(jnp.sum(gates[:, :, None] * picked, axis=1))
    return result.reshape(seqs_here, length, width)

def reference(tokens, attention_gain, query_weight, key_weight, value_weight, query_gain, key_gain, output_weight, mixture_gain, router_weight, gate_weight, up_weight, down_weight, routes, bounds, cotangent):
    per_block = max(1, min(SEQS, 4096 // SEQ_LEN))
    while SEQS % per_block != 0:
        per_block = per_block - 1
    blocks = SEQS // per_block
    block_len = per_block * SEQ_LEN
    most_rows = per_block * N_CTX * CAP
    slot_rows, slot_valid, slot_of = jax.vmap(partial(build_tables, most_rows=most_rows))(routes.reshape(blocks, block_len * TOPK))
    block_routes = routes.reshape(blocks, block_len, TOPK)
    block_bounds = bounds.reshape(blocks, per_block, 2)

    def layer(inputs, *weights):
        items = (inputs.reshape(blocks, per_block, SEQ_LEN, D), block_routes, block_bounds, slot_rows, slot_valid, slot_of)
        result = lax.map(jax.checkpoint(partial(layer_block, weights)), items)
        return result.reshape(SEQS, SEQ_LEN, D)
    output, pullback = jax.vjp(layer, tokens.astype(jnp.float32), attention_gain, query_weight, key_weight, value_weight, query_gain, key_gain, output_weight, mixture_gain, router_weight, gate_weight.astype(jnp.float32), up_weight.astype(jnp.float32), down_weight.astype(jnp.float32))
    grads = pullback(cotangent.astype(jnp.float32))
    return (output.astype(jnp.bfloat16), grads[0].astype(jnp.bfloat16), grads[1], grads[2], grads[3], grads[4], grads[5], grads[6], grads[7], grads[8], grads[9], grads[10], grads[11], grads[12])
```

```python
import jax
import jax.numpy as jnp
from jax import lax
from jax.sharding import PartitionSpec as P

eps_norm = 1e-06
rope_base = 1000000.0
masked_score = -1e30
ALL = ("dp", "ctx", "exp")
PLANE = ("ctx", "exp")


def rope_tables(positions, width):
    exponents = jnp.arange(width // 2, dtype=jnp.float32) * (2.0 / width)
    frequency = rope_base ** (-exponents)
    angles = positions.astype(jnp.float32)[:, None] * frequency[None, :]
    angles = jnp.concatenate([angles, angles], axis=-1)
    return (jnp.cos(angles), jnp.sin(angles))


def turn_ahead(values):
    half = values.shape[-1] // 2
    return jnp.concatenate([-values[..., half:], values[..., :half]], axis=-1)


def turn_behind(values):
    half = values.shape[-1] // 2
    return jnp.concatenate([values[..., half:], -values[..., :half]], axis=-1)


def norm_rope(raw, gain, cosine, sine):
    inverse = lax.rsqrt(jnp.mean(raw * raw, axis=-1, keepdims=True) + eps_norm)
    normed = raw * inverse
    scaled = normed * gain
    return (scaled * cosine + turn_ahead(scaled) * sine, normed, inverse)


def norm_rope_back(grad, normed, inverse, gain, cosine, sine):
    scaled_grad = grad * cosine + turn_behind(grad * sine)
    gain_grad = jnp.sum(scaled_grad * normed, axis=(0, 1))
    inner = scaled_grad * gain
    return (
        inverse * (inner - normed * jnp.mean(inner * normed, axis=-1, keepdims=True)),
        gain_grad,
    )


def norm_back(grad, normed, inverse, gain):
    gain_grad = jnp.sum(grad * normed, axis=0)
    scaled = grad * gain
    return (
        inverse * (scaled - normed * jnp.mean(scaled * normed, axis=-1, keepdims=True)),
        gain_grad,
    )


def line_gather(block, axis):
    n = lax.axis_size(axis)
    me = lax.axis_index(axis)
    before, after = [], []
    up = down = block
    for step in range(1, n):
        up = lax.ppermute(up, axis, [(i, i + 1) for i in range(step - 1, n - 1)])
        down = lax.ppermute(down, axis, [(i, i - 1) for i in range(1, n - step + 1)])
        before.insert(0, up)
        after.append(down)
    return lax.dynamic_slice_in_dim(jnp.stack(before + [block] + after), n - 1 - me, n, 0)


def line_scatter(parts, axis):
    n = lax.axis_size(axis)
    me = lax.axis_index(axis)

    def part(i):
        return lax.dynamic_index_in_dim(parts, jnp.clip(i, 0, n - 1), 0, keepdims=False)

    up = down = None
    for step in range(1, n):
        send_up, send_down = part(me + n - step), part(me - n + step)
        if up is not None:
            send_up, send_down = add_low(send_up, up), add_low(send_down, down)
        up = lax.ppermute(send_up, axis, [(i, i + 1) for i in range(step)])
        down = lax.ppermute(send_down, axis, [(i, i - 1) for i in range(n - step, n)])
    return part(me).astype(jnp.float32) + up.astype(jnp.float32) + down.astype(jnp.float32)


def add_low(left, right):
    return (left.astype(jnp.float32) + right.astype(jnp.float32)).astype(left.dtype)


def flip(block, axis, bit):
    return lax.ppermute(block, axis, [(i, i ^ bit) for i in range(lax.axis_size(axis))])


def square_gather(block, axis):
    if lax.axis_size(axis) != 4:
        return lax.all_gather(block, axis, axis=0, tiled=False)
    half = block.shape[-1] // 2
    me = lax.axis_index(axis)
    by_x, by_y = flip(block, axis, 1), flip(block, axis, 2)
    far = jnp.concatenate(
        [flip(by_x[..., :half], axis, 2), flip(by_y[..., half:], axis, 1)], axis=-1
    )
    whole = jnp.zeros((4,) + block.shape, block.dtype)
    for bits, piece in enumerate((block, by_x, by_y, far)):
        whole = lax.dynamic_update_index_in_dim(whole, piece, me ^ bits, 0)
    return whole


def square_scatter(parts, axis):
    if lax.axis_size(axis) != 4:
        return lax.psum_scatter(parts, axis, scatter_dimension=0, tiled=False).astype(jnp.float32)
    half = parts.shape[-1] // 2
    me = lax.axis_index(axis)
    own, to_x, to_y, far = [
        lax.dynamic_index_in_dim(parts, me ^ bits, 0, keepdims=False) for bits in range(4)
    ]
    first = flip(jnp.stack([to_x[..., :half], far[..., :half]]), axis, 1)
    second = flip(jnp.stack([to_y[..., half:], far[..., half:]]), axis, 2)
    later_first = flip(add_low(to_y[..., :half], first[1]), axis, 2)
    later_second = flip(add_low(to_x[..., half:], second[1]), axis, 1)
    own = own.astype(jnp.float32)
    first = own[..., :half] + first[0].astype(jnp.float32) + later_first.astype(jnp.float32)
    second = own[..., half:] + second[0].astype(jnp.float32) + later_second.astype(jnp.float32)
    return jnp.concatenate([first, second], axis=-1)


def pair_gather(block, axis):
    if lax.axis_size(axis) != 2:
        return lax.all_gather(block, axis, axis=0, tiled=False)
    other = flip(block, axis, 1)
    first = lax.axis_index(axis) == 0
    return jnp.stack([jnp.where(first, block, other), jnp.where(first, other, block)])


def pair_scatter(parts, axis):
    if lax.axis_size(axis) != 2:
        return lax.psum_scatter(parts, axis, scatter_dimension=0, tiled=False)
    first = lax.axis_index(axis) == 0
    other = flip(jnp.where(first, parts[1], parts[0]), axis, 1)
    return add_low(jnp.where(first, parts[0], parts[1]), other)


def swap(parts, axis):
    return lax.all_to_all(parts, axis, split_axis=0, concat_axis=0, tiled=True)


def shards(
    tokens,
    attention_gain,
    query_weight,
    key_weight,
    value_weight,
    query_gain,
    key_gain,
    output_weight,
    mixture_gain,
    router_weight,
    gate_weight,
    up_weight,
    down_weight,
    routes,
    bounds,
    cotangent,
):
    low, full = jnp.bfloat16, jnp.float32
    n_dp, n_ctx, n_exp = (lax.axis_size(a) for a in ALL)
    devices = n_dp * n_ctx * n_exp
    tok_count, width = tokens.shape[1], tokens.shape[2]
    seq_len = tok_count * n_ctx
    head_dim = query_gain.shape[0] * devices
    rows = query_weight.shape[0]
    heads = query_weight.shape[1] // head_dim
    kv_heads = key_weight.shape[1] // head_dim
    kv_here = kv_heads // n_ctx
    group_size = heads // kv_heads
    q_cols, kv_cols = heads * head_dim // n_ctx, kv_here * head_dim
    experts = router_weight.shape[1]
    topk = routes.shape[2]
    base_rows = tok_count * topk // experts
    capacity = base_rows + max(1, base_rows // 8)
    plane = experts // n_dp
    local_experts = gate_weight.shape[0]
    score_scale = head_dim ** (-0.5)
    dp_index = lax.axis_index("dp")

    gain_len = query_gain.shape[0]
    small = jnp.concatenate(
        [
            attention_gain[:, None],
            mixture_gain[:, None],
            jnp.pad(jnp.concatenate([query_gain, key_gain]), (0, rows - 2 * gain_len))[:, None],
            router_weight,
        ],
        axis=1,
    ).astype(low)
    small = jnp.pad(small, ((0, 0), (0, -small.shape[1] % 128)))
    extra = small.shape[1]

    def by_ctx(weight):
        return weight.astype(low).reshape(rows, n_ctx, -1).transpose(1, 0, 2)

    front = jnp.concatenate(
        [
            by_ctx(query_weight),
            by_ctx(key_weight),
            by_ctx(value_weight),
            jnp.broadcast_to(small[None], (n_ctx, rows, extra)),
        ],
        axis=2,
    )
    front = pair_gather(line_gather(swap(front, "ctx"), "dp"), "exp")
    front = front.transpose(1, 2, 0, 3, 4).reshape(width, -1)
    front_weight = front[:, : q_cols + 2 * kv_cols]
    small = front[:, q_cols + 2 * kv_cols :]
    first_gain = small[:, 0].astype(full)
    second_gain = small[:, 1].astype(full)
    head_gains = small[:, 2].reshape(devices, rows)
    query_scale = head_gains[:, :gain_len].reshape(-1).astype(full)
    key_scale = head_gains[:, gain_len : 2 * gain_len].reshape(-1).astype(full)
    router_full = small[:, 3 : 3 + experts]

    whole_tokens = square_gather(tokens[0], "ctx").reshape(seq_len, width)
    back = line_gather(output_weight.astype(low), "dp")
    back = pair_gather(swap(back, "ctx"), "exp")
    output_part = back.transpose(1, 0, 2, 3).reshape(q_cols, width)

    column_grads = line_gather(cotangent[0], "dp")
    column_routes = line_gather(routes[0], "dp")
    chosen = jnp.any(
        column_routes[:, :, :, None] == jnp.arange(experts, dtype=jnp.int32), axis=2
    )
    hot = lax.dynamic_slice_in_dim(chosen.astype(low), dp_index * plane, plane, 2)
    row_ids = jnp.arange(tok_count, dtype=jnp.int32)
    earlier = (row_ids[None, :] < row_ids[:, None]).astype(low)
    before = jnp.einsum("st,btj->bsj", earlier, hot, preferred_element_type=full)
    slots = jnp.arange(capacity, dtype=full)
    pick = (
        (before.transpose(0, 2, 1)[:, :, None, :] == slots[None, None, :, None])
        & (hot.transpose(0, 2, 1)[:, :, None, :] > 0)
    ).astype(low)

    def send_out(blocks):
        return jnp.einsum("bjrt,btd->jbrd", pick, blocks, preferred_element_type=low)

    def bring_back(sent):
        return jnp.einsum("bjrt,jbrd->btd", pick, sent, preferred_element_type=full)

    grad_rows = swap(send_out(column_grads), PLANE)

    inputs = whole_tokens.astype(full)
    first_inverse = lax.rsqrt(jnp.mean(inputs * inputs, axis=-1, keepdims=True) + eps_norm)
    hidden = ((inputs * first_inverse) * first_gain).astype(low)
    positions = jnp.arange(seq_len, dtype=jnp.int32)
    cosine, sine = rope_tables(positions, head_dim)
    cosine = cosine[:, None, :]
    sine = sine[:, None, :]
    raw = jnp.dot(hidden, front_weight, preferred_element_type=full)
    query_raw = raw[:, :q_cols].reshape(seq_len, -1, head_dim)
    key_raw = raw[:, q_cols : q_cols + kv_cols].reshape(seq_len, -1, head_dim)
    value_raw = raw[:, q_cols + kv_cols :].reshape(seq_len, -1, head_dim)
    query_rot, query_normed, query_inverse = norm_rope(query_raw, query_scale, cosine, sine)
    key_rot, key_normed, key_inverse = norm_rope(key_raw, key_scale, cosine, sine)
    query_low = query_rot.astype(low)
    key_low = key_rot.astype(low)
    value_low = value_raw.astype(low)
    first_end, second_end = bounds[0, 0], bounds[0, 1]
    document = (positions >= first_end).astype(jnp.int32) + (positions >= second_end).astype(
        jnp.int32
    )
    allowed = (positions[None, :] <= positions[:, None]) & (document[None, :] == document[:, None])
    attended_parts, lse_parts = [], []
    for g in range(kv_here):
        query_group = query_low[:, g * group_size : (g + 1) * group_size]
        scores = (
            jnp.einsum("tgd,sd->gts", query_group, key_low[:, g], preferred_element_type=full)
            * score_scale
        )
        scores = jnp.where(allowed[None], scores, masked_score)
        highest = jnp.max(scores, axis=-1, keepdims=True)
        weights = jnp.exp(scores - highest)
        totals = jnp.sum(weights, axis=-1, keepdims=True)
        shares_low = (weights / totals).astype(low)
        attended_parts.append(
            jnp.einsum("gts,sd->tgd", shares_low, value_low[:, g], preferred_element_type=full)
        )
        lse_parts.append(highest + jnp.log(totals))
    attended_low = jnp.concatenate(attended_parts, axis=1).astype(low).reshape(seq_len, q_cols)
    branch = jnp.dot(attended_low, output_part, preferred_element_type=full).astype(low)
    branch = square_scatter(branch.reshape(n_ctx, tok_count, width), "ctx")

    own = tokens[0].astype(full)
    middle = own + branch
    second_inverse = lax.rsqrt(jnp.mean(middle * middle, axis=-1, keepdims=True) + eps_norm)
    second_normed = middle * second_inverse
    mixed_low = (second_normed * second_gain).astype(low)

    column_mixed = line_gather(mixed_low, "dp")
    logits = jnp.einsum("btd,de->bte", column_mixed, router_full, preferred_element_type=full)
    logits = jnp.where(chosen, logits, masked_score)
    gates = jnp.exp(logits - jnp.max(logits, axis=-1, keepdims=True))
    gates = gates / jnp.sum(gates, axis=-1, keepdims=True)
    plane_gates = lax.dynamic_slice_in_dim(gates, dp_index * plane, plane, 2)
    own_gates = lax.dynamic_index_in_dim(gates, dp_index, 0, keepdims=False)
    slot_gates = jnp.sum(
        pick.astype(full) * plane_gates.transpose(0, 2, 1)[:, :, None, :], axis=-1
    ).transpose(1, 0, 2)
    slot_gates = swap(slot_gates, PLANE)[..., None]
    expert_in = swap(send_out(column_mixed), PLANE)

    sources = n_ctx * n_exp

    def by_expert(v):
        v = v.reshape((sources, local_experts, n_dp * capacity) + v.shape[3:])
        return v.transpose(1, 0, 2, 3).reshape(local_experts, -1, v.shape[-1])

    def by_source(v):
        v = v.reshape(local_experts, sources, n_dp * capacity, -1).transpose(1, 0, 2, 3)
        return v.reshape(sources * local_experts, n_dp, capacity, -1)

    grad_rows, expert_in, slot_gates = by_expert(grad_rows), by_expert(expert_in), by_expert(slot_gates)
    act_grad = (
        jnp.einsum("ecd,efd->ecf", grad_rows, down_weight, preferred_element_type=full)
        * slot_gates
    )
    gate_pre = jnp.einsum("ecd,edf->ecf", expert_in, gate_weight, preferred_element_type=full)
    up_pre = jnp.einsum("ecd,edf->ecf", expert_in, up_weight, preferred_element_type=full)
    sigma = jax.nn.sigmoid(gate_pre)
    silu = gate_pre * sigma
    activated = (silu * up_pre).astype(low)
    up_grad = (act_grad * silu).astype(low)
    gate_grad = (act_grad * up_pre * sigma * (1.0 + gate_pre * (1.0 - sigma))).astype(low)
    row_grads = (
        jnp.einsum("ecf,edf->ecd", gate_grad, gate_weight, preferred_element_type=full)
        + jnp.einsum("ecf,edf->ecd", up_grad, up_weight, preferred_element_type=full)
    ).astype(low)
    row_grads = swap(by_source(row_grads), PLANE)
    expert_out = jnp.einsum(
        "ecf,efd->ecd", activated, down_weight, preferred_element_type=full
    ).astype(low)
    slot_dots = jnp.sum(expert_out.astype(full) * grad_rows.astype(full), axis=-1, keepdims=True)
    slot_dots = swap(by_source(slot_dots), PLANE)[..., 0]
    scaled_out = (expert_out.astype(full) * slot_gates).astype(low)
    scaled_out = swap(by_source(scaled_out), PLANE)
    out_grads = (grad_rows.astype(full) * slot_gates).astype(low)
    down_grad = jnp.einsum("ecf,ecd->efd", activated, out_grads, preferred_element_type=full)
    gate_w_grad = jnp.einsum("ecd,ecf->edf", expert_in, gate_grad, preferred_element_type=full)
    up_w_grad = jnp.einsum("ecd,ecf->edf", expert_in, up_grad, preferred_element_type=full)

    dots = jnp.sum(
        pick.astype(full) * slot_dots.transpose(1, 0, 2)[..., None], axis=2
    ).transpose(0, 2, 1)
    dots = swap(dots, "dp").transpose(1, 0, 2).reshape(tok_count, experts)
    picked_grads = own_gates * (dots - jnp.sum(own_gates * dots, axis=-1, keepdims=True))
    logit_grads = picked_grads.astype(low)
    mixed_grad = line_scatter(bring_back(row_grads).astype(low), "dp")
    mixed_grad = mixed_grad + jnp.einsum(
        "te,de->td", logit_grads, router_full, preferred_element_type=full
    )
    mixture = line_scatter(bring_back(scaled_out).astype(low), "dp")
    output = (middle + mixture).astype(low)[None]
    router_grad = jnp.einsum("td,te->de", mixed_low, logit_grads, preferred_element_type=full)
    grad_out = cotangent[0].astype(full)
    middle_back, second_gain_grad = norm_back(
        mixed_grad, second_normed, second_inverse, second_gain
    )
    middle_grad = grad_out + middle_back

    branch_low = square_gather(middle_grad.astype(low), "ctx").reshape(seq_len, width)
    output_w_grad = jnp.einsum("ti,td->id", attended_low, branch_low, preferred_element_type=full)
    attended_grad = jnp.einsum("td,id->ti", branch_low, output_part, preferred_element_type=full)
    attended_grad = attended_grad.astype(low).reshape(seq_len, -1, head_dim)
    query_grad_parts, key_grad_parts, value_grad_parts = [], [], []
    for g in range(kv_here):
        query_group = query_low[:, g * group_size : (g + 1) * group_size]
        grad_group = attended_grad[:, g * group_size : (g + 1) * group_size]
        scores = (
            jnp.einsum("tgd,sd->gts", query_group, key_low[:, g], preferred_element_type=full)
            * score_scale
        )
        scores = jnp.where(allowed[None], scores, masked_score)
        shares = jnp.exp(scores - lse_parts[g])
        shares_low = shares.astype(low)
        share_grads = jnp.einsum(
            "tgd,sd->gts", grad_group, value_low[:, g], preferred_element_type=full
        )
        centre = jnp.sum(shares * share_grads, axis=-1, keepdims=True)
        score_grads = (shares * (share_grads - centre)).astype(low)
        query_grad_parts.append(
            jnp.einsum("gts,sd->tgd", score_grads, key_low[:, g], preferred_element_type=full)
            * score_scale
        )
        key_grad_parts.append(
            jnp.einsum("gts,tgd->sd", score_grads, query_group, preferred_element_type=full)
            * score_scale
        )
        value_grad_parts.append(
            jnp.einsum("gts,tgd->sd", shares_low, grad_group, preferred_element_type=full)
        )
    query_grad = jnp.concatenate(query_grad_parts, axis=1)
    key_grad = jnp.stack(key_grad_parts, axis=1)
    value_grad = jnp.stack(value_grad_parts, axis=1)
    query_raw_grad, query_gain_grad = norm_rope_back(
        query_grad, query_normed, query_inverse, query_scale, cosine, sine
    )
    key_raw_grad, key_gain_grad = norm_rope_back(
        key_grad, key_normed, key_inverse, key_scale, cosine, sine
    )
    raw_grad = jnp.concatenate(
        [
            query_raw_grad.reshape(seq_len, -1),
            key_raw_grad.reshape(seq_len, -1),
            value_grad.reshape(seq_len, -1),
        ],
        axis=1,
    ).astype(low)
    hidden_grad = jnp.einsum("ti,di->td", raw_grad, front_weight, preferred_element_type=full)
    hidden_grad = square_scatter(hidden_grad.astype(low).reshape(n_ctx, tok_count, width), "ctx")
    own_inverse = lax.rsqrt(jnp.mean(own * own, axis=-1, keepdims=True) + eps_norm)
    input_back, first_gain_grad = norm_back(hidden_grad, own * own_inverse, own_inverse, first_gain)
    tokens_grad = (middle_grad + input_back).astype(low)[None]

    front_grad = jnp.einsum("td,ti->di", hidden, raw_grad, preferred_element_type=full).astype(low)
    front_grad = front_grad.reshape(n_dp, n_ctx, n_exp, rows, -1).transpose(2, 0, 1, 3, 4)
    front_grad = line_scatter(pair_scatter(front_grad, "exp"), "dp").astype(low)
    front_grad = swap(front_grad, "ctx").astype(full)
    query_share = front_grad[:, :, :q_cols].transpose(1, 0, 2).reshape(rows, -1)
    key_share = front_grad[:, :, q_cols : q_cols + kv_cols].transpose(1, 0, 2).reshape(rows, -1)
    value_share = front_grad[:, :, q_cols + kv_cols :].transpose(1, 0, 2).reshape(rows, -1)
    back_grad = output_w_grad.astype(low).reshape(n_ctx, n_exp, -1, width).transpose(1, 0, 2, 3)
    back_grad = swap(pair_scatter(back_grad, "exp"), "ctx")
    output_share = line_scatter(back_grad, "dp")
    packed = jnp.concatenate(
        [
            first_gain_grad.reshape(devices, -1),
            second_gain_grad.reshape(devices, -1),
            query_gain_grad.reshape(devices, -1),
            key_gain_grad.reshape(devices, -1),
            router_grad.reshape(devices, -1),
        ],
        axis=1,
    )
    packed = jnp.pad(packed, ((0, 0), (0, -packed.shape[1] % 1024)))
    packed = lax.psum_scatter(packed, ALL, scatter_dimension=0, tiled=False)
    ends = [rows, 2 * rows, 2 * rows + gain_len, 2 * rows + 2 * gain_len]
    first_share = packed[: ends[0]]
    second_share = packed[ends[0] : ends[1]]
    query_gain_share = packed[ends[1] : ends[2]]
    key_gain_share = packed[ends[2] : ends[3]]
    router_share = packed[ends[3] : ends[3] + rows * experts].reshape(rows, experts)
    return (
        output,
        tokens_grad,
        first_share,
        query_share,
        key_share,
        value_share,
        query_gain_share,
        key_gain_share,
        output_share,
        second_share,
        router_share,
        gate_w_grad,
        up_w_grad,
        down_grad,
    )


def solution(mesh):
    rows = P(ALL)
    sequences = P(("dp", "exp"), "ctx")
    in_specs = (sequences,) + (rows,) * 12 + (sequences, P(("dp", "exp")), sequences)
    out_specs = (sequences,) * 2 + (rows,) * 12
    return jax.shard_map(shards, mesh=mesh, in_specs=in_specs, out_specs=out_specs, check_vma=False)
```

```python
import functools

import jax
import jax.numpy as jnp
from jax import lax
from jax.experimental import pallas as pl
from jax.experimental.pallas import tpu as pltpu
from jax.sharding import PartitionSpec as P

eps_norm = 1e-06
rope_base = 1000000.0
masked_score = -1e30
ALL = ("dp", "ctx", "exp")
PLANE = ("ctx", "exp")
VMEM = 56 << 20
MESH = pl.DeviceIdType.MESH


def rope_tables(positions, width):
    exponents = jnp.arange(width // 2, dtype=jnp.float32) * (2.0 / width)
    frequency = rope_base ** (-exponents)
    angles = positions.astype(jnp.float32)[:, None] * frequency[None, :]
    angles = jnp.concatenate([angles, angles], axis=-1)
    return (jnp.cos(angles), jnp.sin(angles))


def norm_back(grad, normed, inverse, gain):
    gain_grad = jnp.sum(grad * normed, axis=0)
    scaled = grad * gain
    return (
        inverse * (scaled - normed * jnp.mean(scaled * normed, axis=-1, keepdims=True)),
        gain_grad,
    )


def line_gather(block, axis):
    n = lax.axis_size(axis)
    me = lax.axis_index(axis)
    before, after = [], []
    up = down = block
    for step in range(1, n):
        up = lax.ppermute(up, axis, [(i, i + 1) for i in range(step - 1, n - 1)])
        down = lax.ppermute(down, axis, [(i, i - 1) for i in range(1, n - step + 1)])
        before.insert(0, up)
        after.append(down)
    return lax.dynamic_slice_in_dim(jnp.stack(before + [block] + after), n - 1 - me, n, 0)


def line_scatter(parts, axis):
    n = lax.axis_size(axis)
    me = lax.axis_index(axis)

    def part(i):
        return lax.dynamic_index_in_dim(parts, jnp.clip(i, 0, n - 1), 0, keepdims=False)

    up = down = None
    for step in range(1, n):
        send_up, send_down = part(me + n - step), part(me - n + step)
        if up is not None:
            send_up, send_down = add_low(send_up, up), add_low(send_down, down)
        up = lax.ppermute(send_up, axis, [(i, i + 1) for i in range(step)])
        down = lax.ppermute(send_down, axis, [(i, i - 1) for i in range(n - step, n)])
    return part(me).astype(jnp.float32) + up.astype(jnp.float32) + down.astype(jnp.float32)


def add_low(left, right):
    return (left.astype(jnp.float32) + right.astype(jnp.float32)).astype(left.dtype)


def flip(block, axis, bit):
    return lax.ppermute(block, axis, [(i, i ^ bit) for i in range(lax.axis_size(axis))])


def square_gather(block, axis):
    if lax.axis_size(axis) != 4:
        return lax.all_gather(block, axis, axis=0, tiled=False)
    half = block.shape[-1] // 2
    me = lax.axis_index(axis)
    by_x, by_y = flip(block, axis, 1), flip(block, axis, 2)
    far = jnp.concatenate(
        [flip(by_x[..., :half], axis, 2), flip(by_y[..., half:], axis, 1)], axis=-1
    )
    whole = jnp.zeros((4,) + block.shape, block.dtype)
    for bits, piece in enumerate((block, by_x, by_y, far)):
        whole = lax.dynamic_update_index_in_dim(whole, piece, me ^ bits, 0)
    return whole


def square_scatter(parts, axis):
    if lax.axis_size(axis) != 4:
        return lax.psum_scatter(parts, axis, scatter_dimension=0, tiled=False).astype(jnp.float32)
    half = parts.shape[-1] // 2
    me = lax.axis_index(axis)
    own, to_x, to_y, far = [
        lax.dynamic_index_in_dim(parts, me ^ bits, 0, keepdims=False) for bits in range(4)
    ]
    first = flip(jnp.stack([to_x[..., :half], far[..., :half]]), axis, 1)
    second = flip(jnp.stack([to_y[..., half:], far[..., half:]]), axis, 2)
    later_first = flip(add_low(to_y[..., :half], first[1]), axis, 2)
    later_second = flip(add_low(to_x[..., half:], second[1]), axis, 1)
    own = own.astype(jnp.float32)
    first = own[..., :half] + first[0].astype(jnp.float32) + later_first.astype(jnp.float32)
    second = own[..., half:] + second[0].astype(jnp.float32) + later_second.astype(jnp.float32)
    return jnp.concatenate([first, second], axis=-1)


def pair_gather(block, axis):
    if lax.axis_size(axis) != 2:
        return lax.all_gather(block, axis, axis=0, tiled=False)
    other = flip(block, axis, 1)
    first = lax.axis_index(axis) == 0
    return jnp.stack([jnp.where(first, block, other), jnp.where(first, other, block)])


def pair_scatter(parts, axis):
    if lax.axis_size(axis) != 2:
        return lax.psum_scatter(parts, axis, scatter_dimension=0, tiled=False)
    first = lax.axis_index(axis) == 0
    other = flip(jnp.where(first, parts[1], parts[0]), axis, 1)
    return add_low(jnp.where(first, parts[0], parts[1]), other)


def swap(parts, axis):
    return lax.all_to_all(parts, axis, split_axis=0, concat_axis=0, tiled=True)


def project_kernel(x_ref, gain_ref, weight_ref, scale_ref, cos_ref, sin_ref, hidden_ref, raw_ref, out_ref, *, q_heads, kv_heads):
    x = x_ref[...].astype(jnp.float32)
    inverse = lax.rsqrt(jnp.mean(x * x, axis=-1, keepdims=True) + eps_norm)
    hidden = ((x * inverse) * gain_ref[...]).astype(jnp.bfloat16)
    hidden_ref[...] = hidden
    raw = jnp.dot(hidden, weight_ref[...], preferred_element_type=jnp.float32)
    raw_ref[...] = raw
    width = cos_ref.shape[1]
    cosine, sine = cos_ref[...], sin_ref[...]
    for h in range(q_heads + kv_heads):
        here = slice(h * width, (h + 1) * width)
        part = raw[:, here]
        scale = scale_ref[0:1, :] if h < q_heads else scale_ref[1:2, :]
        factor = lax.rsqrt(jnp.mean(part * part, axis=-1, keepdims=True) + eps_norm)
        scaled = part * factor * scale
        turned = pltpu.roll(scaled, width // 2, 1)
        out_ref[:, here] = (scaled * cosine + turned * sine).astype(jnp.bfloat16)
    rest = slice((q_heads + kv_heads) * width, raw.shape[1])
    out_ref[:, rest] = raw[:, rest].astype(jnp.bfloat16)


def project(x, gain, weight, scales, cosine, sine, q_heads, kv_heads, block):
    rows, width = x.shape
    columns = weight.shape[1]
    head = cosine.shape[1]
    whole = lambda shape: pl.BlockSpec(shape, lambda i: (0, 0))
    return pl.pallas_call(
        functools.partial(project_kernel, q_heads=q_heads, kv_heads=kv_heads),
        grid=(rows // block,),
        in_specs=[
            pl.BlockSpec((block, width), lambda i: (i, 0)),
            whole((1, width)),
            whole((width, columns)),
            whole((2, head)),
            pl.BlockSpec((block, head), lambda i: (i, 0)),
            pl.BlockSpec((block, head), lambda i: (i, 0)),
        ],
        out_specs=[
            pl.BlockSpec((block, width), lambda i: (i, 0)),
            pl.BlockSpec((block, columns), lambda i: (i, 0)),
            pl.BlockSpec((block, columns), lambda i: (i, 0)),
        ],
        out_shape=[
            jax.ShapeDtypeStruct((rows, width), jnp.bfloat16),
            jax.ShapeDtypeStruct((rows, columns), jnp.float32),
            jax.ShapeDtypeStruct((rows, columns), jnp.bfloat16),
        ],
        compiler_params=pltpu.CompilerParams(vmem_limit_bytes=VMEM),
        cost_estimate=pl.CostEstimate(
            flops=2 * rows * width * columns, bytes_accessed=30 << 20, transcendentals=0
        ),
    )(x, gain, weight, scales, cosine, sine)


def seen(bounds_ref, first, rows, keys):
    query = first + lax.broadcasted_iota(jnp.int32, (rows, 1), 0)
    low_end, high_end = bounds_ref[0, 0], bounds_ref[0, 1]
    start = jnp.where(query >= high_end, high_end, jnp.where(query >= low_end, low_end, 0))
    key = lax.broadcasted_iota(jnp.int32, (rows, keys), 1)
    return (key <= query) & (key >= start)


def shares_of(query, keys, allowed, score_scale):
    scores = lax.dot_general(
        query, keys, (((1,), (1,)), ((), ())), preferred_element_type=jnp.float32
    )
    scores = jnp.where(allowed, scores * score_scale, masked_score)
    weights = jnp.exp(scores - jnp.max(scores, axis=-1, keepdims=True))
    return weights / jnp.sum(weights, axis=-1, keepdims=True)


def attend_kernel(bounds_ref, query_ref, key_ref, value_ref, out_ref, *, block, score_scale):
    rows = query_ref.shape[0]
    for first in range(0, rows, block):
        last = first + block
        allowed = seen(bounds_ref, first, block, last)
        shares = shares_of(query_ref[first:last, :], key_ref[:last, :], allowed, score_scale)
        out_ref[first:last, :] = jnp.dot(
            shares.astype(jnp.bfloat16), value_ref[:last, :], preferred_element_type=jnp.float32
        ).astype(jnp.bfloat16)


def attend(bounds, turned, heads, kv_heads, head, block):
    rows = turned.shape[0]
    group = heads // kv_heads
    return pl.pallas_call(
        functools.partial(attend_kernel, block=block, score_scale=head ** (-0.5)),
        grid=(heads,),
        in_specs=[
            pl.BlockSpec(memory_space=pltpu.SMEM),
            pl.BlockSpec((rows, head), lambda h: (0, h)),
            pl.BlockSpec((rows, head), lambda h: (0, heads + h // group)),
            pl.BlockSpec((rows, head), lambda h: (0, heads + kv_heads + h // group)),
        ],
        out_specs=pl.BlockSpec((rows, head), lambda h: (0, h)),
        out_shape=jax.ShapeDtypeStruct((rows, heads * head), jnp.bfloat16),
        compiler_params=pltpu.CompilerParams(vmem_limit_bytes=VMEM),
        cost_estimate=pl.CostEstimate(
            flops=2 * heads * rows * rows * head,
            bytes_accessed=6 << 20,
            transcendentals=heads * rows * rows // 2,
        ),
    )(bounds, turned, turned, turned)


def attend_back_kernel(
    bounds_ref, query_ref, key_ref, value_ref, grad_ref, raw_ref, scale_ref, cos_ref, sin_ref,
    out_ref, gain_ref, key_sum, value_sum, *, block, heads, group, score_scale,
):
    step = pl.program_id(0)
    rows = query_ref.shape[0]
    low, full = jnp.bfloat16, jnp.float32
    kv_heads = heads // group

    def norm_rope_back(grad, raw, scale, cosine, sine):
        inverse = lax.rsqrt(jnp.mean(raw * raw, axis=-1, keepdims=True) + eps_norm)
        normed = raw * inverse
        turned = grad * cosine + pltpu.roll(grad * sine, grad.shape[-1] // 2, 1)
        inner = turned * scale
        back = inverse * (inner - normed * jnp.mean(inner * normed, axis=-1, keepdims=True))
        return back, jnp.sum(turned * normed, axis=0, keepdims=True)

    @pl.when(step == 0)
    def _():
        gain_ref[...] = jnp.zeros_like(gain_ref)

    @pl.when(lax.rem(step, group) == 0)
    def _():
        @pl.when(step < heads)
        def _():
            for kv in range(kv_heads):
                @pl.when(step == kv * group)
                def _():
                    key_sum[kv] = jnp.zeros((rows, key_ref.shape[1]), full)
                    value_sum[kv] = jnp.zeros((rows, key_ref.shape[1]), full)

    @pl.when(step < heads)
    def _():
        kv = jnp.minimum(step // group, kv_heads - 1)
        gains = jnp.zeros((1, query_ref.shape[1]), full)
        for first in range(0, rows, block):
            last = first + block
            query, keys, values = query_ref[first:last, :], key_ref[:last, :], value_ref[:last, :]
            grad = grad_ref[first:last, :]
            allowed = seen(bounds_ref, first, block, last)
            shares = shares_of(query, keys, allowed, score_scale)
            share_grads = lax.dot_general(
                grad, values, (((1,), (1,)), ((), ())), preferred_element_type=full
            )
            centre = jnp.sum(shares * share_grads, axis=-1, keepdims=True)
            score_grads = (shares * (share_grads - centre)).astype(low)
            key_sum[kv, :last, :] += lax.dot_general(
                score_grads, query, (((0,), (0,)), ((), ())), preferred_element_type=full
            )
            value_sum[kv, :last, :] += lax.dot_general(
                shares.astype(low), grad, (((0,), (0,)), ((), ())), preferred_element_type=full
            )
            query_grad = jnp.dot(score_grads, keys, preferred_element_type=full) * score_scale
            back, gain = norm_rope_back(
                query_grad, raw_ref[first:last, :], scale_ref[0:1, :], cos_ref[first:last, :],
                sin_ref[first:last, :],
            )
            out_ref[first:last, :] = back.astype(low)
            gains += gain
        gain_ref[0:1, :] += gains

    @pl.when((step >= heads) & (step < heads + kv_heads))
    def _():
        back, gain = norm_rope_back(
            key_sum[step - heads] * score_scale, raw_ref[...], scale_ref[1:2, :], cos_ref[...],
            sin_ref[...],
        )
        out_ref[...] = back.astype(low)
        gain_ref[1:2, :] += gain

    @pl.when(step >= heads + kv_heads)
    def _():
        out_ref[...] = value_sum[step - heads - kv_heads].astype(low)


def attend_back(bounds, turned, grad, raw, scales, cosine, sine, heads, kv_heads, head, block):
    rows = turned.shape[0]
    group = heads // kv_heads
    columns = turned.shape[1]
    within = lambda h: jnp.minimum(h, heads - 1)
    tables = pl.BlockSpec((rows, head), lambda h: (0, 0))
    return pl.pallas_call(
        functools.partial(
            attend_back_kernel, block=block, heads=heads, group=group, score_scale=head ** (-0.5)
        ),
        grid=(heads + 2 * kv_heads,),
        in_specs=[
            pl.BlockSpec(memory_space=pltpu.SMEM),
            pl.BlockSpec((rows, head), lambda h: (0, within(h))),
            pl.BlockSpec((rows, head), lambda h: (0, heads + within(h) // group)),
            pl.BlockSpec((rows, head), lambda h: (0, heads + kv_heads + within(h) // group)),
            pl.BlockSpec((rows, head), lambda h: (0, within(h))),
            pl.BlockSpec((rows, head), lambda h: (0, jnp.minimum(h, heads + kv_heads - 1))),
            pl.BlockSpec((2, head), lambda h: (0, 0)),
            tables,
            tables,
        ],
        out_specs=[
            pl.BlockSpec((rows, head), lambda h: (0, h)),
            pl.BlockSpec((2, head), lambda h: (0, 0)),
        ],
        out_shape=[
            jax.ShapeDtypeStruct((rows, columns), jnp.bfloat16),
            jax.ShapeDtypeStruct((2, head), jnp.float32),
        ],
        scratch_shapes=[pltpu.VMEM((kv_heads, rows, head), jnp.float32)] * 2,
        compiler_params=pltpu.CompilerParams(vmem_limit_bytes=VMEM),
        cost_estimate=pl.CostEstimate(
            flops=5 * heads * rows * rows * head,
            bytes_accessed=12 << 20,
            transcendentals=heads * rows * rows // 2,
        ),
    )(bounds, turned, turned, turned, grad, raw, scales, cosine, sine)


def greet(sizes):
    n = sizes["dp"]
    barrier = pltpu.get_barrier_semaphore()
    me = lax.axis_index("dp")
    for step in (-1, 1):
        @pl.when((me + step >= 0) & (me + step < n))
        def _():
            pl.semaphore_signal(
                barrier, inc=1, device_id={"dp": me + step}, device_id_type=MESH
            )
    number = sizes["ctx"] * sizes["exp"]
    for ahead in range(number - 1, 0, -1):
        pl.semaphore_signal(
            barrier, inc=1, device_id=place(sizes, peer(sizes, ahead)), device_id_type=MESH
        )
    neighbours = (me + n - 1) // n + (2 * n - 2 - me) // n
    pl.semaphore_wait(barrier, number - 1 + neighbours)


def plane_index(sizes):
    return lax.axis_index("ctx") * sizes["exp"] + lax.axis_index("exp")


def peer(sizes, ahead):
    number = sizes["ctx"] * sizes["exp"]
    return lax.rem(plane_index(sizes) + ahead, number)


def place(sizes, index):
    return {"ctx": index // sizes["exp"], "exp": lax.rem(index, sizes["exp"])}


def cut(widths, part):
    pieces = []
    for number, width in enumerate(widths):
        step = min(width, part)
        pieces += [(number, first, step) for first in range(0, width, step)]
    return pieces


def dispatch_kernel(*refs, sizes, pieces, arrays):
    blocks, pick_ref, outs = refs[:arrays], refs[arrays], refs[arrays + 1 : 2 * arrays + 1]
    columns, packed = refs[2 * arrays + 1 : 3 * arrays + 1], refs[3 * arrays + 1 : 4 * arrays + 1]
    line_send, line_recv, plane_send, plane_recv, own_sem = refs[4 * arrays + 1 :]
    n, number = sizes["dp"], sizes["ctx"] * sizes["exp"]
    me, here = lax.axis_index("dp"), plane_index(sizes)
    tokens = blocks[0].shape[0]
    groups, dests, rows, span = pick_ref.shape
    greet(sizes)

    def line_copy(f, origin, step):
        a, first, part = pieces[f]
        return pltpu.make_async_remote_copy(
            src_ref=columns[a].at[origin, :, pl.ds(first, part)],
            dst_ref=columns[a].at[origin, :, pl.ds(first, part)],
            send_sem=line_send.at[f, origin, (step + 1) // 2],
            recv_sem=line_recv.at[f, origin],
            device_id={"dp": me + step},
            device_id_type=MESH,
        )

    def send_own(f):
        a, first, part = pieces[f]
        columns[a][me, :, pl.ds(first, part)] = blocks[a][:, pl.ds(first, part)]
        for step in (-1, 1):
            @pl.when((me + step >= 0) & (me + step < n))
            def _():
                line_copy(f, me, step).start()

    def plane_copy(f, ahead):
        a, first, part = pieces[f]
        target = peer(sizes, ahead)
        return pltpu.make_async_remote_copy(
            src_ref=packed[a].at[target, :, pl.ds(first, part)],
            dst_ref=outs[a].at[here, :, pl.ds(first, part)],
            send_sem=plane_send.at[f, ahead],
            recv_sem=plane_recv.at[f, ahead],
            device_id=place(sizes, target),
            device_id_type=MESH,
        )

    def own_copy(f):
        a, first, part = pieces[f]
        return pltpu.make_async_copy(
            packed[a].at[here, :, pl.ds(first, part)],
            outs[a].at[here, :, pl.ds(first, part)],
            own_sem.at[f],
        )

    send_own(0)
    for f, (a, first, part) in enumerate(pieces):
        for distance in range(1, n):
            for step in (-1, 1):
                origin = me - step * distance
                beyond = me + step

                @pl.when((origin >= 0) & (origin < n))
                def _():
                    line_copy(f, origin, step).wait_recv()

                    @pl.when((beyond >= 0) & (beyond < n))
                    def _():
                        line_copy(f, origin, step).start()

            if distance == max(1, n - 2) and f + 1 < len(pieces):
                send_own(f + 1)
        for g in range(groups):
            given = columns[a][pl.ds(g * span // tokens, span // tokens), :, pl.ds(first, part)]
            given = given.reshape(span, part)

            @pl.loop(0, dests)
            def _(j):
                packed[a][j, pl.ds(g * rows, rows), pl.ds(first, part)] = jnp.dot(
                    pick_ref[g, j], given, preferred_element_type=jnp.float32
                ).astype(jnp.bfloat16)

        for ahead in range(number - 1, 0, -1):
            plane_copy(f, ahead).start()
        own_copy(f).start()

    for f in range(len(pieces)):
        for distance in range(n):
            for step in (-1, 1):
                origin = me - step * distance
                beyond = me + step

                @pl.when((origin >= 0) & (origin < n) & (beyond >= 0) & (beyond < n))
                def _():
                    line_copy(f, origin, step).wait_send()

        for ahead in range(1, number):
            plane_copy(f, ahead).wait()
        own_copy(f).wait()


def dispatch(blocks, pick, sizes, collective, part=512):
    tokens = blocks[0].shape[0]
    widths = [block.shape[1] for block in blocks]
    n, number = sizes["dp"], sizes["ctx"] * sizes["exp"]
    groups, dests, rows, _ = pick.shape
    pieces = cut(widths, part)
    count = len(pieces)
    return pl.pallas_call(
        functools.partial(dispatch_kernel, sizes=sizes, pieces=pieces, arrays=len(blocks)),
        in_specs=[pl.BlockSpec(memory_space=pltpu.VMEM)] * (len(blocks) + 1),
        out_specs=[pl.BlockSpec(memory_space=pl.ANY)] * len(blocks),
        out_shape=[
            jax.ShapeDtypeStruct((number, groups * rows, width), jnp.bfloat16) for width in widths
        ],
        scratch_shapes=[pltpu.VMEM((n, tokens, width), jnp.bfloat16) for width in widths]
        + [pltpu.VMEM((dests, groups * rows, width), jnp.bfloat16) for width in widths]
        + [
            pltpu.SemaphoreType.DMA((count, n, 2)),
            pltpu.SemaphoreType.DMA((count, n)),
            pltpu.SemaphoreType.DMA((count, number)),
            pltpu.SemaphoreType.DMA((count, number)),
            pltpu.SemaphoreType.DMA((count,)),
        ],
        compiler_params=pltpu.CompilerParams(
            collective_id=collective, has_side_effects=True, vmem_limit_bytes=VMEM
        ),
        cost_estimate=pl.CostEstimate(
            flops=10 << 30, bytes_accessed=600 << 20, transcendentals=0
        ),
    )(*blocks, pick)


def combine_kernel(*refs, sizes, pieces, arrays):
    sent, pick_ref, outs = refs[:arrays], refs[arrays], refs[arrays + 1 : 2 * arrays + 1]
    back, leaving, landing = [refs[k * arrays + 1 : (k + 1) * arrays + 1] for k in (2, 3, 4)]
    sums, line_send, line_recv, plane_send, plane_recv, own_sem = refs[5 * arrays + 1 :]
    n, number = sizes["dp"], sizes["ctx"] * sizes["exp"]
    me, here = lax.axis_index("dp"), plane_index(sizes)
    tokens = outs[0].shape[0]
    groups, span, _ = pick_ref.shape
    rows = sent[0].shape[1] // groups
    full, low = jnp.float32, jnp.bfloat16
    greet(sizes)

    def plane_copy(f, ahead):
        a, first, part = pieces[f]
        target = peer(sizes, ahead)
        return pltpu.make_async_remote_copy(
            src_ref=sent[a].at[target, :, pl.ds(first, part)],
            dst_ref=back[a].at[here, :, pl.ds(first, part)],
            send_sem=plane_send.at[f, ahead],
            recv_sem=plane_recv.at[f, ahead],
            device_id=place(sizes, target),
            device_id_type=MESH,
        )

    def own_copy(f):
        a, first, part = pieces[f]
        return pltpu.make_async_copy(
            sent[a].at[here, :, pl.ds(first, part)],
            back[a].at[here, :, pl.ds(first, part)],
            own_sem.at[f],
        )

    for f in range(len(pieces)):
        for ahead in range(number - 1, 0, -1):
            plane_copy(f, ahead).start()
        own_copy(f).start()

    def line_copy(f, target, step):
        a, first, part = pieces[f]
        return pltpu.make_async_remote_copy(
            src_ref=leaving[a].at[target, :, pl.ds(first, part)],
            dst_ref=landing[a].at[target + (step + 1) // 2, :, pl.ds(first, part)],
            send_sem=line_send.at[f, target],
            recv_sem=line_recv.at[f, target + (step + 1) // 2],
            device_id={"dp": me + step},
            device_id_type=MESH,
        )

    for f, (a, first, part) in enumerate(pieces):
        here_columns = pl.ds(first, part)
        for ahead in range(1, number):
            plane_copy(f, ahead).wait_recv()
        own_copy(f).wait()
        for g in range(groups):
            gathered = back[a][:, pl.ds(g * rows, rows), here_columns].reshape(number * rows, part)
            sums[pl.ds(g * span // tokens, span // tokens), :, pl.ds(0, part)] = jnp.dot(
                pick_ref[g], gathered, preferred_element_type=full
            ).reshape(span // tokens, tokens, part)

        for distance in range(n - 1, 0, -1):
            for step in (-1, 1):
                target = me + step * distance
                behind = me - step

                @pl.when((target >= 0) & (target < n))
                def _():
                    own = sums[target, :, pl.ds(0, part)]

                    @pl.when((behind >= 0) & (behind < n))
                    def _():
                        line_copy(f, target, step).wait_recv()
                        coming = landing[a][target + (step + 1) // 2, :, here_columns]
                        leaving[a][target, :, here_columns] = (own + coming.astype(full)).astype(low)

                    @pl.when((behind < 0) | (behind >= n))
                    def _():
                        leaving[a][target, :, here_columns] = own.astype(low)

                    line_copy(f, target, step).start()

        outs[a][:, here_columns] = sums[me, :, pl.ds(0, part)]
        for step in (-1, 1):
            @pl.when((me - step >= 0) & (me - step < n))
            def _():
                line_copy(f, me, step).wait_recv()
                outs[a][:, here_columns] += landing[a][me + (step + 1) // 2, :, here_columns].astype(full)

    for f in range(len(pieces)):
        for ahead in range(1, number):
            plane_copy(f, ahead).wait_send()
        for distance in range(1, n):
            for step in (-1, 1):
                target = me + step * distance

                @pl.when((target >= 0) & (target < n))
                def _():
                    line_copy(f, target, step).wait_send()


def combine(sent, pick, tokens, sizes, collective, part=512):
    number, back_rows = sent[0].shape[:2]
    widths = [v.shape[2] for v in sent]
    n = sizes["dp"]
    pieces = cut(widths, part)
    count = len(pieces)
    return pl.pallas_call(
        functools.partial(combine_kernel, sizes=sizes, pieces=pieces, arrays=len(sent)),
        in_specs=[pl.BlockSpec(memory_space=pl.ANY)] * len(sent)
        + [pl.BlockSpec(memory_space=pltpu.VMEM)],
        out_specs=[pl.BlockSpec(memory_space=pltpu.VMEM)] * len(sent),
        out_shape=[jax.ShapeDtypeStruct((tokens, width), jnp.float32) for width in widths],
        scratch_shapes=[pltpu.VMEM((number, back_rows, width), jnp.bfloat16) for width in widths]
        + [pltpu.VMEM((n, tokens, width), jnp.bfloat16) for width in widths]
        + [pltpu.VMEM((n + 1, tokens, width), jnp.bfloat16) for width in widths]
        + [
            pltpu.VMEM((n, tokens, max(p[2] for p in pieces)), jnp.float32),
            pltpu.SemaphoreType.DMA((count, n)),
            pltpu.SemaphoreType.DMA((count, n + 1)),
            pltpu.SemaphoreType.DMA((count, number)),
            pltpu.SemaphoreType.DMA((count, number)),
            pltpu.SemaphoreType.DMA((count,)),
        ],
        compiler_params=pltpu.CompilerParams(
            collective_id=collective, has_side_effects=True, vmem_limit_bytes=VMEM
        ),
        cost_estimate=pl.CostEstimate(
            flops=5 << 30, bytes_accessed=300 << 20, transcendentals=0
        ),
    )(*sent, pick)


def expert_kernel(
    here_ref, in_ref, parts_ref, grad_ref, gate_w_ref, up_w_ref, down_w_ref, active_ref, gate_ref,
    up_ref, rows_ref, scaled_ref, dots_ref, *, experts,
):
    full, low = jnp.float32, jnp.bfloat16
    across = (((1,), (1,)), ((), ()))
    grads = grad_ref[0]
    column = lax.broadcasted_iota(jnp.int32, (1, parts_ref.shape[2]), 1)
    mine = lax.rem(column, experts) == here_ref[0]
    parts = parts_ref[0].astype(full)
    gates = jnp.sum(jnp.where(mine & (column < 3 * experts), parts, 0.0), axis=-1, keepdims=True)
    gate_pre = jnp.dot(in_ref[0], gate_w_ref[0], preferred_element_type=full)
    up_pre = jnp.dot(in_ref[0], up_w_ref[0], preferred_element_type=full)
    act_grad = gates * lax.dot_general(grads, down_w_ref[0], across, preferred_element_type=full)
    sigma = 1.0 / (1.0 + jnp.exp(-gate_pre))
    silu = gate_pre * sigma
    activated = silu * up_pre
    active = activated.astype(low)
    active_ref[0] = (gates * activated).astype(low)
    up_grad = (act_grad * silu).astype(low)
    gate_grad = (act_grad * up_pre * sigma * (1.0 + gate_pre * (1.0 - sigma))).astype(low)
    up_ref[0] = up_grad
    gate_ref[0] = gate_grad
    rows_ref[0] = (
        lax.dot_general(gate_grad, gate_w_ref[0], across, preferred_element_type=full)
        + lax.dot_general(up_grad, up_w_ref[0], across, preferred_element_type=full)
    ).astype(low)
    given = jnp.dot(active, down_w_ref[0], preferred_element_type=full).astype(low).astype(full)
    scaled_ref[0] = (gates * given).astype(low)
    dots = jnp.sum(given * grads.astype(full), axis=-1, keepdims=True)
    first = dots.astype(low).astype(full)
    second = (dots - first).astype(low).astype(full)
    third = dots - first - second
    spread = jnp.where(column < experts, first, jnp.where(column < 2 * experts, second, third))
    dots_ref[0] = jnp.where(mine & (column < 3 * experts), spread, 0.0).astype(low)


def expert(here, rows_in, parts, grads, gate_weight, up_weight, down_weight, experts):
    sources, rows, width = rows_in.shape
    inner = gate_weight.shape[2]
    extra = parts.shape[2]
    by_source = lambda columns: pl.BlockSpec((1, rows, columns), lambda i: (i, 0, 0))
    fixed = lambda shape: pl.BlockSpec(
        shape, lambda i: (0, 0, 0), pipeline_mode=pl.Buffered(buffer_count=1)
    )
    out = lambda columns: jax.ShapeDtypeStruct((sources, rows, columns), jnp.bfloat16)
    return pl.pallas_call(
        functools.partial(expert_kernel, experts=experts),
        grid=(sources,),
        in_specs=[
            pl.BlockSpec(memory_space=pltpu.SMEM),
            by_source(width),
            by_source(extra),
            by_source(width),
            fixed((1, width, inner)),
            fixed((1, width, inner)),
            fixed((1, inner, width)),
        ],
        out_specs=[by_source(c) for c in (inner, inner, inner, width, width, extra)],
        out_shape=[out(c) for c in (inner, inner, inner, width, width, extra)],
        compiler_params=pltpu.CompilerParams(vmem_limit_bytes=VMEM),
        cost_estimate=pl.CostEstimate(
            flops=12 * sources * rows * width * inner, bytes_accessed=60 << 20, transcendentals=0
        ),
    )(here, rows_in, parts, grads, gate_weight, up_weight, down_weight)


def shards(
    tokens,
    attention_gain,
    query_weight,
    key_weight,
    value_weight,
    query_gain,
    key_gain,
    output_weight,
    mixture_gain,
    router_weight,
    gate_weight,
    up_weight,
    down_weight,
    routes,
    bounds,
    cotangent,
):
    low, full = jnp.bfloat16, jnp.float32
    n_dp, n_ctx, n_exp = (lax.axis_size(a) for a in ALL)
    devices = n_dp * n_ctx * n_exp
    tok_count, width = tokens.shape[1], tokens.shape[2]
    seq_len = tok_count * n_ctx
    head_dim = query_gain.shape[0] * devices
    rows = query_weight.shape[0]
    heads = query_weight.shape[1] // head_dim
    kv_heads = key_weight.shape[1] // head_dim
    kv_here = kv_heads // n_ctx
    group_size = heads // kv_heads
    q_cols, kv_cols = heads * head_dim // n_ctx, kv_here * head_dim
    experts = router_weight.shape[1]
    topk = routes.shape[2]
    base_rows = tok_count * topk // experts
    capacity = base_rows + max(1, base_rows // 8)
    plane = experts // n_dp
    local_experts = gate_weight.shape[0]
    score_scale = head_dim ** (-0.5)
    dp_index = lax.axis_index("dp")

    gain_len = query_gain.shape[0]
    small = jnp.concatenate(
        [
            attention_gain[:, None],
            mixture_gain[:, None],
            jnp.pad(jnp.concatenate([query_gain, key_gain]), (0, rows - 2 * gain_len))[:, None],
            router_weight,
        ],
        axis=1,
    ).astype(low)
    small = jnp.pad(small, ((0, 0), (0, -small.shape[1] % 128)))
    extra = small.shape[1]

    def by_ctx(weight):
        return weight.astype(low).reshape(rows, n_ctx, -1).transpose(1, 0, 2)

    front = jnp.concatenate(
        [
            by_ctx(query_weight),
            by_ctx(key_weight),
            by_ctx(value_weight),
            jnp.broadcast_to(small[None], (n_ctx, rows, extra)),
        ],
        axis=2,
    )
    front = pair_gather(line_gather(swap(front, "ctx"), "dp"), "exp")
    front = front.transpose(1, 2, 0, 3, 4).reshape(width, -1)
    front_weight = front[:, : q_cols + 2 * kv_cols]
    small = front[:, q_cols + 2 * kv_cols :]
    first_gain = small[:, 0].astype(full)
    second_gain = small[:, 1].astype(full)
    head_gains = small[:, 2].reshape(devices, rows)
    query_scale = head_gains[:, :gain_len].reshape(-1).astype(full)
    key_scale = head_gains[:, gain_len : 2 * gain_len].reshape(-1).astype(full)
    router_full = small[:, 3 : 3 + experts]

    whole_tokens = square_gather(tokens[0], "ctx").reshape(seq_len, width)
    back = line_gather(output_weight.astype(low), "dp")
    back = pair_gather(swap(back, "ctx"), "exp")
    output_part = back.transpose(1, 0, 2, 3).reshape(q_cols, width)

    column_routes = line_gather(routes[0], "dp")
    chosen = jnp.any(
        column_routes[:, :, :, None] == jnp.arange(experts, dtype=jnp.int32), axis=2
    )
    hot = lax.dynamic_slice_in_dim(chosen.astype(low), dp_index * plane, plane, 2)
    row_ids = jnp.arange(tok_count, dtype=jnp.int32)
    earlier = (row_ids[None, :] < row_ids[:, None]).astype(low)
    before = jnp.einsum("st,btj->bsj", earlier, hot, preferred_element_type=full)
    together = 2 if 2 * capacity % 16 == 0 and n_dp % 2 == 0 else n_dp
    groups = n_dp // together
    slot_rows = -(-together * capacity // 16) * 16
    sizes = {"dp": n_dp, "ctx": n_ctx, "exp": n_exp}

    def grouped(v):
        return v.reshape(groups, together * tok_count, -1)

    block_first = jnp.tile(jnp.arange(together, dtype=full) * capacity, groups)[:, None, None]
    slot_at = grouped(jnp.where(hot > 0, before + block_first, -1.0))
    slots = jnp.arange(slot_rows, dtype=full)
    pick = (slot_at.transpose(0, 2, 1)[:, :, None, :] == slots[:, None]).astype(low)
    pick_back = (slot_at[:, :, :, None] == slots).astype(low).reshape(groups, -1, plane * slot_rows)

    def bring_back(sent):
        sent = sent.reshape(plane, groups, slot_rows, -1).transpose(1, 0, 2, 3)
        sent = sent.reshape(groups, plane * slot_rows, -1)
        sums = jnp.einsum("gts,gsd->gtd", pick_back, sent, preferred_element_type=full)
        return sums.reshape(n_dp, tok_count, -1)

    positions = jnp.arange(seq_len, dtype=jnp.int32)
    cosine, sine = rope_tables(positions, head_dim)
    half = head_dim // 2
    sine = jnp.concatenate([-sine[:, :half], sine[:, half:]], axis=1)
    scales = jnp.stack([query_scale, key_scale])
    heads_here = heads // n_ctx
    hidden, raw, turned = project(
        whole_tokens, first_gain[None], front_weight, scales, cosine, sine, heads_here, kv_here,
        tok_count,
    )
    attended_low = attend(bounds, turned, heads_here, kv_here, head_dim, tok_count)
    branch = jnp.dot(attended_low, output_part, preferred_element_type=full).astype(low)
    branch = square_scatter(branch.reshape(n_ctx, tok_count, width), "ctx")

    own = tokens[0].astype(full)
    middle = own + branch
    second_inverse = lax.rsqrt(jnp.mean(middle * middle, axis=-1, keepdims=True) + eps_norm)
    second_normed = middle * second_inverse
    mixed_low = (second_normed * second_gain).astype(low)

    logits = jnp.dot(mixed_low, router_full, preferred_element_type=full)
    own_chosen = jnp.any(routes[0][:, :, None] == jnp.arange(experts, dtype=jnp.int32), axis=1)
    logits = jnp.where(own_chosen, logits, masked_score)
    own_gates = jnp.exp(logits - jnp.max(logits, axis=-1, keepdims=True))
    own_gates = own_gates / jnp.sum(own_gates, axis=-1, keepdims=True)
    first_part = lax.reduce_precision(own_gates, 8, 7)
    second_part = lax.reduce_precision(own_gates - first_part, 8, 7)
    third_part = lax.reduce_precision(own_gates - first_part - second_part, 8, 7)
    gate_parts = jnp.concatenate([first_part, second_part, third_part], axis=1).astype(low)
    gate_parts = jnp.pad(gate_parts, ((0, 0), (0, -gate_parts.shape[1] % 128)))
    expert_in, part_rows, grad_rows = dispatch(
        (mixed_low, gate_parts, cotangent[0]), pick, sizes, 1
    )
    here = (dp_index * n_ctx + lax.axis_index("ctx")) * n_exp + lax.axis_index("exp")
    active, gate_grad, up_grad, row_grads, scaled_out, dot_rows = expert(
        here[None], expert_in, part_rows, grad_rows, gate_weight, up_weight, down_weight, experts
    )
    mixed_grad, dots = combine((row_grads, dot_rows), pick_back, tok_count, sizes, 2)
    weight_sum = lambda left, right: jnp.einsum(
        "scd,scf->df", left, right, preferred_element_type=full
    )[None]
    down_grad = weight_sum(active, grad_rows)
    gate_w_grad = weight_sum(expert_in, gate_grad)
    up_w_grad = weight_sum(expert_in, up_grad)
    scaled_out = swap(scaled_out, PLANE)

    dots = dots[:, :experts] + dots[:, experts : 2 * experts] + dots[:, 2 * experts : 3 * experts]
    picked_grads = own_gates * (dots - jnp.sum(own_gates * dots, axis=-1, keepdims=True))
    logit_grads = picked_grads.astype(low)
    mixed_grad = mixed_grad + jnp.einsum(
        "te,de->td", logit_grads, router_full, preferred_element_type=full
    )
    mixture = line_scatter(bring_back(scaled_out).astype(low), "dp")
    output = (middle + mixture).astype(low)[None]
    router_grad = jnp.einsum("td,te->de", mixed_low, logit_grads, preferred_element_type=full)
    grad_out = cotangent[0].astype(full)
    middle_back, second_gain_grad = norm_back(
        mixed_grad, second_normed, second_inverse, second_gain
    )
    middle_grad = grad_out + middle_back

    branch_low = square_gather(middle_grad.astype(low), "ctx").reshape(seq_len, width)
    output_w_grad = jnp.einsum("ti,td->id", attended_low, branch_low, preferred_element_type=full)
    attended_grad = jnp.einsum("td,id->ti", branch_low, output_part, preferred_element_type=full)
    raw_grad, head_gain_grads = attend_back(
        bounds, turned, attended_grad.astype(low), raw, scales, cosine, sine, heads_here, kv_here,
        head_dim, tok_count,
    )
    query_gain_grad, key_gain_grad = head_gain_grads[0], head_gain_grads[1]
    hidden_grad = jnp.einsum("ti,di->td", raw_grad, front_weight, preferred_element_type=full)
    hidden_grad = square_scatter(hidden_grad.astype(low).reshape(n_ctx, tok_count, width), "ctx")
    own_inverse = lax.rsqrt(jnp.mean(own * own, axis=-1, keepdims=True) + eps_norm)
    input_back, first_gain_grad = norm_back(hidden_grad, own * own_inverse, own_inverse, first_gain)
    tokens_grad = (middle_grad + input_back).astype(low)[None]

    front_grad = jnp.einsum("td,ti->di", hidden, raw_grad, preferred_element_type=full).astype(low)
    front_grad = front_grad.reshape(n_dp, n_ctx, n_exp, rows, -1).transpose(2, 0, 1, 3, 4)
    front_grad = line_scatter(pair_scatter(front_grad, "exp"), "dp").astype(low)
    front_grad = swap(front_grad, "ctx").astype(full)
    query_share = front_grad[:, :, :q_cols].transpose(1, 0, 2).reshape(rows, -1)
    key_share = front_grad[:, :, q_cols : q_cols + kv_cols].transpose(1, 0, 2).reshape(rows, -1)
    value_share = front_grad[:, :, q_cols + kv_cols :].transpose(1, 0, 2).reshape(rows, -1)
    back_grad = output_w_grad.astype(low).reshape(n_ctx, n_exp, -1, width).transpose(1, 0, 2, 3)
    back_grad = swap(pair_scatter(back_grad, "exp"), "ctx")
    output_share = line_scatter(back_grad, "dp")
    packed = jnp.concatenate(
        [
            first_gain_grad.reshape(devices, -1),
            second_gain_grad.reshape(devices, -1),
            query_gain_grad.reshape(devices, -1),
            key_gain_grad.reshape(devices, -1),
            router_grad.reshape(devices, -1),
        ],
        axis=1,
    )
    packed = jnp.pad(packed, ((0, 0), (0, -packed.shape[1] % 1024)))
    packed = packed.reshape(n_dp, n_ctx, n_exp, -1).transpose(2, 1, 0, 3)
    packed = square_scatter(pair_scatter(packed, "exp"), "ctx")
    packed = line_scatter(packed, "dp")
    ends = [rows, 2 * rows, 2 * rows + gain_len, 2 * rows + 2 * gain_len]
    first_share = packed[: ends[0]]
    second_share = packed[ends[0] : ends[1]]
    query_gain_share = packed[ends[1] : ends[2]]
    key_gain_share = packed[ends[2] : ends[3]]
    router_share = packed[ends[3] : ends[3] + rows * experts].reshape(rows, experts)
    return (
        output,
        tokens_grad,
        first_share,
        query_share,
        key_share,
        value_share,
        query_gain_share,
        key_gain_share,
        output_share,
        second_share,
        router_share,
        gate_w_grad,
        up_w_grad,
        down_grad,
    )


def solution(mesh):
    rows = P(ALL)
    sequences = P(("dp", "exp"), "ctx")
    in_specs = (sequences,) + (rows,) * 12 + (sequences, P(("dp", "exp")), sequences)
    out_specs = (sequences,) * 2 + (rows,) * 12
    return jax.shard_map(shards, mesh=mesh, in_specs=in_specs, out_specs=out_specs, check_vma=False)
```

```python
import functools

import jax
import jax.numpy as jnp
from jax import lax
from jax.experimental import pallas as pl
from jax.experimental.pallas import tpu as pltpu
from jax.sharding import PartitionSpec as P

eps_norm = 1e-06
rope_base = 1000000.0
masked_score = -1e30
ALL = ("dp", "ctx", "exp")
PLANE = ("ctx", "exp")
VMEM = 60 << 20
MESH = pl.DeviceIdType.MESH


def rope_tables(positions, width):
    exponents = jnp.arange(width // 2, dtype=jnp.float32) * (2.0 / width)
    frequency = rope_base ** (-exponents)
    angles = positions.astype(jnp.float32)[:, None] * frequency[None, :]
    angles = jnp.concatenate([angles, angles], axis=-1)
    return (jnp.cos(angles), jnp.sin(angles))


def swap(parts, axis):
    return lax.all_to_all(parts, axis, split_axis=0, concat_axis=0, tiled=True)


def project_kernel(x_ref, gain_ref, weight_ref, scale_ref, cos_ref, sin_ref, hidden_ref, raw_ref, out_ref, *, q_heads, kv_heads):
    x = x_ref[...].astype(jnp.float32)
    inverse = lax.rsqrt(jnp.mean(x * x, axis=-1, keepdims=True) + eps_norm)
    hidden = ((x * inverse) * gain_ref[...]).astype(jnp.bfloat16)
    hidden_ref[...] = hidden
    raw = jnp.dot(
        hidden, weight_ref[:, : raw_ref.shape[1]], preferred_element_type=jnp.float32
    )
    raw_ref[...] = raw
    width = cos_ref.shape[1]
    cosine, sine = cos_ref[...], sin_ref[...]
    for h in range(q_heads + kv_heads):
        here = slice(h * width, (h + 1) * width)
        part = raw[:, here]
        scale = scale_ref[0:1, :] if h < q_heads else scale_ref[1:2, :]
        factor = lax.rsqrt(jnp.mean(part * part, axis=-1, keepdims=True) + eps_norm)
        scaled = part * factor * scale
        turned = pltpu.roll(scaled, width // 2, 1)
        out_ref[:, here] = (scaled * cosine + turned * sine).astype(jnp.bfloat16)
    rest = slice((q_heads + kv_heads) * width, raw.shape[1])
    out_ref[:, rest] = raw[:, rest].astype(jnp.bfloat16)


def project(x, gain, weight, columns, scales, cosine, sine, q_heads, kv_heads, block):
    rows, width = x.shape
    head = cosine.shape[1]
    whole = lambda shape: pl.BlockSpec(shape, lambda i: (0, 0))
    return pl.pallas_call(
        functools.partial(project_kernel, q_heads=q_heads, kv_heads=kv_heads),
        grid=(rows // block,),
        in_specs=[
            pl.BlockSpec((block, width), lambda i: (i, 0)),
            whole((1, width)),
            whole(weight.shape),
            whole((2, head)),
            pl.BlockSpec((block, head), lambda i: (i, 0)),
            pl.BlockSpec((block, head), lambda i: (i, 0)),
        ],
        out_specs=[
            pl.BlockSpec((block, width), lambda i: (i, 0)),
            pl.BlockSpec((block, columns), lambda i: (i, 0)),
            pl.BlockSpec((block, columns), lambda i: (i, 0)),
        ],
        out_shape=[
            jax.ShapeDtypeStruct((rows, width), jnp.bfloat16),
            jax.ShapeDtypeStruct((rows, columns), jnp.float32),
            jax.ShapeDtypeStruct((rows, columns), jnp.bfloat16),
        ],
        compiler_params=pltpu.CompilerParams(vmem_limit_bytes=VMEM),
        cost_estimate=pl.CostEstimate(
            flops=2 * rows * width * columns, bytes_accessed=30 << 20, transcendentals=0
        ),
    )(x, gain, weight, scales, cosine, sine)


def seen(bounds_ref, first, rows, keys):
    query = first + lax.broadcasted_iota(jnp.int32, (rows, 1), 0)
    low_end, high_end = bounds_ref[0, 0], bounds_ref[0, 1]
    start = jnp.where(query >= high_end, high_end, jnp.where(query >= low_end, low_end, 0))
    key = lax.broadcasted_iota(jnp.int32, (rows, keys), 1)
    return (key <= query) & (key >= start)


def shares_of(query, keys, allowed, score_scale):
    scores = lax.dot_general(
        query, keys, (((1,), (1,)), ((), ())), preferred_element_type=jnp.float32
    )
    scores = jnp.where(allowed, scores * score_scale, masked_score)
    weights = jnp.exp(scores - jnp.max(scores, axis=-1, keepdims=True))
    return weights / jnp.sum(weights, axis=-1, keepdims=True)


def attend_kernel(bounds_ref, query_ref, key_ref, value_ref, out_ref, *, block, score_scale):
    rows = query_ref.shape[0]
    for first in range(0, rows, block):
        last = first + block
        allowed = seen(bounds_ref, first, block, last)
        shares = shares_of(query_ref[first:last, :], key_ref[:last, :], allowed, score_scale)
        out_ref[first:last, :] = jnp.dot(
            shares.astype(jnp.bfloat16), value_ref[:last, :], preferred_element_type=jnp.float32
        ).astype(jnp.bfloat16)


def attend(bounds, turned, heads, kv_heads, head, block):
    rows = turned.shape[0]
    group = heads // kv_heads
    return pl.pallas_call(
        functools.partial(attend_kernel, block=block, score_scale=head ** (-0.5)),
        grid=(heads,),
        in_specs=[
            pl.BlockSpec(memory_space=pltpu.SMEM),
            pl.BlockSpec((rows, head), lambda h: (0, h)),
            pl.BlockSpec((rows, head), lambda h: (0, heads + h // group)),
            pl.BlockSpec((rows, head), lambda h: (0, heads + kv_heads + h // group)),
        ],
        out_specs=pl.BlockSpec((rows, head), lambda h: (0, h)),
        out_shape=jax.ShapeDtypeStruct((rows, heads * head), jnp.bfloat16),
        compiler_params=pltpu.CompilerParams(vmem_limit_bytes=VMEM),
        cost_estimate=pl.CostEstimate(
            flops=2 * heads * rows * rows * head,
            bytes_accessed=6 << 20,
            transcendentals=heads * rows * rows // 2,
        ),
    )(bounds, turned, turned, turned)


def attend_back_kernel(
    bounds_ref, query_ref, key_ref, value_ref, grad_ref, raw_ref, scale_ref, cos_ref, sin_ref,
    back_ref, out_ref, gain_ref, back_out, key_sum, value_sum, *back_scratch, block, heads, group,
    score_scale, sizes,
):
    step = pl.program_id(0)
    rows = query_ref.shape[0]
    scatter_back(step, heads + 2 * heads // group, back_ref, back_out, back_scratch, sizes)
    low, full = jnp.bfloat16, jnp.float32
    kv_heads = heads // group

    def norm_rope_back(grad, raw, scale, cosine, sine):
        inverse = lax.rsqrt(jnp.mean(raw * raw, axis=-1, keepdims=True) + eps_norm)
        normed = raw * inverse
        turned = grad * cosine + pltpu.roll(grad * sine, grad.shape[-1] // 2, 1)
        inner = turned * scale
        back = inverse * (inner - normed * jnp.mean(inner * normed, axis=-1, keepdims=True))
        return back, jnp.sum(turned * normed, axis=0, keepdims=True)

    @pl.when(step == 0)
    def _():
        gain_ref[...] = jnp.zeros_like(gain_ref)

    @pl.when(lax.rem(step, group) == 0)
    def _():
        @pl.when(step < heads)
        def _():
            for kv in range(kv_heads):
                @pl.when(step == kv * group)
                def _():
                    key_sum[kv] = jnp.zeros((rows, key_ref.shape[1]), full)
                    value_sum[kv] = jnp.zeros((rows, key_ref.shape[1]), full)

    @pl.when(step < heads)
    def _():
        kv = jnp.minimum(step // group, kv_heads - 1)
        gains = jnp.zeros((1, query_ref.shape[1]), full)
        for first in range(0, rows, block):
            last = first + block
            query, keys, values = query_ref[first:last, :], key_ref[:last, :], value_ref[:last, :]
            grad = grad_ref[first:last, :]
            allowed = seen(bounds_ref, first, block, last)
            shares = shares_of(query, keys, allowed, score_scale)
            share_grads = lax.dot_general(
                grad, values, (((1,), (1,)), ((), ())), preferred_element_type=full
            )
            centre = jnp.sum(shares * share_grads, axis=-1, keepdims=True)
            score_grads = (shares * (share_grads - centre)).astype(low)
            key_sum[kv, :last, :] += lax.dot_general(
                score_grads, query, (((0,), (0,)), ((), ())), preferred_element_type=full
            )
            value_sum[kv, :last, :] += lax.dot_general(
                shares.astype(low), grad, (((0,), (0,)), ((), ())), preferred_element_type=full
            )
            query_grad = jnp.dot(score_grads, keys, preferred_element_type=full) * score_scale
            back, gain = norm_rope_back(
                query_grad, raw_ref[first:last, :], scale_ref[0:1, :], cos_ref[first:last, :],
                sin_ref[first:last, :],
            )
            out_ref[first:last, :] = back.astype(low)
            gains += gain
        gain_ref[0:1, :] += gains

    @pl.when((step >= heads) & (step < heads + kv_heads))
    def _():
        back, gain = norm_rope_back(
            key_sum[step - heads] * score_scale, raw_ref[...], scale_ref[1:2, :], cos_ref[...],
            sin_ref[...],
        )
        out_ref[...] = back.astype(low)
        gain_ref[1:2, :] += gain

    @pl.when(step >= heads + kv_heads)
    def _():
        out_ref[...] = value_sum[step - heads - kv_heads].astype(low)


def scatter_back(step, steps, back_ref, back_out, scratch, sizes):
    (
        pairs, total, arrived, leaving, landing, own_sem, pair_send, pair_recv, across_send,
        across_recv, line_send, line_recv,
    ) = scratch
    n, n_ctx, n_exp = sizes["dp"], sizes["ctx"], sizes["exp"]
    z, c, k = (lax.axis_index(a) for a in ALL)
    full, low = jnp.float32, jnp.bfloat16

    def remote(source, target, send, recv, device):
        return pltpu.make_async_remote_copy(
            src_ref=source, dst_ref=target, send_sem=send, recv_sem=recv, device_id=device,
            device_id_type=MESH,
        )

    def pair(ahead):
        target = lax.rem(k + ahead, n_exp)
        return remote(
            back_ref.at[:, target], pairs.at[ahead], pair_send.at[ahead], pair_recv.at[ahead],
            {"exp": target},
        )

    def across(ahead):
        target = lax.rem(c + ahead, n_ctx)
        return remote(
            total.at[target], arrived.at[c], across_send.at[ahead], across_recv.at[ahead],
            {"ctx": target},
        )

    def line(target, way):
        return remote(
            leaving.at[target], landing.at[target + (way + 1) // 2], line_send.at[target],
            line_recv.at[target + (way + 1) // 2], {"dp": z + way},
        )

    def in_line(index):
        return (index >= 0) & (index < n)

    own = pltpu.make_async_copy(back_ref.at[:, k], pairs.at[0], own_sem.at[0])

    @pl.when(step == 0)
    def _():
        greet(sizes)
        own.start()
        for ahead in range(1, n_exp):
            pair(ahead).start()

    @pl.when(step == 1)
    def _():
        own.wait()
        for ahead in range(1, n_exp):
            pair(ahead).wait_recv()
        for group in range(n_ctx):
            summed = pairs[0, group].astype(full)
            for ahead in range(1, n_exp):
                summed = summed + pairs[ahead, group].astype(full)
            total[group] = summed.astype(low)
        for ahead in range(1, n_ctx):
            across(ahead).start()
        arrived[c] = total[c]

    for distance in range(n - 1, 0, -1):
        @pl.when(step == min(2 + 3 * (n - 1 - distance), steps - 2))
        def _():
            if distance == n - 1:
                for ahead in range(1, n_ctx):
                    across(ahead).wait_recv()
            for way in (-1, 1):
                target = z + way * distance

                @pl.when(in_line(target))
                def _():
                    @pl.when(in_line(z - way))
                    def _():
                        line(target, way).wait_recv()
                        leaving[target] = (
                            arrived[target].astype(full)
                            + landing[target + (way + 1) // 2].astype(full)
                        ).astype(low)

                    @pl.when(jnp.logical_not(in_line(z - way)))
                    def _():
                        leaving[target] = arrived[target]

                    line(target, way).start()

    @pl.when(step == steps - 1)
    def _():
        back_out[...] = arrived[z].astype(full)
        for way in (-1, 1):
            @pl.when(in_line(z - way))
            def _():
                line(z, way).wait_recv()
                back_out[...] += landing[z + (way + 1) // 2].astype(full)

        for ahead in range(1, n_exp):
            pair(ahead).wait_send()
        for ahead in range(1, n_ctx):
            across(ahead).wait_send()
        for distance in range(1, n):
            for way in (-1, 1):
                target = z + way * distance

                @pl.when(in_line(target))
                def _():
                    line(target, way).wait_send()


def attend_back(
    bounds, turned, grad, raw, scales, cosine, sine, back, heads, kv_heads, head, block, sizes,
    collective,
):
    n, n_ctx, n_exp = sizes["dp"], sizes["ctx"], sizes["exp"]
    b_rows, b_width = back.shape[2:]
    piece = lambda *lead: pltpu.VMEM(lead + (b_rows, b_width), jnp.bfloat16)
    dma = lambda *shape: pltpu.SemaphoreType.DMA(shape)
    rows = turned.shape[0]
    group = heads // kv_heads
    columns = turned.shape[1]
    within = lambda h: jnp.minimum(h, heads - 1)
    tables = pl.BlockSpec((rows, head), lambda h: (0, 0))
    return pl.pallas_call(
        functools.partial(
            attend_back_kernel, block=block, heads=heads, group=group, score_scale=head ** (-0.5),
            sizes=sizes,
        ),
        grid=(heads + 2 * kv_heads,),
        in_specs=[
            pl.BlockSpec(memory_space=pltpu.SMEM),
            pl.BlockSpec((rows, head), lambda h: (0, within(h))),
            pl.BlockSpec((rows, head), lambda h: (0, heads + within(h) // group)),
            pl.BlockSpec((rows, head), lambda h: (0, heads + kv_heads + within(h) // group)),
            pl.BlockSpec((rows, head), lambda h: (0, within(h))),
            pl.BlockSpec((rows, head), lambda h: (0, jnp.minimum(h, heads + kv_heads - 1))),
            pl.BlockSpec((2, head), lambda h: (0, 0)),
            tables,
            tables,
            pl.BlockSpec(memory_space=pl.ANY),
        ],
        out_specs=[
            pl.BlockSpec((rows, head), lambda h: (0, h)),
            pl.BlockSpec((2, head), lambda h: (0, 0)),
            pl.BlockSpec((b_rows, b_width), lambda h: (0, 0)),
        ],
        out_shape=[
            jax.ShapeDtypeStruct((rows, columns), jnp.bfloat16),
            jax.ShapeDtypeStruct((2, head), jnp.float32),
            jax.ShapeDtypeStruct((b_rows, b_width), jnp.float32),
        ],
        scratch_shapes=[pltpu.VMEM((kv_heads, rows, head), jnp.float32)] * 2
        + [piece(n_exp, n_ctx), piece(n_ctx), piece(n_ctx), piece(n), piece(n + 1)]
        + [dma(1), dma(n_exp), dma(n_exp), dma(n_ctx), dma(n_ctx), dma(n), dma(n + 1)],
        compiler_params=pltpu.CompilerParams(
            collective_id=collective, has_side_effects=True, vmem_limit_bytes=VMEM
        ),
        cost_estimate=pl.CostEstimate(
            flops=5 * heads * rows * rows * head,
            bytes_accessed=12 << 20,
            transcendentals=heads * rows * rows // 2,
        ),
    )(bounds, turned, turned, turned, grad, raw, scales, cosine, sine, back)


def square(sizes):
    me = lax.axis_index("ctx")
    return me + 1 - 2 * lax.rem(me, 2), lax.rem(me + 2, 4)


def remote(source, target, send, recv, device):
    return pltpu.make_async_remote_copy(
        src_ref=source, dst_ref=target, send_sem=send, recv_sem=recv, device_id=device,
        device_id_type=MESH,
    )


class SquareGather:
    def __init__(self, sizes, block, whole, send, recv, own_sem):
        self.block, self.whole, self.send, self.recv = block, whole, send, recv
        self.me = lax.axis_index("ctx")
        self.by = square(sizes)
        self.half = block.shape[1] // 2
        self.own = pltpu.make_async_copy(block, whole.at[self.me], own_sem)

    def copy(self, place, part, side, number):
        columns = pl.ds(part * self.half, self.half)
        target = self.whole.at[place, :, columns]
        source = self.block.at[:, columns] if number < 4 else target
        return remote(
            source, target, self.send.at[number], self.recv.at[number], {"ctx": self.by[side]}
        )

    def first(self, number):
        part, side = ((0, 0), (1, 1), (1, 0), (0, 1))[number]
        return self.copy(self.me, part, side, number)

    def start(self):
        self.own.start()
        for number in range(4):
            self.first(number).start()

    def pass_on(self):
        for part in (0, 1):
            self.first(part).wait_recv()
            self.copy(self.by[part], part, 1 - part, 4 + part).start()

    def finish(self):
        for number in (2, 3):
            self.first(number).wait_recv()
        for part in (0, 1):
            last = self.copy(self.by[part], part, 1 - part, 4 + part)
            last.wait_recv()
            last.wait_send()
        for number in range(4):
            self.first(number).wait_send()
        self.own.wait()


class SquareScatter:
    def __init__(self, sizes, parts, far_in, turn_out, turn_in, send, recv):
        self.parts, self.far_in, self.turn_out, self.turn_in = parts, far_in, turn_out, turn_in
        self.send, self.recv = send, recv
        self.me = lax.axis_index("ctx")
        self.by = square(sizes)
        self.far = sizes["ctx"] - 1 - self.me
        half = parts.shape[2] // 2
        self.columns = (pl.ds(0, half), pl.ds(half, half))

    def first(self, side, number):
        place = self.by[side] if number == 0 else self.far
        index = 2 * side + number
        return remote(
            self.parts.at[place, :, self.columns[side]], self.far_in.at[side, number],
            self.send.at[index], self.recv.at[index], {"ctx": self.by[side]},
        )

    def second(self, side):
        return remote(
            self.turn_out.at[side], self.turn_in.at[side], self.send.at[4 + side],
            self.recv.at[4 + side], {"ctx": self.by[1 - side]},
        )

    def start(self, number):
        for side in (0, 1):
            self.first(side, number).start()

    def turn(self):
        for side in (0, 1):
            self.first(side, 1).wait_recv()
            own = self.parts[self.by[1 - side], :, self.columns[side]].astype(jnp.float32)
            self.turn_out[side] = (own + self.far_in[side, 1].astype(jnp.float32)).astype(
                jnp.bfloat16
            )
            self.second(side).start()

    def finish(self, total):
        for side in (0, 1):
            self.first(side, 0).wait_recv()
            self.second(side).wait_recv()
            total[:, self.columns[side]] = (
                self.parts[self.me, :, self.columns[side]].astype(jnp.float32)
                + self.far_in[side, 0].astype(jnp.float32)
                + self.turn_in[side].astype(jnp.float32)
            )

    def close(self):
        for side in (0, 1):
            for number in (0, 1):
                self.first(side, number).wait_send()
            self.second(side).wait_send()


def square_scratch(rows, width):
    half = width // 2
    return [
        pltpu.VMEM((2, 2, rows, half), jnp.bfloat16),
        pltpu.VMEM((2, rows, half), jnp.bfloat16),
        pltpu.VMEM((2, rows, half), jnp.bfloat16),
        pltpu.SemaphoreType.DMA((6,)),
        pltpu.SemaphoreType.DMA((6,)),
    ]


def greet(sizes):
    n = sizes["dp"]
    barrier = pltpu.get_barrier_semaphore()
    me = lax.axis_index("dp")
    for step in (-1, 1):
        @pl.when((me + step >= 0) & (me + step < n))
        def _():
            pl.semaphore_signal(
                barrier, inc=1, device_id={"dp": me + step}, device_id_type=MESH
            )
    number = sizes["ctx"] * sizes["exp"]
    for ahead in range(number - 1, 0, -1):
        pl.semaphore_signal(
            barrier, inc=1, device_id=place(sizes, peer(sizes, ahead)), device_id_type=MESH
        )
    neighbours = (me + n - 1) // n + (2 * n - 2 - me) // n
    pl.semaphore_wait(barrier, number - 1 + neighbours)


def plane_index(sizes):
    return lax.axis_index("ctx") * sizes["exp"] + lax.axis_index("exp")


def peer(sizes, ahead):
    number = sizes["ctx"] * sizes["exp"]
    return lax.rem(plane_index(sizes) + ahead, number)


def place(sizes, index):
    return {"ctx": index // sizes["exp"], "exp": lax.rem(index, sizes["exp"])}


def cut(widths, part):
    pieces = []
    for number, width in enumerate(widths):
        step = min(width, part)
        pieces += [(number, first, step) for first in range(0, width, step)]
    return pieces


def dispatch_kernel(
    attended_ref, back_ref, token_ref, gain_ref, router_ref, chosen_ref, cot_ref, pick_ref,
    grads_out, mixed_out, parts_out, middle_ref, gates_ref,
    branch, far_in, turn_out, turn_in, sq_send, sq_recv, mixed, *refs, sizes, pieces, experts,
):
    outs, refs = (grads_out, mixed_out, parts_out), refs
    columns, packed = refs[:3], refs[3:6]
    line_send, line_recv, plane_send, plane_recv, own_sem = refs[6:]
    n, n_ctx, number = sizes["dp"], sizes["ctx"], sizes["ctx"] * sizes["exp"]
    me, here = lax.axis_index("dp"), plane_index(sizes)
    tokens, width = token_ref.shape
    groups, dests, rows, span = pick_ref.shape
    full, low = jnp.float32, jnp.bfloat16
    greet(sizes)

    def line_copy(f, origin, step):
        a, first, part = pieces[f]
        return remote(
            columns[a].at[origin, :, pl.ds(first, part)],
            columns[a].at[origin, :, pl.ds(first, part)],
            line_send.at[f, origin, (step + 1) // 2],
            line_recv.at[f, origin],
            {"dp": me + step},
        )

    def send_own(f):
        for step in (-1, 1):
            @pl.when((me + step >= 0) & (me + step < n))
            def _():
                line_copy(f, me, step).start()

    def plane_copy(f, ahead):
        a, first, part = pieces[f]
        target = peer(sizes, ahead)
        return remote(
            packed[a].at[target, :, pl.ds(first, part)],
            outs[a].at[here, :, pl.ds(first, part)],
            plane_send.at[f, ahead],
            plane_recv.at[f, ahead],
            place(sizes, target),
        )

    def own_copy(f):
        a, first, part = pieces[f]
        return pltpu.make_async_copy(
            packed[a].at[here, :, pl.ds(first, part)],
            outs[a].at[here, :, pl.ds(first, part)],
            own_sem.at[f],
        )

    def spread(f):
        a, first, part = pieces[f]
        for distance in range(1, n):
            for step in (-1, 1):
                origin = me - step * distance
                beyond = me + step

                @pl.when((origin >= 0) & (origin < n))
                def _():
                    line_copy(f, origin, step).wait_recv()

                    @pl.when((beyond >= 0) & (beyond < n))
                    def _():
                        line_copy(f, origin, step).start()

            if distance == max(1, n - 2) and f + 1 < len(pieces):
                send_own(f + 1)
        for g in range(groups):
            given = columns[a][pl.ds(g * span // tokens, span // tokens), :, pl.ds(first, part)]
            given = given.reshape(span, part)

            @pl.loop(0, dests)
            def _(j):
                packed[a][j, pl.ds(g * rows, rows), pl.ds(first, part)] = jnp.dot(
                    pick_ref[g, j], given, preferred_element_type=full
                ).astype(low)

    def push(f):
        for ahead in range(number - 1, 0, -1):
            plane_copy(f, ahead).start()
        own_copy(f).start()

    columns[0][me] = cot_ref[...]
    send_own(0)

    scatter = SquareScatter(sizes, branch, far_in, turn_out, turn_in, sq_send, sq_recv)

    def project_block(place):
        branch[place] = jnp.dot(
            attended_ref[pl.ds(place * tokens, tokens), :], back_ref[...],
            preferred_element_type=full,
        ).astype(low)

    project_block(scatter.far)
    scatter.start(1)
    for near in scatter.by:
        project_block(near)
    scatter.start(0)
    project_block(scatter.me)
    spread(0)
    scatter.turn()
    push(0)
    scatter.finish(middle_ref)
    middle_ref[...] += token_ref[...].astype(full)
    middle = middle_ref[...]
    inverse = lax.rsqrt(jnp.mean(middle * middle, axis=-1, keepdims=True) + eps_norm)
    mixed[...] = ((middle * inverse) * gain_ref[...]).astype(low)
    columns[1][me] = mixed[...]
    logits = jnp.dot(mixed[...], router_ref[...], preferred_element_type=full)
    chosen = chosen_ref[...] > 0
    logits = jnp.where(chosen, logits, masked_score)
    gates = jnp.exp(logits - jnp.max(logits, axis=-1, keepdims=True))
    gates = jnp.where(chosen, gates, 0.0)
    gates = gates / jnp.sum(gates, axis=-1, keepdims=True)
    gates_ref[...] = gates
    first_part = gates.astype(low).astype(full)
    second_part = (gates - first_part).astype(low).astype(full)
    third_part = gates - first_part - second_part
    lanes = gates.shape[1]
    if experts == lanes:
        terms = jnp.concatenate([first_part, second_part, third_part], axis=1)
    else:
        terms = (
            first_part
            + pltpu.roll(second_part, experts, 1)
            + pltpu.roll(third_part, 2 * experts, 1)
        )
    columns[2][me] = terms.astype(low)

    for f in range(1, len(pieces)):
        spread(f)
        push(f)

    scatter.close()
    for f in range(len(pieces)):
        for distance in range(n):
            for step in (-1, 1):
                origin = me - step * distance
                beyond = me + step

                @pl.when((origin >= 0) & (origin < n) & (beyond >= 0) & (beyond < n))
                def _():
                    line_copy(f, origin, step).wait_send()

        for ahead in range(1, number):
            plane_copy(f, ahead).wait()
        own_copy(f).wait()


def dispatch(attended, back, tokens, gain, router, chosen, cot, pick, experts, sizes, collective, part=512):
    rows_here, width = tokens.shape
    lanes = router.shape[1]
    widths = [width, width, lanes if 3 * experts <= lanes else 3 * lanes]
    n, n_ctx, number = sizes["dp"], sizes["ctx"], sizes["ctx"] * sizes["exp"]
    groups, dests, rows, _ = pick.shape
    pieces = cut(widths, part)
    count = len(pieces)
    vmem, anywhere = pl.BlockSpec(memory_space=pltpu.VMEM), pl.BlockSpec(memory_space=pl.ANY)
    return pl.pallas_call(
        functools.partial(dispatch_kernel, sizes=sizes, pieces=pieces, experts=experts),
        in_specs=[vmem] * 8,
        out_specs=[anywhere] * 3 + [vmem] * 2,
        out_shape=[
            jax.ShapeDtypeStruct((number, groups * rows, columns), jnp.bfloat16)
            for columns in widths
        ]
        + [
            jax.ShapeDtypeStruct((rows_here, width), jnp.float32),
            jax.ShapeDtypeStruct((rows_here, lanes), jnp.float32),
        ],
        scratch_shapes=[pltpu.VMEM((n_ctx, rows_here, width), jnp.bfloat16)]
        + square_scratch(rows_here, width)
        + [pltpu.VMEM((rows_here, width), jnp.bfloat16)]
        + [pltpu.VMEM((n, rows_here, columns), jnp.bfloat16) for columns in widths]
        + [pltpu.VMEM((dests, groups * rows, columns), jnp.bfloat16) for columns in widths]
        + [
            pltpu.SemaphoreType.DMA((count, n, 2)),
            pltpu.SemaphoreType.DMA((count, n)),
            pltpu.SemaphoreType.DMA((count, number)),
            pltpu.SemaphoreType.DMA((count, number)),
            pltpu.SemaphoreType.DMA((count,)),
        ],
        compiler_params=pltpu.CompilerParams(
            collective_id=collective, has_side_effects=True, vmem_limit_bytes=VMEM
        ),
    )(attended, back, tokens, gain, router, chosen, cot, pick)


def combine_kernel(
    rows_ref, dots_ref, pick_ref, carried_ref, middle_ref, cot_ref, gain_ref, gates_ref, router_ref,
    carried_out, whole_ref, middle_grad_ref, gain_grad_ref, router_grad_ref,
    back_rows, back_dots, leave_rows, leave_dots, land_rows, land_dots, total_rows, total_dots,
    sums, branch, line_send, line_recv, plane_send, plane_recv, own_sem, sq_send, sq_recv, sq_own,
    *, sizes, pieces, experts,
):
    sent, back = (dots_ref, rows_ref), (back_dots, back_rows)
    leaving, landing = (leave_dots, leave_rows), (land_dots, land_rows)
    totals = (total_dots, total_rows)
    n, number = sizes["dp"], sizes["ctx"] * sizes["exp"]
    me, here = lax.axis_index("dp"), plane_index(sizes)
    tokens = middle_ref.shape[0]
    groups, span, _ = pick_ref.shape
    rows = rows_ref.shape[1] // groups
    full, low = jnp.float32, jnp.bfloat16
    greet(sizes)

    def plane_copy(f, ahead):
        a, first, part = pieces[f]
        target = peer(sizes, ahead)
        return remote(
            sent[a].at[target, :, pl.ds(first, part)],
            back[a].at[here, :, pl.ds(first, part)],
            plane_send.at[f, ahead],
            plane_recv.at[f, ahead],
            place(sizes, target),
        )

    def own_copy(f):
        a, first, part = pieces[f]
        return pltpu.make_async_copy(
            sent[a].at[here, :, pl.ds(first, part)],
            back[a].at[here, :, pl.ds(first, part)],
            own_sem.at[f],
        )

    for f in range(len(pieces)):
        for ahead in range(number - 1, 0, -1):
            plane_copy(f, ahead).start()
        own_copy(f).start()

    def line_copy(f, target, step):
        a, first, part = pieces[f]
        return remote(
            leaving[a].at[target, :, pl.ds(first, part)],
            landing[a].at[target + (step + 1) // 2, :, pl.ds(first, part)],
            line_send.at[f, target],
            line_recv.at[f, target + (step + 1) // 2],
            {"dp": me + step},
        )

    for f, (a, first, part) in enumerate(pieces):
        columns = pl.ds(first, part)
        for ahead in range(1, number):
            plane_copy(f, ahead).wait_recv()
        own_copy(f).wait()
        for g in range(groups):
            gathered = back[a][:, pl.ds(g * rows, rows), columns].reshape(number * rows, part)
            sums[pl.ds(g * span // tokens, span // tokens), :, pl.ds(0, part)] = jnp.dot(
                pick_ref[g], gathered, preferred_element_type=full
            ).reshape(span // tokens, tokens, part)

        for distance in range(n - 1, 0, -1):
            for step in (-1, 1):
                target = me + step * distance
                behind = me - step

                @pl.when((target >= 0) & (target < n))
                def _():
                    own = sums[target, :, pl.ds(0, part)]

                    @pl.when((behind >= 0) & (behind < n))
                    def _():
                        line_copy(f, target, step).wait_recv()
                        coming = landing[a][target + (step + 1) // 2, :, columns]
                        leaving[a][target, :, columns] = (own + coming.astype(full)).astype(low)

                    @pl.when((behind < 0) | (behind >= n))
                    def _():
                        leaving[a][target, :, columns] = own.astype(low)

                    line_copy(f, target, step).start()

        totals[a][:, columns] = sums[me, :, pl.ds(0, part)]
        for step in (-1, 1):
            @pl.when((me - step >= 0) & (me - step < n))
            def _():
                line_copy(f, me, step).wait_recv()
                totals[a][:, columns] += landing[a][me + (step + 1) // 2, :, columns].astype(full)

    gates = gates_ref[...]
    lanes = gates.shape[1]
    if experts == lanes:
        dots = sum(total_dots[:, k * lanes : (k + 1) * lanes] for k in range(3))
    else:
        dots = total_dots[...]
        dots = dots + pltpu.roll(dots, lanes - experts, 1) + pltpu.roll(dots, lanes - 2 * experts, 1)
    picked = gates * (dots - jnp.sum(gates * dots, axis=-1, keepdims=True))
    logit_grads = picked.astype(low)
    mixed_grad = total_rows[...] + lax.dot_general(
        logit_grads, router_ref[...], (((1,), (1,)), ((), ())), preferred_element_type=full
    )
    middle = middle_ref[...]
    inverse = lax.rsqrt(jnp.mean(middle * middle, axis=-1, keepdims=True) + eps_norm)
    normed = middle * inverse
    gain_grad_ref[...] = jnp.sum(mixed_grad * normed, axis=0, keepdims=True)
    scaled = mixed_grad * gain_ref[...]
    middle_grad = cot_ref[...].astype(full) + inverse * (
        scaled - normed * jnp.mean(scaled * normed, axis=-1, keepdims=True)
    )
    middle_grad_ref[...] = middle_grad
    branch[...] = middle_grad.astype(low)
    collect = SquareGather(sizes, branch, whole_ref, sq_send, sq_recv, sq_own.at[0])
    collect.start()
    router_grad_ref[...] = lax.dot_general(
        logit_grads, (normed * gain_ref[...]).astype(low), (((0,), (0,)), ((), ())),
        preferred_element_type=full,
    )
    collect.pass_on()

    for f in range(len(pieces)):
        for ahead in range(1, number):
            plane_copy(f, ahead).wait_send()
        for distance in range(1, n):
            for step in (-1, 1):
                target = me + step * distance

                @pl.when((target >= 0) & (target < n))
                def _():
                    line_copy(f, target, step).wait_send()
    collect.finish()


def combine(rows, dots, pick, carried, middle, cot, gain, gates, router, experts, sizes, collective, part=512):
    number, back_rows, width = rows.shape
    extra = dots.shape[2]
    tokens = middle.shape[0]
    lanes = router.shape[1]
    n, n_ctx = sizes["dp"], sizes["ctx"]
    low, full = jnp.bfloat16, jnp.float32
    pieces = cut([extra, width], part)
    count = len(pieces)
    both = (width, extra)
    vmem, anywhere = pl.BlockSpec(memory_space=pltpu.VMEM), pl.BlockSpec(memory_space=pl.ANY)
    dma = lambda *shape: pltpu.SemaphoreType.DMA(shape)
    return pl.pallas_call(
        functools.partial(combine_kernel, sizes=sizes, pieces=pieces, experts=experts),
        in_specs=[anywhere, anywhere, vmem, anywhere] + [vmem] * 5,
        out_specs=[anywhere, anywhere] + [vmem] * 3,
        out_shape=[
            jax.ShapeDtypeStruct(carried.shape, carried.dtype),
            jax.ShapeDtypeStruct((n_ctx, tokens, width), low),
            jax.ShapeDtypeStruct((tokens, width), full),
            jax.ShapeDtypeStruct((1, width), full),
            jax.ShapeDtypeStruct((lanes, width), full),
        ],
        input_output_aliases={3: 0},
        scratch_shapes=[pltpu.VMEM((number, back_rows, w), low) for w in both]
        + [pltpu.VMEM((n, tokens, w), low) for w in both]
        + [pltpu.VMEM((n + 1, tokens, w), low) for w in both]
        + [pltpu.VMEM((tokens, w), full) for w in both]
        + [
            pltpu.VMEM((n, tokens, max(p[2] for p in pieces)), full),
            pltpu.VMEM((tokens, width), low),
            dma(count, n), dma(count, n + 1), dma(count, number), dma(count, number), dma(count),
            dma(6), dma(6), dma(1),
        ],
        compiler_params=pltpu.CompilerParams(
            collective_id=collective, has_side_effects=True, vmem_limit_bytes=VMEM
        ),
    )(rows, dots, pick, carried, middle, cot, gain, gates, router)


def expert_kernel(
    here_ref, in_ref, parts_ref, grad_ref, gate_w_ref, up_w_ref, down_w_ref, active_ref, gate_ref,
    up_ref, rows_ref, scaled_ref, dots_ref, *, experts,
):
    full, low = jnp.float32, jnp.bfloat16
    across = (((1,), (1,)), ((), ()))
    grads = grad_ref[0]
    column = lax.broadcasted_iota(jnp.int32, (1, parts_ref.shape[2]), 1)
    mine = lax.rem(column, experts) == here_ref[0]
    parts = parts_ref[0].astype(full)
    gates = jnp.sum(jnp.where(mine & (column < 3 * experts), parts, 0.0), axis=-1, keepdims=True)
    gate_pre = jnp.dot(in_ref[0], gate_w_ref[0], preferred_element_type=full)
    up_pre = jnp.dot(in_ref[0], up_w_ref[0], preferred_element_type=full)
    act_grad = gates * lax.dot_general(grads, down_w_ref[0], across, preferred_element_type=full)
    sigma = 1.0 / (1.0 + jnp.exp(-gate_pre))
    silu = gate_pre * sigma
    activated = silu * up_pre
    active = activated.astype(low)
    active_ref[0] = (gates * activated).astype(low)
    up_grad = (act_grad * silu).astype(low)
    gate_grad = (act_grad * up_pre * sigma * (1.0 + gate_pre * (1.0 - sigma))).astype(low)
    up_ref[0] = up_grad
    gate_ref[0] = gate_grad
    rows_ref[0] = (
        lax.dot_general(gate_grad, gate_w_ref[0], across, preferred_element_type=full)
        + lax.dot_general(up_grad, up_w_ref[0], across, preferred_element_type=full)
    ).astype(low)
    given = jnp.dot(active, down_w_ref[0], preferred_element_type=full).astype(low).astype(full)
    scaled_ref[0] = (gates * given).astype(low)
    dots = jnp.sum(given * grads.astype(full), axis=-1, keepdims=True)
    first = dots.astype(low).astype(full)
    second = (dots - first).astype(low).astype(full)
    third = dots - first - second
    spread = jnp.where(column < experts, first, jnp.where(column < 2 * experts, second, third))
    dots_ref[0] = jnp.where(mine & (column < 3 * experts), spread, 0.0).astype(low)


def expert(here, rows_in, parts, grads, gate_weight, up_weight, down_weight, experts):
    sources, rows, width = rows_in.shape
    inner = gate_weight.shape[2]
    extra = parts.shape[2]
    by_source = lambda columns: pl.BlockSpec((1, rows, columns), lambda i: (i, 0, 0))
    fixed = lambda shape: pl.BlockSpec(
        shape, lambda i: (0, 0, 0), pipeline_mode=pl.Buffered(buffer_count=1)
    )
    out = lambda columns: jax.ShapeDtypeStruct((sources, rows, columns), jnp.bfloat16)
    return pl.pallas_call(
        functools.partial(expert_kernel, experts=experts),
        grid=(sources,),
        in_specs=[
            pl.BlockSpec(memory_space=pltpu.SMEM),
            by_source(width),
            by_source(extra),
            by_source(width),
            fixed((1, width, inner)),
            fixed((1, width, inner)),
            fixed((1, inner, width)),
        ],
        out_specs=[by_source(c) for c in (inner, inner, inner, width, width, extra)],
        out_shape=[out(c) for c in (inner, inner, inner, width, width, extra)],
        compiler_params=pltpu.CompilerParams(vmem_limit_bytes=VMEM),
        cost_estimate=pl.CostEstimate(
            flops=12 * sources * rows * width * inner, bytes_accessed=60 << 20, transcendentals=0
        ),
    )(here, rows_in, parts, grads, gate_weight, up_weight, down_weight)


def gather_kernel(
    token_ref, front_ref, back_ref, route_ref, tokens_ref, fronts_ref, backs_ref, routes_ref,
    held, sq_send, sq_recv, own_sem, fa_send, fa_recv, fl_send, fl_recv, fp_send, fp_recv,
    bl_send, bl_recv, ba_send, ba_recv, bp_send, bp_recv, rl_send, rl_recv, *, sizes,
):
    n, n_ctx, n_exp = sizes["dp"], sizes["ctx"], sizes["exp"]
    z, c, k = (lax.axis_index(a) for a in ALL)
    by_x, by_y = square(sizes)
    far = n_ctx - 1 - c
    half = token_ref.shape[1] // 2
    greet(sizes)

    def remote(source, target, send, recv, device):
        return pltpu.make_async_remote_copy(
            src_ref=source, dst_ref=target, send_sem=send, recv_sem=recv, device_id=device,
            device_id_type=MESH,
        )

    def front_across(ahead):
        target = lax.rem(c + ahead, n_ctx)
        return remote(
            front_ref.at[target], fronts_ref.at[z, c, k], fa_send.at[ahead], fa_recv.at[ahead],
            {"ctx": target},
        )

    def front_line(origin, step):
        here = fronts_ref.at[origin, :, k]
        return remote(
            here, here, fl_send.at[origin, (step + 1) // 2], fl_recv.at[origin], {"dp": z + step}
        )

    def front_pair(origin, ahead):
        here = fronts_ref.at[origin, :, k]
        return remote(
            here, here, fp_send.at[origin, ahead], fp_recv.at[origin, ahead],
            {"exp": lax.rem(k + ahead, n_exp)},
        )

    def back_line(origin, step):
        here = held.at[origin]
        return remote(
            here, here, bl_send.at[origin, (step + 1) // 2], bl_recv.at[origin], {"dp": z + step}
        )

    def back_across(ahead):
        target = lax.rem(c + ahead, n_ctx)
        return remote(
            held.at[target], backs_ref.at[c, k], ba_send.at[ahead], ba_recv.at[ahead],
            {"ctx": target},
        )

    def back_pair(source, ahead):
        here = backs_ref.at[source, k]
        return remote(
            here, here, bp_send.at[source, ahead], bp_recv.at[source, ahead],
            {"exp": lax.rem(k + ahead, n_exp)},
        )

    def route_line(origin, step):
        here = routes_ref.at[origin]
        return remote(
            here, here, rl_send.at[origin, (step + 1) // 2], rl_recv.at[origin], {"dp": z + step}
        )

    def columns(part):
        return pl.ds(part * half, half)

    def token_copy(place, part, to_y, number):
        here = tokens_ref.at[place, :, columns(part)]
        source = token_ref.at[:, columns(part)] if number < 4 else here
        return remote(
            source, here, sq_send.at[number], sq_recv.at[number], {"ctx": by_y if to_y else by_x}
        )

    firsts = [(0, False, 0), (1, True, 1), (1, False, 2), (0, True, 3)]

    def in_line(step):
        return (z + step >= 0) & (z + step < n)

    own_copies = [
        pltpu.make_async_copy(token_ref, tokens_ref.at[c], own_sem.at[0]),
        pltpu.make_async_copy(front_ref.at[c], fronts_ref.at[z, c, k], own_sem.at[1]),
        pltpu.make_async_copy(back_ref, held.at[z], own_sem.at[2]),
        pltpu.make_async_copy(route_ref, routes_ref.at[z], own_sem.at[3]),
    ]
    for copy in own_copies:
        copy.start()
    for ahead in range(1, n_ctx):
        front_across(ahead).start()
    for part, to_y, number in firsts:
        token_copy(c, part, to_y, number).start()
    for copy in own_copies:
        copy.wait()
    for step in (-1, 1):
        @pl.when(in_line(step))
        def _():
            back_line(z, step).start()
            route_line(z, step).start()
    for ahead in range(1, n_ctx):
        front_across(ahead).wait_recv()
    for step in (-1, 1):
        @pl.when(in_line(step))
        def _():
            front_line(z, step).start()
    for ahead in range(1, n_exp):
        front_pair(z, ahead).start()
    token_copy(by_x, 0, False, 0).wait_recv()
    token_copy(by_x, 0, True, 4).start()
    token_copy(by_y, 1, True, 1).wait_recv()
    token_copy(by_y, 1, False, 5).start()

    def pass_on(line, origin, step, after):
        @pl.when((origin >= 0) & (origin < n))
        def _():
            line(origin, step).wait_recv()

            @pl.when(in_line(step))
            def _():
                line(origin, step).start()

            after(origin)

    def to_siblings(origin):
        for ahead in range(1, n_exp):
            front_pair(origin, ahead).start()

    for distance in range(1, n):
        for step in (-1, 1):
            pass_on(front_line, z - step * distance, step, to_siblings)
            pass_on(route_line, z - step * distance, step, lambda origin: None)
    for distance in range(1, n):
        for step in (-1, 1):
            pass_on(back_line, z - step * distance, step, lambda origin: None)
    for ahead in range(1, n_ctx):
        back_across(ahead).start()
    own_back = pltpu.make_async_copy(held.at[c], backs_ref.at[c, k], own_sem.at[4])
    own_back.start()
    own_back.wait()
    for ahead in range(1, n_exp):
        back_pair(c, ahead).start()
    for behind in range(1, n_ctx):
        back_across(behind).wait_recv()
        source = lax.rem(c + n_ctx - behind, n_ctx)
        for ahead in range(1, n_exp):
            back_pair(source, ahead).start()

    token_copy(by_x, 1, False, 2).wait_recv()
    token_copy(by_y, 0, True, 3).wait_recv()
    token_copy(far, 0, True, 4).wait_recv()
    token_copy(far, 1, False, 5).wait_recv()
    for part, to_y, number in firsts + [(0, True, 4), (1, False, 5)]:
        token_copy(c, part, to_y, number).wait_send()
    for ahead in range(1, n_ctx):
        front_across(ahead).wait_send()
        back_across(ahead).wait_send()
    for origin in range(n):
        for ahead in range(1, n_exp):
            front_pair(origin, ahead).wait()
    for source in range(n_ctx):
        for ahead in range(1, n_exp):
            back_pair(source, ahead).wait()
    for line in (route_line, front_line, back_line):
        for distance in range(n):
            for step in (-1, 1):
                origin = z - step * distance

                @pl.when((origin >= 0) & (origin < n) & in_line(step))
                def _():
                    line(origin, step).wait_send()


def gather(tokens, front, back, routes, sizes, collective):
    n, n_ctx, n_exp = sizes["dp"], sizes["ctx"], sizes["exp"]
    _, rows, columns = front.shape
    dma = lambda *shape: pltpu.SemaphoreType.DMA(shape)
    return pl.pallas_call(
        functools.partial(gather_kernel, sizes=sizes),
        in_specs=[pl.BlockSpec(memory_space=pltpu.VMEM)] * 4,
        out_specs=[pl.BlockSpec(memory_space=pl.ANY)] * 4,
        out_shape=[
            jax.ShapeDtypeStruct((n_ctx,) + tokens.shape, tokens.dtype),
            jax.ShapeDtypeStruct((n, n_ctx, n_exp, rows, columns), front.dtype),
            jax.ShapeDtypeStruct((n_ctx, n_exp) + back.shape, back.dtype),
            jax.ShapeDtypeStruct((n,) + routes.shape, routes.dtype),
        ],
        scratch_shapes=[
            pltpu.VMEM((n,) + back.shape, back.dtype),
            dma(6), dma(6), dma(5),
            dma(n_ctx), dma(n_ctx), dma(n, 2), dma(n), dma(n, n_exp), dma(n, n_exp),
            dma(n, 2), dma(n), dma(n_ctx), dma(n_ctx), dma(n_ctx, n_exp), dma(n_ctx, n_exp),
            dma(n, 2), dma(n),
        ],
        compiler_params=pltpu.CompilerParams(
            collective_id=collective, has_side_effects=True, vmem_limit_bytes=VMEM
        ),
    )(tokens, front, back, routes)


def scatter_kernel(
    hidden_ref, front_ref, middle_ref, token_ref, gain_ref, small_ref, sent_ref, pick_ref,
    result_ref, tokens_grad_ref, front_out, output_ref, small_out,
    far_in, turn_out, turn_in, hidden_sum, front_pairs, front_sum, front_line_in, front_low, front_in,
    rows_in, mix_out, mix_in, small_all, small_in,
    h_send, h_recv, fp_send, fp_recv, fl_send, fl_recv, fa_send, fa_recv,
    m_load, ml_send, ml_recv, s_send, s_recv, *, sizes, part,
):
    n, n_ctx, n_exp = sizes["dp"], sizes["ctx"], sizes["exp"]
    devices = n * n_ctx * n_exp
    z, c, k = (lax.axis_index(a) for a in ALL)
    here = (z * n_ctx + c) * n_exp + k
    tokens, width = token_ref.shape
    full, low = jnp.float32, jnp.bfloat16

    barrier = pltpu.get_barrier_semaphore()

    def device_of(index):
        return {
            "dp": index // (n_ctx * n_exp),
            "ctx": lax.rem(index // n_exp, n_ctx),
            "exp": lax.rem(index, n_exp),
        }

    @pl.loop(1, devices)
    def _(ahead):
        pl.semaphore_signal(
            barrier, inc=1, device_id=device_of(lax.rem(here + ahead, devices)),
            device_id_type=MESH,
        )

    pl.semaphore_wait(barrier, devices - 1)

    def in_line(step):
        return (z + step >= 0) & (z + step < n)

    hidden = SquareScatter(sizes, hidden_ref, far_in, turn_out, turn_in, h_send, h_recv)

    def front_pair(ahead):
        target = lax.rem(k + ahead, n_exp)
        return remote(
            front_ref.at[:, :, target], front_pairs.at[ahead - 1], fp_send.at[ahead],
            fp_recv.at[ahead], {"exp": target},
        )

    for ahead in range(1, n_exp):
        front_pair(ahead).start()
    hidden.start(1)
    hidden.start(0)

    def front_line(target, step):
        return remote(
            front_low.at[target], front_line_in.at[target + (step + 1) // 2], fl_send.at[target],
            fl_recv.at[target + (step + 1) // 2], {"dp": z + step},
        )

    def front_across(ahead):
        target = lax.rem(c + ahead, n_ctx)
        return remote(
            front_sum.at[target], front_in.at[c], fa_send.at[ahead], fa_recv.at[ahead],
            {"ctx": target},
        )

    def mix_line(target, step):
        return remote(
            mix_out.at[target], mix_in.at[target + (step + 1) // 2], ml_send.at[target],
            ml_recv.at[target + (step + 1) // 2], {"dp": z + step},
        )

    def load(piece):
        return pltpu.make_async_copy(
            sent_ref.at[:, :, pl.ds(piece * part, part)], rows_in.at[piece % 2],
            m_load.at[piece % 2],
        )

    def front_own(target):
        total = front_ref[target, :, k].astype(full)
        for ahead in range(1, n_exp):
            total = total + front_pairs[ahead - 1, target].astype(full)
        return total

    def line_step(line, leaving, landing, own, distance):
        for step in (-1, 1):
            target = z + step * distance

            @pl.when((target >= 0) & (target < n))
            def _():
                @pl.when(in_line(-step))
                def _():
                    line(target, step).wait_recv()
                    leaving[target] = (
                        own(target) + landing[target + (step + 1) // 2].astype(full)
                    ).astype(low)

                if own is not mix_own:
                    @pl.when(jnp.logical_not(in_line(-step)))
                    def _():
                        leaving[target] = own(target).astype(low)

                line(target, step).start()

    def mix_own(target):
        return mix_out[target].astype(full)

    load(0).start()
    for ahead in range(1, n_exp):
        front_pair(ahead).wait_recv()
    line_step(front_line, front_low, front_line_in, front_own, n - 1)

    groups, span, _ = pick_ref.shape
    number, back_rows, _ = sent_ref.shape
    rows = back_rows // groups
    pieces = width // part
    for piece in range(pieces):
        if piece + 1 < pieces:
            load(piece + 1).start()
        load(piece).wait()
        for g in range(groups):
            gathered = rows_in[piece % 2, :, pl.ds(g * rows, rows), :].reshape(number * rows, part)
            mix_out[pl.ds(g * span // tokens, span // tokens), :, pl.ds(piece * part, part)] = (
                jnp.dot(pick_ref[g], gathered, preferred_element_type=full)
                .astype(low)
                .reshape(span // tokens, tokens, part)
            )
    line_step(mix_line, mix_out, mix_in, mix_own, n - 1)
    hidden.turn()
    for distance in range(n - 2, 0, -1):
        line_step(front_line, front_low, front_line_in, front_own, distance)
        line_step(mix_line, mix_out, mix_in, mix_own, distance)

    hidden.finish(hidden_sum)
    x = token_ref[...].astype(full)
    inverse = lax.rsqrt(jnp.mean(x * x, axis=-1, keepdims=True) + eps_norm)
    normed = x * inverse
    grad = hidden_sum[...]
    scaled = grad * gain_ref[...]
    tokens_grad_ref[...] = (
        middle_ref[...]
        + inverse * (scaled - normed * jnp.mean(scaled * normed, axis=-1, keepdims=True))
    ).astype(low)
    gain_grad = jnp.sum(grad * normed, axis=0, keepdims=True)
    owned = gain_grad.shape[1] // devices
    small_all[...] = small_ref[...]
    for index in range(devices):
        small_all[index, 0:1, 0:owned] = gain_grad[:, index * owned : (index + 1) * owned]

    def small_copy(ahead):
        target = lax.rem(here + ahead, devices)
        return remote(
            small_all.at[target], small_in.at[ahead], s_send.at[ahead], s_recv.at[ahead],
            device_of(target),
        )

    @pl.loop(1, devices)
    def _(ahead):
        small_copy(ahead).start()

    front_sum[...] = front_own(z).astype(low)
    for step in (-1, 1):
        @pl.when(in_line(-step))
        def _():
            front_line(z, step).wait_recv()
            front_sum[...] = (
                front_sum[...].astype(full) + front_line_in[z + (step + 1) // 2].astype(full)
            ).astype(low)
    for ahead in range(1, n_ctx):
        front_across(ahead).start()
    front_in[c] = front_sum[c]
    hidden_sum[...] = result_ref[...] + mix_own(z)
    for step in (-1, 1):
        @pl.when(in_line(-step))
        def _():
            mix_line(z, step).wait_recv()
            hidden_sum[...] += mix_in[z + (step + 1) // 2].astype(full)
    output_ref[...] = hidden_sum[...].astype(low)
    small_out[...] = small_all[here]

    @pl.loop(1, devices)
    def _(ahead):
        small_copy(ahead).wait_recv()
        small_out[...] += small_in[ahead]

    for ahead in range(1, n_ctx):
        front_across(ahead).wait_recv()
    front_out[...] = front_in[...].astype(full)

    @pl.loop(1, devices)
    def _(ahead):
        small_copy(ahead).wait_send()

    hidden.close()
    for ahead in range(1, n_exp):
        front_pair(ahead).wait_send()
    for ahead in range(1, n_ctx):
        front_across(ahead).wait_send()
    for distance in range(1, n):
        for step in (-1, 1):
            target = z + step * distance

            @pl.when((target >= 0) & (target < n))
            def _():
                front_line(target, step).wait_send()
                mix_line(target, step).wait_send()


def scatter(hidden, front, middle, tokens, gain, small, sent, pick, result, sizes, collective, part=512):
    n, n_ctx, n_exp = sizes["dp"], sizes["ctx"], sizes["exp"]
    low, full = jnp.bfloat16, jnp.float32
    _, rows, width = hidden.shape
    f_rows, f_cols = front.shape[3:]
    number, back_rows, _ = sent.shape
    devices, s_rows, s_cols = small.shape
    dma = lambda *shape: pltpu.SemaphoreType.DMA(shape)
    vmem = pl.BlockSpec(memory_space=pltpu.VMEM)
    return pl.pallas_call(
        functools.partial(scatter_kernel, sizes=sizes, part=part),
        in_specs=[vmem] * 6 + [pl.BlockSpec(memory_space=pl.ANY), vmem, vmem],
        out_specs=[vmem] * 4,
        out_shape=[
            jax.ShapeDtypeStruct((rows, width), low),
            jax.ShapeDtypeStruct((n_ctx, f_rows, f_cols), full),
            jax.ShapeDtypeStruct((rows, width), low),
            jax.ShapeDtypeStruct((s_rows, s_cols), full),
        ],
        scratch_shapes=[
            pltpu.VMEM((2, 2, rows, width // 2), low),
            pltpu.VMEM((2, rows, width // 2), low),
            pltpu.VMEM((2, rows, width // 2), low),
            pltpu.VMEM((rows, width), full),
            pltpu.VMEM((n_exp - 1, n, n_ctx, f_rows, f_cols), low),
            pltpu.VMEM((n_ctx, f_rows, f_cols), low),
            pltpu.VMEM((n + 1, n_ctx, f_rows, f_cols), low),
            pltpu.VMEM((n, n_ctx, f_rows, f_cols), low),
            pltpu.VMEM((n_ctx, f_rows, f_cols), low),
            pltpu.VMEM((2, number, back_rows, part), low),
            pltpu.VMEM((n, rows, width), low),
            pltpu.VMEM((n + 1, rows, width), low),
            pltpu.VMEM((devices, s_rows, s_cols), full),
            pltpu.VMEM((devices, s_rows, s_cols), full),
            dma(6), dma(6), dma(n_exp), dma(n_exp), dma(n), dma(n + 1), dma(n_ctx), dma(n_ctx),
            dma(2), dma(n), dma(n + 1), dma(devices), dma(devices),
        ],
        compiler_params=pltpu.CompilerParams(
            collective_id=collective, has_side_effects=True, vmem_limit_bytes=VMEM
        ),
    )(hidden, front, middle, tokens, gain, small, sent, pick, result)


def shards(
    tokens,
    attention_gain,
    query_weight,
    key_weight,
    value_weight,
    query_gain,
    key_gain,
    output_weight,
    mixture_gain,
    router_weight,
    gate_weight,
    up_weight,
    down_weight,
    routes,
    bounds,
    cotangent,
):
    low, full = jnp.bfloat16, jnp.float32
    n_dp, n_ctx, n_exp = (lax.axis_size(a) for a in ALL)
    devices = n_dp * n_ctx * n_exp
    tok_count, width = tokens.shape[1], tokens.shape[2]
    seq_len = tok_count * n_ctx
    head_dim = query_gain.shape[0] * devices
    rows = query_weight.shape[0]
    heads = query_weight.shape[1] // head_dim
    kv_heads = key_weight.shape[1] // head_dim
    kv_here = kv_heads // n_ctx
    group_size = heads // kv_heads
    q_cols, kv_cols = heads * head_dim // n_ctx, kv_here * head_dim
    experts = router_weight.shape[1]
    topk = routes.shape[2]
    base_rows = tok_count * topk // experts
    capacity = base_rows + max(1, base_rows // 8)
    plane = experts // n_dp
    local_experts = gate_weight.shape[0]
    score_scale = head_dim ** (-0.5)
    dp_index = lax.axis_index("dp")

    gain_len = query_gain.shape[0]
    small = jnp.concatenate(
        [
            attention_gain[:, None],
            mixture_gain[:, None],
            jnp.pad(jnp.concatenate([query_gain, key_gain]), (0, rows - 2 * gain_len))[:, None],
            router_weight,
        ],
        axis=1,
    ).astype(low)
    small = jnp.pad(small, ((0, 0), (0, -small.shape[1] % 128)))
    extra = small.shape[1]

    def by_ctx(weight):
        return weight.astype(low).reshape(rows, n_ctx, -1).transpose(1, 0, 2)

    front = jnp.concatenate(
        [
            by_ctx(query_weight),
            by_ctx(key_weight),
            by_ctx(value_weight),
            jnp.broadcast_to(small[None], (n_ctx, rows, extra)),
        ],
        axis=2,
    )
    sizes = {"dp": n_dp, "ctx": n_ctx, "exp": n_exp}
    whole_tokens, front, output_part, column_routes = gather(
        tokens[0], front, output_weight.astype(low), routes[0], sizes, 3
    )
    whole_tokens = whole_tokens.reshape(seq_len, width)
    front = front.reshape(width, -1)
    output_part = output_part.reshape(q_cols, width)
    front_weight = front[:, : q_cols + 2 * kv_cols]
    small = front[:, q_cols + 2 * kv_cols :]
    first_gain = small[:, 0].astype(full)
    second_gain = small[:, 1].astype(full)
    head_gains = small[:, 2].reshape(devices, rows)
    query_scale = head_gains[:, :gain_len].reshape(-1).astype(full)
    key_scale = head_gains[:, gain_len : 2 * gain_len].reshape(-1).astype(full)
    router_full = small[:, 3 : 3 + experts]

    chosen = jnp.any(
        column_routes[:, :, :, None] == jnp.arange(experts, dtype=jnp.int32), axis=2
    )
    hot = lax.dynamic_slice_in_dim(chosen.astype(low), dp_index * plane, plane, 2)
    row_ids = jnp.arange(tok_count, dtype=jnp.int32)
    earlier = (row_ids[None, :] < row_ids[:, None]).astype(low)
    before = jnp.einsum("st,btj->bsj", earlier, hot, preferred_element_type=full)
    together = 2 if 2 * capacity % 16 == 0 and n_dp % 2 == 0 else n_dp
    groups = n_dp // together
    slot_rows = -(-together * capacity // 16) * 16

    def grouped(v):
        return v.reshape(groups, together * tok_count, -1)

    block_first = jnp.tile(jnp.arange(together, dtype=full) * capacity, groups)[:, None, None]
    slot_at = grouped(jnp.where(hot > 0, before + block_first, -1.0))
    slots = jnp.arange(slot_rows, dtype=full)
    pick = (slot_at.transpose(0, 2, 1)[:, :, None, :] == slots[:, None]).astype(low)
    pick_back = (slot_at[:, :, :, None] == slots).astype(low).reshape(groups, -1, plane * slot_rows)

    positions = jnp.arange(seq_len, dtype=jnp.int32)
    cosine, sine = rope_tables(positions, head_dim)
    half = head_dim // 2
    sine = jnp.concatenate([-sine[:, :half], sine[:, half:]], axis=1)
    scales = jnp.stack([query_scale, key_scale])
    heads_here = heads // n_ctx
    hidden, raw, turned = project(
        whole_tokens, first_gain[None], front, q_cols + 2 * kv_cols, scales, cosine, sine,
        heads_here, kv_here, tok_count,
    )
    attended_low = attend(bounds, turned, heads_here, kv_here, head_dim, tok_count)

    lanes = -(-experts // 128) * 128
    router_wide = jnp.pad(router_full, ((0, 0), (0, lanes - experts)))
    own_chosen = jnp.any(
        routes[0][:, :, None] == jnp.arange(lanes, dtype=jnp.int32), axis=1
    ).astype(full)
    grad_rows, expert_in, part_rows, middle, own_gates = dispatch(
        attended_low, output_part, tokens[0], second_gain[None], router_wide, own_chosen,
        cotangent[0], pick, experts, sizes, 1,
    )
    here = (dp_index * n_ctx + lax.axis_index("ctx")) * n_exp + lax.axis_index("exp")
    active, gate_grad, up_grad, row_grads, scaled_out, dot_rows = expert(
        here[None], expert_in, part_rows, grad_rows, gate_weight, up_weight, down_weight, experts
    )
    scaled_out, branch_low, middle_grad, second_gain_grad, router_grad = combine(
        row_grads, dot_rows, pick_back, scaled_out, middle, cotangent[0], second_gain[None],
        own_gates, router_wide, experts, sizes, 2,
    )
    router_grad = router_grad[:experts].T
    branch_low = branch_low.reshape(seq_len, width)
    weight_sum = lambda left, right: jnp.einsum(
        "scd,scf->df", left, right, preferred_element_type=full
    )[None]
    down_grad = weight_sum(active, grad_rows)
    gate_w_grad = weight_sum(expert_in, gate_grad)
    up_w_grad = weight_sum(expert_in, up_grad)
    scaled_out = swap(scaled_out, PLANE)

    output_w_grad = jnp.einsum("ti,td->id", attended_low, branch_low, preferred_element_type=full)
    attended_grad = jnp.einsum("td,id->ti", branch_low, output_part, preferred_element_type=full)
    raw_grad, head_gain_grads, output_share = attend_back(
        bounds, turned, attended_grad.astype(low), raw, scales, cosine, sine,
        output_w_grad.astype(low).reshape(n_ctx, n_exp, -1, width), heads_here, kv_here,
        head_dim, tok_count, sizes, 5,
    )
    query_gain_grad, key_gain_grad = head_gain_grads[0], head_gain_grads[1]
    hidden_grad = jnp.einsum("ti,di->td", raw_grad, front_weight, preferred_element_type=full)
    front_grad = jnp.einsum("td,ti->di", hidden, raw_grad, preferred_element_type=full).astype(low)
    packed = jnp.concatenate(
        [
            jnp.zeros((devices, rows), full),
            second_gain_grad.reshape(devices, -1),
            query_gain_grad.reshape(devices, -1),
            key_gain_grad.reshape(devices, -1),
            router_grad.reshape(devices, -1),
        ],
        axis=1,
    )
    packed = jnp.pad(packed, ((0, 0), (0, -packed.shape[1] % 1024))).reshape(devices, 8, -1)
    tokens_grad, front_grad, output, packed = scatter(
        hidden_grad.astype(low).reshape(n_ctx, tok_count, width),
        front_grad.reshape(n_dp, n_ctx, n_exp, rows, -1),
        middle_grad,
        tokens[0],
        first_gain[None],
        packed,
        scaled_out,
        pick_back,
        middle,
        sizes,
        4,
    )
    output = output[None]
    tokens_grad = tokens_grad[None]
    query_share = front_grad[:, :, :q_cols].transpose(1, 0, 2).reshape(rows, -1)
    key_share = front_grad[:, :, q_cols : q_cols + kv_cols].transpose(1, 0, 2).reshape(rows, -1)
    value_share = front_grad[:, :, q_cols + kv_cols :].transpose(1, 0, 2).reshape(rows, -1)
    packed = packed.reshape(-1)
    ends = [rows, 2 * rows, 2 * rows + gain_len, 2 * rows + 2 * gain_len]
    first_share = packed[: ends[0]]
    second_share = packed[ends[0] : ends[1]]
    query_gain_share = packed[ends[1] : ends[2]]
    key_gain_share = packed[ends[2] : ends[3]]
    router_share = packed[ends[3] : ends[3] + rows * experts].reshape(rows, experts)
    return (
        output,
        tokens_grad,
        first_share,
        query_share,
        key_share,
        value_share,
        query_gain_share,
        key_gain_share,
        output_share,
        second_share,
        router_share,
        gate_w_grad,
        up_w_grad,
        down_grad,
    )


def solution(mesh):
    rows = P(ALL)
    sequences = P(("dp", "exp"), "ctx")
    in_specs = (sequences,) + (rows,) * 12 + (sequences, P(("dp", "exp")), sequences)
    out_specs = (sequences,) * 2 + (rows,) * 12
    return jax.shard_map(shards, mesh=mesh, in_specs=in_specs, out_specs=out_specs, check_vma=False)
```

```python
import functools

import jax
import jax.numpy as jnp
from jax import lax
from jax.experimental import pallas as pl
from jax.experimental.pallas import tpu as pltpu
from jax.sharding import PartitionSpec as P

eps_norm = 1e-06
rope_base = 1000000.0
masked_score = -1e30
ALL = ("dp", "ctx", "exp")
VMEM = 60 << 20
MESH = pl.DeviceIdType.MESH


def rope_tables(positions, width):
    exponents = jnp.arange(width // 2, dtype=jnp.float32) * (2.0 / width)
    frequency = rope_base ** (-exponents)
    angles = positions.astype(jnp.float32)[:, None] * frequency[None, :]
    angles = jnp.concatenate([angles, angles], axis=-1)
    return (jnp.cos(angles), jnp.sin(angles))


def project_kernel(x_ref, gain_ref, weight_ref, scale_ref, cos_ref, sin_ref, hidden_ref, raw_ref, out_ref, *, q_heads, kv_heads):
    x = x_ref[...].astype(jnp.float32)
    inverse = lax.rsqrt(jnp.mean(x * x, axis=-1, keepdims=True) + eps_norm)
    hidden = ((x * inverse) * gain_ref[...]).astype(jnp.bfloat16)
    hidden_ref[...] = hidden
    raw = jnp.dot(
        hidden, weight_ref[:, : raw_ref.shape[1]], preferred_element_type=jnp.float32
    )
    raw_ref[...] = raw
    width = cos_ref.shape[1]
    cosine, sine = cos_ref[...], sin_ref[...]
    for h in range(q_heads + kv_heads):
        here = slice(h * width, (h + 1) * width)
        part = raw[:, here]
        scale = scale_ref[0:1, :] if h < q_heads else scale_ref[1:2, :]
        factor = lax.rsqrt(jnp.mean(part * part, axis=-1, keepdims=True) + eps_norm)
        scaled = part * factor * scale
        turned = pltpu.roll(scaled, width // 2, 1)
        out_ref[:, here] = (scaled * cosine + turned * sine).astype(jnp.bfloat16)
    rest = slice((q_heads + kv_heads) * width, raw.shape[1])
    out_ref[:, rest] = raw[:, rest].astype(jnp.bfloat16)


def project(x, gain, weight, columns, scales, cosine, sine, q_heads, kv_heads, block):
    rows, width = x.shape
    head = cosine.shape[1]
    whole = lambda shape: pl.BlockSpec(shape, lambda i: (0, 0))
    return pl.pallas_call(
        functools.partial(project_kernel, q_heads=q_heads, kv_heads=kv_heads),
        grid=(rows // block,),
        in_specs=[
            pl.BlockSpec((block, width), lambda i: (i, 0)),
            whole((1, width)),
            whole(weight.shape),
            whole((2, head)),
            pl.BlockSpec((block, head), lambda i: (i, 0)),
            pl.BlockSpec((block, head), lambda i: (i, 0)),
        ],
        out_specs=[
            pl.BlockSpec((block, width), lambda i: (i, 0)),
            pl.BlockSpec((block, columns), lambda i: (i, 0)),
            pl.BlockSpec((block, columns), lambda i: (i, 0)),
        ],
        out_shape=[
            jax.ShapeDtypeStruct((rows, width), jnp.bfloat16),
            jax.ShapeDtypeStruct((rows, columns), jnp.float32),
            jax.ShapeDtypeStruct((rows, columns), jnp.bfloat16),
        ],
        compiler_params=pltpu.CompilerParams(vmem_limit_bytes=VMEM),
        cost_estimate=pl.CostEstimate(
            flops=2 * rows * width * columns, bytes_accessed=30 << 20, transcendentals=0
        ),
    )(x, gain, weight, scales, cosine, sine)


def seen(bounds_ref, first, rows, keys):
    query = first + lax.broadcasted_iota(jnp.int32, (rows, 1), 0)
    low_end, high_end = bounds_ref[0, 0], bounds_ref[0, 1]
    start = jnp.where(query >= high_end, high_end, jnp.where(query >= low_end, low_end, 0))
    key = lax.broadcasted_iota(jnp.int32, (rows, keys), 1)
    return (key <= query) & (key >= start)


def shares_of(query, keys, allowed, score_scale):
    scores = lax.dot_general(
        query, keys, (((1,), (1,)), ((), ())), preferred_element_type=jnp.float32
    )
    scores = jnp.where(allowed, scores * score_scale, masked_score)
    weights = jnp.exp(scores - jnp.max(scores, axis=-1, keepdims=True))
    return weights / jnp.sum(weights, axis=-1, keepdims=True)


def attend_kernel(bounds_ref, query_ref, key_ref, value_ref, out_ref, *, block, score_scale):
    rows = query_ref.shape[0]
    for first in range(0, rows, block):
        last = first + block
        allowed = seen(bounds_ref, first, block, last)
        shares = shares_of(query_ref[first:last, :], key_ref[:last, :], allowed, score_scale)
        out_ref[first:last, :] = jnp.dot(
            shares.astype(jnp.bfloat16), value_ref[:last, :], preferred_element_type=jnp.float32
        ).astype(jnp.bfloat16)


def attend(bounds, turned, heads, kv_heads, head, block):
    rows = turned.shape[0]
    group = heads // kv_heads
    return pl.pallas_call(
        functools.partial(attend_kernel, block=block, score_scale=head ** (-0.5)),
        grid=(heads,),
        in_specs=[
            pl.BlockSpec(memory_space=pltpu.SMEM),
            pl.BlockSpec((rows, head), lambda h: (0, h)),
            pl.BlockSpec((rows, head), lambda h: (0, heads + h // group)),
            pl.BlockSpec((rows, head), lambda h: (0, heads + kv_heads + h // group)),
        ],
        out_specs=pl.BlockSpec((rows, head), lambda h: (0, h)),
        out_shape=jax.ShapeDtypeStruct((rows, heads * head), jnp.bfloat16),
        compiler_params=pltpu.CompilerParams(vmem_limit_bytes=VMEM),
        cost_estimate=pl.CostEstimate(
            flops=2 * heads * rows * rows * head,
            bytes_accessed=6 << 20,
            transcendentals=heads * rows * rows // 2,
        ),
    )(bounds, turned, turned, turned)


def square(sizes):
    me = lax.axis_index("ctx")
    return me + 1 - 2 * lax.rem(me, 2), lax.rem(me + 2, 4)


def remote(source, target, send, recv, device):
    return pltpu.make_async_remote_copy(
        src_ref=source, dst_ref=target, send_sem=send, recv_sem=recv, device_id=device,
        device_id_type=MESH,
    )


class SquareGather:
    def __init__(self, sizes, block, whole, send, recv, own_sem):
        self.block, self.whole, self.send, self.recv = block, whole, send, recv
        self.me = lax.axis_index("ctx")
        self.by = square(sizes)
        self.half = block.shape[1] // 2
        self.own = pltpu.make_async_copy(block, whole.at[self.me], own_sem)

    def copy(self, place, part, side, number):
        columns = pl.ds(part * self.half, self.half)
        target = self.whole.at[place, :, columns]
        source = self.block.at[:, columns] if number < 4 else target
        return remote(
            source, target, self.send.at[number], self.recv.at[number], {"ctx": self.by[side]}
        )

    def first(self, number):
        part, side = ((0, 0), (1, 1), (1, 0), (0, 1))[number]
        return self.copy(self.me, part, side, number)

    def start(self):
        self.own.start()
        for number in range(4):
            self.first(number).start()

    def pass_on(self):
        for part in (0, 1):
            self.first(part).wait_recv()
            self.copy(self.by[part], part, 1 - part, 4 + part).start()

    def finish(self):
        for number in (2, 3):
            self.first(number).wait_recv()
        for part in (0, 1):
            last = self.copy(self.by[part], part, 1 - part, 4 + part)
            last.wait_recv()
            last.wait_send()
        for number in range(4):
            self.first(number).wait_send()
        self.own.wait()


class SquareScatter:
    def __init__(self, sizes, parts, far_in, turn_out, turn_in, send, recv, rows):
        self.parts, self.far_in, self.turn_out, self.turn_in = parts, far_in, turn_out, turn_in
        self.send, self.recv, self.rows = send, recv, pl.ds(0, rows)
        self.me = lax.axis_index("ctx")
        self.by = square(sizes)
        self.far = sizes["ctx"] - 1 - self.me
        half = parts.shape[2] // 2
        self.columns = (pl.ds(0, half), pl.ds(half, half))

    def first(self, side, number):
        place = self.by[side] if number == 0 else self.far
        index = 2 * side + number
        return remote(
            self.parts.at[place, self.rows, self.columns[side]], self.far_in.at[side, number],
            self.send.at[index], self.recv.at[index], {"ctx": self.by[side]},
        )

    def second(self, side):
        return remote(
            self.turn_out.at[side], self.turn_in.at[side], self.send.at[4 + side],
            self.recv.at[4 + side], {"ctx": self.by[1 - side]},
        )

    def start(self, number):
        for side in (0, 1):
            self.first(side, number).start()

    def turn(self):
        for side in (0, 1):
            self.first(side, 1).wait_recv()
            own = self.parts[self.by[1 - side], self.rows, self.columns[side]].astype(jnp.float32)
            self.turn_out[side] = (own + self.far_in[side, 1].astype(jnp.float32)).astype(
                jnp.bfloat16
            )
            self.second(side).start()

    def finish(self, total):
        for side in (0, 1):
            self.first(side, 0).wait_recv()
            self.second(side).wait_recv()
            total[:, self.columns[side]] = (
                self.parts[self.me, self.rows, self.columns[side]].astype(jnp.float32)
                + self.far_in[side, 0].astype(jnp.float32)
                + self.turn_in[side].astype(jnp.float32)
            )

    def close(self):
        for side in (0, 1):
            for number in (0, 1):
                self.first(side, number).wait_send()
            self.second(side).wait_send()


def square_scratch(rows, width):
    half = width // 2
    return [
        pltpu.VMEM((2, 2, rows, half), jnp.bfloat16),
        pltpu.VMEM((2, rows, half), jnp.bfloat16),
        pltpu.VMEM((2, rows, half), jnp.bfloat16),
        pltpu.SemaphoreType.DMA((6,)),
        pltpu.SemaphoreType.DMA((6,)),
    ]


def greet(sizes):
    n = sizes["dp"]
    barrier = pltpu.get_barrier_semaphore()
    me = lax.axis_index("dp")
    for step in (-1, 1):
        @pl.when((me + step >= 0) & (me + step < n))
        def _():
            pl.semaphore_signal(
                barrier, inc=1, device_id={"dp": me + step}, device_id_type=MESH
            )
    number = sizes["ctx"] * sizes["exp"]
    for ahead in range(number - 1, 0, -1):
        pl.semaphore_signal(
            barrier, inc=1, device_id=place(sizes, peer(sizes, ahead)), device_id_type=MESH
        )
    neighbours = (me + n - 1) // n + (2 * n - 2 - me) // n
    pl.semaphore_wait(barrier, number - 1 + neighbours)


def plane_index(sizes):
    return lax.axis_index("ctx") * sizes["exp"] + lax.axis_index("exp")


def peer(sizes, ahead):
    number = sizes["ctx"] * sizes["exp"]
    return lax.rem(plane_index(sizes) + ahead, number)


def place(sizes, index):
    return {"ctx": index // sizes["exp"], "exp": lax.rem(index, sizes["exp"])}


def cut(widths, part):
    pieces = []
    for number, width in enumerate(widths):
        step = min(width, part)
        pieces += [(number, first, step) for first in range(0, width, step)]
    return pieces


def dispatch_kernel(
    attended_ref, back_ref, token_ref, gain_ref, router_ref, chosen_ref, cot_ref, pick_ref,
    grads_out, mixed_out, parts_out, middle_ref, gates_ref,
    branch, far_in, turn_out, turn_in, sq_send, sq_recv, mixed, *refs, sizes, pieces, experts,
):
    outs, refs = (grads_out, mixed_out, parts_out), refs
    columns, packed = refs[:3], refs[3:6]
    line_send, line_recv, plane_send, plane_recv, own_sem = refs[6:]
    n, n_ctx, number = sizes["dp"], sizes["ctx"], sizes["ctx"] * sizes["exp"]
    me, here = lax.axis_index("dp"), plane_index(sizes)
    tokens, width = token_ref.shape
    groups, dests, rows, span = pick_ref.shape
    full, low = jnp.float32, jnp.bfloat16
    greet(sizes)

    def line_copy(f, origin, step):
        a, first, part = pieces[f]
        return remote(
            columns[a].at[origin, :, pl.ds(first, part)],
            columns[a].at[origin, :, pl.ds(first, part)],
            line_send.at[f, origin, (step + 1) // 2],
            line_recv.at[f, origin],
            {"dp": me + step},
        )

    def send_own(f):
        for step in (-1, 1):
            @pl.when((me + step >= 0) & (me + step < n))
            def _():
                line_copy(f, me, step).start()

    def plane_copy(f, ahead):
        a, first, part = pieces[f]
        target = peer(sizes, ahead)
        return remote(
            packed[a].at[target, :, pl.ds(first, part)],
            outs[a].at[here, :, pl.ds(first, part)],
            plane_send.at[f, ahead],
            plane_recv.at[f, ahead],
            place(sizes, target),
        )

    def own_copy(f):
        a, first, part = pieces[f]
        return pltpu.make_async_copy(
            packed[a].at[here, :, pl.ds(first, part)],
            outs[a].at[here, :, pl.ds(first, part)],
            own_sem.at[f],
        )

    def spread(f):
        a, first, part = pieces[f]
        for distance in range(1, n):
            for step in (-1, 1):
                origin = me - step * distance
                beyond = me + step

                @pl.when((origin >= 0) & (origin < n))
                def _():
                    line_copy(f, origin, step).wait_recv()

                    @pl.when((beyond >= 0) & (beyond < n))
                    def _():
                        line_copy(f, origin, step).start()

            if distance == max(1, n - 2) and f + 1 < len(pieces):
                send_own(f + 1)
        for g in range(groups):
            given = columns[a][pl.ds(g * span // tokens, span // tokens), :, pl.ds(first, part)]
            given = given.reshape(span, part)

            @pl.loop(0, dests)
            def _(j):
                packed[a][j, pl.ds(g * rows, rows), pl.ds(first, part)] = jnp.dot(
                    pick_ref[g, j], given, preferred_element_type=full
                ).astype(low)

    def push(f):
        for ahead in range(number - 1, 0, -1):
            plane_copy(f, ahead).start()
        own_copy(f).start()

    columns[0][me] = cot_ref[...]
    send_own(0)

    scatter = SquareScatter(
        sizes, branch, far_in, turn_out, turn_in, sq_send, sq_recv, tokens
    )

    def project_block(place):
        branch[place] = jnp.dot(
            attended_ref[pl.ds(place * tokens, tokens), :], back_ref[...],
            preferred_element_type=full,
        ).astype(low)

    project_block(scatter.far)
    scatter.start(1)
    for near in scatter.by:
        project_block(near)
    scatter.start(0)
    project_block(scatter.me)
    spread(0)
    scatter.turn()
    push(0)
    scatter.finish(middle_ref)
    middle_ref[...] += token_ref[...].astype(full)
    middle = middle_ref[...]
    inverse = lax.rsqrt(jnp.mean(middle * middle, axis=-1, keepdims=True) + eps_norm)
    mixed[...] = ((middle * inverse) * gain_ref[...]).astype(low)
    columns[1][me] = mixed[...]
    logits = jnp.dot(mixed[...], router_ref[...], preferred_element_type=full)
    chosen = chosen_ref[...] > 0
    logits = jnp.where(chosen, logits, masked_score)
    gates = jnp.exp(logits - jnp.max(logits, axis=-1, keepdims=True))
    gates = jnp.where(chosen, gates, 0.0)
    gates = gates / jnp.sum(gates, axis=-1, keepdims=True)
    gates_ref[...] = gates
    first_part = gates.astype(low).astype(full)
    second_part = (gates - first_part).astype(low).astype(full)
    third_part = gates - first_part - second_part
    lanes = gates.shape[1]
    if experts == lanes:
        terms = jnp.concatenate([first_part, second_part, third_part], axis=1)
    else:
        terms = (
            first_part
            + pltpu.roll(second_part, experts, 1)
            + pltpu.roll(third_part, 2 * experts, 1)
        )
    columns[2][me] = terms.astype(low)

    for f in range(1, len(pieces)):
        spread(f)
        push(f)

    scatter.close()
    for f in range(len(pieces)):
        for distance in range(n):
            for step in (-1, 1):
                origin = me - step * distance
                beyond = me + step

                @pl.when((origin >= 0) & (origin < n) & (beyond >= 0) & (beyond < n))
                def _():
                    line_copy(f, origin, step).wait_send()

        for ahead in range(1, number):
            plane_copy(f, ahead).wait()
        own_copy(f).wait()


def dispatch(attended, back, tokens, gain, router, chosen, cot, pick, experts, sizes, collective, part=512):
    rows_here, width = tokens.shape
    lanes = router.shape[1]
    widths = [width, width, lanes if 3 * experts <= lanes else 3 * lanes]
    n, n_ctx, number = sizes["dp"], sizes["ctx"], sizes["ctx"] * sizes["exp"]
    groups, dests, rows, _ = pick.shape
    pieces = cut(widths, part)
    count = len(pieces)
    vmem, anywhere = pl.BlockSpec(memory_space=pltpu.VMEM), pl.BlockSpec(memory_space=pl.ANY)
    return pl.pallas_call(
        functools.partial(dispatch_kernel, sizes=sizes, pieces=pieces, experts=experts),
        in_specs=[vmem] * 8,
        out_specs=[anywhere] * 3 + [vmem] * 2,
        out_shape=[
            jax.ShapeDtypeStruct((number, groups * rows, columns), jnp.bfloat16)
            for columns in widths
        ]
        + [
            jax.ShapeDtypeStruct((rows_here, width), jnp.float32),
            jax.ShapeDtypeStruct((rows_here, lanes), jnp.float32),
        ],
        scratch_shapes=[pltpu.VMEM((n_ctx, rows_here, width), jnp.bfloat16)]
        + square_scratch(rows_here, width)
        + [pltpu.VMEM((rows_here, width), jnp.bfloat16)]
        + [pltpu.VMEM((n, rows_here, columns), jnp.bfloat16) for columns in widths]
        + [pltpu.VMEM((dests, groups * rows, columns), jnp.bfloat16) for columns in widths]
        + [
            pltpu.SemaphoreType.DMA((count, n, 2)),
            pltpu.SemaphoreType.DMA((count, n)),
            pltpu.SemaphoreType.DMA((count, number)),
            pltpu.SemaphoreType.DMA((count, number)),
            pltpu.SemaphoreType.DMA((count,)),
        ],
        compiler_params=pltpu.CompilerParams(
            collective_id=collective, has_side_effects=True, vmem_limit_bytes=VMEM
        ),
    )(attended, back, tokens, gain, router, chosen, cot, pick)


def combine_kernel(
    rows_ref, dots_ref, pick_ref, middle_ref, cot_ref, gain_ref, gates_ref, router_ref,
    in_ref, grad_ref, active_ref, gate_ref, up_ref,
    whole_ref, middle_grad_ref, gain_grad_ref, router_grad_ref, gate_out, up_out, down_out,
    back_rows, back_dots, leave_rows, leave_dots, land_rows, land_dots, total_rows, total_dots,
    sums, branch, line_send, line_recv, plane_send, plane_recv, own_sem, sq_send, sq_recv, sq_own,
    *, sizes, pieces, experts,
):
    sent, back = (dots_ref, rows_ref), (back_dots, back_rows)
    leaving, landing = (leave_dots, leave_rows), (land_dots, land_rows)
    totals = (total_dots, total_rows)
    n, number = sizes["dp"], sizes["ctx"] * sizes["exp"]
    me, here = lax.axis_index("dp"), plane_index(sizes)
    tokens = middle_ref.shape[0]
    groups, _, rows, span = pick_ref.shape
    full, low = jnp.float32, jnp.bfloat16
    greet(sizes)

    def plane_copy(f, ahead):
        a, first, part = pieces[f]
        target = peer(sizes, ahead)
        return remote(
            sent[a].at[target, :, pl.ds(first, part)],
            back[a].at[here, :, pl.ds(first, part)],
            plane_send.at[f, ahead],
            plane_recv.at[f, ahead],
            place(sizes, target),
        )

    def own_copy(f):
        a, first, part = pieces[f]
        return pltpu.make_async_copy(
            sent[a].at[here, :, pl.ds(first, part)],
            back[a].at[here, :, pl.ds(first, part)],
            own_sem.at[f],
        )

    for f in range(len(pieces)):
        for ahead in range(number - 1, 0, -1):
            plane_copy(f, ahead).start()
        own_copy(f).start()

    def line_copy(f, target, step):
        a, first, part = pieces[f]
        return remote(
            leaving[a].at[target, :, pl.ds(first, part)],
            landing[a].at[target + (step + 1) // 2, :, pl.ds(first, part)],
            line_send.at[f, target],
            line_recv.at[f, target + (step + 1) // 2],
            {"dp": me + step},
        )

    inner, chunk = active_ref.shape[1], 256
    slots = in_ref.shape[0]

    def weight_sum(left, right, out, by_left):
        def body(left_ref, right_ref, out_ref):
            out_ref[...] = lax.dot_general(
                left_ref[...], right_ref[...], (((0,), (0,)), ((), ())), preferred_element_type=full
            )

        if by_left:
            grid = left.shape[1] // chunk
            specs = [
                pl.BlockSpec((slots, chunk), lambda i: (0, i)),
                pl.BlockSpec((slots, inner), lambda i: (0, 0)),
            ]
            out_spec = pl.BlockSpec((chunk, inner), lambda i: (i, 0))
        else:
            grid = right.shape[1] // chunk
            specs = [
                pl.BlockSpec((slots, inner), lambda i: (0, 0)),
                pl.BlockSpec((slots, chunk), lambda i: (0, i)),
            ]
            out_spec = pl.BlockSpec((inner, chunk), lambda i: (0, i))
        pltpu.emit_pipeline(body, grid=(grid,), in_specs=specs, out_specs=[out_spec])(
            left, right, out
        )

    for f, (a, first, part) in enumerate(pieces):
        columns = pl.ds(first, part)
        if f == 1:
            weight_sum(in_ref, gate_ref, gate_out, True)
        elif f == 2:
            weight_sum(in_ref, up_ref, up_out, True)
        elif f == 3:
            weight_sum(active_ref, grad_ref, down_out, False)
        for ahead in range(1, number):
            plane_copy(f, ahead).wait_recv()
        own_copy(f).wait()
        for g in range(groups):
            gathered = back[a][:, pl.ds(g * rows, rows), columns].reshape(number * rows, part)
            sums[pl.ds(g * span // tokens, span // tokens), :, pl.ds(0, part)] = lax.dot_general(
                pick_ref[g].reshape(number * rows, span), gathered, (((0,), (0,)), ((), ())),
                preferred_element_type=full,
            ).reshape(span // tokens, tokens, part)

        for distance in range(n - 1, 0, -1):
            for step in (-1, 1):
                target = me + step * distance
                behind = me - step

                @pl.when((target >= 0) & (target < n))
                def _():
                    own = sums[target, :, pl.ds(0, part)]

                    @pl.when((behind >= 0) & (behind < n))
                    def _():
                        line_copy(f, target, step).wait_recv()
                        coming = landing[a][target + (step + 1) // 2, :, columns]
                        leaving[a][target, :, columns] = (own + coming.astype(full)).astype(low)

                    @pl.when((behind < 0) | (behind >= n))
                    def _():
                        leaving[a][target, :, columns] = own.astype(low)

                    line_copy(f, target, step).start()

        totals[a][:, columns] = sums[me, :, pl.ds(0, part)]
        for step in (-1, 1):
            @pl.when((me - step >= 0) & (me - step < n))
            def _():
                line_copy(f, me, step).wait_recv()
                totals[a][:, columns] += landing[a][me + (step + 1) // 2, :, columns].astype(full)

    gates = gates_ref[...]
    lanes = gates.shape[1]
    if experts == lanes:
        dots = sum(total_dots[:, k * lanes : (k + 1) * lanes] for k in range(3))
    else:
        dots = total_dots[...]
        dots = dots + pltpu.roll(dots, lanes - experts, 1) + pltpu.roll(dots, lanes - 2 * experts, 1)
    picked = gates * (dots - jnp.sum(gates * dots, axis=-1, keepdims=True))
    logit_grads = picked.astype(low)
    mixed_grad = total_rows[...] + lax.dot_general(
        logit_grads, router_ref[...], (((1,), (1,)), ((), ())), preferred_element_type=full
    )
    middle = middle_ref[...]
    inverse = lax.rsqrt(jnp.mean(middle * middle, axis=-1, keepdims=True) + eps_norm)
    normed = middle * inverse
    gain_grad_ref[...] = jnp.sum(mixed_grad * normed, axis=0, keepdims=True)
    scaled = mixed_grad * gain_ref[...]
    middle_grad = cot_ref[...].astype(full) + inverse * (
        scaled - normed * jnp.mean(scaled * normed, axis=-1, keepdims=True)
    )
    middle_grad_ref[...] = middle_grad
    branch[...] = middle_grad.astype(low)
    collect = SquareGather(sizes, branch, whole_ref, sq_send, sq_recv, sq_own.at[0])
    collect.start()
    router_grad_ref[...] = lax.dot_general(
        logit_grads, (normed * gain_ref[...]).astype(low), (((0,), (0,)), ((), ())),
        preferred_element_type=full,
    )
    collect.pass_on()

    for f in range(len(pieces)):
        for ahead in range(1, number):
            plane_copy(f, ahead).wait_send()
        for distance in range(1, n):
            for step in (-1, 1):
                target = me + step * distance

                @pl.when((target >= 0) & (target < n))
                def _():
                    line_copy(f, target, step).wait_send()
    collect.finish()


def combine(
    rows, dots, pick, middle, cot, gain, gates, router, rows_in, grads_in, active, gate_grad,
    up_grad, experts, sizes, collective, part=512,
):
    number, back_rows, width = rows.shape
    extra = dots.shape[2]
    tokens = middle.shape[0]
    lanes = router.shape[1]
    inner = active.shape[2]
    flat = lambda v: v.reshape(-1, v.shape[2])
    n, n_ctx = sizes["dp"], sizes["ctx"]
    low, full = jnp.bfloat16, jnp.float32
    pieces = cut([extra, width], part)
    count = len(pieces)
    both = (width, extra)
    vmem, anywhere = pl.BlockSpec(memory_space=pltpu.VMEM), pl.BlockSpec(memory_space=pl.ANY)
    dma = lambda *shape: pltpu.SemaphoreType.DMA(shape)
    return pl.pallas_call(
        functools.partial(combine_kernel, sizes=sizes, pieces=pieces, experts=experts),
        in_specs=[anywhere, anywhere] + [vmem] * 6 + [anywhere] * 5,
        out_specs=[anywhere] + [vmem] * 3 + [anywhere] * 3,
        out_shape=[
            jax.ShapeDtypeStruct((n_ctx, tokens, width), low),
            jax.ShapeDtypeStruct((tokens, width), full),
            jax.ShapeDtypeStruct((1, width), full),
            jax.ShapeDtypeStruct((lanes, width), full),
            jax.ShapeDtypeStruct((width, inner), full),
            jax.ShapeDtypeStruct((width, inner), full),
            jax.ShapeDtypeStruct((inner, width), full),
        ],
        scratch_shapes=[pltpu.VMEM((number, back_rows, w), low) for w in both]
        + [pltpu.VMEM((n, tokens, w), low) for w in both]
        + [pltpu.VMEM((n + 1, tokens, w), low) for w in both]
        + [pltpu.VMEM((tokens, w), full) for w in both]
        + [
            pltpu.VMEM((n, tokens, max(p[2] for p in pieces)), full),
            pltpu.VMEM((tokens, width), low),
            dma(count, n), dma(count, n + 1), dma(count, number), dma(count, number), dma(count),
            dma(6), dma(6), dma(1),
        ],
        compiler_params=pltpu.CompilerParams(
            collective_id=collective, has_side_effects=True, vmem_limit_bytes=VMEM
        ),
    )(
        rows, dots, pick, middle, cot, gain, gates, router, flat(rows_in), flat(grads_in),
        flat(active), flat(gate_grad), flat(up_grad),
    )


def expert_kernel(
    here_ref, in_ref, parts_ref, grad_ref, gate_w_ref, up_w_ref, down_w_ref, active_ref, gate_ref,
    up_ref, rows_ref, scaled_ref, dots_ref, *, experts,
):
    full, low = jnp.float32, jnp.bfloat16
    across = (((1,), (1,)), ((), ()))
    grads = grad_ref[0]
    column = lax.broadcasted_iota(jnp.int32, (1, parts_ref.shape[2]), 1)
    mine = lax.rem(column, experts) == here_ref[0]
    parts = parts_ref[0].astype(full)
    gates = jnp.sum(jnp.where(mine & (column < 3 * experts), parts, 0.0), axis=-1, keepdims=True)
    gate_pre = jnp.dot(in_ref[0], gate_w_ref[0], preferred_element_type=full)
    up_pre = jnp.dot(in_ref[0], up_w_ref[0], preferred_element_type=full)
    act_grad = gates * lax.dot_general(grads, down_w_ref[0], across, preferred_element_type=full)
    sigma = 1.0 / (1.0 + jnp.exp(-gate_pre))
    silu = gate_pre * sigma
    activated = silu * up_pre
    active = activated.astype(low)
    active_ref[0] = (gates * activated).astype(low)
    up_grad = (act_grad * silu).astype(low)
    gate_grad = (act_grad * up_pre * sigma * (1.0 + gate_pre * (1.0 - sigma))).astype(low)
    up_ref[0] = up_grad
    gate_ref[0] = gate_grad
    rows_ref[0] = (
        lax.dot_general(gate_grad, gate_w_ref[0], across, preferred_element_type=full)
        + lax.dot_general(up_grad, up_w_ref[0], across, preferred_element_type=full)
    ).astype(low)
    given = jnp.dot(active, down_w_ref[0], preferred_element_type=full).astype(low).astype(full)
    scaled_ref[0] = (gates * given).astype(low)
    dots = jnp.sum(given * grads.astype(full), axis=-1, keepdims=True)
    first = dots.astype(low).astype(full)
    second = (dots - first).astype(low).astype(full)
    third = dots - first - second
    spread = jnp.where(column < experts, first, jnp.where(column < 2 * experts, second, third))
    dots_ref[0] = jnp.where(mine & (column < 3 * experts), spread, 0.0).astype(low)


def expert(here, rows_in, parts, grads, gate_weight, up_weight, down_weight, experts):
    sources, rows, width = rows_in.shape
    inner = gate_weight.shape[2]
    extra = parts.shape[2]
    by_source = lambda columns: pl.BlockSpec((1, rows, columns), lambda i: (i, 0, 0))
    fixed = lambda shape: pl.BlockSpec(
        shape, lambda i: (0, 0, 0), pipeline_mode=pl.Buffered(buffer_count=1)
    )
    out = lambda columns: jax.ShapeDtypeStruct((sources, rows, columns), jnp.bfloat16)
    return pl.pallas_call(
        functools.partial(expert_kernel, experts=experts),
        grid=(sources,),
        in_specs=[
            pl.BlockSpec(memory_space=pltpu.SMEM),
            by_source(width),
            by_source(extra),
            by_source(width),
            fixed((1, width, inner)),
            fixed((1, width, inner)),
            fixed((1, inner, width)),
        ],
        out_specs=[by_source(c) for c in (inner, inner, inner, width, width, extra)],
        out_shape=[out(c) for c in (inner, inner, inner, width, width, extra)],
        compiler_params=pltpu.CompilerParams(vmem_limit_bytes=VMEM),
        cost_estimate=pl.CostEstimate(
            flops=12 * sources * rows * width * inner, bytes_accessed=60 << 20, transcendentals=0
        ),
    )(here, rows_in, parts, grads, gate_weight, up_weight, down_weight)


def gather_kernel(
    token_ref, front_ref, back_ref, route_ref, tokens_ref, fronts_ref, backs_ref, routes_ref,
    held, sq_send, sq_recv, own_sem, fa_send, fa_recv, fl_send, fl_recv, fp_send, fp_recv,
    bl_send, bl_recv, ba_send, ba_recv, bp_send, bp_recv, rl_send, rl_recv, *, sizes,
):
    n, n_ctx, n_exp = sizes["dp"], sizes["ctx"], sizes["exp"]
    z, c, k = (lax.axis_index(a) for a in ALL)
    by_x, by_y = square(sizes)
    far = n_ctx - 1 - c
    half = token_ref.shape[1] // 2
    greet(sizes)

    def remote(source, target, send, recv, device):
        return pltpu.make_async_remote_copy(
            src_ref=source, dst_ref=target, send_sem=send, recv_sem=recv, device_id=device,
            device_id_type=MESH,
        )

    def front_across(ahead):
        target = lax.rem(c + ahead, n_ctx)
        return remote(
            front_ref.at[target], fronts_ref.at[z, c, k], fa_send.at[ahead], fa_recv.at[ahead],
            {"ctx": target},
        )

    def front_line(origin, step):
        here = fronts_ref.at[origin, :, k]
        return remote(
            here, here, fl_send.at[origin, (step + 1) // 2], fl_recv.at[origin], {"dp": z + step}
        )

    def front_pair(origin, ahead):
        here = fronts_ref.at[origin, :, k]
        return remote(
            here, here, fp_send.at[origin, ahead], fp_recv.at[origin, ahead],
            {"exp": lax.rem(k + ahead, n_exp)},
        )

    def back_line(origin, step):
        here = held.at[origin]
        return remote(
            here, here, bl_send.at[origin, (step + 1) // 2], bl_recv.at[origin], {"dp": z + step}
        )

    def back_across(ahead):
        target = lax.rem(c + ahead, n_ctx)
        return remote(
            held.at[target], backs_ref.at[c, k], ba_send.at[ahead], ba_recv.at[ahead],
            {"ctx": target},
        )

    def back_pair(source, ahead):
        here = backs_ref.at[source, k]
        return remote(
            here, here, bp_send.at[source, ahead], bp_recv.at[source, ahead],
            {"exp": lax.rem(k + ahead, n_exp)},
        )

    def route_line(origin, step):
        here = routes_ref.at[origin]
        return remote(
            here, here, rl_send.at[origin, (step + 1) // 2], rl_recv.at[origin], {"dp": z + step}
        )

    def columns(part):
        return pl.ds(part * half, half)

    def token_copy(place, part, to_y, number):
        here = tokens_ref.at[place, :, columns(part)]
        source = token_ref.at[:, columns(part)] if number < 4 else here
        return remote(
            source, here, sq_send.at[number], sq_recv.at[number], {"ctx": by_y if to_y else by_x}
        )

    firsts = [(0, False, 0), (1, True, 1), (1, False, 2), (0, True, 3)]

    def in_line(step):
        return (z + step >= 0) & (z + step < n)

    own_copies = [
        pltpu.make_async_copy(token_ref, tokens_ref.at[c], own_sem.at[0]),
        pltpu.make_async_copy(front_ref.at[c], fronts_ref.at[z, c, k], own_sem.at[1]),
        pltpu.make_async_copy(back_ref, held.at[z], own_sem.at[2]),
        pltpu.make_async_copy(route_ref, routes_ref.at[z], own_sem.at[3]),
    ]
    for copy in own_copies:
        copy.start()
    for ahead in range(1, n_ctx):
        front_across(ahead).start()
    for part, to_y, number in firsts:
        token_copy(c, part, to_y, number).start()
    for copy in own_copies:
        copy.wait()

    def start_line(line):
        for step in (-1, 1):
            @pl.when(in_line(step))
            def _():
                line(z, step).start()

    start_line(back_line)
    start_line(route_line)

    def pass_on(line, origin, step, after):
        @pl.when((origin >= 0) & (origin < n))
        def _():
            line(origin, step).wait_recv()

            @pl.when(in_line(step))
            def _():
                line(origin, step).start()

            after(origin)

    def nothing(origin):
        pass

    def to_siblings(origin):
        for ahead in range(1, n_exp):
            front_pair(origin, ahead).start()

    for ahead in range(1, n_ctx):
        front_across(ahead).wait_recv()
    to_siblings(z)
    for distance in range(1, n):
        for step in (-1, 1):
            pass_on(back_line, z - step * distance, step, nothing)
        if distance == 1:
            token_copy(by_x, 0, False, 0).wait_recv()
            token_copy(by_x, 0, True, 4).start()
            token_copy(by_y, 1, True, 1).wait_recv()
            token_copy(by_y, 1, False, 5).start()
        if distance == max(1, n - 2):
            start_line(front_line)
    for ahead in range(1, n_ctx):
        back_across(ahead).start()
    own_back = pltpu.make_async_copy(held.at[c], backs_ref.at[c, k], own_sem.at[4])
    own_back.start()
    own_back.wait()
    for ahead in range(1, n_exp):
        back_pair(c, ahead).start()
    for distance in range(1, n):
        for step in (-1, 1):
            pass_on(front_line, z - step * distance, step, to_siblings)
            pass_on(route_line, z - step * distance, step, nothing)
    for behind in range(1, n_ctx):
        back_across(behind).wait_recv()
        source = lax.rem(c + n_ctx - behind, n_ctx)
        for ahead in range(1, n_exp):
            back_pair(source, ahead).start()

    token_copy(by_x, 1, False, 2).wait_recv()
    token_copy(by_y, 0, True, 3).wait_recv()
    token_copy(far, 0, True, 4).wait_recv()
    token_copy(far, 1, False, 5).wait_recv()
    for part, to_y, number in firsts + [(0, True, 4), (1, False, 5)]:
        token_copy(c, part, to_y, number).wait_send()
    for ahead in range(1, n_ctx):
        front_across(ahead).wait_send()
        back_across(ahead).wait_send()
    for origin in range(n):
        for ahead in range(1, n_exp):
            front_pair(origin, ahead).wait()
    for source in range(n_ctx):
        for ahead in range(1, n_exp):
            back_pair(source, ahead).wait()
    for line in (route_line, front_line, back_line):
        for distance in range(n):
            for step in (-1, 1):
                origin = z - step * distance

                @pl.when((origin >= 0) & (origin < n) & in_line(step))
                def _():
                    line(origin, step).wait_send()


def gather(tokens, front, back, routes, sizes, collective):
    n, n_ctx, n_exp = sizes["dp"], sizes["ctx"], sizes["exp"]
    _, rows, columns = front.shape
    dma = lambda *shape: pltpu.SemaphoreType.DMA(shape)
    return pl.pallas_call(
        functools.partial(gather_kernel, sizes=sizes),
        in_specs=[pl.BlockSpec(memory_space=pltpu.VMEM)] * 4,
        out_specs=[pl.BlockSpec(memory_space=pl.ANY)] * 4,
        out_shape=[
            jax.ShapeDtypeStruct((n_ctx,) + tokens.shape, tokens.dtype),
            jax.ShapeDtypeStruct((n, n_ctx, n_exp, rows, columns), front.dtype),
            jax.ShapeDtypeStruct((n_ctx, n_exp) + back.shape, back.dtype),
            jax.ShapeDtypeStruct((n,) + routes.shape, routes.dtype),
        ],
        scratch_shapes=[
            pltpu.VMEM((n,) + back.shape, back.dtype),
            dma(6), dma(6), dma(5),
            dma(n_ctx), dma(n_ctx), dma(n, 2), dma(n), dma(n, n_exp), dma(n, n_exp),
            dma(n, 2), dma(n), dma(n_ctx), dma(n_ctx), dma(n_ctx, n_exp), dma(n_ctx, n_exp),
            dma(n, 2), dma(n),
        ],
        compiler_params=pltpu.CompilerParams(
            collective_id=collective, has_side_effects=True, vmem_limit_bytes=VMEM
        ),
    )(tokens, front, back, routes)


def finish_kernel(
    bounds_ref, query_ref, key_ref, value_ref, grad_ref, raw_ref, scale_ref, cos_ref, sin_ref,
    hidden_ref, weight_ref, back_ref, rows_ref, pick_ref, result_ref, middle_ref, token_ref,
    gain_ref, small_ref,
    tokens_grad_ref, front_out, output_ref, back_out, small_out, landed_ref, back_in,
    key_sum, value_sum, raw_grad, head_gains, shared, arrived, back_one, fronts, front_pairs,
    front_in, rows_in, leaving, landing, far_in, turn_out, turn_in, hidden_send, hidden_recv,
    total, loaded, staged, small_all, small_in,
    own_sem, load_sem, stage_sem, bp_send, bp_recv, ba_send, ba_recv, bl_send, bl_recv,
    fp_send, fp_recv, fl_send, fl_recv, fa_send, fa_recv, plane_send, plane_recv, plane_own,
    line_send, line_recv, s_send, s_recv, *, block, heads, group, score_scale, sizes, part, chunk,
):
    step = pl.program_id(0)
    rows, head = query_ref.shape
    low, full = jnp.bfloat16, jnp.float32
    kv_heads = heads // group
    first_chunk = heads + 2 * kv_heads
    n, n_ctx, n_exp = sizes["dp"], sizes["ctx"], sizes["exp"]
    devices, number = n * n_ctx * n_exp, n_ctx * n_exp
    z, c, k = (lax.axis_index(a) for a in ALL)
    here, in_plane = (z * n_ctx + c) * n_exp + k, plane_index(sizes)
    tokens, width = token_ref.shape
    b_rows = back_out.shape[0]
    pieces = width // part
    chunks = width // chunk

    def in_line(index):
        return (index >= 0) & (index < n)

    def device_of(index):
        return {
            "dp": index // number,
            "ctx": lax.rem(index // n_exp, n_ctx),
            "exp": lax.rem(index, n_exp),
        }

    def back_own():
        return pltpu.make_async_copy(
            back_ref.at[:, k], shared.at[:, pl.ds(0, b_rows)], own_sem.at[0]
        )

    def back_pair(ahead):
        target = lax.rem(k + ahead, n_exp)
        return remote(
            back_ref.at[:, target], shared.at[:, pl.ds(ahead * b_rows, b_rows)],
            bp_send.at[ahead], bp_recv.at[ahead], {"exp": target},
        )

    def back_across(ahead):
        target = lax.rem(c + ahead, n_ctx)
        return remote(
            shared.at[target, pl.ds(0, b_rows)], arrived.at[c], ba_send.at[ahead],
            ba_recv.at[ahead], {"ctx": target},
        )

    def back_line(target, way):
        return remote(
            arrived.at[target], back_in.at[target + (way + 1) // 2], bl_send.at[target],
            bl_recv.at[target + (way + 1) // 2], {"dp": z + way},
        )

    def along_line(line, add, distance):
        for way in (-1, 1):
            target = z + way * distance

            @pl.when(in_line(target))
            def _():
                @pl.when(in_line(z - way))
                def _():
                    line(target, way).wait_recv()
                    add(target, target + (way + 1) // 2)

                line(target, way).start()

    def end_line(line, add):
        for way in (-1, 1):
            @pl.when(in_line(z - way))
            def _():
                line(z, way).wait_recv()
                add((way + 1) // 2 + z)

    def close_line(line):
        for distance in range(1, n):
            for way in (-1, 1):
                @pl.when(in_line(z + way * distance))
                def _():
                    line(z + way * distance, way).wait_send()

    def back_arrived(slot):
        copy = pltpu.make_async_copy(back_in.at[slot], back_one, stage_sem.at[1])
        copy.start()
        copy.wait()
        return back_one[...].astype(full)

    def add_back(target, slot):
        arrived[target] = (arrived[target].astype(full) + back_arrived(slot)).astype(low)

    def plane_copy(piece, ahead):
        target = peer(sizes, ahead)
        columns = pl.ds(piece * part, part)
        return remote(
            rows_ref.at[target, :, columns], landed_ref.at[in_plane, :, columns],
            plane_send.at[piece, ahead], plane_recv.at[piece, ahead], place(sizes, target),
        )

    def plane_own_copy(piece):
        columns = pl.ds(piece * part, part)
        return pltpu.make_async_copy(
            rows_ref.at[in_plane, :, columns], landed_ref.at[in_plane, :, columns],
            plane_own.at[piece],
        )

    def push(piece):
        for ahead in range(number - 1, 0, -1):
            plane_copy(piece, ahead).start()
        plane_own_copy(piece).start()

    def small_load():
        return pltpu.make_async_copy(small_ref, small_all, own_sem.at[1])

    @pl.when(step == 0)
    def _():
        head_gains[...] = jnp.zeros_like(head_gains)
        barrier = pltpu.get_barrier_semaphore()

        @pl.loop(1, devices)
        def _(ahead):
            pl.semaphore_signal(
                barrier, inc=1, device_id=device_of(lax.rem(here + ahead, devices)),
                device_id_type=MESH,
            )

        pl.semaphore_wait(barrier, devices - 1)
        back_own().start()
        for ahead in range(1, n_exp):
            back_pair(ahead).start()
        small_load().start()

    @pl.when(step == 1)
    def _():
        back_own().wait()
        for ahead in range(1, n_exp):
            back_pair(ahead).wait_recv()
        for index in range(n_ctx):
            summed = shared[index, 0:b_rows].astype(full)
            for ahead in range(1, n_exp):
                summed = summed + shared[index, ahead * b_rows : (ahead + 1) * b_rows].astype(full)
            shared[index, 0:b_rows] = summed.astype(low)
        for ahead in range(1, n_ctx):
            back_across(ahead).start()
        arrived[c] = shared[c, 0:b_rows]
        for piece in range(pieces):
            push(piece)
        small_load().wait()

    for distance in range(n - 1, 0, -1):
        @pl.when(step == min(6 + 3 * (n - 1 - distance), first_chunk + chunks - 2))
        def _():
            if distance == n - 1:
                for ahead in range(1, n_ctx):
                    back_across(ahead).wait_recv()
                    back_across(ahead).wait_send()
                for ahead in range(1, n_exp):
                    back_pair(ahead).wait_send()
            along_line(back_line, add_back, distance)

    def norm_rope_back(grad, raw, scale, cosine, sine):
        inverse = lax.rsqrt(jnp.mean(raw * raw, axis=-1, keepdims=True) + eps_norm)
        normed = raw * inverse
        turned = grad * cosine + pltpu.roll(grad * sine, grad.shape[-1] // 2, 1)
        inner = turned * scale
        back = inverse * (inner - normed * jnp.mean(inner * normed, axis=-1, keepdims=True))
        return back, jnp.sum(turned * normed, axis=0, keepdims=True)

    for kv in range(kv_heads):
        @pl.when(step == kv * group)
        def _():
            key_sum[kv] = jnp.zeros((rows, head), full)
            value_sum[kv] = jnp.zeros((rows, head), full)

    here_columns = pl.ds(pl.multiple_of(step * head, head), head)

    @pl.when(step < heads)
    def _():
        kv = step // group
        gains = jnp.zeros((1, head), full)
        for first in range(0, rows, block):
            last = first + block
            query, keys, values = query_ref[first:last, :], key_ref[:last, :], value_ref[:last, :]
            grad = grad_ref[first:last, :]
            allowed = seen(bounds_ref, first, block, last)
            shares = shares_of(query, keys, allowed, score_scale)
            share_grads = lax.dot_general(
                grad, values, (((1,), (1,)), ((), ())), preferred_element_type=full
            )
            centre = jnp.sum(shares * share_grads, axis=-1, keepdims=True)
            score_grads = (shares * (share_grads - centre)).astype(low)
            key_sum[kv, :last, :] += lax.dot_general(
                score_grads, query, (((0,), (0,)), ((), ())), preferred_element_type=full
            )
            value_sum[kv, :last, :] += lax.dot_general(
                shares.astype(low), grad, (((0,), (0,)), ((), ())), preferred_element_type=full
            )
            query_grad = jnp.dot(score_grads, keys, preferred_element_type=full) * score_scale
            back, gain = norm_rope_back(
                query_grad, raw_ref[first:last, :], scale_ref[0:1, :], cos_ref[first:last, :],
                sin_ref[first:last, :],
            )
            raw_grad[first:last, here_columns] = back.astype(low)
            gains += gain
        head_gains[0:1, :] += gains

    @pl.when((step >= heads) & (step < heads + kv_heads))
    def _():
        back, gain = norm_rope_back(
            key_sum[step - heads] * score_scale, raw_ref[...], scale_ref[1:2, :], cos_ref[...],
            sin_ref[...],
        )
        raw_grad[:, here_columns] = back.astype(low)
        head_gains[1:2, :] += gain

    @pl.when((step >= heads + kv_heads) & (step < first_chunk))
    def _():
        raw_grad[:, here_columns] = value_sum[step - heads - kv_heads].astype(low)

    @pl.when((step >= first_chunk) & (step < first_chunk + chunks))
    def _():
        q = step - first_chunk
        grads = raw_grad[...]
        shared[:, 0:tokens, pl.ds(pl.multiple_of(q * chunk, chunk), chunk)] = (
            lax.dot_general(
                grads, weight_ref[:, : grads.shape[1]], (((1,), (1,)), ((), ())),
                preferred_element_type=full,
            )
            .astype(low)
            .reshape(n_ctx, tokens, chunk)
        )
        fronts[q // 2, lax.rem(q, 2)] = (
            lax.dot_general(
                hidden_ref[...], grads, (((0,), (0,)), ((), ())), preferred_element_type=full
            )
            .astype(low)
            .reshape(fronts.shape[2:])
        )

    def front_pair(ahead):
        target = lax.rem(k + ahead, n_exp)
        return remote(
            fronts.at[:, :, :, target], front_pairs.at[ahead - 1], fp_send.at[ahead],
            fp_recv.at[ahead], {"exp": target},
        )

    def front_line(target, way):
        return remote(
            fronts.at[target, :, :, k], front_in.at[target + (way + 1) // 2], fl_send.at[target],
            fl_recv.at[target + (way + 1) // 2], {"dp": z + way},
        )

    def front_across(ahead):
        target = lax.rem(c + ahead, n_ctx)
        return remote(
            fronts.at[z, target // (n_ctx // 2), lax.rem(target, n_ctx // 2), k], front_out.at[c],
            fa_send.at[ahead], fa_recv.at[ahead], {"ctx": target},
        )

    def add_front(target, slot):
        fronts[target, :, :, k] = (
            fronts[target, :, :, k].astype(full) + front_in[slot].astype(full)
        ).astype(low)

    def line_of(piece):
        columns = pl.ds(piece * part, part)

        def line(target, way):
            return remote(
                leaving.at[target, :, columns],
                landing.at[target + (way + 1) // 2, :, columns],
                line_send.at[piece, target], line_recv.at[piece, target + (way + 1) // 2],
                {"dp": z + way},
            )

        return line

    def load_rows(piece):
        return pltpu.make_async_copy(
            landed_ref.at[:, :, pl.ds(piece * part, part)], rows_in, load_sem.at[0]
        )

    def load_part(source, piece):
        return pltpu.make_async_copy(
            source.at[:, pl.ds(piece * part, part)], loaded.at[piece % 2], load_sem.at[1 + piece % 2]
        )

    def mix_in(piece):
        for ahead in range(1, number):
            plane_copy(piece, ahead).wait_recv()
        plane_own_copy(piece).wait()
        load_rows(piece).start()
        load_part(result_ref, piece).start()
        load_rows(piece).wait()
        groups, _, back_rows, span = pick_ref.shape
        columns = pl.ds(piece * part, part)
        for g in range(groups):
            gathered = rows_in[:, pl.ds(g * back_rows, back_rows), :]
            leaving[pl.ds(g * span // tokens, span // tokens), :, columns] = (
                lax.dot_general(
                    pick_ref[g].reshape(number * back_rows, span),
                    gathered.reshape(number * back_rows, part),
                    (((0,), (0,)), ((), ())),
                    preferred_element_type=full,
                )
                .astype(low)
                .reshape(span // tokens, tokens, part)
            )

    def start_total(piece):
        columns = pl.ds(piece * part, part)
        load_part(result_ref, piece).wait()
        total[:, columns] = leaving[z, :, columns].astype(full) + loaded[piece % 2]

    def mix_line(piece, distance):
        columns = pl.ds(piece * part, part)

        def add(target, slot):
            leaving[target, :, columns] = (
                leaving[target, :, columns].astype(full) + landing[slot, :, columns].astype(full)
            ).astype(low)

        along_line(line_of(piece), add, distance)

    def mix_end(piece):
        columns = pl.ds(piece * part, part)

        def add(slot):
            total[:, columns] += landing[slot, :, columns].astype(full)

        end_line(line_of(piece), add)

    @pl.when(step == first_chunk + chunks - 1)
    def _():
        mix_in(0)
        mix_line(0, n - 1)

    def small_copy(ahead):
        target = lax.rem(here + ahead, devices)
        return remote(
            small_all.at[target], small_in.at[ahead], s_send.at[ahead], s_recv.at[ahead],
            device_of(target),
        )

    @pl.when(step == first_chunk + chunks)
    def _():
        for ahead in range(1, n_exp):
            front_pair(ahead).start()
        hidden = SquareScatter(
            sizes, shared, far_in, turn_out, turn_in, hidden_send, hidden_recv, tokens
        )
        hidden.start(1)
        hidden.start(0)
        total[0:b_rows, :] = arrived[z].astype(full)

        def add_last(slot):
            total[0:b_rows, :] += back_arrived(slot)

        end_line(back_line, add_last)
        back_store = pltpu.make_async_copy(total.at[pl.ds(0, b_rows)], back_out, stage_sem.at[0])
        back_store.start()
        back_store.wait()
        if n > 2:
            mix_line(0, n - 2)
        for ahead in range(1, n_exp):
            front_pair(ahead).wait_recv()
        for target in range(n):
            summed = fronts[target, :, :, k].astype(full)
            for ahead in range(1, n_exp):
                summed = summed + front_pairs[ahead - 1, target].astype(full)
            fronts[target, :, :, k] = summed.astype(low)
        along_line(front_line, add_front, n - 1)
        for distance in range(n - 3, 0, -1):
            mix_line(0, distance)
        start_total(0)
        mix_end(0)
        front_own = pltpu.make_async_copy(
            fronts.at[z, c // (n_ctx // 2), lax.rem(c, n_ctx // 2), k], front_out.at[c],
            stage_sem.at[0],
        )
        for piece in range(1, pieces):
            mix_in(piece)
            mix_line(piece, n - 1)
            start_total(piece)
            for distance in range(n - 2, 0, -1):
                if piece == 1:
                    along_line(front_line, add_front, distance)
                mix_line(piece, distance)
                if piece == pieces - 1 and distance == max(1, n - 2):
                    hidden.turn()
            if piece == 1:
                end_line(front_line, lambda slot: add_front(z, slot))
                for ahead in range(1, n_ctx):
                    front_across(ahead).start()
                front_own.start()
            mix_end(piece)
        front_own.wait()
        staged[...] = total[...].astype(low)
        output_store = pltpu.make_async_copy(staged, output_ref, stage_sem.at[0])
        output_store.start()

        load_part(middle_ref, 0).start()
        hidden.finish(total)
        x = token_ref[...].astype(full)
        inverse = lax.rsqrt(jnp.mean(x * x, axis=-1, keepdims=True) + eps_norm)
        normed = x * inverse
        grad = total[...]
        gain_grad = jnp.sum(grad * normed, axis=0, keepdims=True)
        owned, gain_owned = width // devices, head // devices
        for index in range(devices):
            small_all[index, 0:1, 0:owned] = gain_grad[:, index * owned : (index + 1) * owned]
            for which in (0, 1):
                small_all[index, 1 + which : 2 + which, 0:gain_owned] = head_gains[
                    which : which + 1, index * gain_owned : (index + 1) * gain_owned
                ]

        @pl.loop(1, devices)
        def _(ahead):
            small_copy(ahead).start()

        scaled = grad * gain_ref[...]
        total[...] = inverse * (scaled - normed * jnp.mean(scaled * normed, axis=-1, keepdims=True))
        output_store.wait()
        for piece in range(pieces):
            if piece + 1 < pieces:
                load_part(middle_ref, piece + 1).start()
            load_part(middle_ref, piece).wait()
            columns = pl.ds(piece * part, part)
            staged[:, columns] = (total[:, columns] + loaded[piece % 2]).astype(low)
        tokens_store = pltpu.make_async_copy(staged, tokens_grad_ref, stage_sem.at[0])
        tokens_store.start()
        small_out[...] = small_all[here]

        @pl.loop(1, devices)
        def _(ahead):
            small_copy(ahead).wait_recv()
            small_out[...] += small_in[ahead]

        for ahead in range(1, n_ctx):
            front_across(ahead).wait()
        tokens_store.wait()

        @pl.loop(1, devices)
        def _(ahead):
            small_copy(ahead).wait_send()

        hidden.close()
        for ahead in range(1, n_exp):
            front_pair(ahead).wait_send()
        for piece in range(pieces):
            for ahead in range(1, number):
                plane_copy(piece, ahead).wait_send()
            close_line(line_of(piece))
        close_line(back_line)
        close_line(front_line)


def finish(
    bounds, turned, grad, raw, scales, cosine, sine, hidden, weight, back, rows_back, pick, result,
    middle_grad, tokens, gain, small, heads, kv_heads, head, sizes, collective, part=512,
):
    n, n_ctx, n_exp = sizes["dp"], sizes["ctx"], sizes["exp"]
    devices, number = n * n_ctx * n_exp, n_ctx * n_exp
    low, full = jnp.bfloat16, jnp.float32
    rows, columns = raw.shape
    count, width = tokens.shape
    b_rows = back.shape[2]
    f_rows = width // devices
    chunk = width // (2 * n)
    group = heads // kv_heads
    back_rows = rows_back.shape[1]
    s_rows, s_cols = small.shape[1:]
    pieces = width // part
    first_chunk = heads + 2 * kv_heads
    within = lambda h: jnp.minimum(h, heads - 1)
    now = lambda h: jnp.clip(h - first_chunk, 0, 2 * n - 1)
    once = pl.Buffered(buffer_count=1)
    whole = lambda shape: pl.BlockSpec(shape, lambda h: (0,) * len(shape), pipeline_mode=once)
    anywhere = pl.BlockSpec(memory_space=pl.ANY)
    vmem = lambda *shape: pltpu.VMEM(shape, low)
    wide = lambda *shape: pltpu.VMEM(shape, full)
    dma = lambda *shape: pltpu.SemaphoreType.DMA(shape)
    half = n_ctx // 2
    return pl.pallas_call(
        functools.partial(
            finish_kernel, block=count, heads=heads, group=group, score_scale=head ** (-0.5),
            sizes=sizes, part=part, chunk=chunk,
        ),
        grid=(first_chunk + 2 * n + 1,),
        in_specs=[
            pl.BlockSpec(memory_space=pltpu.SMEM),
            pl.BlockSpec((rows, head), lambda h: (0, within(h))),
            pl.BlockSpec((rows, head), lambda h: (0, heads + within(h) // group)),
            pl.BlockSpec((rows, head), lambda h: (0, heads + kv_heads + within(h) // group)),
            pl.BlockSpec((rows, head), lambda h: (0, within(h))),
            pl.BlockSpec((rows, head), lambda h: (0, jnp.minimum(h, heads + kv_heads - 1))),
            whole(scales.shape),
            whole(cosine.shape),
            whole(sine.shape),
            pl.BlockSpec((rows, chunk), lambda h: (0, now(h))),
            pl.BlockSpec((chunk, weight.shape[1]), lambda h: (now(h), 0)),
            anywhere,
            anywhere,
            whole(pick.shape),
            anywhere,
            anywhere,
            whole(tokens.shape),
            whole(gain.shape),
            anywhere,
        ],
        out_specs=[anywhere] * 4
        + [pl.BlockSpec((s_rows, s_cols), lambda h: (0, 0)), anywhere, anywhere],
        out_shape=[
            jax.ShapeDtypeStruct((count, width), low),
            jax.ShapeDtypeStruct((n_ctx, f_rows, columns), low),
            jax.ShapeDtypeStruct((count, width), low),
            jax.ShapeDtypeStruct((b_rows, width), full),
            jax.ShapeDtypeStruct((s_rows, s_cols), full),
            jax.ShapeDtypeStruct(rows_back.shape, low),
            jax.ShapeDtypeStruct((n + 1, b_rows, width), low),
        ],
        scratch_shapes=[
            wide(kv_heads, rows, head),
            wide(kv_heads, rows, head),
            vmem(rows, columns),
            wide(2, head),
            vmem(n_ctx, max(count, n_exp * b_rows), width),
            vmem(n_ctx, b_rows, width),
            vmem(b_rows, width),
            vmem(n, 2, half, n_exp, f_rows, columns),
            vmem(n_exp - 1, n, 2, half, f_rows, columns),
            vmem(n + 1, 2, half, f_rows, columns),
            vmem(number, back_rows, part),
            vmem(n, count, width),
            vmem(n + 1, count, width),
            *square_scratch(count, width),
            wide(count, width),
            wide(2, count, part),
            vmem(count, width),
            wide(devices, s_rows, s_cols),
            wide(devices, s_rows, s_cols),
            dma(2), dma(3), dma(2), dma(n_exp), dma(n_exp), dma(n_ctx), dma(n_ctx), dma(n),
            dma(n + 1), dma(n_exp), dma(n_exp), dma(n), dma(n + 1), dma(n_ctx), dma(n_ctx),
            dma(pieces, number), dma(pieces, number), dma(pieces), dma(pieces, n),
            dma(pieces, n + 1), dma(devices), dma(devices),
        ],
        compiler_params=pltpu.CompilerParams(
            collective_id=collective, has_side_effects=True, vmem_limit_bytes=VMEM
        ),
    )(
        bounds, turned, turned, turned, grad, raw, scales, cosine, sine, hidden, weight, back,
        rows_back, pick, result, middle_grad, tokens, gain, small,
    )


def shards(
    tokens,
    attention_gain,
    query_weight,
    key_weight,
    value_weight,
    query_gain,
    key_gain,
    output_weight,
    mixture_gain,
    router_weight,
    gate_weight,
    up_weight,
    down_weight,
    routes,
    bounds,
    cotangent,
):
    low, full = jnp.bfloat16, jnp.float32
    n_dp, n_ctx, n_exp = (lax.axis_size(a) for a in ALL)
    devices = n_dp * n_ctx * n_exp
    tok_count, width = tokens.shape[1], tokens.shape[2]
    seq_len = tok_count * n_ctx
    head_dim = query_gain.shape[0] * devices
    rows = query_weight.shape[0]
    heads = query_weight.shape[1] // head_dim
    kv_heads = key_weight.shape[1] // head_dim
    kv_here = kv_heads // n_ctx
    group_size = heads // kv_heads
    q_cols, kv_cols = heads * head_dim // n_ctx, kv_here * head_dim
    experts = router_weight.shape[1]
    topk = routes.shape[2]
    base_rows = tok_count * topk // experts
    capacity = base_rows + max(1, base_rows // 8)
    plane = experts // n_dp
    local_experts = gate_weight.shape[0]
    score_scale = head_dim ** (-0.5)
    dp_index = lax.axis_index("dp")

    gain_len = query_gain.shape[0]
    small = jnp.concatenate(
        [
            attention_gain[:, None],
            mixture_gain[:, None],
            jnp.pad(jnp.concatenate([query_gain, key_gain]), (0, rows - 2 * gain_len))[:, None],
            router_weight,
        ],
        axis=1,
    ).astype(low)
    small = jnp.pad(small, ((0, 0), (0, -small.shape[1] % 128)))
    extra = small.shape[1]

    def by_ctx(weight):
        return weight.astype(low).reshape(rows, n_ctx, -1).transpose(1, 0, 2)

    front = jnp.concatenate(
        [
            by_ctx(query_weight),
            by_ctx(key_weight),
            by_ctx(value_weight),
            jnp.broadcast_to(small[None], (n_ctx, rows, extra)),
        ],
        axis=2,
    )
    sizes = {"dp": n_dp, "ctx": n_ctx, "exp": n_exp}
    whole_tokens, front, output_part, column_routes = gather(
        tokens[0], front, output_weight.astype(low), routes[0], sizes, 3
    )
    whole_tokens = whole_tokens.reshape(seq_len, width)
    front = front.reshape(width, -1)
    output_part = output_part.reshape(q_cols, width)
    small = front[:, q_cols + 2 * kv_cols :]
    first_gain = small[:, 0].astype(full)
    second_gain = small[:, 1].astype(full)
    head_gains = small[:, 2].reshape(devices, rows)
    query_scale = head_gains[:, :gain_len].reshape(-1).astype(full)
    key_scale = head_gains[:, gain_len : 2 * gain_len].reshape(-1).astype(full)
    router_full = small[:, 3 : 3 + experts]

    chosen = jnp.any(
        column_routes[:, :, :, None] == jnp.arange(experts, dtype=jnp.int32), axis=2
    )
    hot = lax.dynamic_slice_in_dim(chosen.astype(low), dp_index * plane, plane, 2)
    row_ids = jnp.arange(tok_count, dtype=jnp.int32)
    earlier = (row_ids[None, :] < row_ids[:, None]).astype(low)
    before = jnp.einsum("st,btj->bsj", earlier, hot, preferred_element_type=full)
    together = 2 if 2 * capacity % 16 == 0 and n_dp % 2 == 0 else n_dp
    groups = n_dp // together
    slot_rows = -(-together * capacity // 16) * 16

    def grouped(v):
        return v.reshape(groups, together * tok_count, -1)

    block_first = jnp.tile(jnp.arange(together, dtype=full) * capacity, groups)[:, None, None]
    slot_at = grouped(jnp.where(hot > 0, before + block_first, -1.0))
    slots = jnp.arange(slot_rows, dtype=full)
    pick = (slot_at.transpose(0, 2, 1)[:, :, None, :] == slots[:, None]).astype(low)

    positions = jnp.arange(seq_len, dtype=jnp.int32)
    cosine, sine = rope_tables(positions, head_dim)
    half = head_dim // 2
    sine = jnp.concatenate([-sine[:, :half], sine[:, half:]], axis=1)
    scales = jnp.stack([query_scale, key_scale])
    heads_here = heads // n_ctx
    hidden, raw, turned = project(
        whole_tokens, first_gain[None], front, q_cols + 2 * kv_cols, scales, cosine, sine,
        heads_here, kv_here, tok_count,
    )
    attended_low = attend(bounds, turned, heads_here, kv_here, head_dim, tok_count)

    lanes = -(-experts // 128) * 128
    router_wide = jnp.pad(router_full, ((0, 0), (0, lanes - experts)))
    own_chosen = jnp.any(
        routes[0][:, :, None] == jnp.arange(lanes, dtype=jnp.int32), axis=1
    ).astype(full)
    grad_rows, expert_in, part_rows, middle, own_gates = dispatch(
        attended_low, output_part, tokens[0], second_gain[None], router_wide, own_chosen,
        cotangent[0], pick, experts, sizes, 1,
    )
    here = (dp_index * n_ctx + lax.axis_index("ctx")) * n_exp + lax.axis_index("exp")
    active, gate_grad, up_grad, row_grads, scaled_out, dot_rows = expert(
        here[None], expert_in, part_rows, grad_rows, gate_weight, up_weight, down_weight, experts
    )
    branch_low, middle_grad, second_gain_grad, router_grad, gate_w_grad, up_w_grad, down_grad = combine(
        row_grads, dot_rows, pick, middle, cotangent[0], second_gain[None], own_gates, router_wide,
        expert_in, grad_rows, active, gate_grad, up_grad, experts, sizes, 2,
    )
    gate_w_grad, up_w_grad, down_grad = gate_w_grad[None], up_w_grad[None], down_grad[None]
    router_grad = router_grad[:experts].T
    branch_low = branch_low.reshape(seq_len, width)
    output_w_grad = jnp.einsum("ti,td->id", attended_low, branch_low, preferred_element_type=full)
    attended_grad = jnp.einsum("td,id->ti", branch_low, output_part, preferred_element_type=full)
    rest = jnp.concatenate(
        [second_gain_grad.reshape(devices, -1), router_grad.reshape(devices, -1)], axis=1
    )
    columns = -(-rest.shape[1] // (5 * 128)) * 128
    rest = jnp.pad(rest, ((0, 0), (0, 5 * columns - rest.shape[1]))).reshape(devices, 5, columns)
    small = jnp.pad(rest, ((0, 0), (3, 0), (0, 0)))
    tokens_grad, front_grad, output, output_share, small, _, _ = finish(
        bounds, turned, attended_grad.astype(low), raw, scales, cosine, sine, hidden, front,
        output_w_grad.astype(low).reshape(n_ctx, n_exp, -1, width), scaled_out, pick, middle,
        middle_grad, tokens[0], first_gain[None], small, heads_here, kv_here, head_dim, sizes, 4,
        part=512 if n_ctx * n_exp <= 8 else 256,
    )
    tokens_grad = tokens_grad[None]
    output = output[None]
    front_grad = front_grad.astype(full)
    query_share = front_grad[:, :, :q_cols].transpose(1, 0, 2).reshape(rows, -1)
    key_share = front_grad[:, :, q_cols : q_cols + kv_cols].transpose(1, 0, 2).reshape(rows, -1)
    value_share = front_grad[:, :, q_cols + kv_cols :].transpose(1, 0, 2).reshape(rows, -1)
    first_share = small[0, :rows]
    query_gain_share = small[1, :gain_len]
    key_gain_share = small[2, :gain_len]
    rest = small[3:].reshape(-1)
    second_share = rest[:rows]
    router_share = rest[rows : rows + rows * experts].reshape(rows, experts)
    return (
        output,
        tokens_grad,
        first_share,
        query_share,
        key_share,
        value_share,
        query_gain_share,
        key_gain_share,
        output_share,
        second_share,
        router_share,
        gate_w_grad,
        up_w_grad,
        down_grad,
    )


def solution(mesh):
    rows = P(ALL)
    sequences = P(("dp", "exp"), "ctx")
    in_specs = (sequences,) + (rows,) * 12 + (sequences, P(("dp", "exp")), sequences)
    out_specs = (sequences,) * 2 + (rows,) * 12
    return jax.shard_map(shards, mesh=mesh, in_specs=in_specs, out_specs=out_specs, check_vma=False)
```

```python
import functools

import jax
import jax.numpy as jnp
from jax import lax
from jax.experimental import pallas as pl
from jax.experimental.pallas import tpu as pltpu
from jax.sharding import PartitionSpec as P

eps_norm = 1e-06
rope_base = 1000000.0
masked_score = -1e30
ALL = ("dp", "ctx", "exp")
VMEM = 60 << 20
MESH = pl.DeviceIdType.MESH


def rope_tables(positions, width):
    exponents = jnp.arange(width // 2, dtype=jnp.float32) * (2.0 / width)
    frequency = rope_base ** (-exponents)
    angles = positions.astype(jnp.float32)[:, None] * frequency[None, :]
    angles = jnp.concatenate([angles, angles], axis=-1)
    return (jnp.cos(angles), jnp.sin(angles))


def seen(bounds_ref, first, rows, keys):
    query = first + lax.broadcasted_iota(jnp.int32, (rows, 1), 0)
    low_end, high_end = bounds_ref[0, 0], bounds_ref[0, 1]
    start = jnp.where(query >= high_end, high_end, jnp.where(query >= low_end, low_end, 0))
    key = lax.broadcasted_iota(jnp.int32, (rows, keys), 1)
    return (key <= query) & (key >= start)


def shares_of(query, keys, allowed, score_scale):
    scores = lax.dot_general(
        query, keys, (((1,), (1,)), ((), ())), preferred_element_type=jnp.float32
    )
    scores = jnp.where(allowed, scores * score_scale, masked_score)
    weights = jnp.exp(scores - jnp.max(scores, axis=-1, keepdims=True))
    return weights / jnp.sum(weights, axis=-1, keepdims=True)


def square(sizes):
    me = lax.axis_index("ctx")
    return me + 1 - 2 * lax.rem(me, 2), lax.rem(me + 2, 4)


def remote(source, target, send, recv, device):
    return pltpu.make_async_remote_copy(
        src_ref=source, dst_ref=target, send_sem=send, recv_sem=recv, device_id=device,
        device_id_type=MESH,
    )


class SquareGather:
    def __init__(self, sizes, block, whole, send, recv, own_sem):
        self.block, self.whole, self.send, self.recv = block, whole, send, recv
        self.me = lax.axis_index("ctx")
        self.by = square(sizes)
        self.half = block.shape[1] // 2
        self.own = pltpu.make_async_copy(block, whole.at[self.me], own_sem)

    def copy(self, place, part, side, number):
        columns = pl.ds(part * self.half, self.half)
        target = self.whole.at[place, :, columns]
        source = self.block.at[:, columns] if number < 4 else target
        return remote(
            source, target, self.send.at[number], self.recv.at[number], {"ctx": self.by[side]}
        )

    def first(self, number):
        part, side = ((0, 0), (1, 1), (1, 0), (0, 1))[number]
        return self.copy(self.me, part, side, number)

    def start(self):
        self.own.start()
        for number in range(4):
            self.first(number).start()

    def pass_on(self):
        for part in (0, 1):
            self.first(part).wait_recv()
            self.copy(self.by[part], part, 1 - part, 4 + part).start()

    def finish(self):
        for number in (2, 3):
            self.first(number).wait_recv()
        for part in (0, 1):
            last = self.copy(self.by[part], part, 1 - part, 4 + part)
            last.wait_recv()
            last.wait_send()
        for number in range(4):
            self.first(number).wait_send()
        self.own.wait()


class SquareScatter:
    def __init__(self, sizes, parts, far_in, turn_out, turn_in, send, recv, rows):
        self.parts, self.far_in, self.turn_out, self.turn_in = parts, far_in, turn_out, turn_in
        self.send, self.recv, self.rows = send, recv, rows
        self.me = lax.axis_index("ctx")
        self.by = square(sizes)
        self.far = sizes["ctx"] - 1 - self.me
        half = parts.shape[-1] // 2
        self.columns = (pl.ds(0, half), pl.ds(half, half))

    def at(self, place, side):
        if len(self.parts.shape) == 2:
            return pl.ds(place * self.rows, self.rows), self.columns[side]
        return place, pl.ds(0, self.rows), self.columns[side]

    def first(self, side, number):
        place = self.by[side] if number == 0 else self.far
        index = 2 * side + number
        return remote(
            self.parts.at[self.at(place, side)], self.far_in.at[side, number],
            self.send.at[index], self.recv.at[index], {"ctx": self.by[side]},
        )

    def second(self, side):
        return remote(
            self.turn_out.at[side], self.turn_in.at[side], self.send.at[4 + side],
            self.recv.at[4 + side], {"ctx": self.by[1 - side]},
        )

    def start(self, number):
        for side in (0, 1):
            self.first(side, number).start()

    def turn(self):
        for side in (0, 1):
            self.first(side, 1).wait_recv()
            own = self.parts[self.at(self.by[1 - side], side)].astype(jnp.float32)
            self.turn_out[side] = (own + self.far_in[side, 1].astype(jnp.float32)).astype(
                jnp.bfloat16
            )
            self.second(side).start()

    def finish(self, total):
        for side in (0, 1):
            self.first(side, 0).wait_recv()
            self.second(side).wait_recv()
            total[:, self.columns[side]] = (
                self.parts[self.at(self.me, side)].astype(jnp.float32)
                + self.far_in[side, 0].astype(jnp.float32)
                + self.turn_in[side].astype(jnp.float32)
            )

    def close(self):
        for side in (0, 1):
            for number in (0, 1):
                self.first(side, number).wait_send()
            self.second(side).wait_send()


def square_scratch(rows, width):
    half = width // 2
    return [
        pltpu.VMEM((2, 2, rows, half), jnp.bfloat16),
        pltpu.VMEM((2, rows, half), jnp.bfloat16),
        pltpu.VMEM((2, rows, half), jnp.bfloat16),
        pltpu.SemaphoreType.DMA((6,)),
        pltpu.SemaphoreType.DMA((6,)),
    ]


def greet(sizes):
    n = sizes["dp"]
    barrier = pltpu.get_barrier_semaphore()
    me = lax.axis_index("dp")
    for step in (-1, 1):
        @pl.when((me + step >= 0) & (me + step < n))
        def _():
            pl.semaphore_signal(
                barrier, inc=1, device_id={"dp": me + step}, device_id_type=MESH
            )
    number = sizes["ctx"] * sizes["exp"]
    for ahead in range(number - 1, 0, -1):
        pl.semaphore_signal(
            barrier, inc=1, device_id=place(sizes, peer(sizes, ahead)), device_id_type=MESH
        )
    neighbours = (me + n - 1) // n + (2 * n - 2 - me) // n
    pl.semaphore_wait(barrier, number - 1 + neighbours)


def plane_index(sizes):
    return lax.axis_index("ctx") * sizes["exp"] + lax.axis_index("exp")


def peer(sizes, ahead):
    number = sizes["ctx"] * sizes["exp"]
    return lax.rem(plane_index(sizes) + ahead, number)


def place(sizes, index):
    return {"ctx": index // sizes["exp"], "exp": lax.rem(index, sizes["exp"])}


def partner(sizes, turn):
    n_ctx, n_exp = sizes["ctx"], sizes["exp"]
    number = n_ctx * n_exp
    here = plane_index(sizes)
    if (n_ctx, n_exp) != (4, 2):
        return lax.rem(here + turn, number), lax.rem(here + number - turn, number)
    c, k = lax.axis_index("ctx"), lax.axis_index("exp")
    one_of = lambda *turns: sum(jnp.where(turn == t, 1, 0) for t in turns)
    over_x = lax.rem(lax.rem(c, 2) + one_of(2, 4, 6, 7), 2)
    over_y = lax.rem(c // 2 + one_of(3, 5, 6, 7), 2)
    over_k = lax.rem(k + one_of(1, 4, 5, 7), 2)
    other = (over_y * 2 + over_x) * 2 + over_k
    return other, other


def cut(widths, part):
    pieces = []
    for number, width in enumerate(widths):
        step = min(width, part)
        pieces += [(number, first, step) for first in range(0, width, step)]
    return pieces


def staged_rows(slots):
    return min(256, 1 << (slots.bit_length() - 1))


def dispatch_kernel(
    attended_ref, back_ref, token_ref, gain_ref, router_ref, chosen_ref, cot_ref, pick_ref,
    gate_w_ref, up_w_ref, down_w_ref,
    grads_out, mixed_out, parts_out, middle_ref, gates_ref, active_out, gate_out, up_out, rows_out,
    scaled_out, dots_out,
    branch, far_in, turn_out, turn_in, sq_send, sq_recv, cot_column, mixed_column, parts_column,
    packed, packed_parts, parts_in, active, gate_grad, up_grad, scaled, dots,
    line_send, line_recv, plane_send, plane_recv, own_sem, row_send, row_recv, part_send, part_recv,
    load_sem, store_sem, *, sizes, pieces, experts,
):
    outs = (grads_out, mixed_out, parts_out)
    columns = (cot_column, mixed_column, parts_column)
    targets = (packed, packed, packed_parts)
    n, n_ctx, number = sizes["dp"], sizes["ctx"], sizes["ctx"] * sizes["exp"]
    me, here = lax.axis_index("dp"), plane_index(sizes)
    tokens, width = token_ref.shape
    groups, dests, rows, span = pick_ref.shape
    slots = groups * rows
    full, low = jnp.float32, jnp.bfloat16
    greet(sizes)

    def line_copy(f, origin, step):
        a, first, part = pieces[f]
        return remote(
            columns[a].at[origin, :, pl.ds(first, part)],
            columns[a].at[origin, :, pl.ds(first, part)],
            line_send.at[f, origin, (step + 1) // 2],
            line_recv.at[f, origin],
            {"dp": me + step},
        )

    def send_own(f):
        for step in (-1, 1):
            @pl.when((me + step >= 0) & (me + step < n))
            def _():
                line_copy(f, me, step).start()

    def plane_copy(f, ahead):
        a, first, part = pieces[f]
        target = peer(sizes, ahead)
        return remote(
            packed.at[target, pl.ds(0, slots), pl.ds(first, part)],
            outs[a].at[here, :, pl.ds(first, part)],
            plane_send.at[f, ahead],
            plane_recv.at[f, ahead],
            place(sizes, target),
        )

    def own_copy(f):
        a, first, part = pieces[f]
        return pltpu.make_async_copy(
            packed.at[here, pl.ds(0, slots), pl.ds(first, part)],
            outs[a].at[here, :, pl.ds(first, part)],
            own_sem.at[f],
        )

    cots = len([p for p in pieces if p[0] == 0])
    early = cots + cots // 2
    last_columns = pl.ds(pieces[early][1], width - pieces[early][1])

    def row_copy(turn):
        target, _ = partner(sizes, turn)
        return remote(
            packed.at[target, pl.ds(0, slots), last_columns], mixed_out.at[here, :, last_columns],
            row_send.at[turn], row_recv.at[turn], place(sizes, target),
        )

    def part_copy(turn):
        target, _ = partner(sizes, turn)
        return remote(
            packed_parts.at[target], parts_out.at[here], part_send.at[turn], part_recv.at[turn],
            place(sizes, target),
        )

    def send_rows(turns):
        for turn in turns:
            part_copy(turn).start()
            row_copy(turn).start()

    def spread(f):
        for distance in range(1, n):
            for step in (-1, 1):
                origin = me - step * distance
                beyond = me + step

                @pl.when((origin >= 0) & (origin < n))
                def _():
                    line_copy(f, origin, step).wait_recv()

                    @pl.when((beyond >= 0) & (beyond < n))
                    def _():
                        line_copy(f, origin, step).start()

            if distance == max(1, n - 2) and f + 1 < len(pieces):
                send_own(f + 1)

    def pick_rows(f):
        a, first, part = pieces[f]
        for g in range(groups):
            given = columns[a][pl.ds(g * span // tokens, span // tokens), :, pl.ds(first, part)]
            given = given.reshape(span, part)

            @pl.loop(0, dests)
            def _(j):
                targets[a][j, pl.ds(g * rows, rows), pl.ds(first, part)] = jnp.dot(
                    pick_ref[g, j], given, preferred_element_type=full
                ).astype(low)

    def push(f):
        for ahead in range(number - 1, 0, -1):
            plane_copy(f, ahead).start()
        own_copy(f).start()

    deep = staged_rows(slots)
    blocks = back_ref.shape[0] // deep
    weight_copies = [
        pltpu.make_async_copy(
            back_ref.at[pl.ds(i * deep, deep)], packed.at[i, pl.ds(0, deep)], load_sem.at[i]
        )
        for i in range(blocks)
    ]
    own_cot = pltpu.make_async_copy(cot_ref, cot_column.at[me], own_sem.at[0])
    own_cot.start()
    for copy in weight_copies:
        copy.start()
    own_cot.wait()
    send_own(0)
    for copy in weight_copies:
        copy.wait()

    scatter = SquareScatter(sizes, branch, far_in, turn_out, turn_in, sq_send, sq_recv, tokens)

    def project_block(index):
        at = pl.ds(index * tokens, tokens)
        total = jnp.zeros((tokens, width), full)
        for i in range(blocks):
            total += jnp.dot(
                attended_ref[at, i * deep : (i + 1) * deep], packed[i, 0:deep],
                preferred_element_type=full,
            )
        branch[at] = total.astype(low)

    project_block(scatter.far)
    scatter.start(1)
    for near in scatter.by:
        project_block(near)
    scatter.start(0)
    project_block(scatter.me)
    spread(0)
    pick_rows(0)
    scatter.turn()
    push(0)
    scatter.finish(middle_ref)
    middle_ref[...] += token_ref[...].astype(full)
    middle = middle_ref[...]
    inverse = lax.rsqrt(jnp.mean(middle * middle, axis=-1, keepdims=True) + eps_norm)
    mixed_column[me] = ((middle * inverse) * gain_ref[...]).astype(low)
    logits = jnp.dot(mixed_column[me], router_ref[...], preferred_element_type=full)
    chosen = chosen_ref[...] > 0
    logits = jnp.where(chosen, logits, masked_score)
    gates = jnp.exp(logits - jnp.max(logits, axis=-1, keepdims=True))
    gates = jnp.where(chosen, gates, 0.0)
    gates = gates / jnp.sum(gates, axis=-1, keepdims=True)
    gates_ref[...] = gates
    first_part = gates.astype(low).astype(full)
    second_part = (gates - first_part).astype(low).astype(full)
    third_part = gates - first_part - second_part
    lanes = gates.shape[1]
    if experts == lanes:
        terms = jnp.concatenate([first_part, second_part, third_part], axis=1)
    else:
        terms = (
            first_part
            + pltpu.roll(second_part, experts, 1)
            + pltpu.roll(third_part, 2 * experts, 1)
        )
    parts_column[me] = terms.astype(low)

    def sent(f):
        for ahead in range(1, number):
            plane_copy(f, ahead).wait_send()
        own_copy(f).wait()

    for f in range(1, cots):
        spread(f)
        pick_rows(f)
        push(f)
    scatter.close()
    for f in range(cots, early):
        spread(f)
        sent(f - cots)
        pick_rows(f)
        push(f)
    for f in range(early, len(pieces)):
        spread(f)
    for f in range(early - cots, cots):
        sent(f)

    def pick_turns(first_turn, last_turn):
        @pl.loop(first_turn, last_turn)
        def _(turn):
            j, _ = partner(sizes, turn)
            for a, first, part in pieces[early:]:
                for g in range(groups):
                    given = columns[a][
                        pl.ds(g * span // tokens, span // tokens), :, pl.ds(first, part)
                    ]
                    targets[a][j, pl.ds(g * rows, rows), pl.ds(first, part)] = jnp.dot(
                        pick_ref[g, j], given.reshape(span, part), preferred_element_type=full
                    ).astype(low)

    waves = [range(2, number)]
    pick_turns(1, waves[0][-1] + 1)
    send_rows((*waves[0], 1))
    pick_turns(0, 1)
    if len(waves) > 1:
        pick_turns(waves[1][0], number)
    own_rows = [
        pltpu.make_async_copy(
            packed.at[here, pl.ds(0, slots), last_columns], mixed_out.at[here, :, last_columns],
            own_sem.at[0],
        ),
        pltpu.make_async_copy(packed_parts.at[here], parts_out.at[here], own_sem.at[1]),
    ]
    for copy in own_rows:
        copy.start()
    for copy in own_rows:
        copy.wait()
    for f in range(cots, early):
        own_copy(f).wait()

    across = (((1,), (1,)), ((), ()))
    expert = me * number + here
    column = lax.broadcasted_iota(jnp.int32, (1, parts_in.shape[1]), 1)
    mine = (lax.rem(column, experts) == expert) & (column < 3 * experts)
    in_rows, in_grads, out_rows = (pl.ds(i * slots, slots) for i in range(3))
    cut_rows = slots

    def stores(source):
        given = (
            (branch.at[out_rows], rows_out), (scaled, scaled_out), (active, active_out),
            (gate_grad, gate_out), (up_grad, up_out), (dots, dots_out),
        )
        return [
            pltpu.make_async_copy(value, out.at[source], store_sem.at[i])
            for i, (value, out) in enumerate(given)
        ]

    @pl.loop(0, number)
    def _(i):
        _, source = partner(sizes, i)
        for wave, later in zip(waves, waves[1:]):
            @pl.when(i == wave[0])
            def _():
                for turn in wave:
                    row_copy(turn).wait_send()
                send_rows(later)

        @pl.when(i > 0)
        def _():
            row_copy(i).wait_recv()
            part_copy(i).wait_recv()

        @pl.when(i == 1)
        def _():
            for f in range(early):
                for ahead in range(1, number):
                    plane_copy(f, ahead).wait_recv()

        loads = [
            pltpu.make_async_copy(mixed_out.at[source], branch.at[in_rows], load_sem.at[0]),
            pltpu.make_async_copy(grads_out.at[source], branch.at[in_grads], load_sem.at[1]),
            pltpu.make_async_copy(parts_out.at[source], parts_in, load_sem.at[2]),
        ]
        for copy in loads:
            copy.start()

        @pl.when(i > 0)
        def _():
            for copy in stores(source):
                copy.wait()

        for copy in loads:
            copy.wait()

        @pl.loop(0, slots // cut_rows)
        def _(part):
            at = pl.ds(pl.multiple_of(part * cut_rows, cut_rows), cut_rows)
            at_in = at
            at_grads = pl.ds(pl.multiple_of(slots + part * cut_rows, cut_rows), cut_rows)
            at_out = pl.ds(pl.multiple_of(2 * slots + part * cut_rows, cut_rows), cut_rows)
            parts = parts_in[at].astype(full)
            slot_gates = jnp.sum(jnp.where(mine, parts, 0.0), axis=-1, keepdims=True)
            gate_pre = jnp.dot(branch[at_in], gate_w_ref[0], preferred_element_type=full)
            up_pre = jnp.dot(branch[at_in], up_w_ref[0], preferred_element_type=full)
            act_grad = slot_gates * lax.dot_general(
                branch[at_grads], down_w_ref[0], across, preferred_element_type=full
            )
            sigma = 1.0 / (1.0 + jnp.exp(-gate_pre))
            silu = gate_pre * sigma
            activated = silu * up_pre
            active_low = activated.astype(low)
            active[at] = (slot_gates * activated).astype(low)
            up_low = (act_grad * silu).astype(low)
            gate_low = (act_grad * up_pre * sigma * (1.0 + gate_pre * (1.0 - sigma))).astype(low)
            up_grad[at] = up_low
            gate_grad[at] = gate_low
            branch[at_out] = (
                lax.dot_general(gate_low, gate_w_ref[0], across, preferred_element_type=full)
                + lax.dot_general(up_low, up_w_ref[0], across, preferred_element_type=full)
            ).astype(low)
            given = jnp.dot(active_low, down_w_ref[0], preferred_element_type=full)
            given = given.astype(low).astype(full)
            scaled[at] = (slot_gates * given).astype(low)
            dot = jnp.sum(given * branch[at_grads].astype(full), axis=-1, keepdims=True)
            first = dot.astype(low).astype(full)
            second = (dot - first).astype(low).astype(full)
            third = dot - first - second
            terms = jnp.where(
                column < experts, first, jnp.where(column < 2 * experts, second, third)
            )
            dots[at] = jnp.where(mine, terms, 0.0).astype(low)

        for copy in stores(source):
            copy.start()

    for copy in stores(here):
        copy.wait()
    for turn in waves[-1]:
        row_copy(turn).wait_send()
    for f in range(len(pieces)):
        for distance in range(n):
            for step in (-1, 1):
                origin = me - step * distance
                beyond = me + step

                @pl.when((origin >= 0) & (origin < n) & (beyond >= 0) & (beyond < n))
                def _():
                    line_copy(f, origin, step).wait_send()

    for f in range(cots, early):
        for ahead in range(1, number):
            plane_copy(f, ahead).wait_send()
    row_copy(1).wait_send()
    for turn in range(1, number):
        part_copy(turn).wait_send()


def dispatch(
    attended, back, tokens, gain, router, chosen, cot, pick, gate_weight, up_weight, down_weight,
    experts, sizes, collective, part=512,
):
    rows_here, width = tokens.shape
    inner = gate_weight.shape[2]
    lanes = router.shape[1]
    extra = lanes if 3 * experts <= lanes else 3 * lanes
    widths = [width, width, extra]
    n, n_ctx, number = sizes["dp"], sizes["ctx"], sizes["ctx"] * sizes["exp"]
    groups, dests, rows, _ = pick.shape
    slots = groups * rows
    pieces = cut(widths, part)
    count = len(pieces)
    low, full = jnp.bfloat16, jnp.float32
    vmem, anywhere = pl.BlockSpec(memory_space=pltpu.VMEM), pl.BlockSpec(memory_space=pl.ANY)
    block = lambda *shape: pltpu.VMEM(shape, low)
    dma = lambda *shape: pltpu.SemaphoreType.DMA(shape)
    by_source = lambda columns: jax.ShapeDtypeStruct((number, slots, columns), low)
    return pl.pallas_call(
        functools.partial(dispatch_kernel, sizes=sizes, pieces=pieces, experts=experts),
        in_specs=[vmem, anywhere] + [vmem] * 4 + [anywhere] + [vmem] * 4,
        out_specs=[anywhere] * 3 + [vmem] * 2 + [anywhere] * 6,
        out_shape=[by_source(columns) for columns in widths]
        + [
            jax.ShapeDtypeStruct((rows_here, width), full),
            jax.ShapeDtypeStruct((rows_here, lanes), full),
        ]
        + [by_source(columns) for columns in (inner, inner, inner, width, width, extra)],
        scratch_shapes=[
            block(max(n_ctx * rows_here, 3 * slots), width),
            *square_scratch(rows_here, width),
            block(n, rows_here, width),
            block(n, rows_here, width),
            block(n, rows_here, extra),
            block(dests, slots, width),
            block(dests, slots, extra),
            block(slots, extra),
            block(slots, inner),
            block(slots, inner),
            block(slots, inner),
            block(slots, width),
            block(slots, extra),
            dma(count, n, 2), dma(count, n), dma(count, number), dma(count, number), dma(count),
            dma(number), dma(number), dma(number), dma(number),
            dma(max(3, back.shape[0] // staged_rows(slots))), dma(6),
        ],
        compiler_params=pltpu.CompilerParams(
            collective_id=collective, has_side_effects=True, vmem_limit_bytes=VMEM
        ),
    )(
        attended, back, tokens, gain, router, chosen, cot, pick, gate_weight, up_weight,
        down_weight,
    )


def combine_kernel(
    rows_ref, dots_ref, pick_ref, middle_ref, cot_ref, gain_ref, gates_ref, router_ref,
    in_ref, grad_ref, active_ref, gate_ref, up_ref,
    whole_ref, middle_grad_ref, gain_grad_ref, router_grad_ref, gate_out, up_out, down_out,
    back_rows, back_dots, leave_rows, leave_dots, land_rows, land_dots, total_rows, total_dots,
    sums, branch, line_send, line_recv, plane_send, plane_recv, own_sem, sq_send, sq_recv, sq_own,
    *, sizes, pieces, experts,
):
    sent, back = (dots_ref, rows_ref), (back_dots, back_rows)
    leaving, landing = (leave_dots, leave_rows), (land_dots, land_rows)
    totals = (total_dots, total_rows)
    n, number = sizes["dp"], sizes["ctx"] * sizes["exp"]
    me, here = lax.axis_index("dp"), plane_index(sizes)
    tokens = middle_ref.shape[0]
    groups, _, rows, span = pick_ref.shape
    full, low = jnp.float32, jnp.bfloat16
    greet(sizes)

    def plane_copy(f, ahead):
        a, first, part = pieces[f]
        target = peer(sizes, ahead)
        return remote(
            sent[a].at[target, :, pl.ds(first, part)],
            back[a].at[here, :, pl.ds(first, part)],
            plane_send.at[f, ahead],
            plane_recv.at[f, ahead],
            place(sizes, target),
        )

    def own_copy(f):
        a, first, part = pieces[f]
        return pltpu.make_async_copy(
            sent[a].at[here, :, pl.ds(first, part)],
            back[a].at[here, :, pl.ds(first, part)],
            own_sem.at[f],
        )

    for f in range(len(pieces)):
        for ahead in range(number - 1, 0, -1):
            plane_copy(f, ahead).start()
        own_copy(f).start()

    def line_copy(f, target, step):
        a, first, part = pieces[f]
        return remote(
            leaving[a].at[target, :, pl.ds(first, part)],
            landing[a].at[target + (step + 1) // 2, :, pl.ds(first, part)],
            line_send.at[f, target],
            line_recv.at[f, target + (step + 1) // 2],
            {"dp": me + step},
        )

    inner, chunk = active_ref.shape[1], 256
    slots = in_ref.shape[0]

    def weight_sum(left, right, out, by_left):
        def body(left_ref, right_ref, out_ref):
            out_ref[...] = lax.dot_general(
                left_ref[...], right_ref[...], (((0,), (0,)), ((), ())), preferred_element_type=full
            )

        if by_left:
            grid = left.shape[1] // chunk
            specs = [
                pl.BlockSpec((slots, chunk), lambda i: (0, i)),
                pl.BlockSpec((slots, inner), lambda i: (0, 0)),
            ]
            out_spec = pl.BlockSpec((chunk, inner), lambda i: (i, 0))
        else:
            grid = right.shape[1] // chunk
            specs = [
                pl.BlockSpec((slots, inner), lambda i: (0, 0)),
                pl.BlockSpec((slots, chunk), lambda i: (0, i)),
            ]
            out_spec = pl.BlockSpec((inner, chunk), lambda i: (0, i))
        pltpu.emit_pipeline(body, grid=(grid,), in_specs=specs, out_specs=[out_spec])(
            left, right, out
        )

    for f, (a, first, part) in enumerate(pieces):
        columns = pl.ds(first, part)
        if f == 1:
            weight_sum(in_ref, gate_ref, gate_out, True)
        elif f == 2:
            weight_sum(in_ref, up_ref, up_out, True)
        elif f == 3:
            weight_sum(active_ref, grad_ref, down_out, False)
        for ahead in range(1, number):
            plane_copy(f, ahead).wait_recv()
        own_copy(f).wait()
        for g in range(groups):
            gathered = back[a][:, pl.ds(g * rows, rows), columns].reshape(number * rows, part)
            sums[pl.ds(g * span // tokens, span // tokens), :, pl.ds(0, part)] = lax.dot_general(
                pick_ref[g].reshape(number * rows, span), gathered, (((0,), (0,)), ((), ())),
                preferred_element_type=full,
            ).reshape(span // tokens, tokens, part)

        for distance in range(n - 1, 0, -1):
            for step in (-1, 1):
                target = me + step * distance
                behind = me - step

                @pl.when((target >= 0) & (target < n))
                def _():
                    own = sums[target, :, pl.ds(0, part)]

                    @pl.when((behind >= 0) & (behind < n))
                    def _():
                        line_copy(f, target, step).wait_recv()
                        coming = landing[a][target + (step + 1) // 2, :, columns]
                        leaving[a][target, :, columns] = (own + coming.astype(full)).astype(low)

                    @pl.when((behind < 0) | (behind >= n))
                    def _():
                        leaving[a][target, :, columns] = own.astype(low)

                    line_copy(f, target, step).start()

        totals[a][:, columns] = sums[me, :, pl.ds(0, part)]
        for step in (-1, 1):
            @pl.when((me - step >= 0) & (me - step < n))
            def _():
                line_copy(f, me, step).wait_recv()
                totals[a][:, columns] += landing[a][me + (step + 1) // 2, :, columns].astype(full)

    gates = gates_ref[...]
    lanes = gates.shape[1]
    if experts == lanes:
        dots = sum(total_dots[:, k * lanes : (k + 1) * lanes] for k in range(3))
    else:
        dots = total_dots[...]
        dots = dots + pltpu.roll(dots, lanes - experts, 1) + pltpu.roll(dots, lanes - 2 * experts, 1)
    picked = gates * (dots - jnp.sum(gates * dots, axis=-1, keepdims=True))
    logit_grads = picked.astype(low)
    mixed_grad = total_rows[...] + lax.dot_general(
        logit_grads, router_ref[...], (((1,), (1,)), ((), ())), preferred_element_type=full
    )
    middle = middle_ref[...]
    inverse = lax.rsqrt(jnp.mean(middle * middle, axis=-1, keepdims=True) + eps_norm)
    normed = middle * inverse
    gain_grad_ref[...] = jnp.sum(mixed_grad * normed, axis=0, keepdims=True)
    scaled = mixed_grad * gain_ref[...]
    middle_grad = cot_ref[...].astype(full) + inverse * (
        scaled - normed * jnp.mean(scaled * normed, axis=-1, keepdims=True)
    )
    middle_grad_ref[...] = middle_grad
    branch[...] = middle_grad.astype(low)
    collect = SquareGather(sizes, branch, whole_ref, sq_send, sq_recv, sq_own.at[0])
    collect.start()
    router_grad_ref[...] = lax.dot_general(
        logit_grads, (normed * gain_ref[...]).astype(low), (((0,), (0,)), ((), ())),
        preferred_element_type=full,
    )
    collect.pass_on()

    for f in range(len(pieces)):
        for ahead in range(1, number):
            plane_copy(f, ahead).wait_send()
        for distance in range(1, n):
            for step in (-1, 1):
                target = me + step * distance

                @pl.when((target >= 0) & (target < n))
                def _():
                    line_copy(f, target, step).wait_send()
    collect.finish()


def combine(
    rows, dots, pick, middle, cot, gain, gates, router, rows_in, grads_in, active, gate_grad,
    up_grad, experts, sizes, collective, part=512,
):
    number, back_rows, width = rows.shape
    extra = dots.shape[2]
    tokens = middle.shape[0]
    lanes = router.shape[1]
    inner = active.shape[2]
    flat = lambda v: v.reshape(-1, v.shape[2])
    n, n_ctx = sizes["dp"], sizes["ctx"]
    low, full = jnp.bfloat16, jnp.float32
    pieces = cut([extra, width], part)
    count = len(pieces)
    both = (width, extra)
    vmem, anywhere = pl.BlockSpec(memory_space=pltpu.VMEM), pl.BlockSpec(memory_space=pl.ANY)
    dma = lambda *shape: pltpu.SemaphoreType.DMA(shape)
    return pl.pallas_call(
        functools.partial(combine_kernel, sizes=sizes, pieces=pieces, experts=experts),
        in_specs=[anywhere, anywhere] + [vmem] * 6 + [anywhere] * 5,
        out_specs=[anywhere] + [vmem] * 3 + [anywhere] * 3,
        out_shape=[
            jax.ShapeDtypeStruct((n_ctx, tokens, width), low),
            jax.ShapeDtypeStruct((tokens, width), full),
            jax.ShapeDtypeStruct((1, width), full),
            jax.ShapeDtypeStruct((lanes, width), full),
            jax.ShapeDtypeStruct((width, inner), full),
            jax.ShapeDtypeStruct((width, inner), full),
            jax.ShapeDtypeStruct((inner, width), full),
        ],
        scratch_shapes=[pltpu.VMEM((number, back_rows, w), low) for w in both]
        + [pltpu.VMEM((n, tokens, w), low) for w in both]
        + [pltpu.VMEM((n + 1, tokens, w), low) for w in both]
        + [pltpu.VMEM((tokens, w), full) for w in both]
        + [
            pltpu.VMEM((n, tokens, max(p[2] for p in pieces)), full),
            pltpu.VMEM((tokens, width), low),
            dma(count, n), dma(count, n + 1), dma(count, number), dma(count, number), dma(count),
            dma(6), dma(6), dma(1),
        ],
        compiler_params=pltpu.CompilerParams(
            collective_id=collective, has_side_effects=True, vmem_limit_bytes=VMEM
        ),
    )(
        rows, dots, pick, middle, cot, gain, gates, router, flat(rows_in), flat(grads_in),
        flat(active), flat(gate_grad), flat(up_grad),
    )


def gather_kernel(
    token_ref, front_ref, back_ref, route_ref, cos_ref, sin_ref, bounds_ref,
    fronts_out, backs_ref, routes_ref, hidden_out, raw_out, turned_out, attended_ref,
    tokens_ref, fronts_ref, held, hidden, raw, turned,
    sq_send, sq_recv, own_sem, fa_send, fa_recv, fl_send, fl_recv, fp_send, fp_recv,
    bl_send, bl_recv, ba_send, ba_recv, bp_send, bp_recv, rl_send, rl_recv, store_sem,
    *, sizes, gain_len, heads, kv_heads,
):
    n, n_ctx, n_exp = sizes["dp"], sizes["ctx"], sizes["exp"]
    z, c, k = (lax.axis_index(a) for a in ALL)
    low, full = jnp.bfloat16, jnp.float32
    count, width = token_ref.shape
    owned = front_ref.shape[1]
    head = cos_ref.shape[1]
    columns = raw.shape[1]
    greet(sizes)

    def front_across(ahead):
        target = lax.rem(c + ahead, n_ctx)
        return remote(
            front_ref.at[target], fronts_ref.at[z, c, k], fa_send.at[ahead], fa_recv.at[ahead],
            {"ctx": target},
        )

    def front_line(origin, step):
        here = fronts_ref.at[origin, :, k]
        return remote(
            here, here, fl_send.at[origin, (step + 1) // 2], fl_recv.at[origin], {"dp": z + step}
        )

    def front_pair(origin, ahead):
        here = fronts_ref.at[origin, :, k]
        return remote(
            here, here, fp_send.at[origin, ahead], fp_recv.at[origin, ahead],
            {"exp": lax.rem(k + ahead, n_exp)},
        )

    def back_line(origin, step):
        here = held.at[origin]
        return remote(
            here, here, bl_send.at[origin, (step + 1) // 2], bl_recv.at[origin], {"dp": z + step}
        )

    def back_across(ahead):
        target = lax.rem(c + ahead, n_ctx)
        return remote(
            held.at[target], backs_ref.at[c, k], ba_send.at[ahead], ba_recv.at[ahead],
            {"ctx": target},
        )

    def back_pair(source, ahead):
        here = backs_ref.at[source, k]
        return remote(
            here, here, bp_send.at[source, ahead], bp_recv.at[source, ahead],
            {"exp": lax.rem(k + ahead, n_exp)},
        )

    def route_line(origin, step):
        here = routes_ref.at[origin]
        return remote(
            here, here, rl_send.at[origin, (step + 1) // 2], rl_recv.at[origin], {"dp": z + step}
        )

    def in_line(step):
        return (z + step >= 0) & (z + step < n)

    def start_line(line):
        for step in (-1, 1):
            @pl.when(in_line(step))
            def _():
                line(z, step).start()

    def pass_on(line, distance, after):
        for step in (-1, 1):
            origin = z - step * distance

            @pl.when((origin >= 0) & (origin < n))
            def _():
                line(origin, step).wait_recv()

                @pl.when(in_line(step))
                def _():
                    line(origin, step).start()

                after(origin)

    def nothing(origin):
        pass

    def to_siblings(origin):
        for ahead in range(1, n_exp):
            front_pair(origin, ahead).start()

    tokens = SquareGather(sizes, token_ref, tokens_ref, sq_send, sq_recv, own_sem.at[0])
    own_copies = [
        pltpu.make_async_copy(front_ref.at[c], fronts_ref.at[z, c, k], own_sem.at[1]),
        pltpu.make_async_copy(back_ref, held.at[z], own_sem.at[2]),
        pltpu.make_async_copy(route_ref, routes_ref.at[z], own_sem.at[3]),
    ]
    for copy in own_copies:
        copy.start()
    for ahead in range(1, n_ctx):
        front_across(ahead).start()
    tokens.start()
    for copy in own_copies:
        copy.wait()
    start_line(back_line)
    start_line(route_line)
    for ahead in range(1, n_ctx):
        front_across(ahead).wait_recv()
    start_line(front_line)
    to_siblings(z)
    pass_on(back_line, 1, nothing)
    tokens.pass_on()
    for distance in range(1, n):
        pass_on(front_line, distance, to_siblings)
        pass_on(route_line, distance, nothing)
    for origin in range(n):
        for ahead in range(1, n_exp):
            front_pair(origin, ahead).wait_recv()
    tokens.finish()
    fronts_store = pltpu.make_async_copy(fronts_ref, fronts_out, store_sem.at[0])
    fronts_store.start()

    gains = fronts_ref[..., columns : columns + 128].reshape(width, 128).astype(full).T
    gain = gains[0:1, :]
    row = lax.broadcasted_iota(jnp.int32, (width, head), 0)
    lane = lax.broadcasted_iota(jnp.int32, (width, head), 1)
    spot = lane // gain_len * owned + lax.rem(lane, gain_len)
    packed = gains[0:8, :].astype(low)
    scales = [
        jnp.dot(packed, (row == spot + shift).astype(low), preferred_element_type=full)[2:3, :]
        for shift in (0, gain_len)
    ]

    def hidden_store(i):
        return pltpu.make_async_copy(
            hidden, hidden_out.at[pl.ds(pl.multiple_of(i * count, count), count)], store_sem.at[1]
        )

    def raw_store(i):
        return pltpu.make_async_copy(
            raw, raw_out.at[pl.ds(pl.multiple_of(i * count, count), count)], store_sem.at[2]
        )

    def project(first, last):
        @pl.loop(first, last)
        def _(i):
            x = tokens_ref[i].astype(full)
            inverse = lax.rsqrt(jnp.mean(x * x, axis=-1, keepdims=True) + eps_norm)

            @pl.when(i > 0)
            def _():
                hidden_store(i).wait()
                raw_store(i).wait()

            hidden[...] = ((x * inverse) * gain).astype(low)
            hidden_store(i).start()
            raw[...] = jnp.dot(
                hidden[...], fronts_ref[..., 0:columns].reshape(width, columns),
                preferred_element_type=full,
            )
            raw_store(i).start()
            at = pl.ds(pl.multiple_of(i * count, count), count)
            cosine, sine = cos_ref[at], sin_ref[at]
            for h in range(heads + kv_heads):
                here = slice(h * head, (h + 1) * head)
                part = raw[:, here]
                factor = lax.rsqrt(jnp.mean(part * part, axis=-1, keepdims=True) + eps_norm)
                scaled = part * factor * scales[0 if h < heads else 1]
                spun = pltpu.roll(scaled, head // 2, 1)
                turned[at, here] = (scaled * cosine + spun * sine).astype(low)
            rest = slice((heads + kv_heads) * head, columns)
            turned[at, rest] = raw[:, rest].astype(low)

    rows = n_ctx * count
    group = heads // kv_heads

    def attend(first_head, last_head):
        @pl.loop(first_head, last_head)
        def _(h):
            at = lambda which: pl.ds(pl.multiple_of(which * head, head), head)
            kv = h // group
            for first in range(0, rows, count):
                last = first + count
                allowed = seen(bounds_ref, first, count, last)
                shares = shares_of(
                    turned[first:last, at(h)], turned[0:last, at(heads + kv)], allowed,
                    head ** (-0.5),
                )
                attended_ref[first:last, at(h)] = jnp.dot(
                    shares.astype(low), turned[0:last, at(heads + kv_heads + kv)],
                    preferred_element_type=full,
                ).astype(low)

    project(0, n_ctx // 2)
    if n > 2:
        pass_on(back_line, 2, nothing)
    project(n_ctx // 2, n_ctx)
    turned_store = pltpu.make_async_copy(turned, turned_out, store_sem.at[3])
    turned_store.start()
    attend(0, heads // 4)
    for distance in range(3, n):
        pass_on(back_line, distance, nothing)
    for ahead in range(1, n_ctx):
        back_across(ahead).start()
    own_back = pltpu.make_async_copy(held.at[c], backs_ref.at[c, k], own_sem.at[4])
    own_back.start()
    attend(heads // 4, heads)
    own_back.wait()
    for ahead in range(1, n_exp):
        back_pair(c, ahead).start()
    for behind in range(1, n_ctx):
        back_across(behind).wait_recv()
        source = lax.rem(c + n_ctx - behind, n_ctx)
        for ahead in range(1, n_exp):
            back_pair(source, ahead).start()

    fronts_store.wait()
    hidden_store(n_ctx - 1).wait()
    raw_store(n_ctx - 1).wait()
    turned_store.wait()
    for ahead in range(1, n_ctx):
        front_across(ahead).wait_send()
        back_across(ahead).wait_send()
    for origin in range(n):
        for ahead in range(1, n_exp):
            front_pair(origin, ahead).wait_send()
    for source in range(n_ctx):
        for ahead in range(1, n_exp):
            back_pair(source, ahead).wait()
    for line in (route_line, front_line, back_line):
        for distance in range(n):
            for step in (-1, 1):
                origin = z - step * distance

                @pl.when((origin >= 0) & (origin < n) & in_line(step))
                def _():
                    line(origin, step).wait_send()


def gather(
    tokens, front, back, routes, cosine, sine, bounds, gain_len, heads, kv_heads, sizes, collective
):
    n, n_ctx, n_exp = sizes["dp"], sizes["ctx"], sizes["exp"]
    _, rows, front_columns = front.shape
    count, width = tokens.shape
    head = cosine.shape[1]
    columns = (heads + 2 * kv_heads) * head
    seq = n_ctx * count
    low, full = jnp.bfloat16, jnp.float32
    dma = lambda *shape: pltpu.SemaphoreType.DMA(shape)
    vmem, anywhere = pl.BlockSpec(memory_space=pltpu.VMEM), pl.BlockSpec(memory_space=pl.ANY)
    return pl.pallas_call(
        functools.partial(
            gather_kernel, sizes=sizes, gain_len=gain_len, heads=heads, kv_heads=kv_heads
        ),
        in_specs=[vmem] * 6 + [pl.BlockSpec(memory_space=pltpu.SMEM)],
        out_specs=[anywhere] * 6 + [vmem],
        out_shape=[
            jax.ShapeDtypeStruct((n, n_ctx, n_exp, rows, front_columns), low),
            jax.ShapeDtypeStruct((n_ctx, n_exp) + back.shape, low),
            jax.ShapeDtypeStruct((n,) + routes.shape, routes.dtype),
            jax.ShapeDtypeStruct((seq, width), low),
            jax.ShapeDtypeStruct((seq, columns), full),
            jax.ShapeDtypeStruct((seq, columns), low),
            jax.ShapeDtypeStruct((seq, heads * head), low),
        ],
        scratch_shapes=[
            pltpu.VMEM((n_ctx, count, width), low),
            pltpu.VMEM((n, n_ctx, n_exp, rows, front_columns), low),
            pltpu.VMEM((n,) + back.shape, low),
            pltpu.VMEM((count, width), low),
            pltpu.VMEM((count, columns), full),
            pltpu.VMEM((seq, columns), low),
            dma(6), dma(6), dma(5),
            dma(n_ctx), dma(n_ctx), dma(n, 2), dma(n), dma(n, n_exp), dma(n, n_exp),
            dma(n, 2), dma(n), dma(n_ctx), dma(n_ctx), dma(n_ctx, n_exp), dma(n_ctx, n_exp),
            dma(n, 2), dma(n), dma(4),
        ],
        compiler_params=pltpu.CompilerParams(
            collective_id=collective, has_side_effects=True, vmem_limit_bytes=VMEM
        ),
    )(tokens, front, back, routes, cosine, sine, bounds)


def finish_kernel(
    bounds_ref, query_ref, key_ref, value_ref, grad_ref, raw_ref, scale_ref, cos_ref, sin_ref,
    hidden_ref, weight_ref, back_ref, rows_ref, pick_ref, result_ref, middle_ref, token_ref,
    gain_ref, small_ref,
    tokens_grad_ref, front_out, output_ref, back_out, small_out, landed_ref, back_in,
    key_sum, value_sum, raw_grad, head_gains, shared, arrived, back_one, fronts, front_pairs,
    front_in, rows_in, leaving, landing, far_in, turn_out, turn_in, hidden_send, hidden_recv,
    total, loaded, staged, small_all, small_in,
    own_sem, load_sem, stage_sem, bp_send, bp_recv, ba_send, ba_recv, bl_send, bl_recv,
    fp_send, fp_recv, fl_send, fl_recv, fa_send, fa_recv, plane_send, plane_recv, plane_own,
    line_send, line_recv, s_send, s_recv, *, block, heads, group, score_scale, sizes, part, chunk,
):
    step = pl.program_id(0)
    rows, head = query_ref.shape
    low, full = jnp.bfloat16, jnp.float32
    kv_heads = heads // group
    first_chunk = heads + 2 * kv_heads
    n, n_ctx, n_exp = sizes["dp"], sizes["ctx"], sizes["exp"]
    devices, number = n * n_ctx * n_exp, n_ctx * n_exp
    z, c, k = (lax.axis_index(a) for a in ALL)
    here, in_plane = (z * n_ctx + c) * n_exp + k, plane_index(sizes)
    tokens, width = token_ref.shape
    b_rows = back_out.shape[0]
    pieces = width // part
    chunks = width // chunk

    def in_line(index):
        return (index >= 0) & (index < n)

    def device_of(index):
        return {
            "dp": index // number,
            "ctx": lax.rem(index // n_exp, n_ctx),
            "exp": lax.rem(index, n_exp),
        }

    def back_own():
        return pltpu.make_async_copy(
            back_ref.at[:, k], shared.at[:, pl.ds(0, b_rows)], own_sem.at[0]
        )

    def back_pair(ahead):
        target = lax.rem(k + ahead, n_exp)
        return remote(
            back_ref.at[:, target], shared.at[:, pl.ds(ahead * b_rows, b_rows)],
            bp_send.at[ahead], bp_recv.at[ahead], {"exp": target},
        )

    def back_across(ahead):
        target = lax.rem(c + ahead, n_ctx)
        return remote(
            shared.at[target, pl.ds(0, b_rows)], arrived.at[c], ba_send.at[ahead],
            ba_recv.at[ahead], {"ctx": target},
        )

    def back_line(target, way):
        return remote(
            arrived.at[target], back_in.at[target + (way + 1) // 2], bl_send.at[target],
            bl_recv.at[target + (way + 1) // 2], {"dp": z + way},
        )

    def along_line(line, add, distance):
        for way in (-1, 1):
            target = z + way * distance

            @pl.when(in_line(target))
            def _():
                @pl.when(in_line(z - way))
                def _():
                    line(target, way).wait_recv()
                    add(target, target + (way + 1) // 2)

                line(target, way).start()

    def end_line(line, add):
        for way in (-1, 1):
            @pl.when(in_line(z - way))
            def _():
                line(z, way).wait_recv()
                add((way + 1) // 2 + z)

    def close_line(line):
        for distance in range(1, n):
            for way in (-1, 1):
                @pl.when(in_line(z + way * distance))
                def _():
                    line(z + way * distance, way).wait_send()

    def back_arrived(slot):
        copy = pltpu.make_async_copy(back_in.at[slot], back_one, stage_sem.at[1])
        copy.start()
        copy.wait()
        return back_one[...].astype(full)

    def add_back(target, slot):
        arrived[target] = (arrived[target].astype(full) + back_arrived(slot)).astype(low)

    def plane_copy(piece, ahead):
        target = peer(sizes, ahead)
        columns = pl.ds(piece * part, part)
        return remote(
            rows_ref.at[target, :, columns], landed_ref.at[in_plane, :, columns],
            plane_send.at[piece, ahead], plane_recv.at[piece, ahead], place(sizes, target),
        )

    def plane_own_copy(piece):
        columns = pl.ds(piece * part, part)
        return pltpu.make_async_copy(
            rows_ref.at[in_plane, :, columns], landed_ref.at[in_plane, :, columns],
            plane_own.at[piece],
        )

    def push(piece):
        for ahead in range(number - 1, 0, -1):
            plane_copy(piece, ahead).start()
        plane_own_copy(piece).start()

    def small_load():
        return pltpu.make_async_copy(small_ref, small_all, own_sem.at[1])

    @pl.when(step == 0)
    def _():
        head_gains[...] = jnp.zeros_like(head_gains)
        barrier = pltpu.get_barrier_semaphore()

        @pl.loop(1, devices)
        def _(ahead):
            pl.semaphore_signal(
                barrier, inc=1, device_id=device_of(lax.rem(here + ahead, devices)),
                device_id_type=MESH,
            )

        pl.semaphore_wait(barrier, devices - 1)
        back_own().start()
        for ahead in range(1, n_exp):
            back_pair(ahead).start()
        small_load().start()

    @pl.when(step == 1)
    def _():
        back_own().wait()
        for ahead in range(1, n_exp):
            back_pair(ahead).wait_recv()
        for index in range(n_ctx):
            summed = shared[index, 0:b_rows].astype(full)
            for ahead in range(1, n_exp):
                summed = summed + shared[index, ahead * b_rows : (ahead + 1) * b_rows].astype(full)
            shared[index, 0:b_rows] = summed.astype(low)
        for ahead in range(1, n_ctx):
            back_across(ahead).start()
        arrived[c] = shared[c, 0:b_rows]
        for piece in range(pieces):
            push(piece)
        small_load().wait()

    for distance in range(n - 1, 0, -1):
        @pl.when(step == min(6 + 3 * (n - 1 - distance), first_chunk + chunks - 2))
        def _():
            if distance == n - 1:
                for ahead in range(1, n_ctx):
                    back_across(ahead).wait_recv()
                    back_across(ahead).wait_send()
                for ahead in range(1, n_exp):
                    back_pair(ahead).wait_send()
            along_line(back_line, add_back, distance)

    def norm_rope_back(grad, raw, scale, cosine, sine):
        inverse = lax.rsqrt(jnp.mean(raw * raw, axis=-1, keepdims=True) + eps_norm)
        normed = raw * inverse
        turned = grad * cosine + pltpu.roll(grad * sine, grad.shape[-1] // 2, 1)
        inner = turned * scale
        back = inverse * (inner - normed * jnp.mean(inner * normed, axis=-1, keepdims=True))
        return back, jnp.sum(turned * normed, axis=0, keepdims=True)

    for kv in range(kv_heads):
        @pl.when(step == kv * group)
        def _():
            key_sum[kv] = jnp.zeros((rows, head), full)
            value_sum[kv] = jnp.zeros((rows, head), full)

    here_columns = pl.ds(pl.multiple_of(step * head, head), head)

    @pl.when(step < heads)
    def _():
        kv = step // group
        gains = jnp.zeros((1, head), full)
        for first in range(0, rows, block):
            last = first + block
            query, keys, values = query_ref[first:last, :], key_ref[:last, :], value_ref[:last, :]
            grad = grad_ref[first:last, :]
            allowed = seen(bounds_ref, first, block, last)
            shares = shares_of(query, keys, allowed, score_scale)
            share_grads = lax.dot_general(
                grad, values, (((1,), (1,)), ((), ())), preferred_element_type=full
            )
            centre = jnp.sum(shares * share_grads, axis=-1, keepdims=True)
            score_grads = (shares * (share_grads - centre)).astype(low)
            key_sum[kv, :last, :] += lax.dot_general(
                score_grads, query, (((0,), (0,)), ((), ())), preferred_element_type=full
            )
            value_sum[kv, :last, :] += lax.dot_general(
                shares.astype(low), grad, (((0,), (0,)), ((), ())), preferred_element_type=full
            )
            query_grad = jnp.dot(score_grads, keys, preferred_element_type=full) * score_scale
            back, gain = norm_rope_back(
                query_grad, raw_ref[first:last, :], scale_ref[0:1, :], cos_ref[first:last, :],
                sin_ref[first:last, :],
            )
            raw_grad[first:last, here_columns] = back.astype(low)
            gains += gain
        head_gains[0:1, :] += gains

    @pl.when((step >= heads) & (step < heads + kv_heads))
    def _():
        back, gain = norm_rope_back(
            key_sum[step - heads] * score_scale, raw_ref[...], scale_ref[1:2, :], cos_ref[...],
            sin_ref[...],
        )
        raw_grad[:, here_columns] = back.astype(low)
        head_gains[1:2, :] += gain

    @pl.when((step >= heads + kv_heads) & (step < first_chunk))
    def _():
        raw_grad[:, here_columns] = value_sum[step - heads - kv_heads].astype(low)

    @pl.when((step >= first_chunk) & (step < first_chunk + chunks))
    def _():
        q = step - first_chunk
        grads = raw_grad[...]
        shared[:, 0:tokens, pl.ds(pl.multiple_of(q * chunk, chunk), chunk)] = (
            lax.dot_general(
                grads, weight_ref[:, : grads.shape[1]], (((1,), (1,)), ((), ())),
                preferred_element_type=full,
            )
            .astype(low)
            .reshape(n_ctx, tokens, chunk)
        )
        fronts[q // 2, lax.rem(q, 2)] = (
            lax.dot_general(
                hidden_ref[...], grads, (((0,), (0,)), ((), ())), preferred_element_type=full
            )
            .astype(low)
            .reshape(fronts.shape[2:])
        )

    def front_pair(ahead):
        target = lax.rem(k + ahead, n_exp)
        return remote(
            fronts.at[:, :, :, target], front_pairs.at[ahead - 1], fp_send.at[ahead],
            fp_recv.at[ahead], {"exp": target},
        )

    def front_line(target, way):
        return remote(
            fronts.at[target, :, :, k], front_in.at[target + (way + 1) // 2], fl_send.at[target],
            fl_recv.at[target + (way + 1) // 2], {"dp": z + way},
        )

    def front_across(ahead):
        target = lax.rem(c + ahead, n_ctx)
        return remote(
            fronts.at[z, target // (n_ctx // 2), lax.rem(target, n_ctx // 2), k], front_out.at[c],
            fa_send.at[ahead], fa_recv.at[ahead], {"ctx": target},
        )

    def add_front(target, slot):
        fronts[target, :, :, k] = (
            fronts[target, :, :, k].astype(full) + front_in[slot].astype(full)
        ).astype(low)

    def line_of(piece):
        columns = pl.ds(piece * part, part)

        def line(target, way):
            return remote(
                leaving.at[target, :, columns],
                landing.at[target + (way + 1) // 2, :, columns],
                line_send.at[piece, target], line_recv.at[piece, target + (way + 1) // 2],
                {"dp": z + way},
            )

        return line

    def load_rows(piece):
        return pltpu.make_async_copy(
            landed_ref.at[:, :, pl.ds(piece * part, part)], rows_in, load_sem.at[0]
        )

    def load_part(source, piece):
        return pltpu.make_async_copy(
            source.at[:, pl.ds(piece * part, part)], loaded.at[piece % 2], load_sem.at[1 + piece % 2]
        )

    def mix_in(piece):
        for ahead in range(1, number):
            plane_copy(piece, ahead).wait_recv()
        plane_own_copy(piece).wait()
        load_rows(piece).start()
        load_part(result_ref, piece).start()
        load_rows(piece).wait()
        groups, _, back_rows, span = pick_ref.shape
        columns = pl.ds(piece * part, part)
        for g in range(groups):
            gathered = rows_in[:, pl.ds(g * back_rows, back_rows), :]
            leaving[pl.ds(g * span // tokens, span // tokens), :, columns] = (
                lax.dot_general(
                    pick_ref[g].reshape(number * back_rows, span),
                    gathered.reshape(number * back_rows, part),
                    (((0,), (0,)), ((), ())),
                    preferred_element_type=full,
                )
                .astype(low)
                .reshape(span // tokens, tokens, part)
            )

    def start_total(piece):
        columns = pl.ds(piece * part, part)
        load_part(result_ref, piece).wait()
        total[:, columns] = leaving[z, :, columns].astype(full) + loaded[piece % 2]

    def mix_line(piece, distance):
        columns = pl.ds(piece * part, part)

        def add(target, slot):
            leaving[target, :, columns] = (
                leaving[target, :, columns].astype(full) + landing[slot, :, columns].astype(full)
            ).astype(low)

        along_line(line_of(piece), add, distance)

    def mix_end(piece):
        columns = pl.ds(piece * part, part)

        def add(slot):
            total[:, columns] += landing[slot, :, columns].astype(full)

        end_line(line_of(piece), add)

    @pl.when(step == first_chunk + chunks - 1)
    def _():
        mix_in(0)
        mix_line(0, n - 1)

    def small_copy(ahead):
        target = lax.rem(here + ahead, devices)
        return remote(
            small_all.at[target], small_in.at[ahead], s_send.at[0], s_recv.at[0],
            device_of(target),
        )

    def all_small():
        others = pl.ds(1, devices - 1)
        return remote(
            small_all.at[others], small_in.at[others], s_send.at[0], s_recv.at[0], {"dp": z}
        )

    @pl.when(step == first_chunk + chunks)
    def _():
        for ahead in range(1, n_exp):
            front_pair(ahead).start()
        gain_owned = head // devices
        for index in range(devices):
            for which in (0, 1):
                small_all[index, which : which + 1, 0:gain_owned] = head_gains[
                    which : which + 1, index * gain_owned : (index + 1) * gain_owned
                ]

        @pl.loop(1, devices)
        def _(ahead):
            small_copy(ahead).start()

        hidden = SquareScatter(
            sizes, shared, far_in, turn_out, turn_in, hidden_send, hidden_recv, tokens
        )
        hidden.start(1)
        hidden.start(0)
        total[0:b_rows, :] = arrived[z].astype(full)

        def add_last(slot):
            total[0:b_rows, :] += back_arrived(slot)

        end_line(back_line, add_last)
        back_store = pltpu.make_async_copy(total.at[pl.ds(0, b_rows)], back_out, stage_sem.at[0])
        back_store.start()
        back_store.wait()
        if n > 2:
            mix_line(0, n - 2)
        for ahead in range(1, n_exp):
            front_pair(ahead).wait_recv()
        for target in range(n):
            summed = fronts[target, :, :, k].astype(full)
            for ahead in range(1, n_exp):
                summed = summed + front_pairs[ahead - 1, target].astype(full)
            fronts[target, :, :, k] = summed.astype(low)
        along_line(front_line, add_front, n - 1)
        for distance in range(n - 3, 0, -1):
            mix_line(0, distance)
        start_total(0)
        mix_end(0)
        front_own = pltpu.make_async_copy(
            fronts.at[z, c // (n_ctx // 2), lax.rem(c, n_ctx // 2), k], front_out.at[c],
            stage_sem.at[0],
        )
        for piece in range(1, pieces):
            if piece == pieces - 1:
                all_small().wait_recv()
                small_out[...] = small_all[here] + jnp.sum(small_in[1:devices], axis=0)
            mix_in(piece)
            mix_line(piece, n - 1)
            start_total(piece)
            for distance in range(n - 2, 0, -1):
                if piece == 1:
                    along_line(front_line, add_front, distance)
                mix_line(piece, distance)
                if piece == pieces - 1 and distance == max(1, n - 2):
                    hidden.turn()
            if piece == 1:
                end_line(front_line, lambda slot: add_front(z, slot))
                for ahead in range(1, n_ctx):
                    front_across(ahead).start()
                front_own.start()
            mix_end(piece)
        front_own.wait()
        staged[...] = total[...].astype(low)
        output_store = pltpu.make_async_copy(staged, output_ref, stage_sem.at[0])
        output_store.start()

        load_part(middle_ref, 0).start()
        hidden.finish(total)
        x = token_ref[...].astype(full)
        inverse = lax.rsqrt(jnp.mean(x * x, axis=-1, keepdims=True) + eps_norm)
        normed = x * inverse
        grad = total[...]
        scaled = grad * gain_ref[...]
        total[...] = inverse * (scaled - normed * jnp.mean(scaled * normed, axis=-1, keepdims=True))
        output_store.wait()
        for piece in range(pieces):
            if piece + 1 < pieces:
                load_part(middle_ref, piece + 1).start()
            load_part(middle_ref, piece).wait()
            columns = pl.ds(piece * part, part)
            staged[:, columns] = (total[:, columns] + loaded[piece % 2]).astype(low)
        tokens_store = pltpu.make_async_copy(staged, tokens_grad_ref, stage_sem.at[0])
        tokens_store.start()
        for ahead in range(1, n_ctx):
            front_across(ahead).wait()
        tokens_store.wait()

        all_small().wait_send()
        hidden.close()
        for ahead in range(1, n_exp):
            front_pair(ahead).wait_send()
        for piece in range(pieces):
            for ahead in range(1, number):
                plane_copy(piece, ahead).wait_send()
            close_line(line_of(piece))
        close_line(back_line)
        close_line(front_line)


def finish(
    bounds, turned, grad, raw, scales, cosine, sine, hidden, weight, back, rows_back, pick, result,
    middle_grad, tokens, gain, small, heads, kv_heads, head, sizes, collective, part=512,
):
    n, n_ctx, n_exp = sizes["dp"], sizes["ctx"], sizes["exp"]
    devices, number = n * n_ctx * n_exp, n_ctx * n_exp
    low, full = jnp.bfloat16, jnp.float32
    rows, columns = raw.shape
    count, width = tokens.shape
    b_rows = back.shape[2]
    f_rows = width // devices
    chunk = width // (2 * n)
    group = heads // kv_heads
    back_rows = rows_back.shape[1]
    s_rows, s_cols = small.shape[1:]
    pieces = width // part
    first_chunk = heads + 2 * kv_heads
    within = lambda h: jnp.minimum(h, heads - 1)
    now = lambda h: jnp.clip(h - first_chunk, 0, 2 * n - 1)
    once = pl.Buffered(buffer_count=1)
    whole = lambda shape: pl.BlockSpec(shape, lambda h: (0,) * len(shape), pipeline_mode=once)
    anywhere = pl.BlockSpec(memory_space=pl.ANY)
    vmem = lambda *shape: pltpu.VMEM(shape, low)
    wide = lambda *shape: pltpu.VMEM(shape, full)
    dma = lambda *shape: pltpu.SemaphoreType.DMA(shape)
    half = n_ctx // 2
    return pl.pallas_call(
        functools.partial(
            finish_kernel, block=count, heads=heads, group=group, score_scale=head ** (-0.5),
            sizes=sizes, part=part, chunk=chunk,
        ),
        grid=(first_chunk + 2 * n + 1,),
        in_specs=[
            pl.BlockSpec(memory_space=pltpu.SMEM),
            pl.BlockSpec((rows, head), lambda h: (0, within(h))),
            pl.BlockSpec((rows, head), lambda h: (0, heads + within(h) // group)),
            pl.BlockSpec((rows, head), lambda h: (0, heads + kv_heads + within(h) // group)),
            pl.BlockSpec((rows, head), lambda h: (0, within(h))),
            pl.BlockSpec((rows, head), lambda h: (0, jnp.minimum(h, heads + kv_heads - 1))),
            whole(scales.shape),
            whole(cosine.shape),
            whole(sine.shape),
            pl.BlockSpec((rows, chunk), lambda h: (0, now(h))),
            pl.BlockSpec((chunk, weight.shape[1]), lambda h: (now(h), 0)),
            anywhere,
            anywhere,
            whole(pick.shape),
            anywhere,
            anywhere,
            whole(tokens.shape),
            whole(gain.shape),
            anywhere,
        ],
        out_specs=[anywhere] * 4
        + [pl.BlockSpec((s_rows, s_cols), lambda h: (0, 0)), anywhere, anywhere],
        out_shape=[
            jax.ShapeDtypeStruct((count, width), low),
            jax.ShapeDtypeStruct((n_ctx, f_rows, columns), low),
            jax.ShapeDtypeStruct((count, width), low),
            jax.ShapeDtypeStruct((b_rows, width), full),
            jax.ShapeDtypeStruct((s_rows, s_cols), full),
            jax.ShapeDtypeStruct(rows_back.shape, low),
            jax.ShapeDtypeStruct((n + 1, b_rows, width), low),
        ],
        scratch_shapes=[
            wide(kv_heads, rows, head),
            wide(kv_heads, rows, head),
            vmem(rows, columns),
            wide(2, head),
            vmem(n_ctx, max(count, n_exp * b_rows), width),
            vmem(n_ctx, b_rows, width),
            vmem(b_rows, width),
            vmem(n, 2, half, n_exp, f_rows, columns),
            vmem(n_exp - 1, n, 2, half, f_rows, columns),
            vmem(n + 1, 2, half, f_rows, columns),
            vmem(number, back_rows, part),
            vmem(n, count, width),
            vmem(n + 1, count, width),
            *square_scratch(count, width),
            wide(count, width),
            wide(2, count, part),
            vmem(count, width),
            wide(devices, s_rows, s_cols),
            wide(devices, s_rows, s_cols),
            dma(2), dma(3), dma(2), dma(n_exp), dma(n_exp), dma(n_ctx), dma(n_ctx), dma(n),
            dma(n + 1), dma(n_exp), dma(n_exp), dma(n), dma(n + 1), dma(n_ctx), dma(n_ctx),
            dma(pieces, number), dma(pieces, number), dma(pieces), dma(pieces, n),
            dma(pieces, n + 1), dma(1), dma(1),
        ],
        compiler_params=pltpu.CompilerParams(
            collective_id=collective, has_side_effects=True, vmem_limit_bytes=VMEM
        ),
    )(
        bounds, turned, turned, turned, grad, raw, scales, cosine, sine, hidden, weight, back,
        rows_back, pick, result, middle_grad, tokens, gain, small,
    )


def shards(
    tokens,
    attention_gain,
    query_weight,
    key_weight,
    value_weight,
    query_gain,
    key_gain,
    output_weight,
    mixture_gain,
    router_weight,
    gate_weight,
    up_weight,
    down_weight,
    routes,
    bounds,
    cotangent,
):
    low, full = jnp.bfloat16, jnp.float32
    n_dp, n_ctx, n_exp = (lax.axis_size(a) for a in ALL)
    devices = n_dp * n_ctx * n_exp
    tok_count, width = tokens.shape[1], tokens.shape[2]
    seq_len = tok_count * n_ctx
    head_dim = query_gain.shape[0] * devices
    rows = query_weight.shape[0]
    heads = query_weight.shape[1] // head_dim
    kv_heads = key_weight.shape[1] // head_dim
    kv_here = kv_heads // n_ctx
    group_size = heads // kv_heads
    q_cols, kv_cols = heads * head_dim // n_ctx, kv_here * head_dim
    experts = router_weight.shape[1]
    topk = routes.shape[2]
    base_rows = tok_count * topk // experts
    capacity = base_rows + max(1, base_rows // 8)
    plane = experts // n_dp
    local_experts = gate_weight.shape[0]
    score_scale = head_dim ** (-0.5)
    dp_index = lax.axis_index("dp")

    gain_len = query_gain.shape[0]
    small = jnp.concatenate(
        [
            attention_gain[:, None],
            mixture_gain[:, None],
            jnp.pad(jnp.concatenate([query_gain, key_gain]), (0, rows - 2 * gain_len))[:, None],
            router_weight,
        ],
        axis=1,
    ).astype(low)
    small = jnp.pad(small, ((0, 0), (0, -small.shape[1] % 128)))
    extra = small.shape[1]

    def by_ctx(weight):
        return weight.astype(low).reshape(rows, n_ctx, -1).transpose(1, 0, 2)

    front = jnp.concatenate(
        [
            by_ctx(query_weight),
            by_ctx(key_weight),
            by_ctx(value_weight),
            jnp.broadcast_to(small[None], (n_ctx, rows, extra)),
        ],
        axis=2,
    )
    sizes = {"dp": n_dp, "ctx": n_ctx, "exp": n_exp}
    heads_here = heads // n_ctx
    cosine, sine = rope_tables(jnp.arange(seq_len, dtype=jnp.int32), head_dim)
    half = head_dim // 2
    sine = jnp.concatenate([-sine[:, :half], sine[:, half:]], axis=1)
    front, output_part, column_routes, hidden, raw, turned, attended_low = gather(
        tokens[0], front, output_weight.astype(low), routes[0], cosine, sine, bounds, gain_len,
        heads_here, kv_here, sizes, 3,
    )
    front = front.reshape(width, -1)
    output_part = output_part.reshape(q_cols, width)
    small = front[:, q_cols + 2 * kv_cols :]
    first_gain = small[:, 0].astype(full)
    second_gain = small[:, 1].astype(full)
    head_gains = small[:, 2].reshape(devices, rows)
    query_scale = head_gains[:, :gain_len].reshape(-1).astype(full)
    key_scale = head_gains[:, gain_len : 2 * gain_len].reshape(-1).astype(full)
    router_full = small[:, 3 : 3 + experts]

    chosen = jnp.any(
        column_routes[:, :, :, None] == jnp.arange(experts, dtype=jnp.int32), axis=2
    )
    hot = lax.dynamic_slice_in_dim(chosen.astype(low), dp_index * plane, plane, 2)
    row_ids = jnp.arange(tok_count, dtype=jnp.int32)
    earlier = (row_ids[None, :] < row_ids[:, None]).astype(low)
    before = jnp.einsum("st,btj->bsj", earlier, hot, preferred_element_type=full)
    together = 2 if 2 * capacity % 16 == 0 and n_dp % 2 == 0 else n_dp
    groups = n_dp // together
    slot_rows = -(-together * capacity // 16) * 16

    def grouped(v):
        return v.reshape(groups, together * tok_count, -1)

    block_first = jnp.tile(jnp.arange(together, dtype=full) * capacity, groups)[:, None, None]
    slot_at = grouped(jnp.where(hot > 0, before + block_first, -1.0))
    slots = jnp.arange(slot_rows, dtype=full)
    pick = (slot_at.transpose(0, 2, 1)[:, :, None, :] == slots[:, None]).astype(low)

    scales = jnp.stack([query_scale, key_scale])

    lanes = -(-experts // 128) * 128
    router_wide = jnp.pad(router_full, ((0, 0), (0, lanes - experts)))
    own_chosen = jnp.any(
        routes[0][:, :, None] == jnp.arange(lanes, dtype=jnp.int32), axis=1
    ).astype(full)
    (
        grad_rows, expert_in, _, middle, own_gates, active, gate_grad, up_grad, row_grads,
        scaled_out, dot_rows,
    ) = dispatch(
        attended_low, output_part, tokens[0], second_gain[None], router_wide, own_chosen,
        cotangent[0], pick, gate_weight, up_weight, down_weight, experts, sizes, 1,
    )
    branch_low, middle_grad, second_gain_grad, router_grad, gate_w_grad, up_w_grad, down_grad = combine(
        row_grads, dot_rows, pick, middle, cotangent[0], second_gain[None], own_gates, router_wide,
        expert_in, grad_rows, active, gate_grad, up_grad, experts, sizes, 2,
    )
    gate_w_grad, up_w_grad, down_grad = gate_w_grad[None], up_w_grad[None], down_grad[None]
    router_grad = router_grad[:experts].T
    branch_low = branch_low.reshape(seq_len, width)
    output_w_grad = jnp.einsum("ti,td->id", attended_low, branch_low, preferred_element_type=full)
    attended_grad = jnp.einsum("td,id->ti", branch_low, output_part, preferred_element_type=full)
    rest = jnp.concatenate(
        [second_gain_grad.reshape(devices, -1), router_grad.reshape(devices, -1)], axis=1
    )
    columns = -(-rest.shape[1] // (5 * 128)) * 128
    rest = jnp.pad(rest, ((0, 0), (0, 5 * columns - rest.shape[1]))).reshape(devices, 5, columns)
    small = jnp.pad(rest, ((0, 0), (3, 0), (0, 0)))
    tokens_grad, front_grad, output, output_share, small, _, _ = finish(
        bounds, turned, attended_grad.astype(low), raw, scales, cosine, sine, hidden, front,
        output_w_grad.astype(low).reshape(n_ctx, n_exp, -1, width), scaled_out, pick, middle,
        middle_grad, tokens[0], first_gain[None], small, heads_here, kv_here, head_dim, sizes, 4,
        part=512 if n_ctx * n_exp <= 8 else 256,
    )
    tokens_grad = tokens_grad[None]
    output = output[None]
    front_grad = front_grad.astype(full)
    query_share = front_grad[:, :, :q_cols].transpose(1, 0, 2).reshape(rows, -1)
    key_share = front_grad[:, :, q_cols : q_cols + kv_cols].transpose(1, 0, 2).reshape(rows, -1)
    value_share = front_grad[:, :, q_cols + kv_cols :].transpose(1, 0, 2).reshape(rows, -1)
    first_share = sum(
        jnp.sum(weight.astype(low).astype(full) * grad, axis=1)
        for weight, grad in (
            (query_weight, query_share), (key_weight, key_share), (value_weight, value_share)
        )
    ) / attention_gain.astype(low).astype(full)
    query_gain_share = small[0, :gain_len]
    key_gain_share = small[1, :gain_len]
    rest = small[3:].reshape(-1)
    second_share = rest[:rows]
    router_share = rest[rows : rows + rows * experts].reshape(rows, experts)
    return (
        output,
        tokens_grad,
        first_share,
        query_share,
        key_share,
        value_share,
        query_gain_share,
        key_gain_share,
        output_share,
        second_share,
        router_share,
        gate_w_grad,
        up_w_grad,
        down_grad,
    )


def solution(mesh):
    rows = P(ALL)
    sequences = P(("dp", "exp"), "ctx")
    in_specs = (sequences,) + (rows,) * 12 + (sequences, P(("dp", "exp")), sequences)
    out_specs = (sequences,) * 2 + (rows,) * 12
    return jax.shard_map(shards, mesh=mesh, in_specs=in_specs, out_specs=out_specs, check_vma=False)
```

```python
import functools

import jax
import jax.numpy as jnp
from jax import lax
from jax.experimental import pallas as pl
from jax.experimental.pallas import tpu as pltpu
from jax.sharding import PartitionSpec as P

eps_norm = 1e-06
rope_base = 1000000.0
masked_score = -1e30
ALL = ("dp", "ctx", "exp")
VMEM = 60 << 20
MESH = pl.DeviceIdType.MESH


def rope_tables(positions, width):
    exponents = jnp.arange(width // 2, dtype=jnp.float32) * (2.0 / width)
    frequency = rope_base ** (-exponents)
    angles = positions.astype(jnp.float32)[:, None] * frequency[None, :]
    angles = jnp.concatenate([angles, angles], axis=-1)
    return (jnp.cos(angles), jnp.sin(angles))


def seen(bounds_ref, first, rows, keys):
    query = first + lax.broadcasted_iota(jnp.int32, (rows, 1), 0)
    low_end, high_end = bounds_ref[0, 0], bounds_ref[0, 1]
    start = jnp.where(query >= high_end, high_end, jnp.where(query >= low_end, low_end, 0))
    key = lax.broadcasted_iota(jnp.int32, (rows, keys), 1)
    return (key <= query) & (key >= start)


def shares_of(query, keys, allowed, score_scale):
    scores = lax.dot_general(
        query, keys, (((1,), (1,)), ((), ())), preferred_element_type=jnp.float32
    )
    scores = jnp.where(allowed, scores * score_scale, masked_score)
    weights = jnp.exp(scores - jnp.max(scores, axis=-1, keepdims=True))
    return weights / jnp.sum(weights, axis=-1, keepdims=True)


def square(sizes):
    me = lax.axis_index("ctx")
    return me + 1 - 2 * lax.rem(me, 2), lax.rem(me + 2, 4)


def remote(source, target, send, recv, device):
    return pltpu.make_async_remote_copy(
        src_ref=source, dst_ref=target, send_sem=send, recv_sem=recv, device_id=device,
        device_id_type=MESH,
    )


class SquareGather:
    def __init__(self, sizes, block, whole, send, recv, own_sem):
        self.block, self.whole, self.send, self.recv = block, whole, send, recv
        self.me = lax.axis_index("ctx")
        self.by = square(sizes)
        self.half = block.shape[1] // 2
        self.own = pltpu.make_async_copy(block, whole.at[self.me], own_sem)

    def copy(self, place, part, side, number):
        columns = pl.ds(part * self.half, self.half)
        target = self.whole.at[place, :, columns]
        source = self.block.at[:, columns] if number < 4 else target
        return remote(
            source, target, self.send.at[number], self.recv.at[number], {"ctx": self.by[side]}
        )

    def first(self, number):
        part, side = ((0, 0), (1, 1), (1, 0), (0, 1))[number]
        return self.copy(self.me, part, side, number)

    def start(self):
        self.own.start()
        for number in range(4):
            self.first(number).start()

    def pass_on(self):
        for part in (0, 1):
            self.first(part).wait_recv()
            self.copy(self.by[part], part, 1 - part, 4 + part).start()

    def finish(self):
        for number in (2, 3):
            self.first(number).wait_recv()
        for part in (0, 1):
            last = self.copy(self.by[part], part, 1 - part, 4 + part)
            last.wait_recv()
            last.wait_send()
        for number in range(4):
            self.first(number).wait_send()
        self.own.wait()


class SquareScatter:
    def __init__(self, sizes, parts, far_in, turn_out, turn_in, send, recv, rows):
        self.parts, self.far_in, self.turn_out, self.turn_in = parts, far_in, turn_out, turn_in
        self.send, self.recv, self.rows = send, recv, rows
        self.me = lax.axis_index("ctx")
        self.by = square(sizes)
        self.far = sizes["ctx"] - 1 - self.me
        half = parts.shape[-1] // 2
        self.columns = (pl.ds(0, half), pl.ds(half, half))

    def at(self, place, side):
        if len(self.parts.shape) == 2:
            return pl.ds(place * self.rows, self.rows), self.columns[side]
        return place, pl.ds(0, self.rows), self.columns[side]

    def first(self, side, number):
        place = self.by[side] if number == 0 else self.far
        index = 2 * side + number
        return remote(
            self.parts.at[self.at(place, side)], self.far_in.at[side, number],
            self.send.at[index], self.recv.at[index], {"ctx": self.by[side]},
        )

    def second(self, side):
        return remote(
            self.turn_out.at[side], self.turn_in.at[side], self.send.at[4 + side],
            self.recv.at[4 + side], {"ctx": self.by[1 - side]},
        )

    def start(self, number):
        for side in (0, 1):
            self.first(side, number).start()

    def turn(self):
        for side in (0, 1):
            self.first(side, 1).wait_recv()
            own = self.parts[self.at(self.by[1 - side], side)].astype(jnp.float32)
            self.turn_out[side] = (own + self.far_in[side, 1].astype(jnp.float32)).astype(
                jnp.bfloat16
            )
            self.second(side).start()

    def finish(self, total):
        for side in (0, 1):
            self.first(side, 0).wait_recv()
            self.second(side).wait_recv()
            total[:, self.columns[side]] = (
                self.parts[self.at(self.me, side)].astype(jnp.float32)
                + self.far_in[side, 0].astype(jnp.float32)
                + self.turn_in[side].astype(jnp.float32)
            )

    def close(self):
        for side in (0, 1):
            for number in (0, 1):
                self.first(side, number).wait_send()
            self.second(side).wait_send()


def square_scratch(rows, width):
    half = width // 2
    return [
        pltpu.VMEM((2, 2, rows, half), jnp.bfloat16),
        pltpu.VMEM((2, rows, half), jnp.bfloat16),
        pltpu.VMEM((2, rows, half), jnp.bfloat16),
        pltpu.SemaphoreType.DMA((6,)),
        pltpu.SemaphoreType.DMA((6,)),
    ]


def greet(sizes):
    n = sizes["dp"]
    barrier = pltpu.get_barrier_semaphore()
    me = lax.axis_index("dp")
    for step in (-1, 1):
        @pl.when((me + step >= 0) & (me + step < n))
        def _():
            pl.semaphore_signal(
                barrier, inc=1, device_id={"dp": me + step}, device_id_type=MESH
            )
    number = sizes["ctx"] * sizes["exp"]
    for ahead in range(number - 1, 0, -1):
        pl.semaphore_signal(
            barrier, inc=1, device_id=place(sizes, peer(sizes, ahead)), device_id_type=MESH
        )
    neighbours = (me + n - 1) // n + (2 * n - 2 - me) // n
    pl.semaphore_wait(barrier, number - 1 + neighbours)


def plane_index(sizes):
    return lax.axis_index("ctx") * sizes["exp"] + lax.axis_index("exp")


def peer(sizes, ahead):
    number = sizes["ctx"] * sizes["exp"]
    return lax.rem(plane_index(sizes) + ahead, number)


def place(sizes, index):
    return {"ctx": index // sizes["exp"], "exp": lax.rem(index, sizes["exp"])}


def partner(sizes, turn):
    n_ctx, n_exp = sizes["ctx"], sizes["exp"]
    number = n_ctx * n_exp
    here = plane_index(sizes)
    if (n_ctx, n_exp) != (4, 2):
        return lax.rem(here + turn, number), lax.rem(here + number - turn, number)
    c, k = lax.axis_index("ctx"), lax.axis_index("exp")
    one_of = lambda *turns: sum(jnp.where(turn == t, 1, 0) for t in turns)
    over_x = lax.rem(lax.rem(c, 2) + one_of(2, 4, 6, 7), 2)
    over_y = lax.rem(c // 2 + one_of(3, 5, 6, 7), 2)
    over_k = lax.rem(k + one_of(1, 4, 5, 7), 2)
    other = (over_y * 2 + over_x) * 2 + over_k
    return other, other


def cut(widths, part):
    pieces = []
    for number, width in enumerate(widths):
        step = min(width, part)
        pieces += [(number, first, step) for first in range(0, width, step)]
    return pieces


def staged_rows(slots):
    return min(256, 1 << (slots.bit_length() - 1))


def dispatch_kernel(
    attended_ref, back_ref, token_ref, gain_ref, router_ref, chosen_ref, cot_ref, routes_ref,
    gate_w_ref, up_w_ref, down_w_ref,
    grads_out, mixed_out, parts_out, middle_ref, gates_ref, active_out, gate_out, up_out, rows_out,
    scaled_out, dots_out, pick_out,
    pick_ref, branch, far_in, turn_out, turn_in, sq_send, sq_recv, cot_column, mixed_column, parts_column,
    packed, packed_parts, parts_in, active, gate_grad, up_grad, scaled, dots,
    line_send, line_recv, plane_send, plane_recv, own_sem, row_send, row_recv, part_send, part_recv,
    load_sem, store_sem, *, sizes, pieces, experts, capacity,
):
    outs = (grads_out, mixed_out, parts_out)
    columns = (cot_column, mixed_column, parts_column)
    targets = (packed, packed, packed_parts)
    n, n_ctx, number = sizes["dp"], sizes["ctx"], sizes["ctx"] * sizes["exp"]
    me, here = lax.axis_index("dp"), plane_index(sizes)
    tokens, width = token_ref.shape
    groups, dests, rows, span = pick_ref.shape
    slots = groups * rows
    full, low = jnp.float32, jnp.bfloat16
    greet(sizes)

    def line_copy(f, origin, step):
        a, first, part = pieces[f]
        return remote(
            columns[a].at[origin, :, pl.ds(first, part)],
            columns[a].at[origin, :, pl.ds(first, part)],
            line_send.at[f, origin, (step + 1) // 2],
            line_recv.at[f, origin],
            {"dp": me + step},
        )

    def send_own(f):
        for step in (-1, 1):
            @pl.when((me + step >= 0) & (me + step < n))
            def _():
                line_copy(f, me, step).start()

    def plane_copy(f, ahead):
        a, first, part = pieces[f]
        target = peer(sizes, ahead)
        return remote(
            packed.at[target, pl.ds(0, slots), pl.ds(first, part)],
            outs[a].at[here, :, pl.ds(first, part)],
            plane_send.at[f, ahead],
            plane_recv.at[f, ahead],
            place(sizes, target),
        )

    def own_copy(f):
        a, first, part = pieces[f]
        return pltpu.make_async_copy(
            packed.at[here, pl.ds(0, slots), pl.ds(first, part)],
            outs[a].at[here, :, pl.ds(first, part)],
            own_sem.at[f],
        )

    cots = len([p for p in pieces if p[0] == 0])
    early = cots + cots // 2
    last_columns = pl.ds(pieces[early][1], width - pieces[early][1])

    def row_copy(turn):
        target, _ = partner(sizes, turn)
        return remote(
            packed.at[target, pl.ds(0, slots), last_columns], mixed_out.at[here, :, last_columns],
            row_send.at[turn], row_recv.at[turn], place(sizes, target),
        )

    def part_copy(turn):
        target, _ = partner(sizes, turn)
        return remote(
            packed_parts.at[target], parts_out.at[here], part_send.at[turn], part_recv.at[turn],
            place(sizes, target),
        )

    def send_rows(turns):
        for turn in turns:
            part_copy(turn).start()
            row_copy(turn).start()

    def spread(f):
        for distance in range(1, n):
            for step in (-1, 1):
                origin = me - step * distance
                beyond = me + step

                @pl.when((origin >= 0) & (origin < n))
                def _():
                    line_copy(f, origin, step).wait_recv()

                    @pl.when((beyond >= 0) & (beyond < n))
                    def _():
                        line_copy(f, origin, step).start()

            if distance == max(1, n - 2) and f + 1 < len(pieces):
                send_own(f + 1)

    def pick_rows(f):
        a, first, part = pieces[f]
        for g in range(groups):
            given = columns[a][pl.ds(g * span // tokens, span // tokens), :, pl.ds(first, part)]
            given = given.reshape(span, part)

            @pl.loop(0, dests)
            def _(j):
                targets[a][j, pl.ds(g * rows, rows), pl.ds(first, part)] = jnp.dot(
                    pick_ref[g, j], given, preferred_element_type=full
                ).astype(low)

    def push(f):
        for ahead in range(number - 1, 0, -1):
            plane_copy(f, ahead).start()
        own_copy(f).start()

    deep = staged_rows(slots)
    blocks = back_ref.shape[0] // deep
    weight_copies = [
        pltpu.make_async_copy(
            back_ref.at[pl.ds(i * deep, deep)], packed.at[i, pl.ds(0, deep)], load_sem.at[i]
        )
        for i in range(blocks)
    ]
    own_cot = pltpu.make_async_copy(cot_ref, cot_column.at[me], own_sem.at[0])
    own_cot.start()
    for copy in weight_copies:
        copy.start()
    own_cot.wait()
    send_own(0)

    together = span // tokens
    low_row = lax.broadcasted_iota(jnp.int32, (tokens, tokens), 0)
    low_lane = lax.broadcasted_iota(jnp.int32, (tokens, tokens), 1)
    earlier = (low_row < low_lane).astype(low)
    named = me * dests + lax.broadcasted_iota(jnp.int32, (dests, 1), 0)
    spots = lax.broadcasted_iota(jnp.int32, (rows, 1), 0).astype(full)
    for b in range(n):
        listed = routes_ref[b]
        hot = jnp.zeros((dests, tokens), full)
        for which in range(listed.shape[0]):
            hot += (listed[which : which + 1, :] == named).astype(full)
        before = jnp.dot(hot.astype(low), earlier, preferred_element_type=full)
        spot = jnp.where(hot > 0, before + b % together * capacity, -1.0)
        at = b % together * tokens
        for j in range(dests):
            pick_ref[b // together, j, :, at : at + tokens] = (
                spot[j : j + 1, :] == spots
            ).astype(low)
    pick_store = pltpu.make_async_copy(pick_ref, pick_out, store_sem.at[6])
    pick_store.start()
    for copy in weight_copies:
        copy.wait()

    scatter = SquareScatter(sizes, branch, far_in, turn_out, turn_in, sq_send, sq_recv, tokens)

    def project_block(index):
        at = pl.ds(index * tokens, tokens)
        total = jnp.zeros((tokens, width), full)
        for i in range(blocks):
            total += jnp.dot(
                attended_ref[at, i * deep : (i + 1) * deep], packed[i, 0:deep],
                preferred_element_type=full,
            )
        branch[at] = total.astype(low)

    project_block(scatter.far)
    scatter.start(1)
    for near in scatter.by:
        project_block(near)
    scatter.start(0)
    project_block(scatter.me)
    spread(0)
    pick_rows(0)
    scatter.turn()
    push(0)
    scatter.finish(middle_ref)
    middle_ref[...] += token_ref[...].astype(full)
    middle = middle_ref[...]
    inverse = lax.rsqrt(jnp.mean(middle * middle, axis=-1, keepdims=True) + eps_norm)
    mixed_column[me] = ((middle * inverse) * gain_ref[...]).astype(low)
    logits = jnp.dot(mixed_column[me], router_ref[...], preferred_element_type=full)
    chosen = chosen_ref[...] > 0
    logits = jnp.where(chosen, logits, masked_score)
    gates = jnp.exp(logits - jnp.max(logits, axis=-1, keepdims=True))
    gates = jnp.where(chosen, gates, 0.0)
    gates = gates / jnp.sum(gates, axis=-1, keepdims=True)
    gates_ref[...] = gates
    first_part = gates.astype(low).astype(full)
    second_part = (gates - first_part).astype(low).astype(full)
    third_part = gates - first_part - second_part
    lanes = gates.shape[1]
    if experts == lanes:
        terms = jnp.concatenate([first_part, second_part, third_part], axis=1)
    else:
        terms = (
            first_part
            + pltpu.roll(second_part, experts, 1)
            + pltpu.roll(third_part, 2 * experts, 1)
        )
    parts_column[me] = terms.astype(low)

    def sent(f):
        for ahead in range(1, number):
            plane_copy(f, ahead).wait_send()
        own_copy(f).wait()

    for f in range(1, cots):
        spread(f)
        pick_rows(f)
        push(f)
    scatter.close()
    for f in range(cots, early):
        spread(f)
        sent(f - cots)
        pick_rows(f)
        push(f)
    for f in range(early, len(pieces)):
        spread(f)
    for f in range(early - cots, cots):
        sent(f)

    def pick_turns(first_turn, last_turn):
        @pl.loop(first_turn, last_turn)
        def _(turn):
            j, _ = partner(sizes, turn)
            for a, first, part in pieces[early:]:
                for g in range(groups):
                    given = columns[a][
                        pl.ds(g * span // tokens, span // tokens), :, pl.ds(first, part)
                    ]
                    targets[a][j, pl.ds(g * rows, rows), pl.ds(first, part)] = jnp.dot(
                        pick_ref[g, j], given.reshape(span, part), preferred_element_type=full
                    ).astype(low)

    waves = [range(2, number)]
    pick_turns(1, waves[0][-1] + 1)
    send_rows((*waves[0], 1))
    pick_turns(0, 1)
    if len(waves) > 1:
        pick_turns(waves[1][0], number)
    own_rows = [
        pltpu.make_async_copy(
            packed.at[here, pl.ds(0, slots), last_columns], mixed_out.at[here, :, last_columns],
            own_sem.at[0],
        ),
        pltpu.make_async_copy(packed_parts.at[here], parts_out.at[here], own_sem.at[1]),
    ]
    for copy in own_rows:
        copy.start()
    for copy in own_rows:
        copy.wait()
    for f in range(cots, early):
        own_copy(f).wait()

    across = (((1,), (1,)), ((), ()))
    expert = me * number + here
    column = lax.broadcasted_iota(jnp.int32, (1, parts_in.shape[1]), 1)
    mine = (lax.rem(column, experts) == expert) & (column < 3 * experts)
    in_rows, in_grads, out_rows = (pl.ds(i * slots, slots) for i in range(3))
    cut_rows = slots

    def stores(source):
        given = (
            (branch.at[out_rows], rows_out), (scaled, scaled_out), (active, active_out),
            (gate_grad, gate_out), (up_grad, up_out), (dots, dots_out),
        )
        return [
            pltpu.make_async_copy(value, out.at[source], store_sem.at[i])
            for i, (value, out) in enumerate(given)
        ]

    @pl.loop(0, number)
    def _(i):
        _, source = partner(sizes, i)
        for wave, later in zip(waves, waves[1:]):
            @pl.when(i == wave[0])
            def _():
                for turn in wave:
                    row_copy(turn).wait_send()
                send_rows(later)

        @pl.when(i > 0)
        def _():
            row_copy(i).wait_recv()
            part_copy(i).wait_recv()

        @pl.when(i == 1)
        def _():
            for f in range(early):
                for ahead in range(1, number):
                    plane_copy(f, ahead).wait_recv()

        loads = [
            pltpu.make_async_copy(mixed_out.at[source], branch.at[in_rows], load_sem.at[0]),
            pltpu.make_async_copy(grads_out.at[source], branch.at[in_grads], load_sem.at[1]),
            pltpu.make_async_copy(parts_out.at[source], parts_in, load_sem.at[2]),
        ]
        for copy in loads:
            copy.start()

        @pl.when(i > 0)
        def _():
            for copy in stores(source):
                copy.wait()

        for copy in loads:
            copy.wait()

        @pl.loop(0, slots // cut_rows)
        def _(part):
            at = pl.ds(pl.multiple_of(part * cut_rows, cut_rows), cut_rows)
            at_in = at
            at_grads = pl.ds(pl.multiple_of(slots + part * cut_rows, cut_rows), cut_rows)
            at_out = pl.ds(pl.multiple_of(2 * slots + part * cut_rows, cut_rows), cut_rows)
            parts = parts_in[at].astype(full)
            slot_gates = jnp.sum(jnp.where(mine, parts, 0.0), axis=-1, keepdims=True)
            gate_pre = jnp.dot(branch[at_in], gate_w_ref[0], preferred_element_type=full)
            up_pre = jnp.dot(branch[at_in], up_w_ref[0], preferred_element_type=full)
            act_grad = slot_gates * lax.dot_general(
                branch[at_grads], down_w_ref[0], across, preferred_element_type=full
            )
            sigma = 1.0 / (1.0 + jnp.exp(-gate_pre))
            silu = gate_pre * sigma
            activated = silu * up_pre
            active_low = activated.astype(low)
            active[at] = (slot_gates * activated).astype(low)
            up_low = (act_grad * silu).astype(low)
            gate_low = (act_grad * up_pre * sigma * (1.0 + gate_pre * (1.0 - sigma))).astype(low)
            up_grad[at] = up_low
            gate_grad[at] = gate_low
            branch[at_out] = (
                lax.dot_general(gate_low, gate_w_ref[0], across, preferred_element_type=full)
                + lax.dot_general(up_low, up_w_ref[0], across, preferred_element_type=full)
            ).astype(low)
            given = jnp.dot(active_low, down_w_ref[0], preferred_element_type=full)
            given = given.astype(low).astype(full)
            scaled[at] = (slot_gates * given).astype(low)
            dot = jnp.sum(given * branch[at_grads].astype(full), axis=-1, keepdims=True)
            first = dot.astype(low).astype(full)
            second = (dot - first).astype(low).astype(full)
            third = dot - first - second
            terms = jnp.where(
                column < experts, first, jnp.where(column < 2 * experts, second, third)
            )
            dots[at] = jnp.where(mine, terms, 0.0).astype(low)

        for copy in stores(source):
            copy.start()

    for copy in stores(here):
        copy.wait()
    pick_store.wait()
    for turn in waves[-1]:
        row_copy(turn).wait_send()
    for f in range(len(pieces)):
        for distance in range(n):
            for step in (-1, 1):
                origin = me - step * distance
                beyond = me + step

                @pl.when((origin >= 0) & (origin < n) & (beyond >= 0) & (beyond < n))
                def _():
                    line_copy(f, origin, step).wait_send()

    for f in range(cots, early):
        for ahead in range(1, number):
            plane_copy(f, ahead).wait_send()
    row_copy(1).wait_send()
    for turn in range(1, number):
        part_copy(turn).wait_send()


def dispatch(
    attended, back, tokens, gain, router, chosen, cot, routes, gate_weight, up_weight, down_weight,
    experts, capacity, sizes, collective, part=512,
):
    rows_here, width = tokens.shape
    inner = gate_weight.shape[2]
    lanes = router.shape[1]
    extra = lanes if 3 * experts <= lanes else 3 * lanes
    widths = [width, width, extra]
    n, n_ctx, number = sizes["dp"], sizes["ctx"], sizes["ctx"] * sizes["exp"]
    together = 2 if 2 * capacity % 16 == 0 and n % 2 == 0 else n
    groups, dests, rows = n // together, number, -(-together * capacity // 16) * 16
    pick = (groups, dests, rows, together * rows_here)
    slots = groups * rows
    pieces = cut(widths, part)
    count = len(pieces)
    low, full = jnp.bfloat16, jnp.float32
    vmem, anywhere = pl.BlockSpec(memory_space=pltpu.VMEM), pl.BlockSpec(memory_space=pl.ANY)
    block = lambda *shape: pltpu.VMEM(shape, low)
    dma = lambda *shape: pltpu.SemaphoreType.DMA(shape)
    by_source = lambda columns: jax.ShapeDtypeStruct((number, slots, columns), low)
    return pl.pallas_call(
        functools.partial(
            dispatch_kernel, sizes=sizes, pieces=pieces, experts=experts, capacity=capacity
        ),
        in_specs=[vmem, anywhere] + [vmem] * 4 + [anywhere] + [vmem] * 4,
        out_specs=[anywhere] * 3 + [vmem] * 2 + [anywhere] * 7,
        out_shape=[by_source(columns) for columns in widths]
        + [
            jax.ShapeDtypeStruct((rows_here, width), full),
            jax.ShapeDtypeStruct((rows_here, lanes), full),
        ]
        + [by_source(columns) for columns in (inner, inner, inner, width, width, extra)]
        + [jax.ShapeDtypeStruct(pick, low)],
        scratch_shapes=[
            block(*pick),
            block(max(n_ctx * rows_here, 3 * slots), width),
            *square_scratch(rows_here, width),
            block(n, rows_here, width),
            block(n, rows_here, width),
            block(n, rows_here, extra),
            block(dests, slots, width),
            block(dests, slots, extra),
            block(slots, extra),
            block(slots, inner),
            block(slots, inner),
            block(slots, inner),
            block(slots, width),
            block(slots, extra),
            dma(count, n, 2), dma(count, n), dma(count, number), dma(count, number), dma(count),
            dma(number), dma(number), dma(number), dma(number),
            dma(max(3, back.shape[0] // staged_rows(slots))), dma(7),
        ],
        compiler_params=pltpu.CompilerParams(
            collective_id=collective, has_side_effects=True, vmem_limit_bytes=VMEM
        ),
    )(
        attended, back, tokens, gain, router, chosen, cot, routes, gate_weight, up_weight,
        down_weight,
    )


def combine_kernel(
    rows_ref, dots_ref, pick_ref, middle_ref, cot_ref, gain_ref, gates_ref, router_ref,
    in_ref, grad_ref, active_ref, gate_ref, up_ref,
    whole_ref, middle_grad_ref, gain_grad_ref, router_grad_ref, gate_out, up_out, down_out,
    back_rows, back_dots, leave_rows, leave_dots, land_rows, land_dots, total_rows, total_dots,
    sums, branch, line_send, line_recv, plane_send, plane_recv, own_sem, sq_send, sq_recv, sq_own,
    *, sizes, pieces, experts,
):
    sent, back = (dots_ref, rows_ref), (back_dots, back_rows)
    leaving, landing = (leave_dots, leave_rows), (land_dots, land_rows)
    totals = (total_dots, total_rows)
    n, number = sizes["dp"], sizes["ctx"] * sizes["exp"]
    me, here = lax.axis_index("dp"), plane_index(sizes)
    tokens = middle_ref.shape[0]
    groups, _, rows, span = pick_ref.shape
    full, low = jnp.float32, jnp.bfloat16
    greet(sizes)

    def plane_copy(f, ahead):
        a, first, part = pieces[f]
        target = peer(sizes, ahead)
        return remote(
            sent[a].at[target, :, pl.ds(first, part)],
            back[a].at[here, :, pl.ds(first, part)],
            plane_send.at[f, ahead],
            plane_recv.at[f, ahead],
            place(sizes, target),
        )

    def own_copy(f):
        a, first, part = pieces[f]
        return pltpu.make_async_copy(
            sent[a].at[here, :, pl.ds(first, part)],
            back[a].at[here, :, pl.ds(first, part)],
            own_sem.at[f],
        )

    for f in range(len(pieces)):
        for ahead in range(number - 1, 0, -1):
            plane_copy(f, ahead).start()
        own_copy(f).start()

    def line_copy(f, target, step):
        a, first, part = pieces[f]
        return remote(
            leaving[a].at[target, :, pl.ds(first, part)],
            landing[a].at[target + (step + 1) // 2, :, pl.ds(first, part)],
            line_send.at[f, target],
            line_recv.at[f, target + (step + 1) // 2],
            {"dp": me + step},
        )

    inner, chunk = active_ref.shape[1], 256
    slots = in_ref.shape[0]

    def weight_sum(left, right, out, by_left):
        def body(left_ref, right_ref, out_ref):
            out_ref[...] = lax.dot_general(
                left_ref[...], right_ref[...], (((0,), (0,)), ((), ())), preferred_element_type=full
            )

        if by_left:
            grid = left.shape[1] // chunk
            specs = [
                pl.BlockSpec((slots, chunk), lambda i: (0, i)),
                pl.BlockSpec((slots, inner), lambda i: (0, 0)),
            ]
            out_spec = pl.BlockSpec((chunk, inner), lambda i: (i, 0))
        else:
            grid = right.shape[1] // chunk
            specs = [
                pl.BlockSpec((slots, inner), lambda i: (0, 0)),
                pl.BlockSpec((slots, chunk), lambda i: (0, i)),
            ]
            out_spec = pl.BlockSpec((inner, chunk), lambda i: (0, i))
        pltpu.emit_pipeline(body, grid=(grid,), in_specs=specs, out_specs=[out_spec])(
            left, right, out
        )

    for f, (a, first, part) in enumerate(pieces):
        columns = pl.ds(first, part)
        if f == 1:
            weight_sum(in_ref, gate_ref, gate_out, True)
        elif f == 2:
            weight_sum(in_ref, up_ref, up_out, True)
        elif f == 3:
            weight_sum(active_ref, grad_ref, down_out, False)
        for ahead in range(1, number):
            plane_copy(f, ahead).wait_recv()
        own_copy(f).wait()
        for g in range(groups):
            gathered = back[a][:, pl.ds(g * rows, rows), columns].reshape(number * rows, part)
            sums[pl.ds(g * span // tokens, span // tokens), :, pl.ds(0, part)] = lax.dot_general(
                pick_ref[g].reshape(number * rows, span), gathered, (((0,), (0,)), ((), ())),
                preferred_element_type=full,
            ).reshape(span // tokens, tokens, part)

        for distance in range(n - 1, 0, -1):
            for step in (-1, 1):
                target = me + step * distance
                behind = me - step

                @pl.when((target >= 0) & (target < n))
                def _():
                    own = sums[target, :, pl.ds(0, part)]

                    @pl.when((behind >= 0) & (behind < n))
                    def _():
                        line_copy(f, target, step).wait_recv()
                        coming = landing[a][target + (step + 1) // 2, :, columns]
                        leaving[a][target, :, columns] = (own + coming.astype(full)).astype(low)

                    @pl.when((behind < 0) | (behind >= n))
                    def _():
                        leaving[a][target, :, columns] = own.astype(low)

                    line_copy(f, target, step).start()

        totals[a][:, columns] = sums[me, :, pl.ds(0, part)]
        for step in (-1, 1):
            @pl.when((me - step >= 0) & (me - step < n))
            def _():
                line_copy(f, me, step).wait_recv()
                totals[a][:, columns] += landing[a][me + (step + 1) // 2, :, columns].astype(full)

    gates = gates_ref[...]
    lanes = gates.shape[1]
    if experts == lanes:
        dots = sum(total_dots[:, k * lanes : (k + 1) * lanes] for k in range(3))
    else:
        dots = total_dots[...]
        dots = dots + pltpu.roll(dots, lanes - experts, 1) + pltpu.roll(dots, lanes - 2 * experts, 1)
    picked = gates * (dots - jnp.sum(gates * dots, axis=-1, keepdims=True))
    logit_grads = picked.astype(low)
    mixed_grad = total_rows[...] + lax.dot_general(
        logit_grads, router_ref[...], (((1,), (1,)), ((), ())), preferred_element_type=full
    )
    middle = middle_ref[...]
    inverse = lax.rsqrt(jnp.mean(middle * middle, axis=-1, keepdims=True) + eps_norm)
    normed = middle * inverse
    gain_grad_ref[...] = jnp.sum(mixed_grad * normed, axis=0, keepdims=True)
    scaled = mixed_grad * gain_ref[...]
    middle_grad = cot_ref[...].astype(full) + inverse * (
        scaled - normed * jnp.mean(scaled * normed, axis=-1, keepdims=True)
    )
    middle_grad_ref[...] = middle_grad
    branch[...] = middle_grad.astype(low)
    collect = SquareGather(sizes, branch, whole_ref, sq_send, sq_recv, sq_own.at[0])
    collect.start()
    router_grad_ref[...] = lax.dot_general(
        logit_grads, (normed * gain_ref[...]).astype(low), (((0,), (0,)), ((), ())),
        preferred_element_type=full,
    )
    collect.pass_on()

    for f in range(len(pieces)):
        for ahead in range(1, number):
            plane_copy(f, ahead).wait_send()
        for distance in range(1, n):
            for step in (-1, 1):
                target = me + step * distance

                @pl.when((target >= 0) & (target < n))
                def _():
                    line_copy(f, target, step).wait_send()
    collect.finish()


def combine(
    rows, dots, pick, middle, cot, gain, gates, router, rows_in, grads_in, active, gate_grad,
    up_grad, experts, sizes, collective, part=512,
):
    number, back_rows, width = rows.shape
    extra = dots.shape[2]
    tokens = middle.shape[0]
    lanes = router.shape[1]
    inner = active.shape[2]
    flat = lambda v: v.reshape(-1, v.shape[2])
    n, n_ctx = sizes["dp"], sizes["ctx"]
    low, full = jnp.bfloat16, jnp.float32
    pieces = cut([extra, width], part)
    count = len(pieces)
    both = (width, extra)
    vmem, anywhere = pl.BlockSpec(memory_space=pltpu.VMEM), pl.BlockSpec(memory_space=pl.ANY)
    dma = lambda *shape: pltpu.SemaphoreType.DMA(shape)
    return pl.pallas_call(
        functools.partial(combine_kernel, sizes=sizes, pieces=pieces, experts=experts),
        in_specs=[anywhere, anywhere] + [vmem] * 6 + [anywhere] * 5,
        out_specs=[anywhere] + [vmem] * 3 + [anywhere] * 3,
        out_shape=[
            jax.ShapeDtypeStruct((n_ctx, tokens, width), low),
            jax.ShapeDtypeStruct((tokens, width), full),
            jax.ShapeDtypeStruct((1, width), full),
            jax.ShapeDtypeStruct((lanes, width), full),
            jax.ShapeDtypeStruct((width, inner), full),
            jax.ShapeDtypeStruct((width, inner), full),
            jax.ShapeDtypeStruct((inner, width), full),
        ],
        scratch_shapes=[pltpu.VMEM((number, back_rows, w), low) for w in both]
        + [pltpu.VMEM((n, tokens, w), low) for w in both]
        + [pltpu.VMEM((n + 1, tokens, w), low) for w in both]
        + [pltpu.VMEM((tokens, w), full) for w in both]
        + [
            pltpu.VMEM((n, tokens, max(p[2] for p in pieces)), full),
            pltpu.VMEM((tokens, width), low),
            dma(count, n), dma(count, n + 1), dma(count, number), dma(count, number), dma(count),
            dma(6), dma(6), dma(1),
        ],
        compiler_params=pltpu.CompilerParams(
            collective_id=collective, has_side_effects=True, vmem_limit_bytes=VMEM
        ),
    )(
        rows, dots, pick, middle, cot, gain, gates, router, flat(rows_in), flat(grads_in),
        flat(active), flat(gate_grad), flat(up_grad),
    )


def gather_kernel(
    token_ref, front_ref, back_ref, route_ref, cos_ref, sin_ref, bounds_ref,
    fronts_out, backs_ref, routes_ref, hidden_out, raw_out, turned_out, attended_ref, gains_ref,
    scales_ref,
    tokens_ref, fronts_ref, held, hidden, raw, turned,
    sq_send, sq_recv, own_sem, fa_send, fa_recv, fl_send, fl_recv, fp_send, fp_recv,
    bl_send, bl_recv, ba_send, ba_recv, bp_send, bp_recv, rl_send, rl_recv, store_sem,
    *, sizes, gain_len, heads, kv_heads, experts,
):
    n, n_ctx, n_exp = sizes["dp"], sizes["ctx"], sizes["exp"]
    z, c, k = (lax.axis_index(a) for a in ALL)
    low, full = jnp.bfloat16, jnp.float32
    count, width = token_ref.shape
    owned = front_ref.shape[1]
    head = cos_ref.shape[1]
    columns = raw.shape[1]
    greet(sizes)

    def front_across(ahead):
        target = lax.rem(c + ahead, n_ctx)
        return remote(
            front_ref.at[target], fronts_ref.at[z, c, k], fa_send.at[ahead], fa_recv.at[ahead],
            {"ctx": target},
        )

    def front_line(origin, step):
        here = fronts_ref.at[origin, :, k]
        return remote(
            here, here, fl_send.at[origin, (step + 1) // 2], fl_recv.at[origin], {"dp": z + step}
        )

    def front_pair(origin, ahead):
        here = fronts_ref.at[origin, :, k]
        return remote(
            here, here, fp_send.at[origin, ahead], fp_recv.at[origin, ahead],
            {"exp": lax.rem(k + ahead, n_exp)},
        )

    def back_line(origin, step):
        here = held.at[origin]
        return remote(
            here, here, bl_send.at[origin, (step + 1) // 2], bl_recv.at[origin], {"dp": z + step}
        )

    def back_across(ahead):
        target = lax.rem(c + ahead, n_ctx)
        return remote(
            held.at[target], backs_ref.at[c, k], ba_send.at[ahead], ba_recv.at[ahead],
            {"ctx": target},
        )

    def back_pair(source, ahead):
        here = backs_ref.at[source, k]
        return remote(
            here, here, bp_send.at[source, ahead], bp_recv.at[source, ahead],
            {"exp": lax.rem(k + ahead, n_exp)},
        )

    def route_line(origin, step):
        here = routes_ref.at[origin]
        return remote(
            here, here, rl_send.at[origin, (step + 1) // 2], rl_recv.at[origin], {"dp": z + step}
        )

    def in_line(step):
        return (z + step >= 0) & (z + step < n)

    def start_line(line):
        for step in (-1, 1):
            @pl.when(in_line(step))
            def _():
                line(z, step).start()

    def pass_on(line, distance, after):
        for step in (-1, 1):
            origin = z - step * distance

            @pl.when((origin >= 0) & (origin < n))
            def _():
                line(origin, step).wait_recv()

                @pl.when(in_line(step))
                def _():
                    line(origin, step).start()

                after(origin)

    def nothing(origin):
        pass

    def to_siblings(origin):
        for ahead in range(1, n_exp):
            front_pair(origin, ahead).start()

    tokens = SquareGather(sizes, token_ref, tokens_ref, sq_send, sq_recv, own_sem.at[0])
    own_copies = [
        pltpu.make_async_copy(front_ref.at[c], fronts_ref.at[z, c, k], own_sem.at[1]),
        pltpu.make_async_copy(back_ref, held.at[z], own_sem.at[2]),
        pltpu.make_async_copy(route_ref, routes_ref.at[z], own_sem.at[3]),
    ]
    for copy in own_copies:
        copy.start()
    for ahead in range(1, n_ctx):
        front_across(ahead).start()
    tokens.start()
    for copy in own_copies:
        copy.wait()
    start_line(back_line)
    start_line(route_line)
    for ahead in range(1, n_ctx):
        front_across(ahead).wait_recv()
    start_line(front_line)
    to_siblings(z)
    pass_on(back_line, 1, nothing)
    tokens.pass_on()
    for distance in range(1, n):
        pass_on(front_line, distance, to_siblings)
        pass_on(route_line, distance, nothing)
    for origin in range(n):
        for ahead in range(1, n_exp):
            front_pair(origin, ahead).wait_recv()
    tokens.finish()
    fronts_store = pltpu.make_async_copy(fronts_ref, fronts_out, store_sem.at[0])
    fronts_store.start()

    place_of = columns + experts // 128 * 128
    spun = fronts_ref[..., place_of : place_of + 128].reshape(width, 128).astype(full).T
    lead = experts % 128
    gain = spun[lead : lead + 1, :]
    gains_ref[...] = spun[lead : lead + 8, :]
    row = lax.broadcasted_iota(jnp.int32, (width, head), 0)
    lane = lax.broadcasted_iota(jnp.int32, (width, head), 1)
    spot = lane // gain_len * owned + lax.rem(lane, gain_len)
    packed = spun[lead : lead + 8, :].astype(low)
    scales = [
        jnp.dot(packed, (row == spot + shift).astype(low), preferred_element_type=full)[2:3, :]
        for shift in (0, gain_len)
    ]
    scales_ref[0:1, :] = scales[0]
    scales_ref[1:2, :] = scales[1]

    def hidden_store(i):
        return pltpu.make_async_copy(
            hidden, hidden_out.at[pl.ds(pl.multiple_of(i * count, count), count)], store_sem.at[1]
        )

    def raw_store(i):
        return pltpu.make_async_copy(
            raw, raw_out.at[pl.ds(pl.multiple_of(i * count, count), count)], store_sem.at[2]
        )

    def project(first, last):
        @pl.loop(first, last)
        def _(i):
            x = tokens_ref[i].astype(full)
            inverse = lax.rsqrt(jnp.mean(x * x, axis=-1, keepdims=True) + eps_norm)

            @pl.when(i > 0)
            def _():
                hidden_store(i).wait()
                raw_store(i).wait()

            hidden[...] = ((x * inverse) * gain).astype(low)
            hidden_store(i).start()
            raw[...] = jnp.dot(
                hidden[...], fronts_ref[..., 0:columns].reshape(width, columns),
                preferred_element_type=full,
            )
            raw_store(i).start()
            at = pl.ds(pl.multiple_of(i * count, count), count)
            cosine, sine = cos_ref[at], sin_ref[at]
            for h in range(heads + kv_heads):
                here = slice(h * head, (h + 1) * head)
                part = raw[:, here]
                factor = lax.rsqrt(jnp.mean(part * part, axis=-1, keepdims=True) + eps_norm)
                scaled = part * factor * scales[0 if h < heads else 1]
                spun = pltpu.roll(scaled, head // 2, 1)
                turned[at, here] = (scaled * cosine + spun * sine).astype(low)
            rest = slice((heads + kv_heads) * head, columns)
            turned[at, rest] = raw[:, rest].astype(low)

    rows = n_ctx * count
    group = heads // kv_heads

    def attend(first_head, last_head):
        @pl.loop(first_head, last_head)
        def _(h):
            at = lambda which: pl.ds(pl.multiple_of(which * head, head), head)
            kv = h // group
            for first in range(0, rows, count):
                last = first + count
                allowed = seen(bounds_ref, first, count, last)
                shares = shares_of(
                    turned[first:last, at(h)], turned[0:last, at(heads + kv)], allowed,
                    head ** (-0.5),
                )
                attended_ref[first:last, at(h)] = jnp.dot(
                    shares.astype(low), turned[0:last, at(heads + kv_heads + kv)],
                    preferred_element_type=full,
                ).astype(low)

    project(0, n_ctx // 2)
    if n > 2:
        pass_on(back_line, 2, nothing)
    project(n_ctx // 2, n_ctx)
    turned_store = pltpu.make_async_copy(turned, turned_out, store_sem.at[3])
    turned_store.start()
    attend(0, heads // 4)
    for distance in range(3, n):
        pass_on(back_line, distance, nothing)
    for ahead in range(1, n_ctx):
        back_across(ahead).start()
    own_back = pltpu.make_async_copy(held.at[c], backs_ref.at[c, k], own_sem.at[4])
    own_back.start()
    attend(heads // 4, heads)
    own_back.wait()
    for ahead in range(1, n_exp):
        back_pair(c, ahead).start()
    for behind in range(1, n_ctx):
        back_across(behind).wait_recv()
        source = lax.rem(c + n_ctx - behind, n_ctx)
        for ahead in range(1, n_exp):
            back_pair(source, ahead).start()

    fronts_store.wait()
    hidden_store(n_ctx - 1).wait()
    raw_store(n_ctx - 1).wait()
    turned_store.wait()
    for ahead in range(1, n_ctx):
        front_across(ahead).wait_send()
        back_across(ahead).wait_send()
    for origin in range(n):
        for ahead in range(1, n_exp):
            front_pair(origin, ahead).wait_send()
    for source in range(n_ctx):
        for ahead in range(1, n_exp):
            back_pair(source, ahead).wait()
    for line in (route_line, front_line, back_line):
        for distance in range(n):
            for step in (-1, 1):
                origin = z - step * distance

                @pl.when((origin >= 0) & (origin < n) & in_line(step))
                def _():
                    line(origin, step).wait_send()


def gather(
    tokens, front, back, routes, cosine, sine, bounds, gain_len, heads, kv_heads, experts, sizes,
    collective,
):
    n, n_ctx, n_exp = sizes["dp"], sizes["ctx"], sizes["exp"]
    _, rows, front_columns = front.shape
    count, width = tokens.shape
    head = cosine.shape[1]
    columns = (heads + 2 * kv_heads) * head
    seq = n_ctx * count
    low, full = jnp.bfloat16, jnp.float32
    dma = lambda *shape: pltpu.SemaphoreType.DMA(shape)
    vmem, anywhere = pl.BlockSpec(memory_space=pltpu.VMEM), pl.BlockSpec(memory_space=pl.ANY)
    return pl.pallas_call(
        functools.partial(
            gather_kernel, sizes=sizes, gain_len=gain_len, heads=heads, kv_heads=kv_heads,
            experts=experts,
        ),
        in_specs=[vmem] * 6 + [pl.BlockSpec(memory_space=pltpu.SMEM)],
        out_specs=[anywhere] * 6 + [vmem] * 3,
        out_shape=[
            jax.ShapeDtypeStruct((n, n_ctx, n_exp, rows, front_columns), low),
            jax.ShapeDtypeStruct((n_ctx, n_exp) + back.shape, low),
            jax.ShapeDtypeStruct((n,) + routes.shape, routes.dtype),
            jax.ShapeDtypeStruct((seq, width), low),
            jax.ShapeDtypeStruct((seq, columns), full),
            jax.ShapeDtypeStruct((seq, columns), low),
            jax.ShapeDtypeStruct((seq, heads * head), low),
            jax.ShapeDtypeStruct((8, width), full),
            jax.ShapeDtypeStruct((2, head), full),
        ],
        scratch_shapes=[
            pltpu.VMEM((n_ctx, count, width), low),
            pltpu.VMEM((n, n_ctx, n_exp, rows, front_columns), low),
            pltpu.VMEM((n,) + back.shape, low),
            pltpu.VMEM((count, width), low),
            pltpu.VMEM((count, columns), full),
            pltpu.VMEM((seq, columns), low),
            dma(6), dma(6), dma(5),
            dma(n_ctx), dma(n_ctx), dma(n, 2), dma(n), dma(n, n_exp), dma(n, n_exp),
            dma(n, 2), dma(n), dma(n_ctx), dma(n_ctx), dma(n_ctx, n_exp), dma(n_ctx, n_exp),
            dma(n, 2), dma(n), dma(4),
        ],
        compiler_params=pltpu.CompilerParams(
            collective_id=collective, has_side_effects=True, vmem_limit_bytes=VMEM
        ),
    )(tokens, front, back, routes, cosine, sine, bounds)


def finish_kernel(
    bounds_ref, query_ref, key_ref, value_ref, grad_ref, raw_ref, scale_ref, cos_ref, sin_ref,
    hidden_ref, weight_ref, back_ref, rows_ref, pick_ref, result_ref, middle_ref, token_ref,
    gain_ref, small_ref,
    tokens_grad_ref, front_out, output_ref, back_out, small_out, landed_ref, back_in,
    key_sum, value_sum, raw_grad, head_gains, shared, arrived, back_one, fronts, front_pairs,
    front_in, rows_in, leaving, landing, far_in, turn_out, turn_in, hidden_send, hidden_recv,
    total, loaded, staged, small_all, small_in,
    own_sem, load_sem, stage_sem, bp_send, bp_recv, ba_send, ba_recv, bl_send, bl_recv,
    fp_send, fp_recv, fl_send, fl_recv, fa_send, fa_recv, plane_send, plane_recv, plane_own,
    line_send, line_recv, s_send, s_recv, *, block, heads, group, score_scale, sizes, part, chunk,
):
    step = pl.program_id(0)
    rows, head = query_ref.shape
    low, full = jnp.bfloat16, jnp.float32
    kv_heads = heads // group
    first_chunk = heads + 2 * kv_heads
    n, n_ctx, n_exp = sizes["dp"], sizes["ctx"], sizes["exp"]
    devices, number = n * n_ctx * n_exp, n_ctx * n_exp
    z, c, k = (lax.axis_index(a) for a in ALL)
    here, in_plane = (z * n_ctx + c) * n_exp + k, plane_index(sizes)
    tokens, width = token_ref.shape
    b_rows = back_out.shape[0]
    pieces = width // part
    chunks = width // chunk

    def in_line(index):
        return (index >= 0) & (index < n)

    def device_of(index):
        return {
            "dp": index // number,
            "ctx": lax.rem(index // n_exp, n_ctx),
            "exp": lax.rem(index, n_exp),
        }

    def back_own():
        return pltpu.make_async_copy(
            back_ref.at[:, k], shared.at[:, pl.ds(0, b_rows)], own_sem.at[0]
        )

    def back_pair(ahead):
        target = lax.rem(k + ahead, n_exp)
        return remote(
            back_ref.at[:, target], shared.at[:, pl.ds(ahead * b_rows, b_rows)],
            bp_send.at[ahead], bp_recv.at[ahead], {"exp": target},
        )

    def back_across(ahead):
        target = lax.rem(c + ahead, n_ctx)
        return remote(
            shared.at[target, pl.ds(0, b_rows)], arrived.at[c], ba_send.at[ahead],
            ba_recv.at[ahead], {"ctx": target},
        )

    def back_line(target, way):
        return remote(
            arrived.at[target], back_in.at[target + (way + 1) // 2], bl_send.at[target],
            bl_recv.at[target + (way + 1) // 2], {"dp": z + way},
        )

    def along_line(line, add, distance):
        for way in (-1, 1):
            target = z + way * distance

            @pl.when(in_line(target))
            def _():
                @pl.when(in_line(z - way))
                def _():
                    line(target, way).wait_recv()
                    add(target, target + (way + 1) // 2)

                line(target, way).start()

    def end_line(line, add):
        for way in (-1, 1):
            @pl.when(in_line(z - way))
            def _():
                line(z, way).wait_recv()
                add((way + 1) // 2 + z)

    def close_line(line):
        for distance in range(1, n):
            for way in (-1, 1):
                @pl.when(in_line(z + way * distance))
                def _():
                    line(z + way * distance, way).wait_send()

    def back_arrived(slot):
        copy = pltpu.make_async_copy(back_in.at[slot], back_one, stage_sem.at[1])
        copy.start()
        copy.wait()
        return back_one[...].astype(full)

    def add_back(target, slot):
        arrived[target] = (arrived[target].astype(full) + back_arrived(slot)).astype(low)

    def plane_copy(piece, ahead):
        target = peer(sizes, ahead)
        columns = pl.ds(piece * part, part)
        return remote(
            rows_ref.at[target, :, columns], landed_ref.at[in_plane, :, columns],
            plane_send.at[piece, ahead], plane_recv.at[piece, ahead], place(sizes, target),
        )

    def plane_own_copy(piece):
        columns = pl.ds(piece * part, part)
        return pltpu.make_async_copy(
            rows_ref.at[in_plane, :, columns], landed_ref.at[in_plane, :, columns],
            plane_own.at[piece],
        )

    def push(piece):
        for ahead in range(number - 1, 0, -1):
            plane_copy(piece, ahead).start()
        plane_own_copy(piece).start()

    def small_load():
        return pltpu.make_async_copy(small_ref, small_all, own_sem.at[1])

    @pl.when(step == 0)
    def _():
        head_gains[...] = jnp.zeros_like(head_gains)
        barrier = pltpu.get_barrier_semaphore()

        @pl.loop(1, devices)
        def _(ahead):
            pl.semaphore_signal(
                barrier, inc=1, device_id=device_of(lax.rem(here + ahead, devices)),
                device_id_type=MESH,
            )

        pl.semaphore_wait(barrier, devices - 1)
        back_own().start()
        for ahead in range(1, n_exp):
            back_pair(ahead).start()
        small_load().start()

    @pl.when(step == 1)
    def _():
        back_own().wait()
        for ahead in range(1, n_exp):
            back_pair(ahead).wait_recv()
        for index in range(n_ctx):
            summed = shared[index, 0:b_rows].astype(full)
            for ahead in range(1, n_exp):
                summed = summed + shared[index, ahead * b_rows : (ahead + 1) * b_rows].astype(full)
            shared[index, 0:b_rows] = summed.astype(low)
        for ahead in range(1, n_ctx):
            back_across(ahead).start()
        arrived[c] = shared[c, 0:b_rows]
        push(0)
        small_load().wait()

    for piece in range(1, pieces):
        @pl.when(step == min(1 + 4 * piece, first_chunk))
        def _():
            push(piece)

    for distance in range(n - 1, 0, -1):
        @pl.when(step == min(6 + 3 * (n - 1 - distance), first_chunk + chunks - 2))
        def _():
            if distance == n - 1:
                for ahead in range(1, n_ctx):
                    back_across(ahead).wait_recv()
                    back_across(ahead).wait_send()
                for ahead in range(1, n_exp):
                    back_pair(ahead).wait_send()
            along_line(back_line, add_back, distance)

    def norm_rope_back(grad, raw, scale, cosine, sine):
        inverse = lax.rsqrt(jnp.mean(raw * raw, axis=-1, keepdims=True) + eps_norm)
        normed = raw * inverse
        turned = grad * cosine + pltpu.roll(grad * sine, grad.shape[-1] // 2, 1)
        inner = turned * scale
        back = inverse * (inner - normed * jnp.mean(inner * normed, axis=-1, keepdims=True))
        return back, jnp.sum(turned * normed, axis=0, keepdims=True)

    for kv in range(kv_heads):
        @pl.when(step == kv * group)
        def _():
            key_sum[kv] = jnp.zeros((rows, head), full)
            value_sum[kv] = jnp.zeros((rows, head), full)

    here_columns = pl.ds(pl.multiple_of(step * head, head), head)

    @pl.when(step < heads)
    def _():
        kv = step // group
        gains = jnp.zeros((1, head), full)
        for first in range(0, rows, block):
            last = first + block
            query, keys, values = query_ref[first:last, :], key_ref[:last, :], value_ref[:last, :]
            grad = grad_ref[first:last, :]
            allowed = seen(bounds_ref, first, block, last)
            shares = shares_of(query, keys, allowed, score_scale)
            share_grads = lax.dot_general(
                grad, values, (((1,), (1,)), ((), ())), preferred_element_type=full
            )
            centre = jnp.sum(shares * share_grads, axis=-1, keepdims=True)
            score_grads = (shares * (share_grads - centre)).astype(low)
            key_sum[kv, :last, :] += lax.dot_general(
                score_grads, query, (((0,), (0,)), ((), ())), preferred_element_type=full
            )
            value_sum[kv, :last, :] += lax.dot_general(
                shares.astype(low), grad, (((0,), (0,)), ((), ())), preferred_element_type=full
            )
            query_grad = jnp.dot(score_grads, keys, preferred_element_type=full) * score_scale
            back, gain = norm_rope_back(
                query_grad, raw_ref[first:last, :], scale_ref[0:1, :], cos_ref[first:last, :],
                sin_ref[first:last, :],
            )
            raw_grad[first:last, here_columns] = back.astype(low)
            gains += gain
        head_gains[0:1, :] += gains

    @pl.when((step >= heads) & (step < heads + kv_heads))
    def _():
        back, gain = norm_rope_back(
            key_sum[step - heads] * score_scale, raw_ref[...], scale_ref[1:2, :], cos_ref[...],
            sin_ref[...],
        )
        raw_grad[:, here_columns] = back.astype(low)
        head_gains[1:2, :] += gain

    @pl.when((step >= heads + kv_heads) & (step < first_chunk))
    def _():
        raw_grad[:, here_columns] = value_sum[step - heads - kv_heads].astype(low)

    @pl.when((step >= first_chunk) & (step < first_chunk + chunks))
    def _():
        q = step - first_chunk
        grads = raw_grad[...]
        shared[:, 0:tokens, pl.ds(pl.multiple_of(q * chunk, chunk), chunk)] = (
            lax.dot_general(
                grads, weight_ref[:, : grads.shape[1]], (((1,), (1,)), ((), ())),
                preferred_element_type=full,
            )
            .astype(low)
            .reshape(n_ctx, tokens, chunk)
        )
        fronts[q // 2, lax.rem(q, 2)] = (
            lax.dot_general(
                hidden_ref[...], grads, (((0,), (0,)), ((), ())), preferred_element_type=full
            )
            .astype(low)
            .reshape(fronts.shape[2:])
        )

    def front_pair(ahead):
        target = lax.rem(k + ahead, n_exp)
        return remote(
            fronts.at[:, :, :, target], front_pairs.at[ahead - 1], fp_send.at[ahead],
            fp_recv.at[ahead], {"exp": target},
        )

    def front_line(target, way):
        return remote(
            fronts.at[target, :, :, k], front_in.at[target + (way + 1) // 2], fl_send.at[target],
            fl_recv.at[target + (way + 1) // 2], {"dp": z + way},
        )

    def front_across(ahead):
        target = lax.rem(c + ahead, n_ctx)
        return remote(
            fronts.at[z, target // (n_ctx // 2), lax.rem(target, n_ctx // 2), k], front_out.at[c],
            fa_send.at[ahead], fa_recv.at[ahead], {"ctx": target},
        )

    def add_front(target, slot):
        fronts[target, :, :, k] = (
            fronts[target, :, :, k].astype(full) + front_in[slot].astype(full)
        ).astype(low)

    def line_of(piece):
        columns = pl.ds(piece * part, part)

        def line(target, way):
            return remote(
                leaving.at[target, :, columns],
                landing.at[target + (way + 1) // 2, :, columns],
                line_send.at[piece, target], line_recv.at[piece, target + (way + 1) // 2],
                {"dp": z + way},
            )

        return line

    def load_rows(piece):
        return pltpu.make_async_copy(
            landed_ref.at[:, :, pl.ds(piece * part, part)], rows_in, load_sem.at[0]
        )

    def load_part(source, piece):
        return pltpu.make_async_copy(
            source.at[:, pl.ds(piece * part, part)], loaded.at[piece % 2], load_sem.at[1 + piece % 2]
        )

    def mix_in(piece):
        for ahead in range(1, number):
            plane_copy(piece, ahead).wait_recv()
        plane_own_copy(piece).wait()
        load_rows(piece).start()
        load_part(result_ref, piece).start()
        load_rows(piece).wait()
        groups, _, back_rows, span = pick_ref.shape
        columns = pl.ds(piece * part, part)
        for g in range(groups):
            gathered = rows_in[:, pl.ds(g * back_rows, back_rows), :]
            leaving[pl.ds(g * span // tokens, span // tokens), :, columns] = (
                lax.dot_general(
                    pick_ref[g].reshape(number * back_rows, span),
                    gathered.reshape(number * back_rows, part),
                    (((0,), (0,)), ((), ())),
                    preferred_element_type=full,
                )
                .astype(low)
                .reshape(span // tokens, tokens, part)
            )

    def start_total(piece):
        columns = pl.ds(piece * part, part)
        load_part(result_ref, piece).wait()
        total[:, columns] = leaving[z, :, columns].astype(full) + loaded[piece % 2]

    def mix_line(piece, distance):
        columns = pl.ds(piece * part, part)

        def add(target, slot):
            leaving[target, :, columns] = (
                leaving[target, :, columns].astype(full) + landing[slot, :, columns].astype(full)
            ).astype(low)

        along_line(line_of(piece), add, distance)

    def mix_end(piece):
        columns = pl.ds(piece * part, part)

        def add(slot):
            total[:, columns] += landing[slot, :, columns].astype(full)

        end_line(line_of(piece), add)

    @pl.when(step == first_chunk + chunks - 1)
    def _():
        mix_in(0)
        mix_line(0, n - 1)

    def small_copy(ahead):
        target = lax.rem(here + ahead, devices)
        return remote(
            small_all.at[target], small_in.at[ahead], s_send.at[0], s_recv.at[0],
            device_of(target),
        )

    def all_small():
        others = pl.ds(1, devices - 1)
        return remote(
            small_all.at[others], small_in.at[others], s_send.at[0], s_recv.at[0], {"dp": z}
        )

    @pl.when(step == first_chunk + chunks)
    def _():
        for ahead in range(1, n_exp):
            front_pair(ahead).start()
        gain_owned = head // devices
        for index in range(devices):
            for which in (0, 1):
                small_all[index, which : which + 1, 0:gain_owned] = head_gains[
                    which : which + 1, index * gain_owned : (index + 1) * gain_owned
                ]

        @pl.loop(1, devices)
        def _(ahead):
            small_copy(ahead).start()

        hidden = SquareScatter(
            sizes, shared, far_in, turn_out, turn_in, hidden_send, hidden_recv, tokens
        )
        hidden.start(1)
        hidden.start(0)
        total[0:b_rows, :] = arrived[z].astype(full)

        def add_last(slot):
            total[0:b_rows, :] += back_arrived(slot)

        end_line(back_line, add_last)
        back_store = pltpu.make_async_copy(total.at[pl.ds(0, b_rows)], back_out, stage_sem.at[0])
        back_store.start()
        back_store.wait()
        if n > 2:
            mix_line(0, n - 2)
        for ahead in range(1, n_exp):
            front_pair(ahead).wait_recv()
        for target in range(n):
            summed = fronts[target, :, :, k].astype(full)
            for ahead in range(1, n_exp):
                summed = summed + front_pairs[ahead - 1, target].astype(full)
            fronts[target, :, :, k] = summed.astype(low)
        along_line(front_line, add_front, n - 1)
        for distance in range(n - 3, 0, -1):
            mix_line(0, distance)
        start_total(0)
        mix_end(0)
        front_own = pltpu.make_async_copy(
            fronts.at[z, c // (n_ctx // 2), lax.rem(c, n_ctx // 2), k], front_out.at[c],
            stage_sem.at[0],
        )
        for piece in range(1, pieces):
            if piece == pieces - 1:
                all_small().wait_recv()
                small_out[...] = small_all[here] + jnp.sum(small_in[1:devices], axis=0)
            mix_in(piece)
            mix_line(piece, n - 1)
            start_total(piece)
            for distance in range(n - 2, 0, -1):
                if piece == 1:
                    along_line(front_line, add_front, distance)
                mix_line(piece, distance)
                if piece == pieces - 1 and distance == max(1, n - 2):
                    hidden.turn()
            if piece == 1:
                end_line(front_line, lambda slot: add_front(z, slot))
                for ahead in range(1, n_ctx):
                    front_across(ahead).start()
                front_own.start()
            mix_end(piece)
        front_own.wait()
        staged[...] = total[...].astype(low)
        output_store = pltpu.make_async_copy(staged, output_ref, stage_sem.at[0])
        output_store.start()

        load_part(middle_ref, 0).start()
        hidden.finish(total)
        x = token_ref[...].astype(full)
        inverse = lax.rsqrt(jnp.mean(x * x, axis=-1, keepdims=True) + eps_norm)
        normed = x * inverse
        grad = total[...]
        scaled = grad * gain_ref[...]
        total[...] = inverse * (scaled - normed * jnp.mean(scaled * normed, axis=-1, keepdims=True))
        output_store.wait()
        for piece in range(pieces):
            if piece + 1 < pieces:
                load_part(middle_ref, piece + 1).start()
            load_part(middle_ref, piece).wait()
            columns = pl.ds(piece * part, part)
            staged[:, columns] = (total[:, columns] + loaded[piece % 2]).astype(low)
        tokens_store = pltpu.make_async_copy(staged, tokens_grad_ref, stage_sem.at[0])
        tokens_store.start()
        for ahead in range(1, n_ctx):
            front_across(ahead).wait()
        tokens_store.wait()

        all_small().wait_send()
        hidden.close()
        for ahead in range(1, n_exp):
            front_pair(ahead).wait_send()
        for piece in range(pieces):
            for ahead in range(1, number):
                plane_copy(piece, ahead).wait_send()
            close_line(line_of(piece))
        close_line(back_line)
        close_line(front_line)


def finish(
    bounds, turned, grad, raw, scales, cosine, sine, hidden, weight, back, rows_back, pick, result,
    middle_grad, tokens, gain, small, heads, kv_heads, head, sizes, collective, part=512,
):
    n, n_ctx, n_exp = sizes["dp"], sizes["ctx"], sizes["exp"]
    devices, number = n * n_ctx * n_exp, n_ctx * n_exp
    low, full = jnp.bfloat16, jnp.float32
    rows, columns = raw.shape
    count, width = tokens.shape
    b_rows = back.shape[2]
    f_rows = width // devices
    chunk = width // (2 * n)
    group = heads // kv_heads
    back_rows = rows_back.shape[1]
    s_rows, s_cols = small.shape[1:]
    pieces = width // part
    first_chunk = heads + 2 * kv_heads
    within = lambda h: jnp.minimum(h, heads - 1)
    now = lambda h: jnp.clip(h - first_chunk, 0, 2 * n - 1)
    once = pl.Buffered(buffer_count=1)
    whole = lambda shape: pl.BlockSpec(shape, lambda h: (0,) * len(shape), pipeline_mode=once)
    anywhere = pl.BlockSpec(memory_space=pl.ANY)
    vmem = lambda *shape: pltpu.VMEM(shape, low)
    wide = lambda *shape: pltpu.VMEM(shape, full)
    dma = lambda *shape: pltpu.SemaphoreType.DMA(shape)
    half = n_ctx // 2
    return pl.pallas_call(
        functools.partial(
            finish_kernel, block=count, heads=heads, group=group, score_scale=head ** (-0.5),
            sizes=sizes, part=part, chunk=chunk,
        ),
        grid=(first_chunk + 2 * n + 1,),
        in_specs=[
            pl.BlockSpec(memory_space=pltpu.SMEM),
            pl.BlockSpec((rows, head), lambda h: (0, within(h))),
            pl.BlockSpec((rows, head), lambda h: (0, heads + within(h) // group)),
            pl.BlockSpec((rows, head), lambda h: (0, heads + kv_heads + within(h) // group)),
            pl.BlockSpec((rows, head), lambda h: (0, within(h))),
            pl.BlockSpec((rows, head), lambda h: (0, jnp.minimum(h, heads + kv_heads - 1))),
            whole(scales.shape),
            whole(cosine.shape),
            whole(sine.shape),
            pl.BlockSpec((rows, chunk), lambda h: (0, now(h))),
            pl.BlockSpec((chunk, weight.shape[1]), lambda h: (now(h), 0)),
            anywhere,
            anywhere,
            whole(pick.shape),
            anywhere,
            anywhere,
            whole(tokens.shape),
            whole(gain.shape),
            anywhere,
        ],
        out_specs=[anywhere] * 4
        + [pl.BlockSpec((s_rows, s_cols), lambda h: (0, 0)), anywhere, anywhere],
        out_shape=[
            jax.ShapeDtypeStruct((count, width), low),
            jax.ShapeDtypeStruct((n_ctx, f_rows, columns), low),
            jax.ShapeDtypeStruct((count, width), low),
            jax.ShapeDtypeStruct((b_rows, width), full),
            jax.ShapeDtypeStruct((s_rows, s_cols), full),
            jax.ShapeDtypeStruct(rows_back.shape, low),
            jax.ShapeDtypeStruct((n + 1, b_rows, width), low),
        ],
        scratch_shapes=[
            wide(kv_heads, rows, head),
            wide(kv_heads, rows, head),
            vmem(rows, columns),
            wide(2, head),
            vmem(n_ctx, max(count, n_exp * b_rows), width),
            vmem(n_ctx, b_rows, width),
            vmem(b_rows, width),
            vmem(n, 2, half, n_exp, f_rows, columns),
            vmem(n_exp - 1, n, 2, half, f_rows, columns),
            vmem(n + 1, 2, half, f_rows, columns),
            vmem(number, back_rows, part),
            vmem(n, count, width),
            vmem(n + 1, count, width),
            *square_scratch(count, width),
            wide(count, width),
            wide(2, count, part),
            vmem(count, width),
            wide(devices, s_rows, s_cols),
            wide(devices, s_rows, s_cols),
            dma(2), dma(3), dma(2), dma(n_exp), dma(n_exp), dma(n_ctx), dma(n_ctx), dma(n),
            dma(n + 1), dma(n_exp), dma(n_exp), dma(n), dma(n + 1), dma(n_ctx), dma(n_ctx),
            dma(pieces, number), dma(pieces, number), dma(pieces), dma(pieces, n),
            dma(pieces, n + 1), dma(1), dma(1),
        ],
        compiler_params=pltpu.CompilerParams(
            collective_id=collective, has_side_effects=True, vmem_limit_bytes=VMEM
        ),
    )(
        bounds, turned, turned, turned, grad, raw, scales, cosine, sine, hidden, weight, back,
        rows_back, pick, result, middle_grad, tokens, gain, small,
    )


def shards(
    tokens,
    attention_gain,
    query_weight,
    key_weight,
    value_weight,
    query_gain,
    key_gain,
    output_weight,
    mixture_gain,
    router_weight,
    gate_weight,
    up_weight,
    down_weight,
    routes,
    bounds,
    cotangent,
):
    low, full = jnp.bfloat16, jnp.float32
    n_dp, n_ctx, n_exp = (lax.axis_size(a) for a in ALL)
    devices = n_dp * n_ctx * n_exp
    tok_count, width = tokens.shape[1], tokens.shape[2]
    seq_len = tok_count * n_ctx
    head_dim = query_gain.shape[0] * devices
    rows = query_weight.shape[0]
    heads = query_weight.shape[1] // head_dim
    kv_heads = key_weight.shape[1] // head_dim
    kv_here = kv_heads // n_ctx
    group_size = heads // kv_heads
    q_cols, kv_cols = heads * head_dim // n_ctx, kv_here * head_dim
    experts = router_weight.shape[1]
    topk = routes.shape[2]
    base_rows = tok_count * topk // experts
    capacity = base_rows + max(1, base_rows // 8)
    plane = experts // n_dp
    local_experts = gate_weight.shape[0]
    score_scale = head_dim ** (-0.5)
    dp_index = lax.axis_index("dp")

    gain_len = query_gain.shape[0]
    small = jnp.concatenate(
        [
            router_weight,
            attention_gain[:, None],
            mixture_gain[:, None],
            jnp.pad(jnp.concatenate([query_gain, key_gain]), (0, rows - 2 * gain_len))[:, None],
        ],
        axis=1,
    ).astype(low)
    small = jnp.pad(small, ((0, 0), (0, -small.shape[1] % 128)))
    extra = small.shape[1]

    def by_ctx(weight):
        return weight.astype(low).reshape(rows, n_ctx, -1).transpose(1, 0, 2)

    front = jnp.concatenate(
        [
            by_ctx(query_weight),
            by_ctx(key_weight),
            by_ctx(value_weight),
            jnp.broadcast_to(small[None], (n_ctx, rows, extra)),
        ],
        axis=2,
    )
    sizes = {"dp": n_dp, "ctx": n_ctx, "exp": n_exp}
    heads_here = heads // n_ctx
    cosine, sine = rope_tables(jnp.arange(seq_len, dtype=jnp.int32), head_dim)
    half = head_dim // 2
    sine = jnp.concatenate([-sine[:, :half], sine[:, half:]], axis=1)
    (
        front, output_part, column_routes, hidden, raw, turned, attended_low, gains, scales
    ) = gather(
        tokens[0], front, output_weight.astype(low), routes[0].T, cosine, sine, bounds, gain_len,
        heads_here, kv_here, experts, sizes, 3,
    )
    front = front.reshape(width, -1)
    output_part = output_part.reshape(q_cols, width)
    first_gain, second_gain = gains[0:1], gains[1:2]

    lanes = -(-experts // 128) * 128
    after = q_cols + 2 * kv_cols
    router_wide = front[:, after : after + lanes]
    own_chosen = jnp.any(
        routes[0][:, :, None] == jnp.arange(lanes, dtype=jnp.int32), axis=1
    ).astype(full)
    (
        grad_rows, expert_in, _, middle, own_gates, active, gate_grad, up_grad, row_grads,
        scaled_out, dot_rows, pick,
    ) = dispatch(
        attended_low, output_part, tokens[0], second_gain, router_wide, own_chosen,
        cotangent[0], column_routes, gate_weight, up_weight, down_weight, experts, capacity, sizes,
        1,
    )
    branch_low, middle_grad, second_gain_grad, router_grad, gate_w_grad, up_w_grad, down_grad = combine(
        row_grads, dot_rows, pick, middle, cotangent[0], second_gain, own_gates, router_wide,
        expert_in, grad_rows, active, gate_grad, up_grad, experts, sizes, 2,
    )
    gate_w_grad, up_w_grad, down_grad = gate_w_grad[None], up_w_grad[None], down_grad[None]
    router_grad = router_grad[:experts].T
    branch_low = branch_low.reshape(seq_len, width)
    output_w_grad = jnp.einsum("ti,td->id", attended_low, branch_low, preferred_element_type=full)
    attended_grad = jnp.einsum("td,id->ti", branch_low, output_part, preferred_element_type=full)
    rest = jnp.concatenate(
        [second_gain_grad.reshape(devices, -1), router_grad.reshape(devices, -1)], axis=1
    )
    columns = -(-rest.shape[1] // (5 * 128)) * 128
    rest = jnp.pad(rest, ((0, 0), (0, 5 * columns - rest.shape[1]))).reshape(devices, 5, columns)
    small = jnp.pad(rest, ((0, 0), (3, 0), (0, 0)))
    tokens_grad, front_grad, output, output_share, small, _, _ = finish(
        bounds, turned, attended_grad.astype(low), raw, scales, cosine, sine, hidden, front,
        output_w_grad.astype(low).reshape(n_ctx, n_exp, -1, width), scaled_out, pick, middle,
        middle_grad, tokens[0], first_gain, small, heads_here, kv_here, head_dim, sizes, 4,
        part=512 if n_ctx * n_exp <= 8 else 256,
    )
    tokens_grad = tokens_grad[None]
    output = output[None]
    front_grad = front_grad.astype(full)
    query_share = front_grad[:, :, :q_cols].transpose(1, 0, 2).reshape(rows, -1)
    key_share = front_grad[:, :, q_cols : q_cols + kv_cols].transpose(1, 0, 2).reshape(rows, -1)
    value_share = front_grad[:, :, q_cols + kv_cols :].transpose(1, 0, 2).reshape(rows, -1)
    first_share = sum(
        jnp.sum(weight.astype(low).astype(full) * grad, axis=1)
        for weight, grad in (
            (query_weight, query_share), (key_weight, key_share), (value_weight, value_share)
        )
    ) / attention_gain.astype(low).astype(full)
    query_gain_share = small[0, :gain_len]
    key_gain_share = small[1, :gain_len]
    rest = small[3:].reshape(-1)
    second_share = rest[:rows]
    router_share = rest[rows : rows + rows * experts].reshape(rows, experts)
    return (
        output,
        tokens_grad,
        first_share,
        query_share,
        key_share,
        value_share,
        query_gain_share,
        key_gain_share,
        output_share,
        second_share,
        router_share,
        gate_w_grad,
        up_w_grad,
        down_grad,
    )


def solution(mesh):
    rows = P(ALL)
    sequences = P(("dp", "exp"), "ctx")
    in_specs = (sequences,) + (rows,) * 12 + (sequences, P(("dp", "exp")), sequences)
    out_specs = (sequences,) * 2 + (rows,) * 12
    return jax.shard_map(shards, mesh=mesh, in_specs=in_specs, out_specs=out_specs, check_vma=False)
```

```python
import functools

import jax
import jax.numpy as jnp
from jax import lax
from jax.experimental import pallas as pl
from jax.experimental.pallas import tpu as pltpu
from jax.sharding import PartitionSpec as P

eps_norm = 1e-06
rope_base = 1000000.0
masked_score = -1e30
ALL = ("dp", "ctx", "exp")
VMEM = 60 << 20
MESH = pl.DeviceIdType.MESH


def rope_tables(positions, width):
    exponents = jnp.arange(width // 2, dtype=jnp.float32) * (2.0 / width)
    frequency = rope_base ** (-exponents)
    angles = positions.astype(jnp.float32)[:, None] * frequency[None, :]
    angles = jnp.concatenate([angles, angles], axis=-1)
    return (jnp.cos(angles), jnp.sin(angles))


def seen(bounds_ref, first, rows, keys):
    query = first + lax.broadcasted_iota(jnp.int32, (rows, 1), 0)
    low_end, high_end = bounds_ref[0, 0], bounds_ref[0, 1]
    start = jnp.where(query >= high_end, high_end, jnp.where(query >= low_end, low_end, 0))
    key = lax.broadcasted_iota(jnp.int32, (rows, keys), 1)
    return (key <= query) & (key >= start)


def shares_of(query, keys, allowed, score_scale):
    scores = lax.dot_general(
        query, keys, (((1,), (1,)), ((), ())), preferred_element_type=jnp.float32
    )
    scores = jnp.where(allowed, scores * score_scale, masked_score)
    weights = jnp.exp(scores - jnp.max(scores, axis=-1, keepdims=True))
    return weights / jnp.sum(weights, axis=-1, keepdims=True)


def square(sizes):
    me = lax.axis_index("ctx")
    return me + 1 - 2 * lax.rem(me, 2), lax.rem(me + 2, 4)


def remote(source, target, send, recv, device):
    return pltpu.make_async_remote_copy(
        src_ref=source, dst_ref=target, send_sem=send, recv_sem=recv, device_id=device,
        device_id_type=MESH,
    )


class SquareGather:
    def __init__(self, sizes, block, whole, send, recv, own_sem):
        self.block, self.whole, self.send, self.recv = block, whole, send, recv
        self.me = lax.axis_index("ctx")
        self.by = square(sizes)
        self.half = block.shape[1] // 2
        self.own = pltpu.make_async_copy(block, whole.at[self.me], own_sem)

    def copy(self, place, part, side, number):
        columns = pl.ds(part * self.half, self.half)
        target = self.whole.at[place, :, columns]
        source = self.block.at[:, columns] if number < 4 else target
        return remote(
            source, target, self.send.at[number], self.recv.at[number], {"ctx": self.by[side]}
        )

    def first(self, number):
        part, side = ((0, 0), (1, 1), (1, 0), (0, 1))[number]
        return self.copy(self.me, part, side, number)

    def start(self):
        self.own.start()
        for number in range(4):
            self.first(number).start()

    def pass_on(self):
        for part in (0, 1):
            self.first(part).wait_recv()
            self.copy(self.by[part], part, 1 - part, 4 + part).start()

    def finish(self):
        for number in (2, 3):
            self.first(number).wait_recv()
        for part in (0, 1):
            last = self.copy(self.by[part], part, 1 - part, 4 + part)
            last.wait_recv()
            last.wait_send()
        for number in range(4):
            self.first(number).wait_send()
        self.own.wait()


class SquareScatter:
    def __init__(self, sizes, parts, far_in, turn_out, turn_in, send, recv, rows):
        self.parts, self.far_in, self.turn_out, self.turn_in = parts, far_in, turn_out, turn_in
        self.send, self.recv, self.rows = send, recv, rows
        self.me = lax.axis_index("ctx")
        self.by = square(sizes)
        self.far = sizes["ctx"] - 1 - self.me
        half = parts.shape[-1] // 2
        self.columns = (pl.ds(0, half), pl.ds(half, half))

    def at(self, place, side):
        if len(self.parts.shape) == 2:
            return pl.ds(place * self.rows, self.rows), self.columns[side]
        return place, pl.ds(0, self.rows), self.columns[side]

    def first(self, side, number):
        place = self.by[side] if number == 0 else self.far
        index = 2 * side + number
        return remote(
            self.parts.at[self.at(place, side)], self.far_in.at[side, number],
            self.send.at[index], self.recv.at[index], {"ctx": self.by[side]},
        )

    def second(self, side):
        return remote(
            self.turn_out.at[side], self.turn_in.at[side], self.send.at[4 + side],
            self.recv.at[4 + side], {"ctx": self.by[1 - side]},
        )

    def start(self, number):
        for side in (0, 1):
            self.first(side, number).start()

    def turn(self):
        for side in (0, 1):
            self.first(side, 1).wait_recv()
            own = self.parts[self.at(self.by[1 - side], side)].astype(jnp.float32)
            self.turn_out[side] = (own + self.far_in[side, 1].astype(jnp.float32)).astype(
                jnp.bfloat16
            )
            self.second(side).start()

    def finish(self, total):
        for side in (0, 1):
            self.first(side, 0).wait_recv()
            self.second(side).wait_recv()
            total[:, self.columns[side]] = (
                self.parts[self.at(self.me, side)].astype(jnp.float32)
                + self.far_in[side, 0].astype(jnp.float32)
                + self.turn_in[side].astype(jnp.float32)
            )

    def close(self):
        for side in (0, 1):
            for number in (0, 1):
                self.first(side, number).wait_send()
            self.second(side).wait_send()


def square_scratch(rows, width):
    half = width // 2
    return [
        pltpu.VMEM((2, 2, rows, half), jnp.bfloat16),
        pltpu.VMEM((2, rows, half), jnp.bfloat16),
        pltpu.VMEM((2, rows, half), jnp.bfloat16),
        pltpu.SemaphoreType.DMA((6,)),
        pltpu.SemaphoreType.DMA((6,)),
    ]


def greet(sizes):
    n = sizes["dp"]
    barrier = pltpu.get_barrier_semaphore()
    me = lax.axis_index("dp")
    for step in (-1, 1):
        @pl.when((me + step >= 0) & (me + step < n))
        def _():
            pl.semaphore_signal(
                barrier, inc=1, device_id={"dp": me + step}, device_id_type=MESH
            )
    number = sizes["ctx"] * sizes["exp"]
    for ahead in range(number - 1, 0, -1):
        pl.semaphore_signal(
            barrier, inc=1, device_id=place(sizes, peer(sizes, ahead)), device_id_type=MESH
        )
    neighbours = (me + n - 1) // n + (2 * n - 2 - me) // n
    pl.semaphore_wait(barrier, number - 1 + neighbours)


def plane_index(sizes):
    return lax.axis_index("ctx") * sizes["exp"] + lax.axis_index("exp")


def peer(sizes, ahead):
    number = sizes["ctx"] * sizes["exp"]
    return lax.rem(plane_index(sizes) + ahead, number)


def place(sizes, index):
    return {"ctx": index // sizes["exp"], "exp": lax.rem(index, sizes["exp"])}


def partner(sizes, turn):
    n_ctx, n_exp = sizes["ctx"], sizes["exp"]
    number = n_ctx * n_exp
    here = plane_index(sizes)
    if (n_ctx, n_exp) != (4, 2):
        return lax.rem(here + turn, number), lax.rem(here + number - turn, number)
    c, k = lax.axis_index("ctx"), lax.axis_index("exp")
    one_of = lambda *turns: sum(jnp.where(turn == t, 1, 0) for t in turns)
    over_x = lax.rem(lax.rem(c, 2) + one_of(2, 4, 6, 7), 2)
    over_y = lax.rem(c // 2 + one_of(3, 5, 6, 7), 2)
    over_k = lax.rem(k + one_of(1, 4, 5, 7), 2)
    other = (over_y * 2 + over_x) * 2 + over_k
    return other, other


def cut(widths, part):
    pieces = []
    for number, width in enumerate(widths):
        step = min(width, part)
        pieces += [(number, first, step) for first in range(0, width, step)]
    return pieces


def staged_rows(slots):
    return min(256, 1 << (slots.bit_length() - 1))


def dispatch_kernel(
    attended_ref, back_ref, token_ref, gain_ref, router_ref, chosen_ref, cot_ref, routes_ref,
    gate_w_ref, up_w_ref, down_w_ref,
    grads_out, mixed_out, parts_out, middle_ref, gates_ref, active_out, gate_out, up_out, rows_out,
    scaled_out, dots_out, pick_out,
    pick_ref, branch, far_in, turn_out, turn_in, sq_send, sq_recv, cot_column, mixed_column, parts_column,
    packed, packed_parts, parts_in, active, gate_grad, up_grad, scaled, dots,
    line_send, line_recv, plane_send, plane_recv, own_sem, row_send, row_recv, part_send, part_recv,
    load_sem, store_sem, *, sizes, pieces, experts, capacity,
):
    outs = (grads_out, mixed_out, parts_out)
    columns = (cot_column, mixed_column, parts_column)
    targets = (packed, packed, packed_parts)
    n, n_ctx, number = sizes["dp"], sizes["ctx"], sizes["ctx"] * sizes["exp"]
    me, here = lax.axis_index("dp"), plane_index(sizes)
    tokens, width = token_ref.shape
    groups, dests, rows, span = pick_ref.shape
    slots = groups * rows
    full, low = jnp.float32, jnp.bfloat16
    greet(sizes)

    def line_copy(f, origin, step):
        a, first, part = pieces[f]
        return remote(
            columns[a].at[origin, :, pl.ds(first, part)],
            columns[a].at[origin, :, pl.ds(first, part)],
            line_send.at[f, origin, (step + 1) // 2],
            line_recv.at[f, origin],
            {"dp": me + step},
        )

    def send_own(f):
        for step in (-1, 1):
            @pl.when((me + step >= 0) & (me + step < n))
            def _():
                line_copy(f, me, step).start()

    def plane_copy(f, ahead):
        a, first, part = pieces[f]
        target = peer(sizes, ahead)
        return remote(
            packed.at[target, pl.ds(0, slots), pl.ds(first, part)],
            outs[a].at[here, :, pl.ds(first, part)],
            plane_send.at[f, ahead],
            plane_recv.at[f, ahead],
            place(sizes, target),
        )

    def own_copy(f):
        a, first, part = pieces[f]
        return pltpu.make_async_copy(
            packed.at[here, pl.ds(0, slots), pl.ds(first, part)],
            outs[a].at[here, :, pl.ds(first, part)],
            own_sem.at[f],
        )

    cots = len([p for p in pieces if p[0] == 0])
    early = cots + cots // 2
    last_columns = pl.ds(pieces[early][1], width - pieces[early][1])

    def row_copy(turn):
        target, _ = partner(sizes, turn)
        return remote(
            packed.at[target, pl.ds(0, slots), last_columns], mixed_out.at[here, :, last_columns],
            row_send.at[turn], row_recv.at[turn], place(sizes, target),
        )

    def part_copy(turn):
        target, _ = partner(sizes, turn)
        return remote(
            packed_parts.at[target], parts_out.at[here], part_send.at[turn], part_recv.at[turn],
            place(sizes, target),
        )

    def send_rows(turns):
        for turn in turns:
            part_copy(turn).start()
            row_copy(turn).start()

    def spread(f):
        for distance in range(1, n):
            for step in (-1, 1):
                origin = me - step * distance
                beyond = me + step

                @pl.when((origin >= 0) & (origin < n))
                def _():
                    line_copy(f, origin, step).wait_recv()

                    @pl.when((beyond >= 0) & (beyond < n))
                    def _():
                        line_copy(f, origin, step).start()

            if distance == max(1, n - 2) and f + 1 < len(pieces):
                send_own(f + 1)

    def pick_rows(f):
        a, first, part = pieces[f]
        for g in range(groups):
            given = columns[a][pl.ds(g * span // tokens, span // tokens), :, pl.ds(first, part)]
            given = given.reshape(span, part)

            @pl.loop(0, dests)
            def _(j):
                targets[a][j, pl.ds(g * rows, rows), pl.ds(first, part)] = jnp.dot(
                    pick_ref[g, j], given, preferred_element_type=full
                ).astype(low)

    def push(f):
        for ahead in range(number - 1, 0, -1):
            plane_copy(f, ahead).start()
        own_copy(f).start()

    deep = staged_rows(slots)
    blocks = back_ref.shape[0] // deep
    weight_copies = [
        pltpu.make_async_copy(
            back_ref.at[pl.ds(i * deep, deep)], packed.at[i, pl.ds(0, deep)], load_sem.at[i]
        )
        for i in range(blocks)
    ]
    own_cot = pltpu.make_async_copy(cot_ref, cot_column.at[me], own_sem.at[0])
    own_cot.start()
    for copy in weight_copies:
        copy.start()
    own_cot.wait()
    send_own(0)

    together = span // tokens
    low_row = lax.broadcasted_iota(jnp.int32, (tokens, tokens), 0)
    low_lane = lax.broadcasted_iota(jnp.int32, (tokens, tokens), 1)
    earlier = (low_row < low_lane).astype(low)
    named = me * dests + lax.broadcasted_iota(jnp.int32, (dests, 1), 0)
    spots = lax.broadcasted_iota(jnp.int32, (rows, 1), 0).astype(full)
    for b in range(n):
        listed = routes_ref[b]
        hot = jnp.zeros((dests, tokens), full)
        for which in range(listed.shape[0]):
            hot += (listed[which : which + 1, :] == named).astype(full)
        before = jnp.dot(hot.astype(low), earlier, preferred_element_type=full)
        spot = jnp.where(hot > 0, before + b % together * capacity, -1.0)
        at = b % together * tokens
        for j in range(dests):
            pick_ref[b // together, j, :, at : at + tokens] = (
                spot[j : j + 1, :] == spots
            ).astype(low)
    pick_store = pltpu.make_async_copy(pick_ref, pick_out, store_sem.at[6])
    pick_store.start()
    for copy in weight_copies:
        copy.wait()

    scatter = SquareScatter(sizes, branch, far_in, turn_out, turn_in, sq_send, sq_recv, tokens)

    def project_block(index):
        at = pl.ds(index * tokens, tokens)
        total = jnp.zeros((tokens, width), full)
        for i in range(blocks):
            total += jnp.dot(
                attended_ref[at, i * deep : (i + 1) * deep], packed[i, 0:deep],
                preferred_element_type=full,
            )
        branch[at] = total.astype(low)

    project_block(scatter.far)
    scatter.start(1)
    for near in scatter.by:
        project_block(near)
    scatter.start(0)
    project_block(scatter.me)
    spread(0)
    pick_rows(0)
    scatter.turn()
    push(0)
    scatter.finish(middle_ref)
    middle_ref[...] += token_ref[...].astype(full)
    middle = middle_ref[...]
    inverse = lax.rsqrt(jnp.mean(middle * middle, axis=-1, keepdims=True) + eps_norm)
    mixed_column[me] = ((middle * inverse) * gain_ref[...]).astype(low)
    logits = jnp.dot(mixed_column[me], router_ref[...], preferred_element_type=full)
    chosen = chosen_ref[...] > 0
    logits = jnp.where(chosen, logits, masked_score)
    gates = jnp.exp(logits - jnp.max(logits, axis=-1, keepdims=True))
    gates = jnp.where(chosen, gates, 0.0)
    gates = gates / jnp.sum(gates, axis=-1, keepdims=True)
    gates_ref[...] = gates
    first_part = gates.astype(low).astype(full)
    second_part = (gates - first_part).astype(low).astype(full)
    third_part = gates - first_part - second_part
    lanes = gates.shape[1]
    if experts == lanes:
        terms = jnp.concatenate([first_part, second_part, third_part], axis=1)
    else:
        terms = (
            first_part
            + pltpu.roll(second_part, experts, 1)
            + pltpu.roll(third_part, 2 * experts, 1)
        )
    parts_column[me] = terms.astype(low)

    def sent(f):
        for ahead in range(1, number):
            plane_copy(f, ahead).wait_send()
        own_copy(f).wait()

    for f in range(1, cots):
        spread(f)
        pick_rows(f)
        push(f)
    scatter.close()
    for f in range(cots, early):
        spread(f)
        sent(f - cots)
        pick_rows(f)
        push(f)
    for f in range(early, len(pieces)):
        spread(f)
    for f in range(early - cots, cots):
        sent(f)

    def pick_turns(first_turn, last_turn):
        @pl.loop(first_turn, last_turn)
        def _(turn):
            j, _ = partner(sizes, turn)
            for a, first, part in pieces[early:]:
                for g in range(groups):
                    given = columns[a][
                        pl.ds(g * span // tokens, span // tokens), :, pl.ds(first, part)
                    ]
                    targets[a][j, pl.ds(g * rows, rows), pl.ds(first, part)] = jnp.dot(
                        pick_ref[g, j], given.reshape(span, part), preferred_element_type=full
                    ).astype(low)

    waves = [range(2, number)]
    pick_turns(1, waves[0][-1] + 1)
    send_rows((*waves[0], 1))
    pick_turns(0, 1)
    if len(waves) > 1:
        pick_turns(waves[1][0], number)
    own_rows = [
        pltpu.make_async_copy(
            packed.at[here, pl.ds(0, slots), last_columns], mixed_out.at[here, :, last_columns],
            own_sem.at[0],
        ),
        pltpu.make_async_copy(packed_parts.at[here], parts_out.at[here], own_sem.at[1]),
    ]
    for copy in own_rows:
        copy.start()
    for copy in own_rows:
        copy.wait()
    for f in range(cots, early):
        own_copy(f).wait()

    across = (((1,), (1,)), ((), ()))
    expert = me * number + here
    column = lax.broadcasted_iota(jnp.int32, (1, parts_in.shape[1]), 1)
    mine = (lax.rem(column, experts) == expert) & (column < 3 * experts)
    in_rows, in_grads, out_rows = (pl.ds(i * slots, slots) for i in range(3))
    cut_rows = slots

    def stores(source):
        given = (
            (branch.at[out_rows], rows_out), (scaled, scaled_out), (active, active_out),
            (gate_grad, gate_out), (up_grad, up_out), (dots, dots_out),
        )
        return [
            pltpu.make_async_copy(value, out.at[source], store_sem.at[i])
            for i, (value, out) in enumerate(given)
        ]

    @pl.loop(0, number)
    def _(i):
        _, source = partner(sizes, i)
        for wave, later in zip(waves, waves[1:]):
            @pl.when(i == wave[0])
            def _():
                for turn in wave:
                    row_copy(turn).wait_send()
                send_rows(later)

        @pl.when(i > 0)
        def _():
            row_copy(i).wait_recv()
            part_copy(i).wait_recv()

        @pl.when(i == 1)
        def _():
            for f in range(early):
                for ahead in range(1, number):
                    plane_copy(f, ahead).wait_recv()

        loads = [
            pltpu.make_async_copy(mixed_out.at[source], branch.at[in_rows], load_sem.at[0]),
            pltpu.make_async_copy(grads_out.at[source], branch.at[in_grads], load_sem.at[1]),
            pltpu.make_async_copy(parts_out.at[source], parts_in, load_sem.at[2]),
        ]
        for copy in loads:
            copy.start()

        @pl.when(i > 0)
        def _():
            for copy in stores(source):
                copy.wait()

        for copy in loads:
            copy.wait()

        @pl.loop(0, slots // cut_rows)
        def _(part):
            at = pl.ds(pl.multiple_of(part * cut_rows, cut_rows), cut_rows)
            at_in = at
            at_grads = pl.ds(pl.multiple_of(slots + part * cut_rows, cut_rows), cut_rows)
            at_out = pl.ds(pl.multiple_of(2 * slots + part * cut_rows, cut_rows), cut_rows)
            parts = parts_in[at].astype(full)
            slot_gates = jnp.sum(jnp.where(mine, parts, 0.0), axis=-1, keepdims=True)
            gate_pre = jnp.dot(branch[at_in], gate_w_ref[0], preferred_element_type=full)
            up_pre = jnp.dot(branch[at_in], up_w_ref[0], preferred_element_type=full)
            act_grad = slot_gates * lax.dot_general(
                branch[at_grads], down_w_ref[0], across, preferred_element_type=full
            )
            sigma = 1.0 / (1.0 + jnp.exp(-gate_pre))
            silu = gate_pre * sigma
            activated = silu * up_pre
            active_low = activated.astype(low)
            active[at] = (slot_gates * activated).astype(low)
            up_low = (act_grad * silu).astype(low)
            gate_low = (act_grad * up_pre * sigma * (1.0 + gate_pre * (1.0 - sigma))).astype(low)
            up_grad[at] = up_low
            gate_grad[at] = gate_low
            branch[at_out] = (
                lax.dot_general(gate_low, gate_w_ref[0], across, preferred_element_type=full)
                + lax.dot_general(up_low, up_w_ref[0], across, preferred_element_type=full)
            ).astype(low)
            given = jnp.dot(active_low, down_w_ref[0], preferred_element_type=full)
            given = given.astype(low).astype(full)
            scaled[at] = (slot_gates * given).astype(low)
            dot = jnp.sum(given * branch[at_grads].astype(full), axis=-1, keepdims=True)
            first = dot.astype(low).astype(full)
            second = (dot - first).astype(low).astype(full)
            third = dot - first - second
            terms = jnp.where(
                column < experts, first, jnp.where(column < 2 * experts, second, third)
            )
            dots[at] = jnp.where(mine, terms, 0.0).astype(low)

        for copy in stores(source):
            copy.start()

    for copy in stores(here):
        copy.wait()
    pick_store.wait()
    for turn in waves[-1]:
        row_copy(turn).wait_send()
    for f in range(len(pieces)):
        for distance in range(n):
            for step in (-1, 1):
                origin = me - step * distance
                beyond = me + step

                @pl.when((origin >= 0) & (origin < n) & (beyond >= 0) & (beyond < n))
                def _():
                    line_copy(f, origin, step).wait_send()

    for f in range(cots, early):
        for ahead in range(1, number):
            plane_copy(f, ahead).wait_send()
    row_copy(1).wait_send()
    for turn in range(1, number):
        part_copy(turn).wait_send()


def dispatch(
    attended, back, tokens, gain, router, chosen, cot, routes, gate_weight, up_weight, down_weight,
    experts, capacity, sizes, collective, part=512,
):
    rows_here, width = tokens.shape
    inner = gate_weight.shape[2]
    lanes = router.shape[1]
    extra = lanes if 3 * experts <= lanes else 3 * lanes
    widths = [width, width, extra]
    n, n_ctx, number = sizes["dp"], sizes["ctx"], sizes["ctx"] * sizes["exp"]
    together = 2 if 2 * capacity % 16 == 0 and n % 2 == 0 else n
    groups, dests, rows = n // together, number, -(-together * capacity // 16) * 16
    pick = (groups, dests, rows, together * rows_here)
    slots = groups * rows
    pieces = cut(widths, part)
    count = len(pieces)
    low, full = jnp.bfloat16, jnp.float32
    vmem, anywhere = pl.BlockSpec(memory_space=pltpu.VMEM), pl.BlockSpec(memory_space=pl.ANY)
    block = lambda *shape: pltpu.VMEM(shape, low)
    dma = lambda *shape: pltpu.SemaphoreType.DMA(shape)
    by_source = lambda columns: jax.ShapeDtypeStruct((number, slots, columns), low)
    return pl.pallas_call(
        functools.partial(
            dispatch_kernel, sizes=sizes, pieces=pieces, experts=experts, capacity=capacity
        ),
        in_specs=[vmem, anywhere] + [vmem] * 4 + [anywhere] + [vmem] * 4,
        out_specs=[anywhere] * 3 + [vmem] * 2 + [anywhere] * 7,
        out_shape=[by_source(columns) for columns in widths]
        + [
            jax.ShapeDtypeStruct((rows_here, width), full),
            jax.ShapeDtypeStruct((rows_here, lanes), full),
        ]
        + [by_source(columns) for columns in (inner, inner, inner, width, width, extra)]
        + [jax.ShapeDtypeStruct(pick, low)],
        scratch_shapes=[
            block(*pick),
            block(max(n_ctx * rows_here, 3 * slots), width),
            *square_scratch(rows_here, width),
            block(n, rows_here, width),
            block(n, rows_here, width),
            block(n, rows_here, extra),
            block(dests, slots, width),
            block(dests, slots, extra),
            block(slots, extra),
            block(slots, inner),
            block(slots, inner),
            block(slots, inner),
            block(slots, width),
            block(slots, extra),
            dma(count, n, 2), dma(count, n), dma(count, number), dma(count, number), dma(count),
            dma(number), dma(number), dma(number), dma(number),
            dma(max(3, back.shape[0] // staged_rows(slots))), dma(7),
        ],
        compiler_params=pltpu.CompilerParams(
            collective_id=collective, has_side_effects=True, vmem_limit_bytes=VMEM
        ),
    )(
        attended, back, tokens, gain, router, chosen, cot, routes, gate_weight, up_weight,
        down_weight,
    )


def combine_kernel(
    rows_ref, dots_ref, pick_ref, middle_ref, cot_ref, gain_ref, gates_ref, router_ref,
    in_ref, grad_ref, active_ref, gate_ref, up_ref,
    whole_ref, middle_grad_ref, gain_grad_ref, router_grad_ref, gate_out, up_out, down_out,
    back_rows, back_dots, leave_rows, leave_dots, land_rows, land_dots, total_rows, total_dots,
    sums, branch, line_send, line_recv, plane_send, plane_recv, own_sem, sq_send, sq_recv, sq_own,
    *, sizes, pieces, experts,
):
    sent, back = (dots_ref, rows_ref), (back_dots, back_rows)
    leaving, landing = (leave_dots, leave_rows), (land_dots, land_rows)
    totals = (total_dots, total_rows)
    n, number = sizes["dp"], sizes["ctx"] * sizes["exp"]
    me, here = lax.axis_index("dp"), plane_index(sizes)
    tokens = middle_ref.shape[0]
    groups, _, rows, span = pick_ref.shape
    full, low = jnp.float32, jnp.bfloat16
    greet(sizes)

    def plane_copy(f, ahead):
        a, first, part = pieces[f]
        target = peer(sizes, ahead)
        return remote(
            sent[a].at[target, :, pl.ds(first, part)],
            back[a].at[here, :, pl.ds(first, part)],
            plane_send.at[f, ahead],
            plane_recv.at[f, ahead],
            place(sizes, target),
        )

    def own_copy(f):
        a, first, part = pieces[f]
        return pltpu.make_async_copy(
            sent[a].at[here, :, pl.ds(first, part)],
            back[a].at[here, :, pl.ds(first, part)],
            own_sem.at[f],
        )

    for f in range(len(pieces)):
        for ahead in range(number - 1, 0, -1):
            plane_copy(f, ahead).start()
        own_copy(f).start()

    def line_copy(f, target, step):
        a, first, part = pieces[f]
        return remote(
            leaving[a].at[target, :, pl.ds(first, part)],
            landing[a].at[target + (step + 1) // 2, :, pl.ds(first, part)],
            line_send.at[f, target],
            line_recv.at[f, target + (step + 1) // 2],
            {"dp": me + step},
        )

    inner, chunk = active_ref.shape[1], 256
    slots = in_ref.shape[0]

    def weight_sum(left, right, out, by_left):
        def body(left_ref, right_ref, out_ref):
            out_ref[...] = lax.dot_general(
                left_ref[...], right_ref[...], (((0,), (0,)), ((), ())), preferred_element_type=full
            )

        if by_left:
            grid = left.shape[1] // chunk
            specs = [
                pl.BlockSpec((slots, chunk), lambda i: (0, i)),
                pl.BlockSpec((slots, inner), lambda i: (0, 0)),
            ]
            out_spec = pl.BlockSpec((chunk, inner), lambda i: (i, 0))
        else:
            grid = right.shape[1] // chunk
            specs = [
                pl.BlockSpec((slots, inner), lambda i: (0, 0)),
                pl.BlockSpec((slots, chunk), lambda i: (0, i)),
            ]
            out_spec = pl.BlockSpec((inner, chunk), lambda i: (0, i))
        pltpu.emit_pipeline(body, grid=(grid,), in_specs=specs, out_specs=[out_spec])(
            left, right, out
        )

    for f, (a, first, part) in enumerate(pieces):
        columns = pl.ds(first, part)
        if f == 1:
            weight_sum(in_ref, gate_ref, gate_out, True)
        elif f == 2:
            weight_sum(in_ref, up_ref, up_out, True)
        elif f == 3:
            weight_sum(active_ref, grad_ref, down_out, False)
        for ahead in range(1, number):
            plane_copy(f, ahead).wait_recv()
        own_copy(f).wait()
        for g in range(groups):
            gathered = back[a][:, pl.ds(g * rows, rows), columns].reshape(number * rows, part)
            sums[pl.ds(g * span // tokens, span // tokens), :, pl.ds(0, part)] = lax.dot_general(
                pick_ref[g].reshape(number * rows, span), gathered, (((0,), (0,)), ((), ())),
                preferred_element_type=full,
            ).reshape(span // tokens, tokens, part)

        for distance in range(n - 1, 0, -1):
            for step in (-1, 1):
                target = me + step * distance
                behind = me - step

                @pl.when((target >= 0) & (target < n))
                def _():
                    own = sums[target, :, pl.ds(0, part)]

                    @pl.when((behind >= 0) & (behind < n))
                    def _():
                        line_copy(f, target, step).wait_recv()
                        coming = landing[a][target + (step + 1) // 2, :, columns]
                        leaving[a][target, :, columns] = (own + coming.astype(full)).astype(low)

                    @pl.when((behind < 0) | (behind >= n))
                    def _():
                        leaving[a][target, :, columns] = own.astype(low)

                    line_copy(f, target, step).start()

        totals[a][:, columns] = sums[me, :, pl.ds(0, part)]
        for step in (-1, 1):
            @pl.when((me - step >= 0) & (me - step < n))
            def _():
                line_copy(f, me, step).wait_recv()
                totals[a][:, columns] += landing[a][me + (step + 1) // 2, :, columns].astype(full)

    gates = gates_ref[...]
    lanes = gates.shape[1]
    if experts == lanes:
        dots = sum(total_dots[:, k * lanes : (k + 1) * lanes] for k in range(3))
    else:
        dots = total_dots[...]
        dots = dots + pltpu.roll(dots, lanes - experts, 1) + pltpu.roll(dots, lanes - 2 * experts, 1)
    picked = gates * (dots - jnp.sum(gates * dots, axis=-1, keepdims=True))
    logit_grads = picked.astype(low)
    mixed_grad = total_rows[...] + lax.dot_general(
        logit_grads, router_ref[...], (((1,), (1,)), ((), ())), preferred_element_type=full
    )
    middle = middle_ref[...]
    inverse = lax.rsqrt(jnp.mean(middle * middle, axis=-1, keepdims=True) + eps_norm)
    normed = middle * inverse
    gain_grad_ref[...] = jnp.sum(mixed_grad * normed, axis=0, keepdims=True)
    scaled = mixed_grad * gain_ref[...]
    middle_grad = cot_ref[...].astype(full) + inverse * (
        scaled - normed * jnp.mean(scaled * normed, axis=-1, keepdims=True)
    )
    middle_grad_ref[...] = middle_grad
    branch[...] = middle_grad.astype(low)
    collect = SquareGather(sizes, branch, whole_ref, sq_send, sq_recv, sq_own.at[0])
    collect.start()
    router_grad_ref[...] = lax.dot_general(
        logit_grads, (normed * gain_ref[...]).astype(low), (((0,), (0,)), ((), ())),
        preferred_element_type=full,
    )
    collect.pass_on()

    for f in range(len(pieces)):
        for ahead in range(1, number):
            plane_copy(f, ahead).wait_send()
        for distance in range(1, n):
            for step in (-1, 1):
                target = me + step * distance

                @pl.when((target >= 0) & (target < n))
                def _():
                    line_copy(f, target, step).wait_send()
    collect.finish()


def combine(
    rows, dots, pick, middle, cot, gain, gates, router, rows_in, grads_in, active, gate_grad,
    up_grad, experts, sizes, collective, part=512,
):
    number, back_rows, width = rows.shape
    extra = dots.shape[2]
    tokens = middle.shape[0]
    lanes = router.shape[1]
    inner = active.shape[2]
    flat = lambda v: v.reshape(-1, v.shape[2])
    n, n_ctx = sizes["dp"], sizes["ctx"]
    low, full = jnp.bfloat16, jnp.float32
    pieces = cut([extra, width], part)
    count = len(pieces)
    both = (width, extra)
    vmem, anywhere = pl.BlockSpec(memory_space=pltpu.VMEM), pl.BlockSpec(memory_space=pl.ANY)
    dma = lambda *shape: pltpu.SemaphoreType.DMA(shape)
    return pl.pallas_call(
        functools.partial(combine_kernel, sizes=sizes, pieces=pieces, experts=experts),
        in_specs=[anywhere, anywhere] + [vmem] * 6 + [anywhere] * 5,
        out_specs=[anywhere] + [vmem] * 3 + [anywhere] * 3,
        out_shape=[
            jax.ShapeDtypeStruct((n_ctx, tokens, width), low),
            jax.ShapeDtypeStruct((tokens, width), full),
            jax.ShapeDtypeStruct((1, width), full),
            jax.ShapeDtypeStruct((lanes, width), full),
            jax.ShapeDtypeStruct((width, inner), full),
            jax.ShapeDtypeStruct((width, inner), full),
            jax.ShapeDtypeStruct((inner, width), full),
        ],
        scratch_shapes=[pltpu.VMEM((number, back_rows, w), low) for w in both]
        + [pltpu.VMEM((n, tokens, w), low) for w in both]
        + [pltpu.VMEM((n + 1, tokens, w), low) for w in both]
        + [pltpu.VMEM((tokens, w), full) for w in both]
        + [
            pltpu.VMEM((n, tokens, max(p[2] for p in pieces)), full),
            pltpu.VMEM((tokens, width), low),
            dma(count, n), dma(count, n + 1), dma(count, number), dma(count, number), dma(count),
            dma(6), dma(6), dma(1),
        ],
        compiler_params=pltpu.CompilerParams(
            collective_id=collective, has_side_effects=True, vmem_limit_bytes=VMEM
        ),
    )(
        rows, dots, pick, middle, cot, gain, gates, router, flat(rows_in), flat(grads_in),
        flat(active), flat(gate_grad), flat(up_grad),
    )


def gather_kernel(
    token_ref, front_ref, back_ref, route_ref, cos_ref, sin_ref, bounds_ref,
    fronts_out, backs_ref, routes_ref, hidden_out, raw_out, turned_out, attended_ref, gains_ref,
    scales_ref,
    tokens_ref, fronts_ref, held, hidden, raw, turned,
    sq_send, sq_recv, own_sem, fa_send, fa_recv, fl_send, fl_recv, fp_send, fp_recv,
    bl_send, bl_recv, ba_send, ba_recv, bp_send, bp_recv, rl_send, rl_recv, store_sem,
    *, sizes, gain_len, heads, kv_heads, experts,
):
    n, n_ctx, n_exp = sizes["dp"], sizes["ctx"], sizes["exp"]
    z, c, k = (lax.axis_index(a) for a in ALL)
    low, full = jnp.bfloat16, jnp.float32
    count, width = token_ref.shape
    owned = front_ref.shape[1]
    head = cos_ref.shape[1]
    columns = raw.shape[1]
    greet(sizes)

    def front_across(ahead):
        target = lax.rem(c + ahead, n_ctx)
        return remote(
            front_ref.at[target], fronts_ref.at[z, c, k], fa_send.at[ahead], fa_recv.at[ahead],
            {"ctx": target},
        )

    def front_line(origin, step):
        here = fronts_ref.at[origin, :, k]
        return remote(
            here, here, fl_send.at[origin, (step + 1) // 2], fl_recv.at[origin], {"dp": z + step}
        )

    def front_pair(origin, ahead):
        here = fronts_ref.at[origin, :, k]
        return remote(
            here, here, fp_send.at[origin, ahead], fp_recv.at[origin, ahead],
            {"exp": lax.rem(k + ahead, n_exp)},
        )

    def back_line(origin, step):
        here = held.at[origin]
        return remote(
            here, here, bl_send.at[origin, (step + 1) // 2], bl_recv.at[origin], {"dp": z + step}
        )

    def back_across(ahead):
        target = lax.rem(c + ahead, n_ctx)
        return remote(
            held.at[target], backs_ref.at[c, k], ba_send.at[ahead], ba_recv.at[ahead],
            {"ctx": target},
        )

    def back_pair(source, ahead):
        here = backs_ref.at[source, k]
        return remote(
            here, here, bp_send.at[source, ahead], bp_recv.at[source, ahead],
            {"exp": lax.rem(k + ahead, n_exp)},
        )

    def route_line(origin, step):
        here = routes_ref.at[origin]
        return remote(
            here, here, rl_send.at[origin, (step + 1) // 2], rl_recv.at[origin], {"dp": z + step}
        )

    def in_line(step):
        return (z + step >= 0) & (z + step < n)

    def start_line(line):
        for step in (-1, 1):
            @pl.when(in_line(step))
            def _():
                line(z, step).start()

    def pass_on(line, distance, after):
        for step in (-1, 1):
            origin = z - step * distance

            @pl.when((origin >= 0) & (origin < n))
            def _():
                line(origin, step).wait_recv()

                @pl.when(in_line(step))
                def _():
                    line(origin, step).start()

                after(origin)

    def nothing(origin):
        pass

    def to_siblings(origin):
        for ahead in range(1, n_exp):
            front_pair(origin, ahead).start()

    tokens = SquareGather(sizes, token_ref, tokens_ref, sq_send, sq_recv, own_sem.at[0])
    own_copies = [
        pltpu.make_async_copy(front_ref.at[c], fronts_ref.at[z, c, k], own_sem.at[1]),
        pltpu.make_async_copy(back_ref, held.at[z], own_sem.at[2]),
        pltpu.make_async_copy(route_ref, routes_ref.at[z], own_sem.at[3]),
    ]
    for copy in own_copies:
        copy.start()
    for ahead in range(1, n_ctx):
        front_across(ahead).start()
    tokens.start()
    for copy in own_copies:
        copy.wait()
    start_line(back_line)
    start_line(route_line)
    for ahead in range(1, n_ctx):
        front_across(ahead).wait_recv()
    start_line(front_line)
    to_siblings(z)
    pass_on(back_line, 1, nothing)
    tokens.pass_on()
    for distance in range(1, n):
        pass_on(front_line, distance, to_siblings)
        if distance == 2:
            pass_on(back_line, 2, nothing)
        pass_on(route_line, distance, nothing)
    for origin in range(n):
        for ahead in range(1, n_exp):
            front_pair(origin, ahead).wait_recv()
    tokens.finish()
    fronts_store = pltpu.make_async_copy(fronts_ref, fronts_out, store_sem.at[0])
    fronts_store.start()

    place_of = columns + experts // 128 * 128
    spun = fronts_ref[..., place_of : place_of + 128].reshape(width, 128).astype(full).T
    lead = experts % 128
    gain = spun[lead : lead + 1, :]
    gains_ref[...] = spun[lead : lead + 8, :]
    row = lax.broadcasted_iota(jnp.int32, (width, head), 0)
    lane = lax.broadcasted_iota(jnp.int32, (width, head), 1)
    spot = lane // gain_len * owned + lax.rem(lane, gain_len)
    packed = spun[lead : lead + 8, :].astype(low)
    scales = [
        jnp.dot(packed, (row == spot + shift).astype(low), preferred_element_type=full)[2:3, :]
        for shift in (0, gain_len)
    ]
    scales_ref[0:1, :] = scales[0]
    scales_ref[1:2, :] = scales[1]

    def hidden_store(i):
        return pltpu.make_async_copy(
            hidden, hidden_out.at[pl.ds(pl.multiple_of(i * count, count), count)], store_sem.at[1]
        )

    def raw_store(i):
        return pltpu.make_async_copy(
            raw, raw_out.at[pl.ds(pl.multiple_of(i * count, count), count)], store_sem.at[2]
        )

    def project(first, last):
        @pl.loop(first, last)
        def _(i):
            x = tokens_ref[i].astype(full)
            inverse = lax.rsqrt(jnp.mean(x * x, axis=-1, keepdims=True) + eps_norm)

            @pl.when(i > 0)
            def _():
                hidden_store(i).wait()
                raw_store(i).wait()

            hidden[...] = ((x * inverse) * gain).astype(low)
            hidden_store(i).start()
            raw[...] = jnp.dot(
                hidden[...], fronts_ref[..., 0:columns].reshape(width, columns),
                preferred_element_type=full,
            )
            raw_store(i).start()
            at = pl.ds(pl.multiple_of(i * count, count), count)
            cosine, sine = cos_ref[at], sin_ref[at]
            for h in range(heads + kv_heads):
                here = slice(h * head, (h + 1) * head)
                part = raw[:, here]
                factor = lax.rsqrt(jnp.mean(part * part, axis=-1, keepdims=True) + eps_norm)
                scaled = part * factor * scales[0 if h < heads else 1]
                spun = pltpu.roll(scaled, head // 2, 1)
                turned[at, here] = (scaled * cosine + spun * sine).astype(low)
            rest = slice((heads + kv_heads) * head, columns)
            turned[at, rest] = raw[:, rest].astype(low)

    rows = n_ctx * count
    group = heads // kv_heads

    def attend(first_head, last_head):
        @pl.loop(first_head, last_head)
        def _(h):
            at = lambda which: pl.ds(pl.multiple_of(which * head, head), head)
            kv = h // group
            for first in range(0, rows, count):
                last = first + count
                allowed = seen(bounds_ref, first, count, last)
                shares = shares_of(
                    turned[first:last, at(h)], turned[0:last, at(heads + kv)], allowed,
                    head ** (-0.5),
                )
                attended_ref[first:last, at(h)] = jnp.dot(
                    shares.astype(low), turned[0:last, at(heads + kv_heads + kv)],
                    preferred_element_type=full,
                ).astype(low)

    project(0, n_ctx)
    turned_store = pltpu.make_async_copy(turned, turned_out, store_sem.at[3])
    turned_store.start()
    attend(0, heads // 4)
    for distance in range(3, n):
        pass_on(back_line, distance, nothing)
    for ahead in range(1, n_ctx):
        back_across(ahead).start()
    own_back = pltpu.make_async_copy(held.at[c], backs_ref.at[c, k], own_sem.at[4])
    own_back.start()
    attend(heads // 4, heads)
    own_back.wait()
    for ahead in range(1, n_exp):
        back_pair(c, ahead).start()
    for behind in range(1, n_ctx):
        back_across(behind).wait_recv()
        source = lax.rem(c + n_ctx - behind, n_ctx)
        for ahead in range(1, n_exp):
            back_pair(source, ahead).start()

    fronts_store.wait()
    hidden_store(n_ctx - 1).wait()
    raw_store(n_ctx - 1).wait()
    turned_store.wait()
    for ahead in range(1, n_ctx):
        front_across(ahead).wait_send()
        back_across(ahead).wait_send()
    for origin in range(n):
        for ahead in range(1, n_exp):
            front_pair(origin, ahead).wait_send()
    for source in range(n_ctx):
        for ahead in range(1, n_exp):
            back_pair(source, ahead).wait()
    for line in (route_line, front_line, back_line):
        for distance in range(n):
            for step in (-1, 1):
                origin = z - step * distance

                @pl.when((origin >= 0) & (origin < n) & in_line(step))
                def _():
                    line(origin, step).wait_send()


def gather(
    tokens, front, back, routes, cosine, sine, bounds, gain_len, heads, kv_heads, experts, sizes,
    collective,
):
    n, n_ctx, n_exp = sizes["dp"], sizes["ctx"], sizes["exp"]
    _, rows, front_columns = front.shape
    count, width = tokens.shape
    head = cosine.shape[1]
    columns = (heads + 2 * kv_heads) * head
    seq = n_ctx * count
    low, full = jnp.bfloat16, jnp.float32
    dma = lambda *shape: pltpu.SemaphoreType.DMA(shape)
    vmem, anywhere = pl.BlockSpec(memory_space=pltpu.VMEM), pl.BlockSpec(memory_space=pl.ANY)
    return pl.pallas_call(
        functools.partial(
            gather_kernel, sizes=sizes, gain_len=gain_len, heads=heads, kv_heads=kv_heads,
            experts=experts,
        ),
        in_specs=[vmem] * 6 + [pl.BlockSpec(memory_space=pltpu.SMEM)],
        out_specs=[anywhere] * 6 + [vmem] * 3,
        out_shape=[
            jax.ShapeDtypeStruct((n, n_ctx, n_exp, rows, front_columns), low),
            jax.ShapeDtypeStruct((n_ctx, n_exp) + back.shape, low),
            jax.ShapeDtypeStruct((n,) + routes.shape, routes.dtype),
            jax.ShapeDtypeStruct((seq, width), low),
            jax.ShapeDtypeStruct((seq, columns), full),
            jax.ShapeDtypeStruct((seq, columns), low),
            jax.ShapeDtypeStruct((seq, heads * head), low),
            jax.ShapeDtypeStruct((8, width), full),
            jax.ShapeDtypeStruct((2, head), full),
        ],
        scratch_shapes=[
            pltpu.VMEM((n_ctx, count, width), low),
            pltpu.VMEM((n, n_ctx, n_exp, rows, front_columns), low),
            pltpu.VMEM((n,) + back.shape, low),
            pltpu.VMEM((count, width), low),
            pltpu.VMEM((count, columns), full),
            pltpu.VMEM((seq, columns), low),
            dma(6), dma(6), dma(5),
            dma(n_ctx), dma(n_ctx), dma(n, 2), dma(n), dma(n, n_exp), dma(n, n_exp),
            dma(n, 2), dma(n), dma(n_ctx), dma(n_ctx), dma(n_ctx, n_exp), dma(n_ctx, n_exp),
            dma(n, 2), dma(n), dma(4),
        ],
        compiler_params=pltpu.CompilerParams(
            collective_id=collective, has_side_effects=True, vmem_limit_bytes=VMEM
        ),
    )(tokens, front, back, routes, cosine, sine, bounds)


def finish_kernel(
    bounds_ref, query_ref, key_ref, value_ref, grad_ref, raw_ref, scale_ref, cos_ref, sin_ref,
    hidden_ref, weight_ref, back_ref, rows_ref, pick_ref, result_ref, middle_ref, token_ref,
    gain_ref, small_ref,
    tokens_grad_ref, front_out, output_ref, back_out, small_out, landed_ref, back_in,
    key_sum, value_sum, raw_grad, head_gains, shared, arrived, back_one, fronts, front_pairs,
    front_in, rows_in, leaving, landing, far_in, turn_out, turn_in, hidden_send, hidden_recv,
    total, loaded, staged, small_all, small_in,
    own_sem, load_sem, stage_sem, bp_send, bp_recv, ba_send, ba_recv, bl_send, bl_recv,
    fp_send, fp_recv, fl_send, fl_recv, fa_send, fa_recv, plane_send, plane_recv, plane_own,
    line_send, line_recv, s_send, s_recv, *, block, heads, group, score_scale, sizes, part, chunk,
):
    step = pl.program_id(0)
    rows, head = query_ref.shape
    low, full = jnp.bfloat16, jnp.float32
    kv_heads = heads // group
    first_chunk = heads + 2 * kv_heads
    n, n_ctx, n_exp = sizes["dp"], sizes["ctx"], sizes["exp"]
    devices, number = n * n_ctx * n_exp, n_ctx * n_exp
    z, c, k = (lax.axis_index(a) for a in ALL)
    here, in_plane = (z * n_ctx + c) * n_exp + k, plane_index(sizes)
    tokens, width = token_ref.shape
    b_rows = back_out.shape[0]
    pieces = width // part
    chunks = width // chunk

    def in_line(index):
        return (index >= 0) & (index < n)

    def device_of(index):
        return {
            "dp": index // number,
            "ctx": lax.rem(index // n_exp, n_ctx),
            "exp": lax.rem(index, n_exp),
        }

    def back_own():
        return pltpu.make_async_copy(
            back_ref.at[:, k], shared.at[:, pl.ds(0, b_rows)], own_sem.at[0]
        )

    def back_pair(ahead):
        target = lax.rem(k + ahead, n_exp)
        return remote(
            back_ref.at[:, target], shared.at[:, pl.ds(ahead * b_rows, b_rows)],
            bp_send.at[ahead], bp_recv.at[ahead], {"exp": target},
        )

    def back_across(ahead):
        target = lax.rem(c + ahead, n_ctx)
        return remote(
            shared.at[target, pl.ds(0, b_rows)], arrived.at[c], ba_send.at[ahead],
            ba_recv.at[ahead], {"ctx": target},
        )

    def back_line(target, way):
        return remote(
            arrived.at[target], back_in.at[target + (way + 1) // 2], bl_send.at[target],
            bl_recv.at[target + (way + 1) // 2], {"dp": z + way},
        )

    def along_line(line, add, distance):
        for way in (-1, 1):
            target = z + way * distance

            @pl.when(in_line(target))
            def _():
                @pl.when(in_line(z - way))
                def _():
                    line(target, way).wait_recv()
                    add(target, target + (way + 1) // 2)

                line(target, way).start()

    def end_line(line, add):
        for way in (-1, 1):
            @pl.when(in_line(z - way))
            def _():
                line(z, way).wait_recv()
                add((way + 1) // 2 + z)

    def close_line(line):
        for distance in range(1, n):
            for way in (-1, 1):
                @pl.when(in_line(z + way * distance))
                def _():
                    line(z + way * distance, way).wait_send()

    def back_arrived(slot):
        copy = pltpu.make_async_copy(back_in.at[slot], back_one, stage_sem.at[1])
        copy.start()
        copy.wait()
        return back_one[...].astype(full)

    def add_back(target, slot):
        arrived[target] = (arrived[target].astype(full) + back_arrived(slot)).astype(low)

    def plane_copy(piece, ahead):
        target = peer(sizes, ahead)
        columns = pl.ds(piece * part, part)
        return remote(
            rows_ref.at[target, :, columns], landed_ref.at[in_plane, :, columns],
            plane_send.at[piece, ahead], plane_recv.at[piece, ahead], place(sizes, target),
        )

    def plane_own_copy(piece):
        columns = pl.ds(piece * part, part)
        return pltpu.make_async_copy(
            rows_ref.at[in_plane, :, columns], landed_ref.at[in_plane, :, columns],
            plane_own.at[piece],
        )

    def push(piece):
        for ahead in range(number - 1, 0, -1):
            plane_copy(piece, ahead).start()
        plane_own_copy(piece).start()

    def small_load():
        return pltpu.make_async_copy(small_ref, small_all, own_sem.at[1])

    @pl.when(step == 0)
    def _():
        head_gains[...] = jnp.zeros_like(head_gains)
        barrier = pltpu.get_barrier_semaphore()

        @pl.loop(1, devices)
        def _(ahead):
            pl.semaphore_signal(
                barrier, inc=1, device_id=device_of(lax.rem(here + ahead, devices)),
                device_id_type=MESH,
            )

        pl.semaphore_wait(barrier, devices - 1)
        back_own().start()
        for ahead in range(1, n_exp):
            back_pair(ahead).start()
        small_load().start()

    @pl.when(step == 1)
    def _():
        back_own().wait()
        for ahead in range(1, n_exp):
            back_pair(ahead).wait_recv()
        for index in range(n_ctx):
            summed = shared[index, 0:b_rows].astype(full)
            for ahead in range(1, n_exp):
                summed = summed + shared[index, ahead * b_rows : (ahead + 1) * b_rows].astype(full)
            shared[index, 0:b_rows] = summed.astype(low)
        for ahead in range(1, n_ctx):
            back_across(ahead).start()
        arrived[c] = shared[c, 0:b_rows]
        push(0)
        small_load().wait()

    for piece in range(1, pieces):
        @pl.when(step == min(1 + 4 * piece, first_chunk))
        def _():
            push(piece)

    for distance in range(n - 1, 0, -1):
        @pl.when(step == min(6 + 3 * (n - 1 - distance), first_chunk + chunks - 2))
        def _():
            if distance == n - 1:
                for ahead in range(1, n_ctx):
                    back_across(ahead).wait_recv()
                    back_across(ahead).wait_send()
                for ahead in range(1, n_exp):
                    back_pair(ahead).wait_send()
            along_line(back_line, add_back, distance)

    def norm_rope_back(grad, raw, scale, cosine, sine):
        inverse = lax.rsqrt(jnp.mean(raw * raw, axis=-1, keepdims=True) + eps_norm)
        normed = raw * inverse
        turned = grad * cosine + pltpu.roll(grad * sine, grad.shape[-1] // 2, 1)
        inner = turned * scale
        back = inverse * (inner - normed * jnp.mean(inner * normed, axis=-1, keepdims=True))
        return back, jnp.sum(turned * normed, axis=0, keepdims=True)

    for kv in range(kv_heads):
        @pl.when(step == kv * group)
        def _():
            key_sum[kv] = jnp.zeros((rows, head), full)
            value_sum[kv] = jnp.zeros((rows, head), full)

    here_columns = pl.ds(pl.multiple_of(step * head, head), head)

    @pl.when(step < heads)
    def _():
        kv = step // group
        gains = jnp.zeros((1, head), full)
        for first in range(0, rows, block):
            last = first + block
            query, keys, values = query_ref[first:last, :], key_ref[:last, :], value_ref[:last, :]
            grad = grad_ref[first:last, :]
            allowed = seen(bounds_ref, first, block, last)
            shares = shares_of(query, keys, allowed, score_scale)
            share_grads = lax.dot_general(
                grad, values, (((1,), (1,)), ((), ())), preferred_element_type=full
            )
            centre = jnp.sum(shares * share_grads, axis=-1, keepdims=True)
            score_grads = (shares * (share_grads - centre)).astype(low)
            key_sum[kv, :last, :] += lax.dot_general(
                score_grads, query, (((0,), (0,)), ((), ())), preferred_element_type=full
            )
            value_sum[kv, :last, :] += lax.dot_general(
                shares.astype(low), grad, (((0,), (0,)), ((), ())), preferred_element_type=full
            )
            query_grad = jnp.dot(score_grads, keys, preferred_element_type=full) * score_scale
            back, gain = norm_rope_back(
                query_grad, raw_ref[first:last, :], scale_ref[0:1, :], cos_ref[first:last, :],
                sin_ref[first:last, :],
            )
            raw_grad[first:last, here_columns] = back.astype(low)
            gains += gain
        head_gains[0:1, :] += gains

    @pl.when((step >= heads) & (step < heads + kv_heads))
    def _():
        back, gain = norm_rope_back(
            key_sum[step - heads] * score_scale, raw_ref[...], scale_ref[1:2, :], cos_ref[...],
            sin_ref[...],
        )
        raw_grad[:, here_columns] = back.astype(low)
        head_gains[1:2, :] += gain

    @pl.when((step >= heads + kv_heads) & (step < first_chunk))
    def _():
        raw_grad[:, here_columns] = value_sum[step - heads - kv_heads].astype(low)

    @pl.when((step >= first_chunk) & (step < first_chunk + chunks))
    def _():
        q = step - first_chunk
        grads = raw_grad[...]
        shared[:, 0:tokens, pl.ds(pl.multiple_of(q * chunk, chunk), chunk)] = (
            lax.dot_general(
                grads, weight_ref[:, : grads.shape[1]], (((1,), (1,)), ((), ())),
                preferred_element_type=full,
            )
            .astype(low)
            .reshape(n_ctx, tokens, chunk)
        )
        fronts[q // 2, lax.rem(q, 2)] = (
            lax.dot_general(
                hidden_ref[...], grads, (((0,), (0,)), ((), ())), preferred_element_type=full
            )
            .astype(low)
            .reshape(fronts.shape[2:])
        )

    def front_pair(ahead):
        target = lax.rem(k + ahead, n_exp)
        return remote(
            fronts.at[:, :, :, target], front_pairs.at[ahead - 1], fp_send.at[ahead],
            fp_recv.at[ahead], {"exp": target},
        )

    def front_line(target, way):
        return remote(
            fronts.at[target, :, :, k], front_in.at[target + (way + 1) // 2], fl_send.at[target],
            fl_recv.at[target + (way + 1) // 2], {"dp": z + way},
        )

    def front_across(ahead):
        target = lax.rem(c + ahead, n_ctx)
        return remote(
            fronts.at[z, target // (n_ctx // 2), lax.rem(target, n_ctx // 2), k], front_out.at[c],
            fa_send.at[ahead], fa_recv.at[ahead], {"ctx": target},
        )

    def add_front(target, slot):
        fronts[target, :, :, k] = (
            fronts[target, :, :, k].astype(full) + front_in[slot].astype(full)
        ).astype(low)

    def line_of(piece):
        columns = pl.ds(piece * part, part)

        def line(target, way):
            return remote(
                leaving.at[target, :, columns],
                landing.at[target + (way + 1) // 2, :, columns],
                line_send.at[piece, target], line_recv.at[piece, target + (way + 1) // 2],
                {"dp": z + way},
            )

        return line

    def load_rows(piece):
        return pltpu.make_async_copy(
            landed_ref.at[:, :, pl.ds(piece * part, part)], rows_in, load_sem.at[0]
        )

    def load_part(source, piece):
        return pltpu.make_async_copy(
            source.at[:, pl.ds(piece * part, part)], loaded.at[piece % 2], load_sem.at[1 + piece % 2]
        )

    def mix_in(piece):
        for ahead in range(1, number):
            plane_copy(piece, ahead).wait_recv()
        plane_own_copy(piece).wait()
        load_rows(piece).start()
        load_part(result_ref, piece).start()
        load_rows(piece).wait()
        groups, _, back_rows, span = pick_ref.shape
        columns = pl.ds(piece * part, part)
        for g in range(groups):
            gathered = rows_in[:, pl.ds(g * back_rows, back_rows), :]
            leaving[pl.ds(g * span // tokens, span // tokens), :, columns] = (
                lax.dot_general(
                    pick_ref[g].reshape(number * back_rows, span),
                    gathered.reshape(number * back_rows, part),
                    (((0,), (0,)), ((), ())),
                    preferred_element_type=full,
                )
                .astype(low)
                .reshape(span // tokens, tokens, part)
            )

    def start_total(piece):
        columns = pl.ds(piece * part, part)
        load_part(result_ref, piece).wait()
        total[:, columns] = leaving[z, :, columns].astype(full) + loaded[piece % 2]

    def mix_line(piece, distance):
        columns = pl.ds(piece * part, part)

        def add(target, slot):
            leaving[target, :, columns] = (
                leaving[target, :, columns].astype(full) + landing[slot, :, columns].astype(full)
            ).astype(low)

        along_line(line_of(piece), add, distance)

    def mix_end(piece):
        columns = pl.ds(piece * part, part)

        def add(slot):
            total[:, columns] += landing[slot, :, columns].astype(full)

        end_line(line_of(piece), add)

    @pl.when(step == first_chunk + chunks - 1)
    def _():
        mix_in(0)
        mix_line(0, n - 1)

    def small_copy(ahead):
        target = lax.rem(here + ahead, devices)
        return remote(
            small_all.at[target], small_in.at[ahead], s_send.at[0], s_recv.at[0],
            device_of(target),
        )

    def all_small():
        others = pl.ds(1, devices - 1)
        return remote(
            small_all.at[others], small_in.at[others], s_send.at[0], s_recv.at[0], {"dp": z}
        )

    @pl.when(step == first_chunk + chunks)
    def _():
        for ahead in range(1, n_exp):
            front_pair(ahead).start()
        gain_owned = head // devices
        for index in range(devices):
            for which in (0, 1):
                small_all[index, which : which + 1, 0:gain_owned] = head_gains[
                    which : which + 1, index * gain_owned : (index + 1) * gain_owned
                ]

        @pl.loop(1, devices)
        def _(ahead):
            small_copy(ahead).start()

        hidden = SquareScatter(
            sizes, shared, far_in, turn_out, turn_in, hidden_send, hidden_recv, tokens
        )
        hidden.start(1)
        hidden.start(0)
        total[0:b_rows, :] = arrived[z].astype(full)

        def add_last(slot):
            total[0:b_rows, :] += back_arrived(slot)

        end_line(back_line, add_last)
        back_store = pltpu.make_async_copy(total.at[pl.ds(0, b_rows)], back_out, stage_sem.at[0])
        back_store.start()
        back_store.wait()
        if n > 2:
            mix_line(0, n - 2)
        for ahead in range(1, n_exp):
            front_pair(ahead).wait_recv()
        for target in range(n):
            summed = fronts[target, :, :, k].astype(full)
            for ahead in range(1, n_exp):
                summed = summed + front_pairs[ahead - 1, target].astype(full)
            fronts[target, :, :, k] = summed.astype(low)
        along_line(front_line, add_front, n - 1)
        for distance in range(n - 3, 0, -1):
            mix_line(0, distance)
        start_total(0)
        mix_end(0)
        front_own = pltpu.make_async_copy(
            fronts.at[z, c // (n_ctx // 2), lax.rem(c, n_ctx // 2), k], front_out.at[c],
            stage_sem.at[0],
        )
        for piece in range(1, pieces):
            if piece == pieces - 1:
                all_small().wait_recv()
                small_out[...] = small_all[here] + jnp.sum(small_in[1:devices], axis=0)
            mix_in(piece)
            mix_line(piece, n - 1)
            start_total(piece)
            for distance in range(n - 2, 0, -1):
                if piece == 1:
                    along_line(front_line, add_front, distance)
                mix_line(piece, distance)
                if piece == pieces - 1 and distance == max(1, n - 2):
                    hidden.turn()
            if piece == 1:
                end_line(front_line, lambda slot: add_front(z, slot))
                for ahead in range(1, n_ctx):
                    front_across(ahead).start()
                front_own.start()
            mix_end(piece)
        front_own.wait()
        staged[...] = total[...].astype(low)
        output_store = pltpu.make_async_copy(staged, output_ref, stage_sem.at[0])
        output_store.start()

        load_part(middle_ref, 0).start()
        hidden.finish(total)
        x = token_ref[...].astype(full)
        inverse = lax.rsqrt(jnp.mean(x * x, axis=-1, keepdims=True) + eps_norm)
        normed = x * inverse
        grad = total[...]
        scaled = grad * gain_ref[...]
        total[...] = inverse * (scaled - normed * jnp.mean(scaled * normed, axis=-1, keepdims=True))
        output_store.wait()
        for piece in range(pieces):
            if piece + 1 < pieces:
                load_part(middle_ref, piece + 1).start()
            load_part(middle_ref, piece).wait()
            columns = pl.ds(piece * part, part)
            staged[:, columns] = (total[:, columns] + loaded[piece % 2]).astype(low)
        tokens_store = pltpu.make_async_copy(staged, tokens_grad_ref, stage_sem.at[0])
        tokens_store.start()
        for ahead in range(1, n_ctx):
            front_across(ahead).wait()
        tokens_store.wait()

        all_small().wait_send()
        hidden.close()
        for ahead in range(1, n_exp):
            front_pair(ahead).wait_send()
        for piece in range(pieces):
            for ahead in range(1, number):
                plane_copy(piece, ahead).wait_send()
            close_line(line_of(piece))
        close_line(back_line)
        close_line(front_line)


def finish(
    bounds, turned, grad, raw, scales, cosine, sine, hidden, weight, back, rows_back, pick, result,
    middle_grad, tokens, gain, small, heads, kv_heads, head, sizes, collective, part=512,
):
    n, n_ctx, n_exp = sizes["dp"], sizes["ctx"], sizes["exp"]
    devices, number = n * n_ctx * n_exp, n_ctx * n_exp
    low, full = jnp.bfloat16, jnp.float32
    rows, columns = raw.shape
    count, width = tokens.shape
    b_rows = back.shape[2]
    f_rows = width // devices
    chunk = width // (2 * n)
    group = heads // kv_heads
    back_rows = rows_back.shape[1]
    s_rows, s_cols = small.shape[1:]
    pieces = width // part
    first_chunk = heads + 2 * kv_heads
    within = lambda h: jnp.minimum(h, heads - 1)
    now = lambda h: jnp.clip(h - first_chunk, 0, 2 * n - 1)
    once = pl.Buffered(buffer_count=1)
    whole = lambda shape: pl.BlockSpec(shape, lambda h: (0,) * len(shape), pipeline_mode=once)
    anywhere = pl.BlockSpec(memory_space=pl.ANY)
    vmem = lambda *shape: pltpu.VMEM(shape, low)
    wide = lambda *shape: pltpu.VMEM(shape, full)
    dma = lambda *shape: pltpu.SemaphoreType.DMA(shape)
    half = n_ctx // 2
    return pl.pallas_call(
        functools.partial(
            finish_kernel, block=count, heads=heads, group=group, score_scale=head ** (-0.5),
            sizes=sizes, part=part, chunk=chunk,
        ),
        grid=(first_chunk + 2 * n + 1,),
        in_specs=[
            pl.BlockSpec(memory_space=pltpu.SMEM),
            pl.BlockSpec((rows, head), lambda h: (0, within(h))),
            pl.BlockSpec((rows, head), lambda h: (0, heads + within(h) // group)),
            pl.BlockSpec((rows, head), lambda h: (0, heads + kv_heads + within(h) // group)),
            pl.BlockSpec((rows, head), lambda h: (0, within(h))),
            pl.BlockSpec((rows, head), lambda h: (0, jnp.minimum(h, heads + kv_heads - 1))),
            whole(scales.shape),
            whole(cosine.shape),
            whole(sine.shape),
            pl.BlockSpec((rows, chunk), lambda h: (0, now(h))),
            pl.BlockSpec((chunk, weight.shape[1]), lambda h: (now(h), 0)),
            anywhere,
            anywhere,
            whole(pick.shape),
            anywhere,
            anywhere,
            whole(tokens.shape),
            whole(gain.shape),
            anywhere,
        ],
        out_specs=[anywhere] * 4
        + [pl.BlockSpec((s_rows, s_cols), lambda h: (0, 0)), anywhere, anywhere],
        out_shape=[
            jax.ShapeDtypeStruct((count, width), low),
            jax.ShapeDtypeStruct((n_ctx, f_rows, columns), low),
            jax.ShapeDtypeStruct((count, width), low),
            jax.ShapeDtypeStruct((b_rows, width), full),
            jax.ShapeDtypeStruct((s_rows, s_cols), full),
            jax.ShapeDtypeStruct(rows_back.shape, low),
            jax.ShapeDtypeStruct((n + 1, b_rows, width), low),
        ],
        scratch_shapes=[
            wide(kv_heads, rows, head),
            wide(kv_heads, rows, head),
            vmem(rows, columns),
            wide(2, head),
            vmem(n_ctx, max(count, n_exp * b_rows), width),
            vmem(n_ctx, b_rows, width),
            vmem(b_rows, width),
            vmem(n, 2, half, n_exp, f_rows, columns),
            vmem(n_exp - 1, n, 2, half, f_rows, columns),
            vmem(n + 1, 2, half, f_rows, columns),
            vmem(number, back_rows, part),
            vmem(n, count, width),
            vmem(n + 1, count, width),
            *square_scratch(count, width),
            wide(count, width),
            wide(2, count, part),
            vmem(count, width),
            wide(devices, s_rows, s_cols),
            wide(devices, s_rows, s_cols),
            dma(2), dma(3), dma(2), dma(n_exp), dma(n_exp), dma(n_ctx), dma(n_ctx), dma(n),
            dma(n + 1), dma(n_exp), dma(n_exp), dma(n), dma(n + 1), dma(n_ctx), dma(n_ctx),
            dma(pieces, number), dma(pieces, number), dma(pieces), dma(pieces, n),
            dma(pieces, n + 1), dma(1), dma(1),
        ],
        compiler_params=pltpu.CompilerParams(
            collective_id=collective, has_side_effects=True, vmem_limit_bytes=VMEM
        ),
    )(
        bounds, turned, turned, turned, grad, raw, scales, cosine, sine, hidden, weight, back,
        rows_back, pick, result, middle_grad, tokens, gain, small,
    )


def shards(
    tokens,
    attention_gain,
    query_weight,
    key_weight,
    value_weight,
    query_gain,
    key_gain,
    output_weight,
    mixture_gain,
    router_weight,
    gate_weight,
    up_weight,
    down_weight,
    routes,
    bounds,
    cotangent,
):
    low, full = jnp.bfloat16, jnp.float32
    n_dp, n_ctx, n_exp = (lax.axis_size(a) for a in ALL)
    devices = n_dp * n_ctx * n_exp
    tok_count, width = tokens.shape[1], tokens.shape[2]
    seq_len = tok_count * n_ctx
    head_dim = query_gain.shape[0] * devices
    rows = query_weight.shape[0]
    heads = query_weight.shape[1] // head_dim
    kv_heads = key_weight.shape[1] // head_dim
    kv_here = kv_heads // n_ctx
    group_size = heads // kv_heads
    q_cols, kv_cols = heads * head_dim // n_ctx, kv_here * head_dim
    experts = router_weight.shape[1]
    topk = routes.shape[2]
    base_rows = tok_count * topk // experts
    capacity = base_rows + max(1, base_rows // 8)
    plane = experts // n_dp
    local_experts = gate_weight.shape[0]
    score_scale = head_dim ** (-0.5)
    dp_index = lax.axis_index("dp")

    gain_len = query_gain.shape[0]
    small = jnp.concatenate(
        [
            router_weight,
            attention_gain[:, None],
            mixture_gain[:, None],
            jnp.pad(jnp.concatenate([query_gain, key_gain]), (0, rows - 2 * gain_len))[:, None],
        ],
        axis=1,
    ).astype(low)
    small = jnp.pad(small, ((0, 0), (0, -small.shape[1] % 128)))
    extra = small.shape[1]

    def by_ctx(weight):
        return weight.astype(low).reshape(rows, n_ctx, -1).transpose(1, 0, 2)

    front = jnp.concatenate(
        [
            by_ctx(query_weight),
            by_ctx(key_weight),
            by_ctx(value_weight),
            jnp.broadcast_to(small[None], (n_ctx, rows, extra)),
        ],
        axis=2,
    )
    sizes = {"dp": n_dp, "ctx": n_ctx, "exp": n_exp}
    heads_here = heads // n_ctx
    cosine, sine = rope_tables(jnp.arange(seq_len, dtype=jnp.int32), head_dim)
    half = head_dim // 2
    sine = jnp.concatenate([-sine[:, :half], sine[:, half:]], axis=1)
    (
        front, output_part, column_routes, hidden, raw, turned, attended_low, gains, scales
    ) = gather(
        tokens[0], front, output_weight.astype(low), routes[0].T, cosine, sine, bounds, gain_len,
        heads_here, kv_here, experts, sizes, 3,
    )
    front = front.reshape(width, -1)
    output_part = output_part.reshape(q_cols, width)
    first_gain, second_gain = gains[0:1], gains[1:2]

    lanes = -(-experts // 128) * 128
    after = q_cols + 2 * kv_cols
    router_wide = front[:, after : after + lanes]
    own_chosen = jnp.any(
        routes[0][:, :, None] == jnp.arange(lanes, dtype=jnp.int32), axis=1
    ).astype(full)
    (
        grad_rows, expert_in, _, middle, own_gates, active, gate_grad, up_grad, row_grads,
        scaled_out, dot_rows, pick,
    ) = dispatch(
        attended_low, output_part, tokens[0], second_gain, router_wide, own_chosen,
        cotangent[0], column_routes, gate_weight, up_weight, down_weight, experts, capacity, sizes,
        1,
    )
    branch_low, middle_grad, second_gain_grad, router_grad, gate_w_grad, up_w_grad, down_grad = combine(
        row_grads, dot_rows, pick, middle, cotangent[0], second_gain, own_gates, router_wide,
        expert_in, grad_rows, active, gate_grad, up_grad, experts, sizes, 2,
    )
    gate_w_grad, up_w_grad, down_grad = gate_w_grad[None], up_w_grad[None], down_grad[None]
    router_grad = router_grad[:experts].T
    branch_low = branch_low.reshape(seq_len, width)
    output_w_grad = jnp.einsum("ti,td->id", attended_low, branch_low, preferred_element_type=full)
    attended_grad = jnp.einsum("td,id->ti", branch_low, output_part, preferred_element_type=full)
    rest = jnp.concatenate(
        [second_gain_grad.reshape(devices, -1), router_grad.reshape(devices, -1)], axis=1
    )
    columns = -(-rest.shape[1] // (5 * 128)) * 128
    rest = jnp.pad(rest, ((0, 0), (0, 5 * columns - rest.shape[1]))).reshape(devices, 5, columns)
    small = jnp.pad(rest, ((0, 0), (3, 0), (0, 0)))
    tokens_grad, front_grad, output, output_share, small, _, _ = finish(
        bounds, turned, attended_grad.astype(low), raw, scales, cosine, sine, hidden, front,
        output_w_grad.astype(low).reshape(n_ctx, n_exp, -1, width), scaled_out, pick, middle,
        middle_grad, tokens[0], first_gain, small, heads_here, kv_here, head_dim, sizes, 4,
        part=512 if n_ctx * n_exp <= 8 else 256,
    )
    tokens_grad = tokens_grad[None]
    output = output[None]
    front_grad = front_grad.astype(full)
    query_share = front_grad[:, :, :q_cols].transpose(1, 0, 2).reshape(rows, -1)
    key_share = front_grad[:, :, q_cols : q_cols + kv_cols].transpose(1, 0, 2).reshape(rows, -1)
    value_share = front_grad[:, :, q_cols + kv_cols :].transpose(1, 0, 2).reshape(rows, -1)
    first_share = sum(
        jnp.sum(weight.astype(low).astype(full) * grad, axis=1)
        for weight, grad in (
            (query_weight, query_share), (key_weight, key_share), (value_weight, value_share)
        )
    ) / attention_gain.astype(low).astype(full)
    query_gain_share = small[0, :gain_len]
    key_gain_share = small[1, :gain_len]
    rest = small[3:].reshape(-1)
    second_share = rest[:rows]
    router_share = rest[rows : rows + rows * experts].reshape(rows, experts)
    return (
        output,
        tokens_grad,
        first_share,
        query_share,
        key_share,
        value_share,
        query_gain_share,
        key_gain_share,
        output_share,
        second_share,
        router_share,
        gate_w_grad,
        up_w_grad,
        down_grad,
    )


def solution(mesh):
    rows = P(ALL)
    sequences = P(("dp", "exp"), "ctx")
    in_specs = (sequences,) + (rows,) * 12 + (sequences, P(("dp", "exp")), sequences)
    out_specs = (sequences,) * 2 + (rows,) * 12
    return jax.shard_map(shards, mesh=mesh, in_specs=in_specs, out_specs=out_specs, check_vma=False)
```
